32 devices in a mesh: dp: 4 (over z), fsdp: 8 (over y, x, core).
Axes of the slice: x: 2, y: 2, z: 4, core: 2. Of those that a mesh axis runs over, the one named last changes fastest.
Arguments:
- layer_input: bfloat16 [32, 472, 768], P(('dp', 'fsdp')), may hold values from -6 to 6
- mask_index: int32 [32, 232], P(('dp', 'fsdp')), may hold values from 0 to 471, as said below
- distract: int32 [32, 232, 100], P(('dp', 'fsdp')), may hold values from 0 to 231, as said below
- code_choice: int32 [32, 232, 2], P(('dp', 'fsdp')), may hold values from 0 to 319
- params: float32 [7421952], P(('dp', 'fsdp')), may hold values from -4 to 4
- moment_one: float32 [7421952], P(('dp', 'fsdp')), may hold values from -5.9604645e-07 to 5.9604645e-07
- moment_two: float32 [7421952], P(('dp', 'fsdp')), may hold values from 2.748603e-15 to 1.0994412e-14
- vectors: float32 [9728], replicated, may hold values from -1 to 3
- vector_one: float32 [9728], replicated, may hold values from -2.3841858e-06 to 2.3841858e-06
- vector_two: float32 [9728], replicated, may hold values from 4.3923754e-14 to 1.7515607e-13
Outputs:
- total_loss: float32 [], replicated
- grad_norm: float32 [], replicated
- layer_output: bfloat16 [32, 472, 768], P(('dp', 'fsdp'))
- input_grad: float32 [32, 472, 768], P(('dp', 'fsdp'))
- refreshed_weights: float32 [7421952], P(('dp', 'fsdp'))
- params_bfloat_copy: bfloat16 [7421952], P(('dp', 'fsdp'))
- new_moment_one: float32 [7421952], P(('dp', 'fsdp'))
- new_moment_two: float32 [7421952], P(('dp', 'fsdp'))
- new_vectors: float32 [9728], replicated
- new_vector_one: float32 [9728], replicated
- new_vector_two: float32 [9728], replicated
The draws below stay inside these ranges and needn't reach their ends.
Inputs may be any that keep to these rules, and one draw needn't show every extreme that they name: `mask_index`: each utterance's 232 positions are distinct and increasing. `distract`: for each masked frame, 100 distinct indices of other masked frames of the same utterance, never its own.
All inputs are finite; a program needn't handle non-finite values.
Results may differ from the reference program's by a relative error of at most 0.014.
The reference program's roundings to bfloat16 on the way count: a program that leaves them out, or rounds other values in their place, can miss the bound.
Values may be sent and summed in bfloat16 or wider, within the bound.
A program may use at most 192 MiB of HBM per device.

```python
import math
import jax
import jax.numpy as jnp
from jax import lax

D = 768
H = 12
HD = 64
FF = 3072
FINAL = 256
G = 2
V = 320
CD = 128
NEGS = 100
LEN = 472
MASKED = 232
STEP = 10
UTTS = 32
PFLAT = 7421952
NVEC = 9728


def draw_params(key, part):
    key = jax.random.fold_in(key, 11)
    mask_positions = jnp.arange(PFLAT)
    counts = [3 * D * D, D * D, D * FF, FF * D, D * FINAL, G * CD * V, G * CD * FINAL]
    factors = [1.5 / D ** 0.5, 6.0 / D ** 0.5, 1.0 / D ** 0.5, 1.0 / FF ** 0.5, 1.0 / D ** 0.5, 1.0, 1.0 / (G * CD) ** 0.5]
    scale_all = jnp.zeros((PFLAT,), jnp.float32)
    offset = 0
    for count_one, factor in zip(counts, factors):
        inside = (mask_positions >= offset) & (mask_positions < offset + count_one)
        scale_all = jnp.where(inside, factor, scale_all)
        offset = offset + count_one
    sample = jnp.clip(jax.random.normal(key, (PFLAT,), jnp.float32), -4.0, 4.0)
    return sample * scale_all


def draw_vectors(key, part):
    key = jax.random.fold_in(key, 12)
    first_key, second_key, third_key = jax.random.split(key, 3)
    biases = 0.1 * jnp.clip(jax.random.normal(first_key, (NVEC,), jnp.float32), -4.0, 4.0)
    ramp = jnp.arange(D).astype(jnp.float32) / (D - 1)
    bottom, height = (0.6, 1.2)
    gain_first = (bottom + height * ramp) * (1.0 + 0.1 * jax.random.uniform(second_key, (D,), jnp.float32, -1.0, 1.0))
    gain_second = (bottom + height * ramp) * (1.0 + 0.1 * jax.random.uniform(third_key, (D,), jnp.float32, -1.0, 1.0))
    return jnp.concatenate([biases[:3 * D], gain_first, biases[4 * D:6 * D + FF], gain_second, biases[7 * D + FF:]])


def draw_mask_index(key, part):
    key = jax.random.fold_in(key, 13)
    ranking = jax.random.randint(key, (UTTS, LEN), 0, 1 << 20) * 1024 + jnp.arange(LEN, dtype=jnp.int32)
    order = jnp.argsort(ranking, axis=1)[:, :MASKED]
    return jnp.sort(order, axis=1).astype(jnp.int32)


def draw_distract(key, part):
    key = jax.random.fold_in(key, 14)
    ranking = jax.random.randint(key, (UTTS, MASKED, MASKED - 1), 0, 1 << 20) * 256 + jnp.arange(MASKED - 1, dtype=jnp.int32)
    picked = jnp.argsort(ranking, axis=2)[:, :, :NEGS].astype(jnp.int32)
    own = jnp.arange(MASKED, dtype=jnp.int32)[None, :, None]
    return (picked + (picked >= own).astype(jnp.int32)).astype(jnp.int32)


def with_ends(drawn, own_key, smallest, high):
    longest = drawn.shape.index(max(drawn.shape))
    spots = []
    for shift in (0, 1):
        where = [jax.random.randint(jax.random.fold_in(own_key, axis), (), 0, length) for axis, length in enumerate(drawn.shape)]
        where[longest] = (where[longest] + shift) % drawn.shape[longest]
        spots.append(tuple(where))
    return drawn.at[spots[0]].set(smallest).at[spots[1]].set(high)


def steps_of(key, shape, cuts, low, top_value):
    gain = 1.0
    for position, parts in cuts:
        heights = jax.random.uniform(jax.random.fold_in(jax.random.fold_in(key, 6), position), (parts,), jnp.float32, low / len(cuts), top_value / len(cuts))
        gain = gain * jnp.repeat(jnp.exp(heights), shape[position] // parts).reshape((-1,) + (1,) * (len(shape) - 1 - position))
    return gain


def centred(key, shape, spread, bound, cuts=(), kind=jnp.bfloat16):
    result = spread * jax.random.normal(key, shape, jnp.float32)
    if cuts:
        result = result * steps_of(key, shape, cuts, -0.22, 0.18)
    return jnp.clip(result, -bound, bound).astype(kind)


def setup_inputs(seed: int = 0) -> dict:
    seeds = jax.random.split(jax.random.key(seed), 11)
    layer_input = centred(seeds[0], (UTTS, LEN, D), 1.0, 6.0, ((0, 32),))
    mask_index = draw_mask_index(jax.random.fold_in(seeds[10], 71), 0)
    distract = draw_distract(jax.random.fold_in(seeds[10], 71), 0)
    code_choice = with_ends(jax.random.randint(seeds[3], (UTTS, MASKED, G), 0, V), jax.random.fold_in(seeds[3], 1), 0, V - 1).astype(jnp.int32)
    params = draw_params(jax.random.fold_in(seeds[10], 71), 0)
    moment_one = centred(seeds[5], (PFLAT,), (0.000111 / PFLAT ** 0.5), 5.960464477539062e-07, ((0, 32),), jnp.float32)
    moment_two = jnp.clip(jnp.exp(math.log(1.0994412269428513e-14) - 1.3862944 * jax.random.uniform(seeds[6], (PFLAT,), jnp.float32) ** steps_of(seeds[6], (PFLAT,), ((0, 32),), -0.2, 0.2)), 2.748603067357128e-15, 1.0994412269428513e-14)
    vectors = draw_vectors(jax.random.fold_in(seeds[10], 71), 0)
    vector_one = centred(seeds[8], (NVEC,), (0.000444 / PFLAT ** 0.5), 2.384185791015625e-06, (), jnp.float32)
    vector_two = jnp.clip(jnp.exp(jax.random.uniform(seeds[9], (NVEC,), jnp.float32, math.log(4.3923754065346154e-14), math.log(1.7515607291396923e-13))), 4.3923754065346154e-14, 1.7515607291396923e-13)
    return {"layer_input": layer_input, "mask_index": mask_index, "distract": distract, "code_choice": code_choice, "params": params, "moment_one": moment_one, "moment_two": moment_two, "vectors": vectors, "vector_one": vector_one, "vector_two": vector_two}


@jax.custom_vjp
def low(v):
    return lax.optimization_barrier(v.astype(jnp.bfloat16)).astype(jnp.float32)

@jax.custom_vjp
def low_back(v):
    return v

def low_keep(v):
    return (low(v), None)

def low_pass(kept, grad):
    return (grad,)

def back_keep(v):
    return (v, None)

def back_low(kept, grad):
    return (low(grad),)
low.defvjp(low_keep, low_pass)
low_back.defvjp(back_keep, back_low)
eps_norm = 1e-05
eps_cos = 1e-06
softness_divisor = 0.1
beta_one = 0.9
beta_two = 0.98
adam_eps = 1e-08
decay_rate = 0.01
rate_matrix = 0.03
rate_vector = 0.2
clip_level = 0.001
group_utts = 8

def unpack(flat_values):
    shapes = [(D, 3 * D), (D, D), (D, FF), (FF, D), (D, FINAL), (G * CD, V), (G * CD, FINAL)]
    pieces = []
    offset = 0
    for height, width in shapes:
        pieces.append(flat_values[offset:offset + height * width].reshape(height, width))
        offset = offset + height * width
    return pieces

def split_vectors(vector_all):
    lengths = [D, D, D, D, D, FF, D, D, D, FINAL, FINAL]
    pieces = []
    offset = 0
    for length in lengths:
        pieces.append(vector_all[offset:offset + length])
        offset = offset + length
    return pieces

def matmul(left, right):
    return jnp.einsum('...i,ij->...j', left, right, precision=lax.Precision.HIGHEST)

def layer_norm(values, scale_gain, shift_bias):
    centered = values - lax.optimization_barrier(jnp.mean(values, axis=-1, keepdims=True))
    variance = lax.optimization_barrier(jnp.mean(centered * centered, axis=-1, keepdims=True))
    return centered * lax.rsqrt(variance + eps_norm) * scale_gain + shift_bias

def pick_rows(source, index_rows):
    return source[index_rows]

def contrast_loss(chosen, targets, distract):
    encoder_unit_heading = chosen * lax.rsqrt(lax.optimization_barrier(jnp.sum(chosen * chosen, axis=-1, keepdims=True)) + eps_cos)
    quantized_unit_heading = targets * lax.rsqrt(lax.optimization_barrier(jnp.sum(targets * targets, axis=-1, keepdims=True)) + eps_cos)
    angular_agreement = jnp.einsum('rby,roy->rbo', encoder_unit_heading, quantized_unit_heading, precision=lax.Precision.HIGHEST) / softness_divisor
    positive = jnp.diagonal(angular_agreement, axis1=1, axis2=2)
    negative = jnp.take_along_axis(angular_agreement, distract, axis=2)
    logits_all = jnp.concatenate([positive[..., None], negative], axis=-1)
    return jnp.sum(jax.nn.logsumexp(logits_all, axis=-1) - positive)

def adamw_update(master, first_moment, second, gradient, step_rate):
    first_new = beta_one * first_moment + (1.0 - beta_one) * gradient
    second_new = beta_two * second + (1.0 - beta_two) * gradient * gradient
    first_hat = first_new / (1.0 - beta_one ** STEP)
    second_hat = second_new / (1.0 - beta_two ** STEP)
    master_new = master * (1.0 - step_rate * decay_rate) - step_rate * first_hat / (jnp.sqrt(second_hat) + adam_eps)
    return (master_new, first_new, second_new)

def group_forward(inputs, mask_index, distract, code_choice, matrices, vector_list):
    qkv_weight, out_weight, up_weight, down_weight, proj_weight, codebook, code_weight = matrices
    bias_query, bias_value, bias_out, gain_one, shift_one, bias_up, bias_down, gain_two, shift_two, bias_proj, bias_code = vector_list
    count_utts = inputs.shape[0]
    projected = matmul(inputs, qkv_weight)
    queries = low(low_back(projected[..., :D] + bias_query)).reshape(count_utts, LEN, H, HD)
    key_rows = low(low_back(projected[..., D:2 * D])).reshape(count_utts, LEN, H, HD)
    value_rows = low(low_back(projected[..., 2 * D:] + bias_value)).reshape(count_utts, LEN, H, HD)
    scores = low_back(jnp.einsum('blhe,bmhe->bhlm', queries, key_rows, precision=lax.Precision.HIGHEST) * 0.125)
    probs_low = low(jax.nn.softmax(scores, axis=-1))
    attended = jnp.einsum('bhlm,bmhe->blhe', probs_low, value_rows, precision=lax.Precision.HIGHEST)
    attended = low(low_back(attended.reshape(count_utts, LEN, D)))
    branch = low_back(matmul(attended, out_weight) + bias_out)
    normed = layer_norm(inputs + branch, gain_one, shift_one)
    hidden = low_back(matmul(low(normed), up_weight) + bias_up)
    active = low(jax.nn.gelu(hidden, approximate=False))
    second = low_back(matmul(active, down_weight) + bias_down)
    output = low(layer_norm(normed + second, gain_two, shift_two))
    context = low_back(matmul(output, proj_weight) + bias_proj)
    choose = (code_choice[..., None] == jnp.arange(V, dtype=jnp.int32)).astype(jnp.float32)
    code_vectors = jnp.einsum('bmgv,gcv->bmgc', choose, codebook.reshape(G, CD, V), precision=lax.Precision.HIGHEST)
    code_vectors = code_vectors.reshape(count_utts, MASKED, G * CD)
    targets = low_back(matmul(code_vectors, code_weight) + bias_code)
    chosen = jax.vmap(pick_rows)(context, mask_index)
    return (contrast_loss(chosen, targets, distract), output)

def reference(layer_input, mask_index, distract, code_choice, params, moment_one, moment_two, vectors, vector_one, vector_two):
    total_masked = layer_input.shape[0] * MASKED
    frames_wide = layer_input.astype(jnp.float32)
    weights_f = params.astype(jnp.bfloat16).astype(jnp.float32)

    def forward(inputs_all, flat_values, vector_all):
        matrices = unpack(flat_values)
        vector_list = split_vectors(vector_all)

        def step_group(carry, group_data):
            group_loss, output = jax.checkpoint(group_forward)(group_data[0], group_data[1], group_data[2], group_data[3], matrices, vector_list)
            return (carry + group_loss, output)
        grouped = tuple((source_array.reshape((-1, group_utts) + source_array.shape[1:]) for source_array in (inputs_all, mask_index, distract, code_choice)))
        loss_sum, outputs = lax.scan(step_group, jnp.zeros((), jnp.float32), grouped)
        total = loss_sum / total_masked
        return (total, outputs.reshape(inputs_all.shape))
    total, pullback, outputs = jax.vjp(forward, frames_wide, weights_f, vectors, has_aux=True)
    input_grad, flat_grad, vector_gradient = pullback(jnp.ones((), jnp.float32))
    grad_norm = jnp.sqrt(jnp.sum(flat_grad * flat_grad) + jnp.sum(vector_gradient * vector_gradient))
    factor = jnp.minimum(1.0, clip_level / (grad_norm + 1e-06))
    refreshed_weights, new_one, new_two = adamw_update(params, moment_one, moment_two, flat_grad * factor, rate_matrix)
    new_vectors, new_vector_first, new_vector_second = adamw_update(vectors, vector_one, vector_two, vector_gradient * factor, rate_vector)
    return (total, grad_norm, outputs.astype(jnp.bfloat16), input_grad, refreshed_weights, refreshed_weights.astype(jnp.bfloat16), new_one, new_two, new_vectors, new_vector_first, new_vector_second)
```

```python
from functools import partial

import jax
import jax.numpy as jnp
from jax import lax
from jax.experimental import pallas as pl
from jax.experimental.pallas import tpu as pltpu
from jax.sharding import PartitionSpec as P

MESH = pl.DeviceIdType.MESH
NROW = 9664
GROW = NROW + 256

D = 768
H = 12
HD = 64
FF = 3072
FINAL = 256
G = 2
V = 320
CD = 128
LEN = 472
MASKED = 232
STEP = 10


eps_norm = 1e-05
eps_cos = 1e-06
softness_divisor = 0.1
beta_one = 0.9
beta_two = 0.98
adam_eps = 1e-08
decay_rate = 0.01
rate_matrix = 0.03
rate_vector = 0.2
clip_level = 0.001


def unpack(flat_values):
    shapes = [(D, 3 * D), (D, D), (D, FF), (FF, D), (D, FINAL), (G * CD, V), (G * CD, FINAL)]
    pieces = []
    offset = 0
    for height, width in shapes:
        pieces.append(flat_values[offset : offset + height * width].reshape(height, width))
        offset = offset + height * width
    return pieces


def split_vectors(vector_all):
    lengths = [D, D, D, D, D, FF, D, D, D, FINAL, FINAL]
    pieces = []
    offset = 0
    for length in lengths:
        pieces.append(vector_all[offset : offset + length])
        offset = offset + length
    return pieces


def layer_norm(values, scale_gain, shift_bias):
    centered = values - jnp.mean(values, axis=-1, keepdims=True)
    variance = jnp.mean(centered * centered, axis=-1, keepdims=True)
    return centered * lax.rsqrt(variance + eps_norm) * scale_gain + shift_bias


def contrast(chosen, targets, distract, weight):
    hi = dict(precision=lax.Precision.HIGHEST)
    frames = jnp.arange(MASKED, dtype=jnp.int32)
    allowed = jnp.any(distract[:, :, None] == frames, axis=1) | (frames[:, None] == frames)

    def agreement(chosen, targets):
        left = chosen * lax.rsqrt(jnp.sum(chosen * chosen, axis=-1, keepdims=True) + eps_cos)
        right = targets * lax.rsqrt(jnp.sum(targets * targets, axis=-1, keepdims=True) + eps_cos)
        return jnp.einsum("by,oy->bo", left, right, **hi) / softness_divisor

    similar, back = jax.vjp(agreement, chosen, targets)
    same = frames[:, None] == frames
    positive = jnp.sum(jnp.where(same, similar, 0.0), axis=1)
    top = jnp.max(jnp.where(allowed, similar, -jnp.inf), axis=1)
    parts = jnp.where(allowed, jnp.exp(similar - top[:, None]), 0.0)
    total = jnp.sum(parts, axis=1)
    loss = jnp.sum(top + jnp.log(total) - positive)
    d_similar = weight * (parts / total[:, None] - same.astype(jnp.float32))
    return (loss,) + back(d_similar)


def adamw_update(master, first_moment, second, gradient, step_rate):
    first_new = beta_one * first_moment + (1.0 - beta_one) * gradient
    second_new = beta_two * second + (1.0 - beta_two) * gradient * gradient
    first_hat = first_new / (1.0 - beta_one**STEP)
    second_hat = second_new / (1.0 - beta_two**STEP)
    master_new = master * (1.0 - step_rate * decay_rate) - step_rate * first_hat / (
        jnp.sqrt(second_hat) + adam_eps
    )
    return (master_new, first_new, second_new)


def ag_kernel(p_ref, g_ref, raw, land, sem_raw, R, D, SU, SZ, SV, SD):
    bf16 = jnp.bfloat16
    z = lax.axis_index("dp"); f = lax.axis_index("fsdp")
    c = f % 2; k = f // 2; x = k % 2; y = k // 2
    fc = f + 1 - 2 * c
    fx = f + 2 - 4 * x
    fy = f + 4 - 8 * y
    uf = fx * (1 - c) + fy * c
    vf = fy * (1 - c) + fx * c
    ku = uf // 2; kv = vf // 2; kuv = 3 - k
    Z = 4
    bar = pltpu.get_barrier_semaphore()
    for t in ((z, fc), (z, fx), (z, fy)):
        pl.semaphore_signal(bar, inc=1, device_id=t, device_id_type=MESH)
    @pl.when(z > 0)
    def _(): pl.semaphore_signal(bar, inc=1, device_id=(z - 1, f), device_id_type=MESH)
    @pl.when(z < Z - 1)
    def _(): pl.semaphore_signal(bar, inc=1, device_id=(z + 1, f), device_id_type=MESH)
    pl.semaphore_wait(bar, 3 + (z + Z - 1) // Z + (2 * Z - 2 - z) // Z)

    rawcopy = pltpu.make_async_remote_copy(src_ref=p_ref.at[pl.ds(0, 1812)], dst_ref=land.at[pl.ds(0, 1812)], send_sem=sem_raw.at[0], recv_sem=sem_raw.at[1],
                                           device_id=(z, fc), device_id_type=MESH)
    rawcopy.start()
    @pl.when(c == 0)
    def _(): raw[96:96 + 1812, :] = p_ref[...]
    @pl.when(c == 1)
    def _(): raw[96 + 1812:96 + 3624, :] = p_ref[...]
    rawcopy.wait()
    @pl.when(c == 1)
    def _(): raw[96:96 + 1812, :] = land[0:1812]
    @pl.when(c == 0)
    def _(): raw[96 + 1812:96 + 3624, :] = land[0:1812]
    own = 2416 * z + 608 * k
    for j in range(6):
        g_ref[pl.ds(own, 592), 128*j:128*j+128] = raw[pl.ds(96 + 24 * k + j, 592, stride=6), :].astype(bf16)
        last = raw[pl.ds(96 + (592 + 4 * k) * 6 + j, 16, stride=6), :]
        first = raw[pl.ds(24 * k + j, 16, stride=6), :]
        row = lax.broadcasted_iota(jnp.int32, (16, 128), 0)
        g_ref[pl.ds(NROW + 16 * (4 * z + k), 16), 128*j:128*j+128] = jnp.where(row < 12 - 4 * k, last, first).astype(bf16)

    def spans(plane, kk, cc):
        m = pl.multiple_of(2416 * plane + 608 * kk + 304 * cc, 16)
        ms = 2416 * plane + 608 * kk
        side = NROW + 16 * (4 * plane + kk)
        e = pl.multiple_of((ms + 288) * (1 - cc) + side * cc, 16)
        return ((m, 288), (e, 16))
    def copies(plane, kk, cc, dev, ssem, rsem):
        return [pltpu.make_async_remote_copy(src_ref=g_ref.at[pl.ds(s, n)], dst_ref=g_ref.at[pl.ds(s, n)], send_sem=ssem.at[i], recv_sem=rsem.at[i], device_id=dev, device_id_type=MESH)
                for i, (s, n) in enumerate(spans(plane, kk, cc))]
    up = (z + 1, f); down = (z - 1, f)
    def send(plane, kk, dev, ssem):
        for cp in copies(plane, kk, c, dev, ssem, R.at[4 * plane + kk]): cp.start()
    def d2d(plane, kk):
        for cp in copies(plane, kk, c, (z, fc), SD.at[4 * plane + kk], D.at[4 * plane + kk]): cp.start()
    def recv(plane, kk):
        for cp in copies(plane, kk, c, (z, fc), SD.at[0], R.at[4 * plane + kk]): cp.wait_recv()
    def recvd(plane, kk):
        for cp in copies(plane, kk, 1 - c, (z, fc), SD.at[0], D.at[4 * plane + kk]): cp.wait_recv()
    def sent(plane, kk, ssem):
        for cp in copies(plane, kk, c, (z, fc), ssem, R.at[0]): cp.wait_send()

    send(z, k, (z, uf), SU)
    @pl.when(z < Z - 1)
    def _(): send(z, k, up, SZ.at[0, z, 0])
    @pl.when(z > 0)
    def _(): send(z, k, down, SZ.at[1, z, 0])
    send(z, k, (z, vf), SV.at[z, 0])
    recv(z, ku)
    @pl.when(z < Z - 1)
    def _(): send(z, ku, up, SZ.at[0, z, 1])
    @pl.when(z > 0)
    def _(): send(z, ku, down, SZ.at[1, z, 1])
    send(z, ku, (z, vf), SV.at[z, 1])
    d2d(z, ku)
    for s in range(1, Z + 1):
        if s < Z:
            for i, kk in ((0, k), (1, ku)):
                @pl.when(z - s >= 0)
                def _():
                    recv(z - s, kk)
                    @pl.when(z < Z - 1)
                    def _(): send(z - s, kk, up, SZ.at[0, z - s, i])
                    send(z - s, kk, (z, vf), SV.at[z - s, i])
                    d2d(z - s, kk)
                @pl.when(z + s < Z)
                def _():
                    recv(z + s, kk)
                    @pl.when(z > 0)
                    def _(): send(z + s, kk, down, SZ.at[1, z + s, i])
                    send(z + s, kk, (z, vf), SV.at[z + s, i])
                    d2d(z + s, kk)
        t = s - 1
        for kk in (kv, kuv):
            if t == 0:
                recv(z, kk); d2d(z, kk)
            else:
                @pl.when(z - t >= 0)
                def _(): recv(z - t, kk); d2d(z - t, kk)
                @pl.when(z + t < Z)
                def _(): recv(z + t, kk); d2d(z + t, kk)
    for plane in range(Z):
        for kk in (ku, kv, kuv):
            recvd(plane, kk)
        @pl.when(z != plane)
        def _(): recvd(plane, k)
    sent(z, k, SU)
    for plane in range(Z):
        for i, kk in ((0, k), (1, ku)):
            sent(plane, kk, SV.at[plane, i])
            @pl.when((z < Z - 1) & (plane <= z))
            def _(): sent(plane, kk, SZ.at[0, plane, i])
            @pl.when((z > 0) & (plane >= z))
            def _(): sent(plane, kk, SZ.at[1, plane, i])
        for kk in (ku, kv, kuv):
            sent(plane, kk, SD.at[4 * plane + kk])
        @pl.when(z != plane)
        def _(): sent(plane, k, SD.at[4 * plane + k])
    row = lax.broadcasted_iota(jnp.int32, (16, 768), 0)
    for plane in range(Z):
        for q, bound in ((0, 12), (1, 8), (2, 4)):
            a = g_ref[NROW + 16 * (4 * plane + q):NROW + 16 * (4 * plane + q) + 16, :].astype(jnp.float32)
            b = g_ref[NROW + 16 * (4 * plane + q + 1):NROW + 16 * (4 * plane + q + 1) + 16, :].astype(jnp.float32)
            at = 2416 * plane + 608 * q + 592
            g_ref[at:at + 16, :] = jnp.where(row < bound, a, b).astype(bf16)

def ag(params):
    DMA = pltpu.SemaphoreType.DMA
    return pl.pallas_call(ag_kernel,
        out_shape=jax.ShapeDtypeStruct((GROW, 768), jnp.bfloat16),
        in_specs=[pl.BlockSpec(memory_space=pltpu.VMEM)], out_specs=pl.BlockSpec(memory_space=pltpu.VMEM),
        scratch_shapes=[pltpu.VMEM((96 + 3624 + 96, 128), jnp.float32), pltpu.VMEM((1816, 128), jnp.float32), DMA((2,)),
                        DMA((16, 2)), DMA((16, 2)), DMA((2,)), DMA((2, 4, 2, 2)), DMA((4, 2, 2)), DMA((16, 2))],
        compiler_params=pltpu.CompilerParams(collective_id=0, has_side_effects=True, vmem_limit_bytes=60*2**20))(params.reshape(1812, 128))


HALF = 304

def place():
    z = lax.axis_index("dp"); f = lax.axis_index("fsdp")
    c = f % 2; k = f // 2; x = k % 2; y = k // 2
    fc = f + 1 - 2 * c
    fx = f + 2 - 4 * x
    fy = f + 4 - 8 * y
    uf = fx * (1 - c) + fy * c
    vf = fy * (1 - c) + fx * c
    return z, f, c, k, fc, fx, fy, uf, vf

def greet(z, f, fc, fx, fy, Z):
    bar = pltpu.get_barrier_semaphore()
    for t in ((z, fc), (z, fx), (z, fy)):
        pl.semaphore_signal(bar, inc=1, device_id=t, device_id_type=MESH)
    @pl.when(z > 0)
    def _(): pl.semaphore_signal(bar, inc=1, device_id=(z - 1, f), device_id_type=MESH)
    @pl.when(z < Z - 1)
    def _(): pl.semaphore_signal(bar, inc=1, device_id=(z + 1, f), device_id_type=MESH)
    pl.semaphore_wait(bar, 3 + (z + Z - 1) // Z + (2 * Z - 2 - z) // Z)

def rs_kernel(g_in, vec_in, out, vec_out, sq_out, g, LD, LV, LZ, LU, B, F, vec, vland, sq, sqland,
              s_in, SD, RD, SV, RV, SZ, RZ, SU, SX, SB, SQ):
    bf16 = jnp.bfloat16; f32 = jnp.float32
    z, f, c, k, fc, fx, fy, uf, vf = place()
    ku = uf // 2; kv = vf // 2; kuv = 3 - k
    Z = 4
    cp = pltpu.make_async_copy(g_in, g.at[pl.ds(0, NROW)], s_in)
    cp.start()
    greet(z, f, fc, fx, fy, Z)
    cp.wait()
    row = lax.broadcasted_iota(jnp.int32, (16, 768), 0)
    for plane in range(Z):
        b37, b75, b113 = [g[2416 * plane + 16 * b:2416 * plane + 16 * b + 16, :].astype(f32) for b in (37, 75, 113)]
        for q, v in enumerate((b37, jnp.where(row < 8, b75, b37), jnp.where(row < 4, b113, b75), b113)):
            at = NROW + 16 * (4 * plane + q)
            g[at:at + 16, :] = v.astype(bf16)

    def spans(plane, kk, cc):
        ms = 2416 * plane + 608 * kk
        m = pl.multiple_of(ms + 304 * cc, 16)
        side = NROW + 16 * (4 * plane + kk)
        e = pl.multiple_of((ms + 288) * (1 - cc) + side * cc, 16)
        return (m, e)
    def copies(plane, kk, cc, dst, dev, ssem, rsem):
        m, e = spans(plane, kk, cc)
        return [pltpu.make_async_remote_copy(src_ref=g.at[pl.ds(m, 288)], dst_ref=dst.at[pl.ds(0, 288)], send_sem=ssem.at[0], recv_sem=rsem.at[0], device_id=dev, device_id_type=MESH),
                pltpu.make_async_remote_copy(src_ref=g.at[pl.ds(e, 16)], dst_ref=dst.at[pl.ds(288, 16)], send_sem=ssem.at[1], recv_sem=rsem.at[1], device_id=dev, device_id_type=MESH)]
    def start(cs):
        for q in cs: q.start()
    def add(plane, kk, srcs, final=False):
        m, e = spans(plane, kk, c)
        def one(at, i):
            v = g[pl.ds(at, 16), :].astype(f32)
            for s in srcs:
                v = v + s[pl.ds(i, 16), :].astype(f32)
            if final:
                B[pl.ds(16 + i, 16), :] = v
            else:
                g[pl.ds(at, 16), :] = v.astype(bf16)
        def body(b, _):
            i = pl.multiple_of(16 * b, 16)
            one(pl.multiple_of(m + i, 16), i)
            return 0
        lax.fori_loop(0, 18, body, 0)
        one(e, 288)

    order = (3, 0, 2, 1)
    U = lambda plane, kk: 4 * plane + kk
    for plane in order:
        for kk in (kv, kuv):
            start(copies(plane, kk, 1 - c, LD.at[U(plane, kk)], (z, fc), SD.at[U(plane, kk)], RD.at[U(plane, kk)]))
    for plane in order:
        for kk in (k, ku):
            start(copies(plane, kk, 1 - c, LD.at[U(plane, kk)], (z, fc), SD.at[U(plane, kk)], RD.at[U(plane, kk)]))
    def wait_d(plane, kk):
        for q in copies(plane, kk, 1 - c, LD.at[U(plane, kk)], (z, fc), SD.at[U(plane, kk)], RD.at[U(plane, kk)]): q.wait_recv()
    def landv(plane, kk): return LV.at[U(plane, kk)]
    for plane in order:
        for kk in (kv, kuv):
            wait_d(plane, kk)
            add(plane, kk, [LD.at[U(plane, kk)]])
            start(copies(plane, kk, c, landv(plane, kk), (z, vf), SV.at[U(plane, kk)], RV.at[U(plane, kk)]))
    def zsend(plane, i, kk, up):
        return copies(plane, kk, c, LZ.at[up, U(plane, kk)], (z + (2 * up - 1), f), SZ.at[U(plane, kk)], RZ.at[up, U(plane, kk)])
    def zwait(plane, kk, up):
        for q in copies(plane, kk, c, LZ.at[up, U(plane, kk)], (z, fc), SZ.at[U(plane, kk)], RZ.at[up, U(plane, kk)]): q.wait_recv()
    for plane in order:
        for i, kk in ((0, k), (1, ku)):
            u = U(plane, kk)
            wait_d(plane, kk)
            for q in copies(plane, kk, c, landv(plane, kk), (z, vf), SV.at[u], RV.at[u]): q.wait_recv()
            @pl.when(z < plane)
            def _():
                @pl.when(z > 0)
                def _():
                    zwait(plane, kk, 1)
                    add(plane, kk, [LD.at[u], LV.at[u], LZ.at[1, u]])
                @pl.when(z == 0)
                def _():
                    add(plane, kk, [LD.at[u], LV.at[u]])
                start(zsend(plane, i, kk, 1))
            @pl.when(z > plane)
            def _():
                @pl.when(z < Z - 1)
                def _():
                    zwait(plane, kk, 0)
                    add(plane, kk, [LD.at[u], LV.at[u], LZ.at[0, u]])
                @pl.when(z == Z - 1)
                def _():
                    add(plane, kk, [LD.at[u], LV.at[u]])
                start(zsend(plane, i, kk, 0))
    def gather_z(kk, extra, final):
        u = U(z, kk)
        @pl.when(z == 0)
        def _():
            zwait(z, kk, 0)
            add(z, kk, [LD.at[u], LV.at[u], LZ.at[0, u]] + extra, final)
        @pl.when(z == Z - 1)
        def _():
            zwait(z, kk, 1)
            add(z, kk, [LD.at[u], LV.at[u], LZ.at[1, u]] + extra, final)
        @pl.when((z > 0) & (z < Z - 1))
        def _():
            zwait(z, kk, 0)
            zwait(z, kk, 1)
            add(z, kk, [LD.at[u], LV.at[u], LZ.at[0, u], LZ.at[1, u]] + extra, final)
    gather_z(ku, [], False)
    ucopies = copies(z, ku, c, LU, (z, uf), SU.at[0], SU.at[1])
    start(ucopies)
    for q in copies(z, k, c, LU, (z, uf), SU.at[0], SU.at[1]): q.wait_recv()
    gather_z(k, [LU], True)
    bx = pltpu.make_async_remote_copy(src_ref=B.at[pl.ds(304, 16)], dst_ref=B.at[pl.ds(0, 16)], send_sem=SB.at[0], recv_sem=SB.at[1], device_id=(z, fc), device_id_type=MESH)
    bx.start()
    vec[...] = vec_in[...]
    steps = [(z, fc), (z, fx), (z, fy), (z + 1 - 2 * (z % 2), f), (z + 2 - 4 * (z // 2), f)]
    for i, dev in enumerate(steps):
        q = pltpu.make_async_remote_copy(src_ref=vec, dst_ref=vland.at[i], send_sem=SX.at[i, 0], recv_sem=SX.at[i, 1], device_id=dev, device_id_type=MESH)
        q.start(); q.wait()
        vec[...] = vec[...] + vland[i]
    vec_out[...] = vec[...]
    bx.wait()
    tot = jnp.zeros((8, 128), f32)
    for j in range(6):
        F[pl.ds(j, 320, stride=6), :] = B[:, 128 * j:128 * j + 128]
    for j in range(6):
        v = F[pl.ds(6 * (16 - 2 * c - 4 * k) + j, 302, stride=6), :]
        out[pl.ds(j, 302, stride=6), :] = v
        vv = v * v
        tot = tot + jnp.sum(vv[0:296].reshape(37, 8, 128), axis=0)
        tot = tot + jnp.concatenate([vv[296:302], jnp.zeros((2, 128), f32)], axis=0)
    sq[...] = tot
    for i, dev in enumerate(steps):
        q = pltpu.make_async_remote_copy(src_ref=sq, dst_ref=sqland.at[i], send_sem=SQ.at[i, 0], recv_sem=SQ.at[i, 1], device_id=dev, device_id_type=MESH)
        q.start(); q.wait()
        sq[...] = sq[...] + sqland[i]
    sq_out[...] = sq[...]
    for plane in range(Z):
        for kk in range(4):
            u = U(plane, kk)
            for q in copies(plane, kk, 1 - c, LD.at[u], (z, fc), SD.at[u], RD.at[u]): q.wait_send()
        for kk in (kv, kuv):
            u = U(plane, kk)
            for q in copies(plane, kk, c, LV.at[u], (z, vf), SV.at[u], RV.at[u]): q.wait_send()
        @pl.when(z != plane)
        def _():
            for kk in (k, ku):
                u = U(plane, kk)
                for q in copies(plane, kk, c, LZ.at[0, u], (z, fc), SZ.at[u], RZ.at[0, u]): q.wait_send()
    for q in ucopies: q.wait_send()

def rs(g, vec):
    DMA = pltpu.SemaphoreType.DMA
    f32 = jnp.float32; bf16 = jnp.bfloat16
    V = pl.BlockSpec(memory_space=pltpu.VMEM)
    return pl.pallas_call(rs_kernel,
        out_shape=[jax.ShapeDtypeStruct((1812, 128), f32), jax.ShapeDtypeStruct(vec.shape, f32), jax.ShapeDtypeStruct((8, 128), f32)],
        in_specs=[pl.BlockSpec(memory_space=pl.ANY), V], out_specs=[V, V, V],
        scratch_shapes=[pltpu.VMEM((GROW, 768), bf16), pltpu.VMEM((16, HALF, 768), bf16), pltpu.VMEM((16, HALF, 768), bf16), pltpu.VMEM((2, 16, HALF, 768), bf16),
                        pltpu.VMEM((HALF, 768), bf16), pltpu.VMEM((320, 768), f32), pltpu.VMEM((1920, 128), f32), pltpu.VMEM(vec.shape, f32), pltpu.VMEM((5,) + vec.shape, f32),
                        pltpu.VMEM((8, 128), f32), pltpu.VMEM((5, 8, 128), f32),
                        DMA, DMA((16, 2)), DMA((16, 2)), DMA((16, 2)), DMA((16, 2)), DMA((16, 2)), DMA((2, 16, 2)), DMA((2, 2)), DMA((5, 2)), DMA((2,)), DMA((5, 2))],
        compiler_params=pltpu.CompilerParams(collective_id=1, has_side_effects=True, vmem_limit_bytes=62*2**20))(g, vec)


def column_sum(values):
    return jnp.sum(values.astype(jnp.float32), axis=tuple(range(values.ndim - 1)))


def on_device(
    layer_input,
    mask_index,
    distract,
    code_choice,
    params,
    moment_one,
    moment_two,
    vectors,
    vector_one,
    vector_two,
):
    bf16 = jnp.bfloat16
    f32 = jnp.float32
    count_utts = layer_input.shape[0]
    total_masked = count_utts * lax.axis_size(("dp", "fsdp")) * MASKED
    token_rows = count_utts * LEN
    kernels = lax.axis_size("dp") == 4 and lax.axis_size("fsdp") == 8
    if kernels:
        gathered = ag(params)[:NROW].reshape(-1)
    else:
        gathered = lax.all_gather(params.astype(bf16), ("dp", "fsdp"), axis=0, tiled=True)
    qkv_weight, out_weight, up_weight, down_weight, proj_weight, codebook, code_weight = unpack(
        gathered
    )
    (
        bias_query,
        bias_value,
        bias_out,
        gain_one,
        shift_one,
        bias_up,
        bias_down,
        gain_two,
        shift_two,
        bias_proj,
        bias_code,
    ) = split_vectors(vectors)
    inputs = layer_input.reshape(token_rows, D)
    projected = jnp.dot(inputs, qkv_weight, preferred_element_type=f32)
    query_heads = (projected[:, :D] + bias_query).astype(bf16).reshape(count_utts, LEN, H, HD)
    key_heads = projected[:, D : 2 * D].astype(bf16).reshape(count_utts, LEN, H, HD)
    value_heads = (projected[:, 2 * D :] + bias_value).astype(bf16).reshape(count_utts, LEN, H, HD)
    scores = (
        jnp.einsum("blhe,bmhe->bhlm", query_heads, key_heads, preferred_element_type=f32) * 0.125
    )
    attn_probs = jax.nn.softmax(scores, axis=-1)
    probs_low = attn_probs.astype(bf16)
    attended = jnp.einsum("bhlm,bmhe->blhe", probs_low, value_heads, preferred_element_type=f32)
    attended = attended.astype(bf16).reshape(token_rows, D)
    residual_one = (
        inputs.astype(f32) + jnp.dot(attended, out_weight, preferred_element_type=f32) + bias_out
    )
    normed, back_one = jax.vjp(layer_norm, residual_one, gain_one, shift_one)
    normed_low = normed.astype(bf16)
    hidden = jnp.dot(normed_low, up_weight, preferred_element_type=f32) + bias_up
    active, gelu_back = jax.vjp(partial(jax.nn.gelu, approximate=False), hidden)
    active_low = active.astype(bf16)
    residual_two = normed + jnp.dot(active_low, down_weight, preferred_element_type=f32) + bias_down
    output, back_two = jax.vjp(layer_norm, residual_two, gain_two, shift_two)
    output_low = output.astype(bf16)
    place = (mask_index[0][:, None] == jnp.arange(LEN, dtype=jnp.int32)).astype(bf16)
    picked = jnp.dot(place, output_low, preferred_element_type=f32).astype(bf16)
    chosen = jnp.dot(picked, proj_weight, preferred_element_type=f32) + bias_proj
    choose = (code_choice[..., None] == jnp.arange(V, dtype=jnp.int32)).astype(bf16)
    code_vectors = jnp.einsum(
        "bmgv,gcv->bmgc", choose, codebook.reshape(G, CD, V), preferred_element_type=f32
    )
    code_vectors = code_vectors.astype(bf16).reshape(count_utts, MASKED, G * CD)
    targets = (
        jnp.einsum("bmc,cf->bmf", code_vectors, code_weight, preferred_element_type=f32) + bias_code
    )
    loss_local, d_chosen, d_targets = contrast(chosen, targets[0], distract[0], 1.0 / total_masked)
    d_targets = d_targets[None]
    d_targets_low = d_targets.astype(bf16)
    quantized_offset_slope = column_sum(d_targets_low)
    d_code_weight = jnp.einsum(
        "bmc,bmf->cf", code_vectors, d_targets_low, preferred_element_type=f32
    )
    d_code_vectors = jnp.einsum(
        "bmf,cf->bmc", d_targets_low, code_weight, preferred_element_type=f32
    )
    d_codebook = jnp.einsum(
        "bmgc,bmgv->gcv",
        d_code_vectors.reshape(count_utts, MASKED, G, CD),
        choose.astype(f32),
        precision=lax.Precision.HIGHEST,
    ).reshape(G * CD, V)
    d_chosen_low = d_chosen.astype(bf16)
    d_bias_proj = column_sum(d_chosen_low)
    d_proj_weight = jnp.einsum("td,tf->df", picked, d_chosen_low, preferred_element_type=f32)
    d_context_low = jnp.einsum("mt,mf->tf", place, d_chosen_low, preferred_element_type=f32).astype(bf16)
    result_sensitivity = jnp.einsum(
        "tf,df->td", d_context_low, proj_weight, preferred_element_type=f32
    )
    d_residual_two, d_gain_two, d_shift_two = back_two(result_sensitivity)
    d_second_low = d_residual_two.astype(bf16)
    d_bias_down = column_sum(d_second_low)
    d_down_weight = jnp.einsum("th,td->hd", active_low, d_second_low, preferred_element_type=f32)
    d_active = jnp.einsum("td,hd->th", d_second_low, down_weight, preferred_element_type=f32)
    (d_hidden,) = gelu_back(d_active)
    d_hidden_low = d_hidden.astype(bf16)
    d_bias_up = column_sum(d_hidden_low)
    d_up_weight = jnp.einsum("td,th->dh", normed_low, d_hidden_low, preferred_element_type=f32)
    d_normed = d_residual_two + jnp.einsum(
        "th,dh->td", d_hidden_low, up_weight, preferred_element_type=f32
    )
    d_residual_one, d_gain_one, d_shift_one = back_one(d_normed)
    d_branch_low = d_residual_one.astype(bf16)
    d_bias_out = column_sum(d_branch_low)
    d_out_weight = jnp.einsum("td,te->de", attended, d_branch_low, preferred_element_type=f32)
    d_attended = jnp.einsum("te,de->td", d_branch_low, out_weight, preferred_element_type=f32)
    d_attended = d_attended.astype(bf16).reshape(count_utts, LEN, H, HD)
    d_value = jnp.einsum("bhlm,blhe->bmhe", probs_low, d_attended, preferred_element_type=f32)
    d_probs = jnp.einsum("blhe,bmhe->bhlm", d_attended, value_heads, preferred_element_type=f32)
    d_scores = (
        attn_probs * (d_probs - jnp.sum(attn_probs * d_probs, axis=-1, keepdims=True))
    ).astype(bf16)
    d_query = jnp.einsum("bhlm,bmhe->blhe", d_scores, key_heads, preferred_element_type=f32) * 0.125
    d_key = jnp.einsum("bhlm,blhe->bmhe", d_scores, query_heads, preferred_element_type=f32) * 0.125
    d_projected = jnp.concatenate(
        [
            d_query.reshape(token_rows, D),
            d_key.reshape(token_rows, D),
            d_value.reshape(token_rows, D),
        ],
        axis=1,
    ).astype(bf16)
    d_sums = column_sum(d_projected)
    d_qkv_weight = jnp.einsum("td,te->de", inputs, d_projected, preferred_element_type=f32)
    input_grad = d_residual_one + jnp.einsum(
        "te,de->td", d_projected, qkv_weight, preferred_element_type=f32
    )
    flat_grad = jnp.concatenate(
        [
            matrix_grad.reshape(-1)
            for matrix_grad in (
                d_qkv_weight,
                d_out_weight,
                d_up_weight,
                d_down_weight,
                d_proj_weight,
                d_codebook,
                d_code_weight,
            )
        ]
    )
    vector_gradient = jnp.concatenate(
        [
            d_sums[:D],
            d_sums[2 * D :],
            d_bias_out,
            d_gain_one,
            d_shift_one,
            d_bias_up,
            d_bias_down,
            d_gain_two,
            d_shift_two,
            d_bias_proj,
            quantized_offset_slope,
        ]
    )
    if kernels:
        padded = jnp.concatenate([vector_gradient, jnp.full((512,), loss_local)]).reshape(80, 128)
        grad_shard, sums, squares = rs(flat_grad.astype(bf16).reshape(NROW, 768), padded)
        grad_shard = grad_shard.reshape(-1)
        square_sum = jnp.sum(squares)
        vector_sum = sums.reshape(-1)[:9728]
        loss_sum = sums[79, 0]
    else:
        vector_sum, loss_sum = lax.psum((vector_gradient, loss_local), ("dp", "fsdp"))
        grad_shard = lax.psum_scatter(flat_grad, ("dp", "fsdp"), scatter_dimension=0, tiled=True)
        square_sum = lax.psum(jnp.sum(grad_shard * grad_shard), ("dp", "fsdp"))
    grad_norm = jnp.sqrt(square_sum + jnp.sum(vector_sum * vector_sum))
    factor = jnp.minimum(1.0, clip_level / (grad_norm + 1e-06))
    refreshed_weights, new_one, new_two = adamw_update(
        params, moment_one, moment_two, grad_shard * factor, rate_matrix
    )
    new_vectors, new_vector_first, new_vector_second = adamw_update(
        vectors, vector_one, vector_two, vector_sum * factor, rate_vector
    )
    total_loss = loss_sum / total_masked
    return (
        total_loss,
        grad_norm,
        output_low.reshape(count_utts, LEN, D),
        input_grad.reshape(count_utts, LEN, D),
        refreshed_weights,
        refreshed_weights.astype(bf16),
        new_one,
        new_two,
        new_vectors,
        new_vector_first,
        new_vector_second,
    )


def solution(mesh):
    in_specs = (
        P(("dp", "fsdp"), None, None),
        P(("dp", "fsdp"), None),
        P(("dp", "fsdp"), None, None),
        P(("dp", "fsdp"), None, None),
        P(("dp", "fsdp")),
        P(("dp", "fsdp")),
        P(("dp", "fsdp")),
        P(),
        P(),
        P(),
    )
    out_specs = (
        P(),
        P(),
        P(("dp", "fsdp"), None, None),
        P(("dp", "fsdp"), None, None),
        P(("dp", "fsdp")),
        P(("dp", "fsdp")),
        P(("dp", "fsdp")),
        P(("dp", "fsdp")),
        P(),
        P(),
        P(),
    )
    return jax.shard_map(
        on_device, mesh=mesh, in_specs=in_specs, out_specs=out_specs, check_vma=False
    )
```

```python
import functools

import jax
import jax.numpy as jnp
from jax import lax
from jax.experimental import pallas as pl
from jax.experimental.pallas import tpu as pltpu
from jax.sharding import PartitionSpec as P
D = 768; H = 12; HD = 64; FF = 3072; FINAL = 256; G = 2; V = 320; CD = 128; LEN = 472; MASKED = 232
NROW = 9664; GROW = NROW + 256
T = 512
LT = 480
bf16 = jnp.bfloat16
f32 = jnp.float32
NT = (((1,), (1,)), ((), ()))
BQ, BV, BO, G1, S1, BUP, BDOWN, G2, S2, BPROJ, BCODE = [768 * i for i in range(6)] + [3840 + 3072 + 768 * i for i in range(3)] + [9216, 9472]

def mm(a, b):
    return jnp.dot(a, b, preferred_element_type=f32)

def mm_nt(a, b, precision=None):
    return lax.dot_general(a, b, NT, preferred_element_type=f32, precision=precision)

def hi(a, b):
    return jnp.dot(a, b, preferred_element_type=f32, precision=lax.Precision.HIGHEST)

def split_rows(g, base, parts, nice, first, tmp):
    def body(b, _):
        src = pl.multiple_of(base + b * 64 * parts, 64)
        for j in range(6):
            tmp[j, 0:64 * parts, :] = g[pl.ds(src, 64 * parts), 128 * j:128 * j + 128].astype(f32)
        for t in range(parts):
            at = pl.multiple_of((first + t) * D + b * 64, 64)
            for j in range(6):
                nice[pl.ds(at, 64), 128 * j:128 * j + 128] = tmp[j, pl.ds(t, 64, stride=parts), :].astype(bf16)
        return 0
    lax.fori_loop(0, D // 64, body, 0)

def norm_rows(r, gain, shift, low, wide, hat, rstd):
    def body(b, _):
        at = pl.multiple_of(b * 48, 16)
        v = r[pl.ds(at, 48), :]
        m = jnp.mean(v, axis=-1, keepdims=True)
        c = v - m
        var = jnp.mean(c * c, axis=-1, keepdims=True)
        inv = lax.rsqrt(var + eps_norm)
        xh = c * inv
        o = xh * gain + shift
        hat[pl.ds(at, 48), :] = xh
        rstd[pl.ds(at, 48), :] = jnp.broadcast_to(inv, (48, 128))
        if wide is not None:
            wide[pl.ds(at, 48), :] = o
        low[pl.ds(at, 48), :] = o.astype(bf16)
        return 0
    lax.fori_loop(0, LT // 48, body, 0)

def transpose_to(src, dst, rows, cols):
    def body(n, _):
        at = pl.multiple_of(n * 128, 128)
        dst[pl.ds(at, 128), :] = src[:, pl.ds(at, 128)].T
        return 0
    lax.fori_loop(0, cols // 128, body, 0)

def prepare(x_ref, xp, xT, mask_ref, distract_ref, choice_ref, vec_ref, vec, place, placeT, allowed, choose):
    for i in range(vec_ref.shape[0]):
        vec[0:1, 128 * i:128 * i + 128] = vec_ref[i:i + 1, :]
    xp[...] = jnp.zeros((T, D), bf16)
    xp[0:LEN, :] = x_ref[0]
    transpose_to(xp, xT, T, D)
    zero = jnp.zeros((1, 256 - MASKED), jnp.int32) - 1
    def wide(row):
        return jnp.concatenate([row, zero], axis=1)
    hot = jnp.where(lax.broadcasted_iota(jnp.int32, (T, 256), 0) == wide(mask_ref[...]), 1.0, 0.0)
    placeT[...] = hot.astype(bf16)
    place[...] = hot.T.astype(bf16)
    row = lax.broadcasted_iota(jnp.int32, (256, 256), 0)
    col = lax.broadcasted_iota(jnp.int32, (256, 256), 1)
    allowed[...] = jnp.where((row == col) & (col < MASKED), 1.0, 0.0)
    rows = [wide(distract_ref[i]) for i in range(distract_ref.shape[0])]
    def body(b, _):
        at = pl.multiple_of(8 * b, 8)
        acc = allowed[pl.ds(at, 8), :]
        n = lax.broadcasted_iota(jnp.int32, (8, 256), 0) + at
        for r in rows:
            acc = jnp.where(n == r, 1.0, acc)
        allowed[pl.ds(at, 8), :] = acc
        return 0
    lax.fori_loop(0, MASKED // 8, body, 0)
    allowed[...] = allowed[...].T
    for g in range(2):
        v = jnp.where(lax.broadcasted_iota(jnp.int32, (384, 256), 0) == wide(choice_ref[0, g:g + 1, :]), 1.0, 0.0)
        choose[g] = v.T

def project(xp, nice, vec, q, kk, kT, vv, vT):
    for t, (dst, bias) in enumerate(((q, BQ), (kk, None), (vv, BV))):
        for n in range(3):
            acc = mm(xp[...], nice[t * D:(t + 1) * D, 256 * n:256 * n + 256])
            if bias is not None:
                acc = acc + vec[0:1, bias + 256 * n:bias + 256 * n + 256]
            dst[:, 256 * n:256 * n + 256] = acc.astype(bf16)
    transpose_to(kk, kT, T, D)
    transpose_to(vv, vT, T, D)

def attend(p, q, kk, vT, pT, attT):
    at = pl.multiple_of(128 * p, 128)
    qp = q[:, pl.ds(at, 128)]
    kp = kk[0:LT, pl.ds(at, 128)]
    lane = lax.broadcasted_iota(jnp.int32, (LT, 128), 1)
    for h in range(2):
        kh = jnp.where((lane < 64) == (h == 0), kp, jnp.zeros_like(kp))
        s = mm_nt(kh, qp)[0:LEN] * 0.125
        e = jnp.exp(s - jnp.max(s, axis=0, keepdims=True))
        pr = e * (1.0 / jnp.sum(e, axis=0, keepdims=True))
        pr = jnp.concatenate([pr, jnp.zeros((T - LEN, T), f32)], axis=0).astype(bf16)
        pT[pl.ds(pl.multiple_of((2 * (p % 2) + h) * T, T), T), :] = pr
        rows = pl.ds(pl.multiple_of(128 * p + 64 * h, 64), 64)
        attT[rows, :] = mm(vT[rows, :], pr).astype(bf16)

def out_project(attT, att, xp, wo, vec, res):
    for n in range(6):
        att[:, 128 * n:128 * n + 128] = attT[128 * n:128 * n + 128, :].T
    for n in range(3):
        cols = slice(256 * n, 256 * n + 256)
        acc = mm(att[0:LT, :], wo[:, cols])
        res[:, cols] = xp[0:LT, cols].astype(f32) + acc + vec[0:1, BO + 256 * n:BO + 256 * n + 256]

def up(n, norm_low, nice, vec, act, gp):
    root = 0.7071067811865476
    scale = 0.3989422804014327
    c = n // 3
    w = nice[pl.ds(pl.multiple_of(c * D, D), D), pl.ds(pl.multiple_of((n - 3 * c) * 256, 256), 256)]
    at = pl.multiple_of(n * 256, 256)
    h = mm(norm_low[0:LT, :], w) + vec[0:1, pl.ds(pl.multiple_of(BUP + n * 256, 256), 256)]
    cdf = 0.5 * (1.0 + lax.erf(h * root))
    act[0:LT, pl.ds(at, 256)] = (h * cdf).astype(bf16)
    gp[0:LT, pl.ds(at, 256)] = (cdf + h * (scale * jnp.exp(-0.5 * h * h))).astype(bf16)

def down(act, g, vec, res, wide):
    for n in range(3):
        cols = slice(256 * n, 256 * n + 256)
        acc = mm(act[0:LT, :], g[6144:9216, cols])
        res[:, cols] = wide[:, cols] + acc + vec[0:1, BDOWN + 256 * n:BDOWN + 256 * n + 256]

def small_weights(g, fb, p32, c32, wproj, code, wcode):
    for t in range(3):
        for j in range(2):
            p32[j, pl.ds(t, 256, stride=3), :] = g[9216:9472, 256 * t + 128 * j:256 * t + 128 * j + 128].astype(f32)
    for j in range(2):
        wproj[:, 128 * j:128 * j + 128] = p32[j].astype(bf16)
    for j in range(6):
        fb[pl.ds(j, 192, stride=6), :] = g[9472:9664, 128 * j:128 * j + 128].astype(f32)
    a = [fb[pl.ds(j, 128, stride=5), :] for j in range(5)]
    lo = lax.broadcasted_iota(jnp.int32, (128, 128), 1) < 64
    r2, r3, r4 = [pltpu.roll(v, 64, 1) for v in a[2:]]
    zero = jnp.zeros((128, 128), f32)
    even = [a[0], a[1], jnp.where(lo, a[2], zero)]
    odd = [jnp.where(lo, r2, r3), jnp.where(lo, r3, r4), jnp.where(lo, r4, zero)]
    for j in range(3):
        c32[j, pl.ds(0, 128, stride=2), :] = even[j]
        c32[j, pl.ds(1, 128, stride=2), :] = odd[j]
        code[:, 128 * j:128 * j + 128] = c32[j].astype(bf16)
    for j in range(2):
        wcode[:, 128 * j:128 * j + 128] = fb[pl.ds(640 + j, 256, stride=2), :].astype(bf16)

def contrast(weight, out_low, vec, place, placeT, allowed, choose, wproj, code, wcode, fb, p32, c32, tail, dctx, small):
    picked = mm(place[...], out_low[...]).astype(bf16)
    chosen = mm(picked, wproj[...]) + vec[0:1, BPROJ:BPROJ + 256]
    cv = jnp.concatenate([mm_nt(choose[g].astype(bf16), code[128 * g:128 * g + 128, :]) for g in range(2)], axis=1).astype(bf16)
    targets = mm(cv, wcode[...]) + vec[0:1, BCODE:BCODE + 256]
    n_l = lax.rsqrt(jnp.sum(chosen * chosen, axis=1, keepdims=True) + eps_cos)
    n_r = lax.rsqrt(jnp.sum(targets * targets, axis=1, keepdims=True) + eps_cos)
    left = chosen * n_l
    right = targets * n_r
    sim = mm_nt(left, right, lax.Precision.HIGHEST) / 0.1
    ok = allowed[...] > 0.5
    row = lax.broadcasted_iota(jnp.int32, (256, 256), 0)
    col = lax.broadcasted_iota(jnp.int32, (256, 256), 1)
    eye = jnp.where((row == col) & (row < MASKED), 1.0, 0.0)
    pos = jnp.sum(eye * sim, axis=1, keepdims=True)
    top = jnp.max(jnp.where(ok, sim, -1e30), axis=1, keepdims=True)
    parts = jnp.where(ok, jnp.exp(jnp.minimum(sim - top, 0.0)), 0.0)
    real = lax.broadcasted_iota(jnp.int32, (256, 1), 0) < MASKED
    total = jnp.where(real, jnp.sum(parts, axis=1, keepdims=True), 1.0)
    loss = jnp.sum(jnp.where(real, top + jnp.log(total) - pos, 0.0))
    dsim = (weight / 0.1) * (parts / total - eye)
    dl = hi(dsim, right)
    dr = hi(dsim.T, left)
    d_chosen = (n_l * dl - chosen * (n_l * n_l * n_l) * jnp.sum(chosen * dl, axis=1, keepdims=True)).astype(bf16)
    d_target = (n_r * dr - targets * (n_r * n_r * n_r) * jnp.sum(targets * dr, axis=1, keepdims=True)).astype(bf16)
    small[0:1, :] = jnp.sum(d_chosen.astype(f32), axis=0, keepdims=True)
    small[1:2, :] = jnp.sum(d_target.astype(f32), axis=0, keepdims=True)
    small[2:3, :] = jnp.broadcast_to(loss, (1, 256))
    dctx[...] = mm(placeT[...], d_chosen).astype(bf16)
    dproj = mm(picked.T, d_chosen)
    for j in range(2):
        p32[j] = dproj[:, 128 * j:128 * j + 128]
    for t in range(3):
        for j in range(2):
            tail[0:256, 256 * t + 128 * j:256 * t + 128 * j + 128] = p32[j, pl.ds(t, 256, stride=3), :].astype(bf16)
    dwcode = mm(cv.T, d_target)
    dcv = mm_nt(d_target, wcode[...])
    for g in range(2):
        dc = hi(dcv[:, 128 * g:128 * g + 128].T, choose[g])
        for j in range(3):
            c32[j, 128 * g:128 * g + 128, :] = dc[:, 128 * j:128 * j + 128]
    e = [c32[j, pl.ds(0, 128, stride=2), :] for j in range(3)]
    o = [pltpu.roll(c32[j, pl.ds(1, 128, stride=2), :], 64, 1) for j in range(3)]
    lo = lax.broadcasted_iota(jnp.int32, (128, 128), 1) < 64
    for j, v in enumerate((e[0], e[1], jnp.where(lo, e[2], o[0]), jnp.where(lo, o[0], o[1]), jnp.where(lo, o[1], o[2]))):
        fb[pl.ds(j, 128, stride=5), :] = v
    for j in range(2):
        fb[pl.ds(640 + j, 256, stride=2), :] = dwcode[:, 128 * j:128 * j + 128]
    for j in range(6):
        tail[256:448, 128 * j:128 * j + 128] = fb[pl.ds(j, 192, stride=6), :].astype(bf16)
STEP = 10


eps_norm = 1e-05
eps_cos = 1e-06
softness_divisor = 0.1
beta_one = 0.9
beta_two = 0.98
adam_eps = 1e-08
decay_rate = 0.01
rate_matrix = 0.03
rate_vector = 0.2
clip_level = 0.001


def sum8(v):
    r, n = v.shape
    return jnp.sum(v.reshape(r // 8, 8, n), axis=0)

def norm_back_first(dctx, wproj, gain, hat, rstd, low, acc):
    acc[...] = jnp.zeros((24, D), f32)
    def body(b, _):
        at = pl.multiple_of(b * 48, 16)
        dy = mm_nt(dctx[pl.ds(at, 48), :], wproj[...])
        norm_back_rows(dy, at, gain, hat, hat, rstd, low, acc)
        return 0
    lax.fori_loop(0, LT // 48, body, 0)

def norm_back_rows(dy, at, gain, hat, dst, rstd, low, acc):
    xh = hat[pl.ds(at, 48), :]
    inv = rstd[pl.ds(at, 48), 0:1]
    a = dy * gain
    m1 = jnp.mean(a, axis=-1, keepdims=True)
    m2 = jnp.mean(a * xh, axis=-1, keepdims=True)
    dr = inv * (a - m1 - xh * m2)
    lo = dr.astype(bf16)
    dst[pl.ds(at, 48), :] = dr
    low[pl.ds(at, 48), :] = lo
    acc[0:8, :] += sum8(dy * xh)
    acc[8:16, :] += sum8(dy)
    acc[16:24, :] += sum8(lo.astype(f32))

def norm_back(dy, gain, hat, rstd, low, acc):
    acc[...] = jnp.zeros((24, D), f32)
    def body(b, _):
        at = pl.multiple_of(b * 48, 16)
        norm_back_rows(dy[pl.ds(at, 48), :], at, gain, hat, hat, rstd, low, acc)
        return 0
    lax.fori_loop(0, LT // 48, body, 0)

def put_vec(vg, acc, offsets):
    for i, o in enumerate(offsets):
        vg[0:1, o:o + D] = jnp.sum(acc[8 * i:8 * i + 8, :], axis=0, keepdims=True)

def down_back(n, low2, gg, actT, gp, vg):
    at = pl.multiple_of(n * 256, 256)
    rows = pl.ds(pl.multiple_of(6144 + n * 256, 256), 256)
    d = mm_nt(low2[0:LT, :], gg[rows, :]) * gp[0:LT, pl.ds(at, 256)].astype(f32)
    d = d.astype(bf16)
    gp[0:LT, pl.ds(at, 256)] = d
    vg[0:1, pl.ds(pl.multiple_of(BUP + at, 128), 256)] = jnp.sum(d.astype(f32), axis=0, keepdims=True)
    gg[rows, :] = mm(actT[pl.ds(at, 256), :], low2[...]).astype(bf16)

def up_back_x(n, dh, gg, dr):
    cols = pl.ds(pl.multiple_of(n * 256, 256), 256)
    v = dr[:, cols]
    for c in range(4):
        w = gg[pl.ds(pl.multiple_of(3072 + c * D + n * 256, 256), 256), :]
        v = v + mm_nt(dh[0:LT, c * D:(c + 1) * D], w)
    dr[:, cols] = v

def weave(lhsT, rhs, parts, n, base, gg, tmp, stacked):
    def body(m, _):
        cols = pl.ds(pl.multiple_of(m * 256, 256), 256)
        for t in range(parts):
            r = rhs[t, :, cols] if stacked else rhs[:, pl.ds(pl.multiple_of(t * D + m * 256, 256), 256)]
            acc = mm(lhsT[pl.ds(pl.multiple_of(n * 256, 256), 256), :], r)
            for j in range(2):
                tmp[j, pl.ds(t, 256, stride=parts), :] = acc[:, 128 * j:128 * j + 128]
        for j in range(2):
            gg[pl.ds(pl.multiple_of(base + n * 256 * parts, 256), 256 * parts), pl.ds(pl.multiple_of(m * 256 + 128 * j, 128), 128)] = tmp[j, 0:256 * parts, :].astype(bf16)
        return 0
    lax.fori_loop(0, 3, body, 0)

def out_back(low1, gg, attT, da):
    for n in range(3):
        cols = slice(256 * n, 256 * n + 256)
        da[0:LT, cols] = mm_nt(low1[0:LT, :], gg[2304 + 256 * n:2304 + 256 * n + 256, :]).astype(bf16)
    for n in range(3):
        gg[2304 + 256 * n:2304 + 256 * n + 256, :] = mm(attT[256 * n:256 * n + 256, :], low1[...]).astype(bf16)

def attend_back(p, da, q, kT, vv, ring, dp, dqT):
    at = pl.multiple_of(128 * p, 128)
    lane = lax.broadcasted_iota(jnp.int32, (T, 128), 1)
    dap = da[:, pl.ds(at, 128)]
    qp = q[:, pl.ds(at, 128)]
    vp = vv[0:LT, pl.ds(at, 128)]
    dk = dv = None
    for h in range(2):
        half = (lane < 64) == (h == 0)
        dah = jnp.where(half, dap, jnp.zeros_like(dap))
        qh = jnp.where(half, qp, jnp.zeros_like(qp))
        pr = ring[pl.ds(pl.multiple_of(((2 * p + h) % 6) * T, T), LT), :]
        dpT = mm_nt(vp, dah)
        prf = pr.astype(f32)
        w = prf * dpT
        ds = (w - prf * jnp.sum(w, axis=0, keepdims=True)).astype(bf16)
        a = mm(pr, dah)
        b = mm(ds, qh)
        dv = a if dv is None else dv + a
        dk = b if dk is None else dk + b
        rows = pl.ds(pl.multiple_of(128 * p + 64 * h, 64), 64)
        dqT[rows, :] = (mm(kT[rows, 0:LT], ds) * 0.125).astype(bf16)
    dp[1, 0:LT, pl.ds(at, 128)] = (dk * 0.125).astype(bf16)
    dp[2, 0:LT, pl.ds(at, 128)] = dv.astype(bf16)
    dp[0, :, pl.ds(at, 128)] = dqT[pl.ds(at, 128), :].T

def input_back(n, dp, wq, dr, out):
    cols = slice(256 * n, 256 * n + 256)
    v = dr[:, cols]
    for t in range(3):
        v = v + mm_nt(dp[t, 0:LT, :], wq[t * D + 256 * n:t * D + 256 * n + 256, :])
    out[0, :, cols] = v[0:LEN]
MESH = pl.DeviceIdType.MESH
UP, DOWN, U, V_AXIS, CORE, HERE = range(6)
PLANES = 4
MAIN = 288
EXTRA = 16
HALF = MAIN + EXTRA
PLANE = 2416
UNIT = 608

class Place:
    def __init__(self):
        self.z = lax.axis_index("dp")
        self.f = f = lax.axis_index("fsdp")
        self.c = c = f % 2
        self.k = k = f // 2
        x = k % 2
        y = k // 2
        self.fc = f + 1 - 2 * c
        self.fx = f + 2 - 4 * x
        self.fy = f + 4 - 8 * y
        self.uf = self.fx * (1 - c) + self.fy * c
        self.vf = self.fy * (1 - c) + self.fx * c
        self.roles = (k, self.uf // 2, self.vf // 2, 3 - k)

    def greet(self):
        z = self.z
        bar = pltpu.get_barrier_semaphore()
        for t in (self.fc, self.fx, self.fy):
            pl.semaphore_signal(bar, inc=1, device_id=(z, t), device_id_type=MESH)
        @pl.when(z > 0)
        def _(): pl.semaphore_signal(bar, inc=1, device_id=(z - 1, self.f), device_id_type=MESH)
        @pl.when(z < PLANES - 1)
        def _(): pl.semaphore_signal(bar, inc=1, device_id=(z + 1, self.f), device_id_type=MESH)
        pl.semaphore_wait(bar, 3 + (z + PLANES - 1) // PLANES + (2 * PLANES - 2 - z) // PLANES)

    def greet_all(self, count):
        bar = pltpu.get_barrier_semaphore()
        for j in range(1, count):
            pl.semaphore_signal(bar, inc=1, device_id=(self.z, lax.rem(self.f + j, count)), device_id_type=MESH)
        for j in range(1, PLANES):
            pl.semaphore_signal(bar, inc=1, device_id=(lax.rem(self.z + j, PLANES), self.f), device_id_type=MESH)
        pl.semaphore_wait(bar, count + PLANES - 2)

    def span(self, p, r, c, first):
        kk = self.roles[r]
        m = PLANE * p + UNIT * kk
        return (pl.multiple_of(m + HALF * c + first, 16),
                pl.multiple_of((m + MAIN) * (1 - c) + (NROW + EXTRA * (4 * p + kk)) * c, 16))

def remote(src, dst, ssem, rsem, dev):
    return pltpu.make_async_remote_copy(src_ref=src, dst_ref=dst, send_sem=ssem, recv_sem=rsem, device_id=dev, device_id_type=MESH)

def shared_blocks(g, p, out):
    row = lax.broadcasted_iota(jnp.int32, (16, D), 0)
    if out:
        b = [g[PLANE * p + 16 * q:PLANE * p + 16 * q + 16, :].astype(f32) for q in (37, 75, 113)]
        for q, v in enumerate((b[0], jnp.where(row < 8, b[1], b[0]), jnp.where(row < 4, b[2], b[1]), b[2])):
            g[NROW + 16 * (4 * p + q):NROW + 16 * (4 * p + q) + 16, :] = v.astype(bf16)
    else:
        e = [g[NROW + 16 * (4 * p + q):NROW + 16 * (4 * p + q) + 16, :].astype(f32) for q in range(4)]
        for q, bound in enumerate((12, 8, 4)):
            at = PLANE * p + UNIT * q + 592
            g[at:at + 16, :] = jnp.where(row < bound, e[q], e[q + 1]).astype(bf16)

class Gather:
    def __init__(self, at, g, pieces, R, O, S):
        self.at, self.g, self.pieces, self.R, self.O, self.S = at, g, pieces, R, O, S
        self.index = {}
        self.made = {z: [] for z in range(PLANES)}
        self.seen = set()

    def sem(self, key):
        return self.S.at[self.index.setdefault(key, len(self.index))]

    def copies(self, i, p, r, dev, kind, c):
        _, first, rows, extra = self.pieces[p][i]
        a, e = self.at.span(p, r, c, first)
        unit = 4 * p + self.at.roles[r]
        got = self.O if kind == CORE else self.R
        out = []
        for j, (s, n) in enumerate([(a, rows)] + [(e, EXTRA)] * extra):
            ref = self.g.at[pl.ds(s, n)]
            out.append(remote(ref, ref, self.sem((kind, i, p, r, j)), got.at[unit, i + j], dev))
        return out

    def op(self, zs, kind, i, p, r):
        at = self.at
        if not (p == zs and r == 0) and (zs, i, p, r) not in self.seen:
            self.seen.add((zs, i, p, r))
            for q in self.copies(i, p, r, (zs, at.fc), HERE, at.c): q.wait_recv()
        dev = ((zs + 1, at.f), (zs - 1, at.f), (zs, at.uf), (zs, at.vf), (zs, at.fc))[kind]
        for q in self.copies(i, p, r, dev, kind, at.c): q.start()
        self.made[zs].append((kind, i, p, r))

    def other_core(self, zs, p):
        for r in range(4):
            if p == zs and r == 0: continue
            for i in range(len(self.pieces[p])):
                for q in self.copies(i, p, r, (zs, self.at.fc), CORE, 1 - self.at.c): q.wait_recv()

    def drain(self):
        for zs in range(PLANES):
            @pl.when(self.at.z == zs)
            def _():
                for kind, i, p, r in self.made[zs]:
                    for q in self.copies(i, p, r, (zs, self.at.fc), kind, self.at.c): q.wait_send()

def own_rows(at, g, p_ref, raw, land, sem):
    n = p_ref.shape[0]
    copy = remote(p_ref.at[pl.ds(0, n)], land.at[pl.ds(0, n)], sem.at[0], sem.at[1], (at.z, at.fc))
    copy.start()
    @pl.when(at.c == 0)
    def _(): raw[96:96 + n, :] = p_ref[...]
    @pl.when(at.c == 1)
    def _(): raw[96 + n:96 + 2 * n, :] = p_ref[...]
    copy.wait()
    @pl.when(at.c == 1)
    def _(): raw[96:96 + n, :] = land[0:n]
    @pl.when(at.c == 0)
    def _(): raw[96 + n:96 + 2 * n, :] = land[0:n]
    k = at.k
    own = pl.multiple_of(PLANE * at.z + UNIT * k, 16)
    extra = pl.multiple_of(NROW + EXTRA * (4 * at.z + k), 16)
    row = lax.broadcasted_iota(jnp.int32, (16, 128), 0)
    for j in range(6):
        cols = slice(128 * j, 128 * j + 128)
        g[pl.ds(own, 592), cols] = raw[pl.ds(96 + 24 * k + j, 592, stride=6), :].astype(bf16)
        last = raw[pl.ds(96 + (592 + 4 * k) * 6 + j, 16, stride=6), :]
        first = raw[pl.ds(24 * k + j, 16, stride=6), :]
        g[pl.ds(extra, 16), cols] = jnp.where(row < 12 - 4 * k, last, first).astype(bf16)

K1_OUT = ("w", "wproj", "tail", "dctx", "small", "hat1", "r1", "hat2", "r2", "gp", "actT", "normT", "attT", "q", "kT", "vv", "xT", "pT")
K1_SHAPE = {"w": ((NROW, D), bf16), "wproj": ((D, 256), bf16), "tail": ((448, D), bf16), "dctx": ((T, 256), bf16), "small": ((8, 256), f32),
            "hat1": ((LT, D), f32), "r1": ((LT, 128), f32), "hat2": ((LT, D), f32), "r2": ((LT, 128), f32), "gp": ((T, FF), bf16), "actT": ((FF, T), bf16),
            "normT": ((D, T), bf16), "attT": ((D, T), bf16), "q": ((T, D), bf16), "kT": ((D, T), bf16), "vv": ((T, D), bf16), "xT": ((D, T), bf16),
            "pT": ((H * T, T), bf16)}

def forward_kernel(pieces, events, weight, p_ref, x, mask, dis, cho, vec_ref, *rest):
    n_out = len(K1_OUT)
    hbm = dict(zip(K1_OUT, rest[:n_out]))
    (out, vec, g, raw, land, nice, tmp, wproj, tail, dctx, small, hat1, r1, hat2, r2, gp, actT, normT, attT, q, kT, vv, xT, pT,
     xp, kk, vT, act, res, wide, low1, low2, place, placeT, allowed, choose, fb, p32, c32, code, wcode,
     sem_raw, R, O, S, OS, PS) = rest[n_out:]
    here = dict(wproj=wproj, tail=tail, dctx=dctx, small=small, hat1=hat1, r1=r1, hat2=hat2, r2=r2, gp=gp, actT=actT, normT=normT, attT=attT, q=q, kT=kT, vv=vv, xT=xT, pT=pT)
    outs = []
    count = iter(range(32))
    def put(src, dst):
        cp = pltpu.make_async_copy(src, dst, OS.at[next(count)])
        cp.start()
        outs.append(cp)
    def save(*names):
        for n in names: put(here[n], hbm[n])
    at = Place()
    ga = Gather(at, g, pieces, R, O, S)
    at.greet()
    own_rows(at, g, p_ref, raw, land, sem_raw)
    def slot(i, cond=None):
        for zs in range(PLANES):
            if events[zs][i]:
                @pl.when((at.z == zs) if cond is None else ((at.z == zs) & cond))
                def _():
                    for e in events[zs][i]: ga.op(zs, *e)
    def plane(p):
        for zs in range(PLANES):
            @pl.when(at.z == zs)
            def _(): ga.other_core(zs, p)
        shared_blocks(g, p, False)
    slot(0)
    prepare(x, xp, xT, mask, dis, cho, vec_ref, vec, place, placeT, allowed, choose)
    act[LT:T, :] = jnp.zeros((T - LT, FF), bf16)
    gp[LT:T, :] = jnp.zeros((T - LT, FF), bf16)
    low1[...] = jnp.zeros((T, D), bf16)
    low2[...] = jnp.zeros((T, D), bf16)
    small[...] = jnp.zeros((8, 256), f32)
    save("xT")
    slot(1)
    plane(0)
    split_rows(g, 0, 3, nice, 0, tmp)
    slot(2)
    project(xp, nice, vec, q, kk, kT, vv, vT)
    save("q", "kT", "vv")
    put(nice.at[pl.ds(0, 2304)], hbm["w"].at[pl.ds(0, 2304)])
    nice_out = outs.pop()
    slot(3)
    slot(4)
    def pair_out(p):
        b = p % 2
        return pltpu.make_async_copy(pT.at[pl.ds(pl.multiple_of(2 * T * b, T), 2 * T)], hbm["pT"].at[pl.ds(pl.multiple_of(2 * T * p, T), 2 * T)], PS.at[b])
    def pair(p, _):
        @pl.when(p >= 2)
        def _(): pair_out(p - 2).wait()
        attend(p, q, kk, vT, pT, attT)
        pair_out(p).start()
        for i in range(6): slot(5 + i, p == i)
        return 0
    lax.fori_loop(0, H // 2, pair, 0)
    pair_out(H // 2 - 2).wait()
    pair_out(H // 2 - 1).wait()
    save("attT")
    plane(1)
    out_project(attT, kk, xp, g.at[2304:3072], vec, res)
    put(g.at[pl.ds(2304, 768)], hbm["w"].at[pl.ds(2304, 768)])
    norm_rows(res, vec[0:1, G1:G1 + D], vec[0:1, S1:S1 + D], low1, wide, hat1, r1)
    save("hat1", "r1")
    transpose_to(low1, normT, T, D)
    save("normT")
    slot(11)
    plane(2)
    nice_out.wait()
    split_rows(g, 3072, 4, nice, 0, tmp)
    put(nice, hbm["w"].at[pl.ds(3072, 3072)])
    slot(12)
    def tile(n, _):
        up(n, low1, nice, vec, act, gp)
        for i in range(3): slot(13 + i, n == 3 * i + 2)
        return 0
    lax.fori_loop(0, 12, tile, 0)
    slot(16)
    save("gp")
    transpose_to(act, actT, T, FF)
    save("actT")
    slot(17)
    plane(3)
    put(g.at[pl.ds(6144, 3072)], hbm["w"].at[pl.ds(6144, 3072)])
    down(act, g, vec, res, wide)
    norm_rows(res, vec[0:1, G2:G2 + D], vec[0:1, S2:S2 + D], low2, None, hat2, r2)
    save("hat2", "r2")
    out[0] = low2[0:LEN, :]
    small_weights(g, fb, p32, c32, wproj, code, wcode)
    save("wproj")
    slot(18)
    contrast(weight, low2, vec, place, placeT, allowed, choose, wproj, code, wcode, fb, p32, c32, tail, dctx, small)
    save("tail", "dctx", "small")
    slot(19)
    ga.drain()
    for cp in outs: cp.wait()

def forward(pieces, events, weight, params, x, mask, dis, cho, vec):
    V_ = pl.BlockSpec(memory_space=pltpu.VMEM)
    A_ = pl.BlockSpec(memory_space=pl.ANY)
    VM = pltpu.VMEM
    DMA = pltpu.SemaphoreType.DMA
    sds = jax.ShapeDtypeStruct
    n = params.shape[0] // 128
    most = max(len(ps) for ps in pieces) + 1
    here = [VM(*K1_SHAPE[k]) for k in K1_OUT[1:-1]] + [VM((4 * T, T), bf16)]
    outs = pl.pallas_call(functools.partial(forward_kernel, pieces, events, weight),
        out_shape=[sds(*K1_SHAPE[k]) for k in K1_OUT] + [sds((1, LEN, D), bf16)],
        in_specs=[V_] * 6, out_specs=[A_] * len(K1_OUT) + [V_],
        scratch_shapes=[VM((1, vec.shape[0]), f32), VM((GROW, D), bf16), VM((96 + 2 * n + 96, 128), f32), VM((n + 4, 128), f32), VM((4 * D, D), bf16), VM((6, 256, 128), f32)] + here
            + [VM((T, D), bf16), VM((T, D), bf16), VM((D, T), bf16), VM((T, FF), bf16), VM((LT, D), f32), VM((LT, D), f32), VM((T, D), bf16), VM((T, D), bf16),
               VM((256, T), bf16), VM((T, 256), bf16), VM((256, 256), f32), VM((2, 256, 384), f32), VM((1152, 128), f32), VM((2, 768, 128), f32), VM((3, 256, 128), f32),
               VM((256, 384), bf16), VM((256, 256), bf16),
               DMA((2,)), DMA((16, most)), DMA((16, most)), DMA((320,)), DMA((24,)), DMA((2,))],
        compiler_params=pltpu.CompilerParams(collective_id=0, has_side_effects=True, vmem_limit_bytes=63 * 2**20),
    )(params.reshape(n, 128), x, mask, jnp.transpose(dis, (2, 0, 1)), jnp.swapaxes(cho, 1, 2), vec.reshape(-1, 128))
    return dict(zip(K1_OUT, outs)), outs[-1]
TO_CORE, TO_V, TO_U, TO_Z, KEEP, SMALL = range(6)

class Reduce:
    def __init__(self, at, g, pieces, LD, LV, LZ, LU, total, RD, RV, RZ, RU, S):
        self.at, self.g, self.pieces, self.total = at, g, pieces, total
        self.LD, self.LV, self.LZ, self.LU = LD, LV, LZ, LU
        self.RD, self.RV, self.RZ, self.RU, self.S = RD, RV, RZ, RU, S
        self.index = {}
        self.made = {z: [] for z in range(PLANES)}
        self.seen = set()

    def sem(self, key):
        return self.S.at[self.index.setdefault(key, len(self.index))]

    def copies(self, key, p, r, c, first, rows, extra, land, got, dev):
        a, e = self.at.span(p, r, c, first)
        out = []
        for j, (s, n, to) in enumerate([(a, rows, first)] + [(e, EXTRA, MAIN)] * extra):
            out.append(remote(self.g.at[pl.ds(s, n)], land.at[pl.ds(to, n)], self.sem(key + (j,)), got.at[j], dev))
        return out

    def build(self, zs, op):
        at = self.at
        kind, i, p, r = op
        unit = 4 * p + at.roles[r]
        if kind == TO_CORE:
            return self.copies(op, p, r, 1 - at.c, 0, MAIN, True, self.LD.at[unit], self.RD.at[unit], (zs, at.fc))
        if kind == TO_V:
            n = 2 * p + r - 2
            return self.copies(op, p, r, at.c, 0, MAIN, True, self.LV.at[n], self.RV.at[n], (zs, at.vf))
        _, first, rows, extra = self.pieces[p][i]
        if kind == TO_U:
            return self.copies(op, p, r, at.c, first, rows, extra, self.LU.at[p], self.RU.at[p, i], (zs, at.uf))
        up = p > zs
        to = zs + 1 if up else zs - 1
        n = 8 + r if (not up and to == p) else 2 * p + r
        return self.copies(op, p, r, at.c, first, rows, extra, self.LZ.at[n], self.RZ.at[n, i], (to, at.f))

    def once(self, zs, key, cs):
        if (zs, key) not in self.seen:
            self.seen.add((zs, key))
            for q in cs: q.wait_recv()

    def send(self, zs, op):
        for q in self.build(zs, op): q.start()
        self.made[zs].append(op)

    def add(self, p, r, first, rows, extra, lands, final):
        a, e = self.at.span(p, r, self.at.c, first)
        g, total = self.g, self.total
        def one(s, i):
            v = g[pl.ds(s, 16), :].astype(f32)
            for land in lands:
                v = v + land[pl.ds(i, 16), :].astype(f32)
            if final:
                total[pl.ds(16 + i, 16), :] = v
            else:
                g[pl.ds(s, 16), :] = v.astype(bf16)
        def body(b, _):
            one(pl.multiple_of(a + 16 * b, 16), pl.multiple_of(first + 16 * b, 16))
            return 0
        lax.fori_loop(0, rows // 16, body, 0)
        if extra: one(e, MAIN)

    def op(self, zs, op):
        at = self.at
        kind, i, p, r = op
        if kind == TO_CORE:
            for rr in (2, 3, 0, 1): self.send(zs, (TO_CORE, 0, p, rr))
            return
        unit = 4 * p + at.roles[r]
        self.once(zs, (TO_CORE, p, r), self.copies((HERE,), p, r, at.c, 0, MAIN, True, self.LD.at[unit], self.RD.at[unit], (zs, at.fc)))
        if kind == TO_V:
            self.add(p, r, 0, MAIN, True, [self.LD.at[unit]], False)
            self.send(zs, op)
            return
        n = 2 * p + r
        self.once(zs, (TO_V, p, r), self.copies((HERE,), p, r, at.c, 0, MAIN, True, self.LV.at[n], self.RV.at[n], (zs, at.fc)))
        path, first, rows, extra = self.pieces[p][i]
        lands = [self.LD.at[unit], self.LV.at[n]]
        def arrived(land, got, key):
            self.once(zs, key, self.copies((HERE,), p, r, at.c, first, rows, extra, land, got, (zs, at.fc)))
            lands.append(land)
        if path == 0 or r == 0:
            if p >= zs and zs > 0: arrived(self.LZ.at[n], self.RZ.at[n, i], (UP, i, p, r))
            if p <= zs and zs < PLANES - 1:
                m = 8 + r if p == zs else n
                arrived(self.LZ.at[m], self.RZ.at[m, i], (DOWN, i, p, r))
        if r == 0 and (path == 1 or p == zs):
            arrived(self.LU.at[p], self.RU.at[p, i], (TO_U, i, p))
        self.add(p, r, first, rows, extra, lands, kind == KEEP)
        if kind != KEEP: self.send(zs, op)

    def drain(self):
        for zs in range(PLANES):
            @pl.when(self.at.z == zs)
            def _():
                for op in self.made[zs]:
                    for q in self.build(zs, op): q.wait_send()

class Spread:
    def __init__(self, at, own, land, zland, S, count):
        self.at, self.own, self.land, self.zland, self.S, self.count = at, own, land, zland, S, count

    def round(self, n, me, land, base, dev):
        return [remote(self.own, land.at[me], self.S.at[0, base + j], self.S.at[1, base + j], dev(lax.rem(me + j, n))) for j in range(1, n)]

    def plane(self):
        return self.round(self.count, self.at.f, self.land, 0, lambda t: (self.at.z, t))

    def planes(self):
        return self.round(PLANES, self.at.z, self.zland, self.count, lambda t: (t, self.at.f))

    def first(self):
        for q in self.plane(): q.start()

    def total(self, land, n, me):
        land[me] = self.own[...]
        v = land[0]
        for j in range(1, n): v = v + land[j]
        return v

    def second(self):
        for q in self.plane(): q.wait()
        self.own[...] = self.total(self.land, self.count, self.at.f)
        for q in self.planes(): q.start()

    def last(self):
        for q in self.planes(): q.wait()
        self.own[...] = self.total(self.zland, PLANES, self.at.z)

K2_IN = K1_OUT
K2_HERE = ("wproj", "dctx", "small", "hat1", "r1", "hat2", "r2", "gp", "ring", "normT", "attT", "q", "kT", "vv", "xT", "wq")

def backward_kernel(pieces, events, vec_ref, *rest):
    n_in = len(K2_IN)
    hbm = dict(zip(K2_IN, rest[:n_in]))
    (grad, vsum, sq, ig, g, vec, wproj, dctx, small, hat1, r1, hat2, r2, gp, ring, normT, attT, q, kT, vv, xT, wq,
     low1, low2, acc, tmp, dp, LD, LV, LZ, LU, total, flat, vg, vland, vzland, sqv, sland, szland,
     IS, RD, RV, RZ, RU, S, TS, VS, SS) = rest[n_in:]
    here = dict(wproj=wproj, dctx=dctx, small=small, hat1=hat1, r1=r1, hat2=hat2, r2=r2, gp=gp, normT=normT, attT=attT, q=q, kT=kT, vv=vv, xT=xT)
    loads = {}
    def load(name, src=None, dst=None):
        cp = pltpu.make_async_copy(hbm[name] if src is None else src, here[name] if dst is None else dst, IS.at[len(loads)])
        cp.start()
        loads[name if src is None else (name, len(loads))] = cp
        return cp
    w = hbm["w"]
    first = [load(n) for n in ("dctx", "wproj", "hat2", "r2")]
    second = [load("w", w.at[pl.ds(6144, 3072)], g.at[pl.ds(6144, 3072)]), load("gp"), load("actT", hbm["actT"], ring)]
    tail = load("tail", hbm["tail"], g.at[pl.ds(9216, 448)])
    third = [load("w", w.at[pl.ds(3072, 3072)], g.at[pl.ds(3072, 3072)]), load("normT")]
    fourth = [load("hat1"), load("r1"), load("small")]
    fifth = [load("w", w.at[pl.ds(2304, 768)], g.at[pl.ds(2304, 768)]), load("attT")]
    sixth = [load("q"), load("kT"), load("vv")]
    seventh = [load("xT"), load("w", w.at[pl.ds(0, 2304)], wq)]
    def ready(cs):
        for cp in cs: cp.wait()
    at = Place()
    at.greet_all(vland.shape[0])
    re = Reduce(at, g, pieces, LD, LV, LZ, LU, total, RD, RV, RZ, RU, S)
    vs = Spread(at, vg, vland, vzland, VS, vland.shape[0])
    ss = Spread(at, sqv, sland, szland, SS, vland.shape[0])
    def slot(i, cond=None):
        for zs in range(PLANES):
            if events[zs][i]:
                @pl.when((at.z == zs) if cond is None else ((at.z == zs) & cond))
                def _():
                    for e in events[zs][i]:
                        if e[0] == SMALL: (vs.first, vs.second, vs.last)[e[1]]()
                        else: re.op(zs, e)
    for i in range(vec_ref.shape[0]):
        vec[0:1, 128 * i:128 * i + 128] = vec_ref[i:i + 1, :]
    low2[...] = jnp.zeros((T, D), bf16)
    low1[...] = jnp.zeros((T, D), bf16)
    for t in range(3):
        dp[t] = jnp.zeros((T, D), bf16)
    ready(first)
    norm_back_first(dctx, wproj, vec[0:1, G2:G2 + D], hat2, r2, low2, acc)
    put_vec(vg, acc, (G2, S2, BDOWN))
    ready(second)
    lax.fori_loop(0, 12, lambda n, _: (down_back(n, low2, g, ring, gp, vg), 0)[1], 0)
    ready([tail])
    shared_blocks(g, 3, True)
    def head(h):
        return pltpu.make_async_copy(hbm["pT"].at[pl.ds(pl.multiple_of(h * T, T), T)], ring.at[pl.ds(pl.multiple_of((h % 6) * T, T), T)], TS.at[h % 6])
    for h in range(6): head(h).start()
    slot(1)
    ready(third)
    lax.fori_loop(0, 3, lambda n, _: (up_back_x(n, gp, g, hat2), 0)[1], 0)
    slot(2)
    def woven(n, _):
        weave(normT, gp, 4, 2 - n, 3072, g, tmp, False)
        slot(3, n == 0)
        slot(4, n == 1)
        return 0
    lax.fori_loop(0, 2, woven, 0)
    shared_blocks(g, 2, True)
    slot(5)
    lax.fori_loop(2, 3, woven, 0)
    slot(6)
    ready(fourth)
    norm_back(hat2, vec[0:1, G1:G1 + D], hat1, r1, low1, acc)
    put_vec(vg, acc, (G1, S1, BO))
    ready(fifth)
    da, dqT = low2, normT
    out_back(low1, g, attT, da)
    shared_blocks(g, 1, True)
    slot(7)
    slot(8)
    ready(sixth)
    def pair(p, _):
        head(2 * p).wait()
        head(2 * p + 1).wait()
        attend_back(p, da, q, kT, vv, ring, dp, dqT)
        @pl.when(p < 3)
        def _():
            head(2 * p + 6).start()
            head(2 * p + 7).start()
        for i in range(6): slot(9 + i, p == i)
        return 0
    lax.fori_loop(0, 6, pair, 0)
    ready(seventh)
    def wove(n, _):
        weave(xT, dp, 3, n, 0, g, tmp, True)
        for i in range(3): slot(15 + i, n == i)
        return 0
    lax.fori_loop(0, 3, wove, 0)
    shared_blocks(g, 0, True)
    slot(18)
    vg[0:1, BQ:BQ + D] = jnp.sum(dp[0].astype(f32), axis=0, keepdims=True)
    vg[0:1, BV:BV + D] = jnp.sum(dp[2].astype(f32), axis=0, keepdims=True)
    vg[0:1, BPROJ:BPROJ + 256] = small[0:1, :]
    vg[0:1, BCODE:BCODE + 256] = small[1:2, :]
    vg[0:1, BCODE + 256:BCODE + 512] = small[2:3, :]
    slot(19)
    slot(20)
    for n in range(3):
        input_back(n, dp, wq, hat1, ig)
    slot(21)
    z, c, k = at.z, at.c, at.k
    edge = remote(total.at[pl.ds(HALF, 16)], total.at[pl.ds(0, 16)], TS.at[6], TS.at[7], (z, at.fc))
    edge.start()
    vsum[...] = vg[...]
    edge.wait()
    part = jnp.zeros((8, 128), f32)
    n = grad.shape[0] // 6
    for j in range(6):
        flat[pl.ds(j, 320, stride=6), :] = total[:, 128 * j:128 * j + 128]
    for j in range(6):
        v = flat[pl.ds(6 * (16 - 2 * c - 4 * k) + j, n, stride=6), :]
        grad[pl.ds(j, n, stride=6), :] = v
        v = v * v
        part = part + sum8(v[0:n // 8 * 8])
        if n % 8: part = part + jnp.concatenate([v[n // 8 * 8:], jnp.zeros((8 - n % 8, 128), f32)], axis=0)
    sqv[...] = part
    ss.first()
    ss.second()
    ss.last()
    sq[...] = sqv[...]
    re.drain()

def backward(pieces, events, vec, hbm, count, n):
    V_ = pl.BlockSpec(memory_space=pltpu.VMEM)
    A_ = pl.BlockSpec(memory_space=pl.ANY)
    VM = pltpu.VMEM
    DMA = pltpu.SemaphoreType.DMA
    sds = jax.ShapeDtypeStruct
    most = max(len(ps) for ps in pieces)
    nv = vec.shape[0] + 256
    shape = dict(K1_SHAPE, ring=((FF, T), bf16), wq=((3 * D, D), bf16))
    return pl.pallas_call(functools.partial(backward_kernel, pieces, events),
        out_shape=[sds((n, 128), f32), sds((1, nv), f32), sds((8, 128), f32), sds((1, LEN, D), f32)],
        in_specs=[V_] + [A_] * len(K2_IN), out_specs=[V_] * 4,
        scratch_shapes=[VM((GROW, D), bf16), VM((1, vec.shape[0]), f32)] + [VM(*shape[k]) for k in K2_HERE]
            + [VM((T, D), bf16), VM((T, D), bf16), VM((24, D), f32), VM((2, 1024, 128), f32), VM((3, T, D), bf16),
               VM((16, HALF, D), bf16), VM((8, HALF, D), bf16), VM((10, HALF, D), bf16), VM((4, HALF, D), bf16), VM((HALF + 16, D), f32), VM((6 * (HALF + 16), 128), f32),
               VM((1, nv), f32), VM((count, 1, nv), f32), VM((PLANES, 1, nv), f32), VM((8, 128), f32), VM((count, 8, 128), f32), VM((PLANES, 8, 128), f32),
               DMA((24,)), DMA((16, 2)), DMA((8, 2)), DMA((10, most, 2)), DMA((4, most, 2)), DMA((200,)), DMA((8,)), DMA((2, count + PLANES)), DMA((2, count + PLANES))],
        compiler_params=pltpu.CompilerParams(collective_id=1, has_side_effects=True, vmem_limit_bytes=63 * 2**20),
    )(vec.reshape(-1, 128), *[hbm[k] for k in K2_IN])

PIECES_OUT = (((1, 0, 64, False), (1, 64, 64, False), (1, 128, 80, False), (1, 208, 80, True)), ((0, 0, 80, False), (1, 80, 112, False), (1, 192, 96, True)),
 ((0, 0, 96, False), (0, 96, 96, False), (0, 192, 96, True)), ((0, 0, 112, False), (0, 112, 96, False), (1, 208, 80, True)))
PIECES_BACK = (((0, 0, 80, False), (0, 80, 64, False), (1, 144, 80, False), (1, 224, 64, True)),
 ((0, 0, 80, False), (0, 80, 64, False), (1, 144, 80, False), (1, 224, 64, True)),
 ((0, 0, 80, False), (0, 80, 64, False), (1, 144, 80, False), (1, 224, 64, True)), ((0, 0, 208, False), (1, 208, 80, True)))
SENDS_OUT = ((((0, 0, 0, 0), (2, 0, 0, 0), (2, 1, 0, 0), (0, 1, 0, 0), (2, 2, 0, 0)),
  ((4, 0, 0, 1), (4, 1, 0, 1), (0, 2, 0, 0), (2, 3, 0, 0), (4, 2, 0, 1), (3, 0, 0, 0), (4, 0, 1, 0), (0, 3, 0, 0), (3, 1, 0, 0), (3, 2, 0, 0),
   (3, 3, 0, 0), (4, 3, 0, 1), (4, 0, 0, 2), (3, 0, 0, 1), (4, 1, 0, 2), (4, 1, 1, 0), (3, 1, 0, 1), (4, 2, 0, 2), (3, 2, 0, 1), (3, 3, 0, 1),
   (4, 3, 0, 2), (4, 0, 0, 3), (4, 2, 1, 0), (2, 1, 1, 0), (4, 1, 0, 3), (2, 2, 1, 0), (4, 2, 0, 3), (4, 0, 1, 1), (4, 3, 0, 3), (3, 0, 1, 0),
   (3, 1, 1, 0), (4, 1, 1, 1), (4, 0, 2, 0)),
  ((4, 2, 1, 1), (4, 0, 1, 2), (3, 2, 1, 0), (4, 1, 2, 0), (3, 0, 1, 1)),
  ((4, 1, 1, 2), (4, 2, 1, 2), (3, 1, 1, 1), (4, 0, 1, 3), (3, 2, 1, 1), (4, 2, 2, 0)), (), ((4, 0, 2, 1), (3, 0, 2, 0)),
  ((4, 1, 1, 3), (3, 1, 2, 0)), ((4, 2, 1, 3), (4, 1, 2, 1), (3, 2, 2, 0)), ((4, 0, 2, 2), (3, 0, 2, 1)), ((4, 1, 2, 2), (3, 1, 2, 1)),
  ((4, 2, 2, 2), (4, 2, 2, 1), (3, 2, 2, 1)), ((4, 0, 2, 3), (4, 1, 2, 3), (4, 2, 2, 3), (4, 0, 3, 0), (3, 0, 3, 0), (4, 1, 3, 0), (3, 1, 3, 0)),
  ((4, 0, 3, 2), (4, 2, 3, 0), (4, 1, 3, 2), (2, 2, 3, 0), (3, 2, 3, 0)), (), ((4, 0, 3, 1), (3, 0, 3, 1), (4, 2, 3, 1), (3, 2, 3, 1)),
  ((4, 2, 3, 2), (4, 1, 3, 1), (3, 1, 3, 1)), ((4, 0, 3, 3),), ((4, 2, 3, 3), (4, 1, 3, 3)), (), ()),
 (((0, 0, 1, 0), (1, 0, 1, 0), (2, 0, 1, 0), (2, 1, 1, 0)),
  ((4, 0, 0, 0), (0, 0, 0, 0), (2, 0, 0, 0), (3, 0, 0, 0), (4, 0, 1, 1), (4, 1, 1, 1), (0, 1, 1, 0), (1, 1, 1, 0), (2, 2, 1, 0), (4, 0, 2, 0),
   (4, 1, 0, 0), (2, 1, 0, 0), (1, 2, 1, 0), (4, 0, 0, 1), (3, 1, 0, 0), (4, 0, 0, 2), (0, 1, 0, 0), (3, 0, 0, 1), (4, 2, 0, 0), (4, 1, 2, 0),
   (2, 2, 0, 0), (4, 2, 1, 1), (0, 2, 0, 0), (1, 0, 1, 1), (3, 2, 0, 0), (4, 1, 0, 1), (4, 3, 0, 0), (4, 1, 0, 2), (2, 3, 0, 0), (0, 3, 0, 0),
   (4, 0, 0, 3), (1, 0, 2, 0), (4, 2, 2, 0), (3, 1, 0, 1), (4, 2, 0, 1), (3, 3, 0, 0), (4, 2, 0, 2), (0, 2, 1, 0), (1, 1, 2, 0), (3, 2, 0, 1),
   (4, 0, 2, 1), (4, 3, 0, 1), (3, 3, 0, 1), (4, 1, 0, 3), (3, 0, 1, 0), (1, 2, 2, 0), (4, 1, 2, 1), (0, 0, 1, 1), (4, 3, 0, 2), (3, 1, 1, 0),
   (4, 2, 0, 3), (3, 2, 1, 0), (4, 3, 0, 3), (1, 0, 2, 1), (4, 2, 2, 1), (4, 0, 1, 2), (3, 0, 1, 1)),
  ((4, 1, 1, 2), (4, 2, 1, 2), (3, 1, 1, 1), (1, 1, 2, 1), (3, 2, 1, 1), (4, 0, 3, 0)),
  ((4, 0, 1, 3), (4, 1, 1, 3), (1, 2, 2, 1), (3, 0, 2, 0), (3, 1, 2, 0), (4, 1, 3, 0), (4, 2, 1, 3), (4, 2, 3, 0)), (), ((3, 2, 2, 0), (1, 0, 3, 0)),
  ((4, 0, 2, 2), (3, 0, 2, 1), (4, 0, 3, 1)), ((4, 1, 2, 2), (3, 1, 2, 1), (1, 1, 3, 0), (3, 2, 2, 1)),
  ((4, 2, 2, 2), (4, 0, 2, 3), (4, 1, 3, 1), (1, 2, 3, 0), (2, 2, 3, 0)), ((4, 1, 2, 3), (3, 0, 3, 0)), ((4, 2, 2, 3), (1, 0, 3, 1), (3, 1, 3, 0)),
  ((4, 2, 3, 1), (4, 0, 3, 2), (1, 1, 3, 1), (4, 1, 3, 2), (3, 2, 3, 0), (3, 0, 3, 1)), ((3, 1, 3, 1),), ((4, 2, 3, 2), (3, 2, 3, 1)),
  ((4, 0, 3, 3),), ((4, 1, 3, 3),), ((4, 2, 3, 3),), (), (), ()),
 (((0, 0, 2, 0), (1, 0, 2, 0), (2, 0, 2, 0), (2, 1, 2, 0)),
  ((4, 0, 1, 0), (0, 0, 1, 0), (3, 0, 1, 0), (4, 0, 2, 1), (4, 1, 2, 1), (1, 1, 2, 0), (2, 2, 2, 0), (4, 0, 3, 0), (0, 1, 2, 0), (3, 0, 2, 0),
   (1, 2, 2, 0), (3, 1, 2, 0), (4, 0, 1, 2), (4, 0, 0, 0), (0, 0, 0, 0), (4, 1, 3, 0), (2, 0, 0, 0), (4, 2, 2, 1), (1, 0, 2, 1), (3, 0, 0, 0),
   (0, 2, 2, 0), (4, 0, 2, 2), (3, 2, 2, 0), (4, 1, 1, 0), (4, 2, 3, 0), (4, 1, 2, 2), (2, 1, 1, 0), (1, 1, 2, 1), (4, 0, 0, 1), (4, 1, 0, 0),
   (0, 1, 0, 0), (4, 0, 0, 2), (2, 1, 0, 0), (4, 0, 3, 1), (3, 0, 0, 1), (0, 1, 1, 0), (1, 2, 2, 1), (4, 2, 2, 2), (4, 2, 0, 0), (2, 2, 0, 0),
   (3, 1, 0, 0), (4, 1, 1, 1), (4, 1, 3, 1), (3, 2, 0, 0), (4, 1, 0, 1), (4, 3, 0, 0), (0, 2, 0, 0), (1, 0, 3, 0), (4, 0, 0, 3), (2, 3, 0, 0),
   (4, 2, 0, 1), (3, 1, 0, 1), (0, 3, 0, 0), (4, 1, 0, 2), (3, 3, 0, 0), (4, 2, 1, 0), (1, 1, 3, 0), (4, 2, 0, 2), (3, 2, 0, 1), (4, 3, 0, 1),
   (0, 2, 1, 0), (4, 0, 1, 1), (3, 3, 0, 1), (4, 1, 0, 3), (1, 2, 3, 0), (2, 2, 1, 0), (4, 3, 0, 2), (0, 0, 1, 1), (3, 1, 1, 0), (4, 2, 0, 3),
   (1, 0, 3, 1), (4, 3, 0, 3), (3, 1, 1, 1), (0, 0, 2, 1), (4, 2, 1, 1), (3, 2, 1, 0)),
  ((4, 1, 1, 2), (3, 0, 1, 1), (3, 2, 1, 1), (0, 1, 2, 1), (4, 1, 1, 3), (1, 1, 3, 1)),
  ((4, 2, 1, 2), (4, 0, 1, 3), (0, 2, 2, 1), (3, 0, 2, 1), (4, 2, 1, 3), (3, 1, 2, 1)), (), ((3, 2, 2, 1),), ((4, 0, 2, 3), (2, 2, 3, 0)),
  ((4, 1, 2, 3), (3, 0, 3, 0)), ((4, 2, 2, 3), (3, 1, 3, 0)), ((4, 2, 3, 1), (3, 2, 3, 0)), ((4, 0, 3, 2), (3, 0, 3, 1)),
  ((4, 1, 3, 2), (4, 2, 3, 2), (4, 0, 3, 3), (3, 1, 3, 1), (3, 2, 3, 1)), (), ((4, 1, 3, 3),), ((4, 2, 3, 3),), (), (), (), (), ()),
 (((1, 0, 3, 0), (2, 0, 3, 0)),
  ((4, 0, 3, 1), (1, 1, 3, 0), (2, 1, 3, 0), (2, 2, 3, 0), (4, 0, 2, 0), (1, 2, 3, 0), (3, 0, 2, 0), (3, 0, 3, 0), (4, 1, 3, 1), (1, 0, 3, 1),
   (4, 0, 1, 0), (3, 0, 1, 0), (4, 2, 3, 1), (3, 1, 3, 0), (4, 0, 2, 2), (4, 1, 2, 0), (3, 1, 2, 0), (1, 1, 3, 1), (4, 0, 3, 2), (3, 2, 3, 0),
   (4, 0, 1, 2), (4, 0, 0, 0), (2, 0, 0, 0), (4, 1, 3, 2), (3, 0, 0, 0), (4, 1, 2, 2), (3, 0, 3, 1), (4, 2, 2, 0), (4, 2, 3, 2), (3, 2, 2, 0),
   (4, 0, 0, 1), (4, 1, 0, 0), (4, 0, 0, 2), (2, 1, 0, 0), (3, 0, 0, 1), (4, 0, 3, 3), (3, 1, 0, 0), (4, 1, 1, 0), (2, 1, 1, 0), (4, 2, 2, 2),
   (4, 1, 0, 1), (3, 1, 0, 1), (4, 2, 0, 0), (4, 0, 0, 3), (2, 2, 0, 0), (4, 1, 0, 2), (3, 2, 0, 0), (4, 3, 0, 0), (4, 1, 1, 1), (2, 3, 0, 0),
   (4, 1, 0, 3), (3, 3, 0, 0), (4, 2, 0, 1), (3, 2, 0, 1), (4, 2, 1, 0), (4, 2, 0, 2), (2, 2, 1, 0), (4, 3, 0, 1), (4, 0, 1, 1), (3, 3, 0, 1),
   (4, 3, 0, 2), (3, 1, 1, 0), (4, 2, 0, 3), (4, 0, 2, 1), (3, 1, 1, 1), (4, 2, 1, 1), (4, 3, 0, 3), (3, 2, 1, 0), (4, 1, 2, 1), (4, 1, 1, 2),
   (3, 0, 1, 1)),
  ((4, 1, 1, 3), (3, 2, 1, 1)), ((4, 2, 1, 2), (4, 0, 1, 3), (4, 2, 1, 3), (4, 2, 2, 1), (3, 0, 2, 1), (3, 1, 2, 1)), (), ((3, 2, 2, 1),),
  ((4, 0, 2, 3), (3, 1, 3, 1)), ((4, 1, 2, 3), (3, 2, 3, 1)), ((4, 2, 2, 3),), ((4, 1, 3, 3),), ((4, 2, 3, 3),), (), (), (), (), (), (), (), (), ()))
SENDS_BACK = (((), ((0, 0, 3, 0),), (), ((1, 0, 3, 2), (1, 0, 3, 3)), (), ((0, 0, 2, 0),), (), ((3, 0, 3, 0), (1, 0, 2, 2), (1, 0, 2, 3), (3, 0, 3, 1)),
  ((0, 0, 1, 0),), ((2, 1, 3, 1),), ((3, 0, 2, 0), (1, 0, 1, 2), (3, 1, 2, 0)), ((1, 0, 1, 3),), ((3, 1, 3, 0), (3, 0, 2, 1), (2, 2, 2, 1)),
  ((3, 1, 2, 1), (2, 3, 2, 1)), ((3, 0, 1, 0),), ((3, 1, 1, 0),), ((3, 0, 1, 1), (2, 2, 1, 1), (2, 3, 1, 1)), ((3, 2, 2, 0),), ((0, 0, 0, 0),), (),
  ((5, 0, 0, 0), (3, 3, 2, 0)),
  ((3, 1, 1, 1), (1, 0, 0, 2), (3, 2, 1, 0), (1, 0, 0, 3), (5, 1, 0, 0), (3, 3, 1, 0), (2, 2, 0, 1), (2, 3, 0, 1), (2, 0, 0, 1), (2, 1, 0, 1),
   (5, 2, 0, 0), (4, 0, 0, 0), (4, 2, 0, 0), (4, 1, 0, 0), (4, 3, 0, 0))),
 ((), ((0, 0, 3, 0),), (), ((1, 0, 3, 2), (1, 0, 3, 3)), (), ((0, 0, 2, 0),), (), ((1, 0, 2, 2), (1, 0, 2, 3)), ((0, 0, 1, 0),), ((2, 1, 3, 1),),
  ((1, 0, 1, 2),), ((3, 0, 3, 0), (1, 0, 1, 3)), (), ((2, 2, 2, 1), (3, 0, 3, 1), (2, 3, 2, 1)), ((3, 0, 2, 0),), ((3, 1, 2, 0),), (),
  ((3, 1, 3, 0), (2, 2, 1, 1), (2, 3, 1, 1)), ((0, 0, 0, 0), (3, 0, 2, 1)), (), ((5, 0, 0, 0),),
  ((3, 1, 2, 1), (1, 0, 0, 2), (1, 0, 0, 3), (2, 0, 1, 1), (3, 2, 2, 0), (3, 3, 2, 0), (5, 1, 0, 0), (2, 1, 1, 1), (2, 2, 0, 1), (2, 3, 0, 1),
   (4, 0, 1, 0), (4, 2, 1, 0), (4, 1, 1, 0), (4, 3, 1, 0), (5, 2, 0, 0), (3, 0, 0, 0), (3, 1, 0, 0), (3, 0, 0, 1), (3, 1, 0, 1), (3, 2, 0, 0),
   (3, 3, 0, 0))),
 ((), ((0, 0, 3, 0),), (), ((1, 0, 3, 2), (1, 0, 3, 3)), (), ((0, 0, 2, 0),), (), ((1, 0, 2, 2), (1, 0, 2, 3)), ((0, 0, 1, 0),), ((2, 1, 3, 1),),
  ((1, 0, 1, 2),), (), ((1, 0, 1, 3),), ((2, 2, 2, 1),), ((2, 3, 2, 1),), ((3, 0, 3, 0),), (), (),
  ((0, 0, 0, 0), (3, 0, 1, 0), (2, 2, 1, 1), (2, 3, 1, 1)), (), ((5, 0, 0, 0), (3, 0, 3, 1), (3, 1, 1, 0), (1, 0, 0, 2)),
  ((3, 0, 1, 1), (3, 1, 1, 1), (1, 0, 0, 3), (3, 1, 3, 0), (2, 0, 2, 1), (2, 1, 2, 1), (5, 1, 0, 0), (3, 2, 1, 0), (2, 2, 0, 1), (2, 3, 0, 1),
   (4, 0, 2, 0), (3, 3, 1, 0), (4, 1, 2, 0), (4, 2, 2, 0), (3, 0, 0, 0), (5, 2, 0, 0), (4, 3, 2, 0), (3, 1, 0, 0), (3, 0, 0, 1), (3, 1, 0, 1),
   (3, 2, 0, 0), (3, 3, 0, 0))),
 ((), ((0, 0, 3, 0),), (), ((1, 0, 3, 2), (1, 0, 3, 3)), (), ((0, 0, 2, 0),), (), ((1, 0, 2, 2), (1, 0, 2, 3)), ((0, 0, 1, 0),), ((2, 1, 3, 1),),
  ((1, 0, 1, 2), (3, 0, 2, 0), (3, 1, 2, 0)), ((1, 0, 1, 3),), ((3, 0, 2, 1), (3, 1, 2, 1)), ((2, 2, 2, 1), (2, 3, 2, 1)),
  ((3, 0, 1, 0), (3, 1, 1, 0)), (), (), ((3, 0, 1, 1), (3, 1, 1, 1), (3, 2, 2, 0), (2, 2, 1, 1), (2, 3, 1, 1)), ((0, 0, 0, 0), (3, 3, 2, 0)), (),
  ((5, 0, 0, 0),),
  ((3, 2, 1, 0), (3, 3, 1, 0), (1, 0, 0, 2), (1, 0, 0, 3), (2, 0, 3, 1), (5, 1, 0, 0), (4, 1, 3, 0), (3, 0, 0, 0), (3, 1, 0, 0), (3, 0, 0, 1),
   (3, 1, 0, 1), (5, 2, 0, 0), (2, 2, 0, 1), (2, 3, 0, 1), (4, 0, 3, 0), (3, 2, 0, 0), (3, 3, 0, 0))))

def unpack(flat_values):
    shapes = [(D, 3 * D), (D, D), (D, FF), (FF, D), (D, FINAL), (G * CD, V), (G * CD, FINAL)]
    pieces = []
    offset = 0
    for height, width in shapes:
        pieces.append(flat_values[offset : offset + height * width].reshape(height, width))
        offset = offset + height * width
    return pieces


def split_vectors(vector_all):
    lengths = [D, D, D, D, D, FF, D, D, D, FINAL, FINAL]
    pieces = []
    offset = 0
    for length in lengths:
        pieces.append(vector_all[offset : offset + length])
        offset = offset + length
    return pieces


def layer_norm(values, scale_gain, shift_bias):
    centered = values - jnp.mean(values, axis=-1, keepdims=True)
    variance = jnp.mean(centered * centered, axis=-1, keepdims=True)
    return centered * lax.rsqrt(variance + eps_norm) * scale_gain + shift_bias


def contrast_dense(chosen, targets, distract, weight):
    hi = dict(precision=lax.Precision.HIGHEST)
    frames = jnp.arange(MASKED, dtype=jnp.int32)
    allowed = jnp.any(distract[:, :, None] == frames, axis=1) | (frames[:, None] == frames)

    def agreement(chosen, targets):
        left = chosen * lax.rsqrt(jnp.sum(chosen * chosen, axis=-1, keepdims=True) + eps_cos)
        right = targets * lax.rsqrt(jnp.sum(targets * targets, axis=-1, keepdims=True) + eps_cos)
        return jnp.einsum("by,oy->bo", left, right, **hi) / softness_divisor

    similar, back = jax.vjp(agreement, chosen, targets)
    same = frames[:, None] == frames
    positive = jnp.sum(jnp.where(same, similar, 0.0), axis=1)
    top = jnp.max(jnp.where(allowed, similar, -jnp.inf), axis=1)
    parts = jnp.where(allowed, jnp.exp(similar - top[:, None]), 0.0)
    total = jnp.sum(parts, axis=1)
    loss = jnp.sum(top + jnp.log(total) - positive)
    d_similar = weight * (parts / total[:, None] - same.astype(jnp.float32))
    return (loss,) + back(d_similar)


def adamw_update(master, first_moment, second, gradient, step_rate):
    first_new = beta_one * first_moment + (1.0 - beta_one) * gradient
    second_new = beta_two * second + (1.0 - beta_two) * gradient * gradient
    first_hat = first_new / (1.0 - beta_one**STEP)
    second_hat = second_new / (1.0 - beta_two**STEP)
    master_new = master * (1.0 - step_rate * decay_rate) - step_rate * first_hat / (
        jnp.sqrt(second_hat) + adam_eps
    )
    return (master_new, first_new, second_new)


def column_sum(values):
    return jnp.sum(values.astype(jnp.float32), axis=tuple(range(values.ndim - 1)))


def by_collectives(
    layer_input,
    mask_index,
    distract,
    code_choice,
    params,
    moment_one,
    moment_two,
    vectors,
    vector_one,
    vector_two,
):
    bf16 = jnp.bfloat16
    f32 = jnp.float32
    count_utts = layer_input.shape[0]
    total_masked = count_utts * lax.axis_size(("dp", "fsdp")) * MASKED
    token_rows = count_utts * LEN
    gathered = lax.all_gather(params.astype(bf16), ("dp", "fsdp"), axis=0, tiled=True)
    qkv_weight, out_weight, up_weight, down_weight, proj_weight, codebook, code_weight = unpack(
        gathered
    )
    (
        bias_query,
        bias_value,
        bias_out,
        gain_one,
        shift_one,
        bias_up,
        bias_down,
        gain_two,
        shift_two,
        bias_proj,
        bias_code,
    ) = split_vectors(vectors)
    inputs = layer_input.reshape(token_rows, D)
    projected = jnp.dot(inputs, qkv_weight, preferred_element_type=f32)
    query_heads = (projected[:, :D] + bias_query).astype(bf16).reshape(count_utts, LEN, H, HD)
    key_heads = projected[:, D : 2 * D].astype(bf16).reshape(count_utts, LEN, H, HD)
    value_heads = (projected[:, 2 * D :] + bias_value).astype(bf16).reshape(count_utts, LEN, H, HD)
    scores = (
        jnp.einsum("blhe,bmhe->bhlm", query_heads, key_heads, preferred_element_type=f32) * 0.125
    )
    attn_probs = jax.nn.softmax(scores, axis=-1)
    probs_low = attn_probs.astype(bf16)
    attended = jnp.einsum("bhlm,bmhe->blhe", probs_low, value_heads, preferred_element_type=f32)
    attended = attended.astype(bf16).reshape(token_rows, D)
    residual_one = (
        inputs.astype(f32) + jnp.dot(attended, out_weight, preferred_element_type=f32) + bias_out
    )
    normed, back_one = jax.vjp(layer_norm, residual_one, gain_one, shift_one)
    normed_low = normed.astype(bf16)
    hidden = jnp.dot(normed_low, up_weight, preferred_element_type=f32) + bias_up
    active, gelu_back = jax.vjp(functools.partial(jax.nn.gelu, approximate=False), hidden)
    active_low = active.astype(bf16)
    residual_two = normed + jnp.dot(active_low, down_weight, preferred_element_type=f32) + bias_down
    output, back_two = jax.vjp(layer_norm, residual_two, gain_two, shift_two)
    output_low = output.astype(bf16)
    place = (mask_index[0][:, None] == jnp.arange(LEN, dtype=jnp.int32)).astype(bf16)
    picked = jnp.dot(place, output_low, preferred_element_type=f32).astype(bf16)
    chosen = jnp.dot(picked, proj_weight, preferred_element_type=f32) + bias_proj
    choose = (code_choice[..., None] == jnp.arange(V, dtype=jnp.int32)).astype(bf16)
    code_vectors = jnp.einsum(
        "bmgv,gcv->bmgc", choose, codebook.reshape(G, CD, V), preferred_element_type=f32
    )
    code_vectors = code_vectors.astype(bf16).reshape(count_utts, MASKED, G * CD)
    targets = (
        jnp.einsum("bmc,cf->bmf", code_vectors, code_weight, preferred_element_type=f32) + bias_code
    )
    loss_local, d_chosen, d_targets = contrast_dense(chosen, targets[0], distract[0], 1.0 / total_masked)
    d_targets = d_targets[None]
    d_targets_low = d_targets.astype(bf16)
    quantized_offset_slope = column_sum(d_targets_low)
    d_code_weight = jnp.einsum(
        "bmc,bmf->cf", code_vectors, d_targets_low, preferred_element_type=f32
    )
    d_code_vectors = jnp.einsum(
        "bmf,cf->bmc", d_targets_low, code_weight, preferred_element_type=f32
    )
    d_codebook = jnp.einsum(
        "bmgc,bmgv->gcv",
        d_code_vectors.reshape(count_utts, MASKED, G, CD),
        choose.astype(f32),
        precision=lax.Precision.HIGHEST,
    ).reshape(G * CD, V)
    d_chosen_low = d_chosen.astype(bf16)
    d_bias_proj = column_sum(d_chosen_low)
    d_proj_weight = jnp.einsum("td,tf->df", picked, d_chosen_low, preferred_element_type=f32)
    d_context_low = jnp.einsum("mt,mf->tf", place, d_chosen_low, preferred_element_type=f32).astype(bf16)
    result_sensitivity = jnp.einsum(
        "tf,df->td", d_context_low, proj_weight, preferred_element_type=f32
    )
    d_residual_two, d_gain_two, d_shift_two = back_two(result_sensitivity)
    d_second_low = d_residual_two.astype(bf16)
    d_bias_down = column_sum(d_second_low)
    d_down_weight = jnp.einsum("th,td->hd", active_low, d_second_low, preferred_element_type=f32)
    d_active = jnp.einsum("td,hd->th", d_second_low, down_weight, preferred_element_type=f32)
    (d_hidden,) = gelu_back(d_active)
    d_hidden_low = d_hidden.astype(bf16)
    d_bias_up = column_sum(d_hidden_low)
    d_up_weight = jnp.einsum("td,th->dh", normed_low, d_hidden_low, preferred_element_type=f32)
    d_normed = d_residual_two + jnp.einsum(
        "th,dh->td", d_hidden_low, up_weight, preferred_element_type=f32
    )
    d_residual_one, d_gain_one, d_shift_one = back_one(d_normed)
    d_branch_low = d_residual_one.astype(bf16)
    d_bias_out = column_sum(d_branch_low)
    d_out_weight = jnp.einsum("td,te->de", attended, d_branch_low, preferred_element_type=f32)
    d_attended = jnp.einsum("te,de->td", d_branch_low, out_weight, preferred_element_type=f32)
    d_attended = d_attended.astype(bf16).reshape(count_utts, LEN, H, HD)
    d_value = jnp.einsum("bhlm,blhe->bmhe", probs_low, d_attended, preferred_element_type=f32)
    d_probs = jnp.einsum("blhe,bmhe->bhlm", d_attended, value_heads, preferred_element_type=f32)
    d_scores = (
        attn_probs * (d_probs - jnp.sum(attn_probs * d_probs, axis=-1, keepdims=True))
    ).astype(bf16)
    d_query = jnp.einsum("bhlm,bmhe->blhe", d_scores, key_heads, preferred_element_type=f32) * 0.125
    d_key = jnp.einsum("bhlm,blhe->bmhe", d_scores, query_heads, preferred_element_type=f32) * 0.125
    d_projected = jnp.concatenate(
        [
            d_query.reshape(token_rows, D),
            d_key.reshape(token_rows, D),
            d_value.reshape(token_rows, D),
        ],
        axis=1,
    ).astype(bf16)
    d_sums = column_sum(d_projected)
    d_qkv_weight = jnp.einsum("td,te->de", inputs, d_projected, preferred_element_type=f32)
    input_grad = d_residual_one + jnp.einsum(
        "te,de->td", d_projected, qkv_weight, preferred_element_type=f32
    )
    flat_grad = jnp.concatenate(
        [
            matrix_grad.reshape(-1)
            for matrix_grad in (
                d_qkv_weight,
                d_out_weight,
                d_up_weight,
                d_down_weight,
                d_proj_weight,
                d_codebook,
                d_code_weight,
            )
        ]
    )
    vector_gradient = jnp.concatenate(
        [
            d_sums[:D],
            d_sums[2 * D :],
            d_bias_out,
            d_gain_one,
            d_shift_one,
            d_bias_up,
            d_bias_down,
            d_gain_two,
            d_shift_two,
            d_bias_proj,
            quantized_offset_slope,
        ]
    )
    vector_sum, loss_sum = lax.psum((vector_gradient, loss_local), ("dp", "fsdp"))
    grad_shard = lax.psum_scatter(flat_grad, ("dp", "fsdp"), scatter_dimension=0, tiled=True)
    square_sum = lax.psum(jnp.sum(grad_shard * grad_shard), ("dp", "fsdp"))
    return finish(
        total_masked, square_sum, vector_sum, loss_sum, grad_shard, output_low.reshape(count_utts, LEN, D),
        input_grad.reshape(count_utts, LEN, D), params, moment_one, moment_two, vectors, vector_one, vector_two,
    )


def finish(total_masked, square_sum, vector_sum, loss_sum, grad_shard, output, input_grad, params, moment_one, moment_two, vectors, vector_one, vector_two):
    grad_norm = jnp.sqrt(square_sum + jnp.sum(vector_sum * vector_sum))
    factor = jnp.minimum(1.0, clip_level / (grad_norm + 1e-06))
    refreshed_weights, new_one, new_two = adamw_update(params, moment_one, moment_two, grad_shard * factor, rate_matrix)
    new_vectors, new_vector_first, new_vector_second = adamw_update(vectors, vector_one, vector_two, vector_sum * factor, rate_vector)
    return (
        loss_sum / total_masked,
        grad_norm,
        output,
        input_grad,
        refreshed_weights,
        refreshed_weights.astype(bf16),
        new_one,
        new_two,
        new_vectors,
        new_vector_first,
        new_vector_second,
    )


def by_kernels(layer_input, mask_index, distract, code_choice, params, moment_one, moment_two, vectors, vector_one, vector_two):
    total_masked = layer_input.shape[0] * lax.axis_size(("dp", "fsdp")) * MASKED
    kept, output = forward(PIECES_OUT, SENDS_OUT, 1.0 / total_masked, params, layer_input, mask_index, distract, code_choice, vectors)
    grads, sums, squares, input_grad = backward(PIECES_BACK, SENDS_BACK, vectors, kept, lax.axis_size("fsdp"), params.shape[0] // 128)
    sums = sums.reshape(-1)
    return finish(
        total_masked, jnp.sum(squares), sums[: vectors.shape[0]], sums[vectors.shape[0]], grads.reshape(-1), output, input_grad,
        params, moment_one, moment_two, vectors, vector_one, vector_two,
    )


def solution(mesh):
    in_specs = (
        P(("dp", "fsdp"), None, None),
        P(("dp", "fsdp"), None),
        P(("dp", "fsdp"), None, None),
        P(("dp", "fsdp"), None, None),
        P(("dp", "fsdp")),
        P(("dp", "fsdp")),
        P(("dp", "fsdp")),
        P(),
        P(),
        P(),
    )
    out_specs = (
        P(),
        P(),
        P(("dp", "fsdp"), None, None),
        P(("dp", "fsdp"), None, None),
        P(("dp", "fsdp")),
        P(("dp", "fsdp")),
        P(("dp", "fsdp")),
        P(("dp", "fsdp")),
        P(),
        P(),
        P(),
    )
    fits = mesh.shape["dp"] == PLANES and mesh.shape["fsdp"] == 8
    return jax.shard_map(
        by_kernels if fits else by_collectives, mesh=mesh, in_specs=in_specs, out_specs=out_specs, check_vma=False
    )
```

```python
import functools

import jax
import jax.numpy as jnp
from jax import lax
from jax.experimental import pallas as pl
from jax.experimental.pallas import tpu as pltpu
from jax.sharding import PartitionSpec as P
D = 768; H = 12; HD = 64; FF = 3072; FINAL = 256; G = 2; V = 320; CD = 128; LEN = 472; MASKED = 232
NROW = 9664; GROW = NROW + 256
T = 512
LT = 480
bf16 = jnp.bfloat16
f32 = jnp.float32
NT = (((1,), (1,)), ((), ()))
BQ, BV, BO, G1, S1, BUP, BDOWN, G2, S2, BPROJ, BCODE = [768 * i for i in range(6)] + [3840 + 3072 + 768 * i for i in range(3)] + [9216, 9472]

def mm(a, b):
    return jnp.dot(a, b, preferred_element_type=f32)

def mm_nt(a, b, precision=None):
    return lax.dot_general(a, b, NT, preferred_element_type=f32, precision=precision)

def hi(a, b):
    return jnp.dot(a, b, preferred_element_type=f32, precision=lax.Precision.HIGHEST)

def split_rows(g, base, parts, nice, first, tmp):
    def body(b, _):
        src = pl.multiple_of(base + b * 64 * parts, 64)
        for j in range(6):
            tmp[j, 0:64 * parts, :] = g[pl.ds(src, 64 * parts), 128 * j:128 * j + 128].astype(f32)
        for t in range(parts):
            at = pl.multiple_of((first + t) * D + b * 64, 64)
            for j in range(6):
                nice[pl.ds(at, 64), 128 * j:128 * j + 128] = tmp[j, pl.ds(t, 64, stride=parts), :].astype(bf16)
        return 0
    lax.fori_loop(0, D // 64, body, 0)

def norm_rows(r, gain, shift, low, wide, hat, rstd):
    def body(b, _):
        at = pl.multiple_of(b * 48, 16)
        v = r[pl.ds(at, 48), :]
        m = jnp.mean(v, axis=-1, keepdims=True)
        c = v - m
        var = jnp.mean(c * c, axis=-1, keepdims=True)
        inv = lax.rsqrt(var + eps_norm)
        xh = c * inv
        o = xh * gain + shift
        hat[pl.ds(at, 48), :] = xh
        rstd[pl.ds(at, 48), :] = jnp.broadcast_to(inv, (48, 128))
        if wide is not None:
            wide[pl.ds(at, 48), :] = o
        low[pl.ds(at, 48), :] = o.astype(bf16)
        return 0
    lax.fori_loop(0, LT // 48, body, 0)

def transpose_to(src, dst, rows, cols):
    def body(n, _):
        at = pl.multiple_of(n * 128, 128)
        dst[pl.ds(at, 128), :] = src[:, pl.ds(at, 128)].T
        return 0
    lax.fori_loop(0, cols // 128, body, 0)

def prepare(x_ref, xp, xT, mask_ref, distract_ref, choice_ref, vec_ref, vec, place, placeT, allowed, choose):
    for i in range(vec_ref.shape[0]):
        vec[0:1, 128 * i:128 * i + 128] = vec_ref[i:i + 1, :]
    xp[...] = jnp.zeros((T, D), bf16)
    xp[0:LEN, :] = x_ref[0]
    transpose_to(xp, xT, T, D)
    zero = jnp.zeros((1, 256 - MASKED), jnp.int32) - 1
    def wide(row):
        return jnp.concatenate([row, zero], axis=1)
    hot = jnp.where(lax.broadcasted_iota(jnp.int32, (T, 256), 0) == wide(mask_ref[...]), 1.0, 0.0)
    placeT[...] = hot.astype(bf16)
    place[...] = hot.T.astype(bf16)
    row = lax.broadcasted_iota(jnp.int32, (256, 256), 0)
    col = lax.broadcasted_iota(jnp.int32, (256, 256), 1)
    allowed[...] = jnp.where((row == col) & (col < MASKED), 1.0, 0.0)
    rows = [wide(distract_ref[i]) for i in range(distract_ref.shape[0])]
    def body(b, _):
        at = pl.multiple_of(8 * b, 8)
        acc = allowed[pl.ds(at, 8), :]
        n = lax.broadcasted_iota(jnp.int32, (8, 256), 0) + at
        for r in rows:
            acc = jnp.where(n == r, 1.0, acc)
        allowed[pl.ds(at, 8), :] = acc
        return 0
    lax.fori_loop(0, MASKED // 8, body, 0)
    allowed[...] = allowed[...].T
    for g in range(2):
        v = jnp.where(lax.broadcasted_iota(jnp.int32, (384, 256), 0) == wide(choice_ref[0, g:g + 1, :]), 1.0, 0.0)
        choose[g] = v.T

def project(xp, nice, vec, q, kk, kT, vv, vT):
    for t, (dst, bias) in enumerate(((q, BQ), (kk, None), (vv, BV))):
        for n in range(3):
            acc = mm(xp[...], nice[t * D:(t + 1) * D, 256 * n:256 * n + 256])
            if bias is not None:
                acc = acc + vec[0:1, bias + 256 * n:bias + 256 * n + 256]
            dst[:, 256 * n:256 * n + 256] = acc.astype(bf16)
    transpose_to(kk, kT, T, D)
    transpose_to(vv, vT, T, D)

def attend(p, q, kk, vT, pT, attT):
    at = pl.multiple_of(128 * p, 128)
    qp = q[:, pl.ds(at, 128)]
    kp = kk[0:LT, pl.ds(at, 128)]
    lane = lax.broadcasted_iota(jnp.int32, (LT, 128), 1)
    for h in range(2):
        kh = jnp.where((lane < 64) == (h == 0), kp, jnp.zeros_like(kp))
        s = mm_nt(kh, qp)[0:LEN] * 0.125
        e = jnp.exp(s - jnp.max(s, axis=0, keepdims=True))
        pr = e * (1.0 / jnp.sum(e, axis=0, keepdims=True))
        pr = jnp.concatenate([pr, jnp.zeros((T - LEN, T), f32)], axis=0).astype(bf16)
        pT[pl.ds(pl.multiple_of((2 * (p % 2) + h) * T, T), T), :] = pr
        rows = pl.ds(pl.multiple_of(128 * p + 64 * h, 64), 64)
        attT[rows, :] = mm(vT[rows, :], pr).astype(bf16)

def out_project(attT, att, xp, wo, vec, res):
    for n in range(6):
        att[:, 128 * n:128 * n + 128] = attT[128 * n:128 * n + 128, :].T
    for n in range(3):
        cols = slice(256 * n, 256 * n + 256)
        acc = mm(att[0:LT, :], wo[:, cols])
        res[:, cols] = xp[0:LT, cols].astype(f32) + acc + vec[0:1, BO + 256 * n:BO + 256 * n + 256]

def up(n, norm_low, nice, vec, act, gp):
    root = 0.7071067811865476
    scale = 0.3989422804014327
    c = n // 3
    w = nice[pl.ds(pl.multiple_of(c * D, D), D), pl.ds(pl.multiple_of((n - 3 * c) * 256, 256), 256)]
    at = pl.multiple_of(n * 256, 256)
    h = mm(norm_low[0:LT, :], w) + vec[0:1, pl.ds(pl.multiple_of(BUP + n * 256, 256), 256)]
    cdf = 0.5 * (1.0 + lax.erf(h * root))
    act[0:LT, pl.ds(at, 256)] = (h * cdf).astype(bf16)
    gp[0:LT, pl.ds(at, 256)] = (cdf + h * (scale * jnp.exp(-0.5 * h * h))).astype(bf16)

def down(act, g, vec, res, wide):
    for n in range(3):
        cols = slice(256 * n, 256 * n + 256)
        acc = mm(act[0:LT, :], g[6144:9216, cols])
        res[:, cols] = wide[:, cols] + acc + vec[0:1, BDOWN + 256 * n:BDOWN + 256 * n + 256]

def small_weights(g, fb, p32, c32, wproj, code, wcode):
    for t in range(3):
        for j in range(2):
            p32[j, pl.ds(t, 256, stride=3), :] = g[9216:9472, 256 * t + 128 * j:256 * t + 128 * j + 128].astype(f32)
    for j in range(2):
        wproj[:, 128 * j:128 * j + 128] = p32[j].astype(bf16)
    for j in range(6):
        fb[pl.ds(j, 192, stride=6), :] = g[9472:9664, 128 * j:128 * j + 128].astype(f32)
    a = [fb[pl.ds(j, 128, stride=5), :] for j in range(5)]
    lo = lax.broadcasted_iota(jnp.int32, (128, 128), 1) < 64
    r2, r3, r4 = [pltpu.roll(v, 64, 1) for v in a[2:]]
    zero = jnp.zeros((128, 128), f32)
    even = [a[0], a[1], jnp.where(lo, a[2], zero)]
    odd = [jnp.where(lo, r2, r3), jnp.where(lo, r3, r4), jnp.where(lo, r4, zero)]
    for j in range(3):
        c32[j, pl.ds(0, 128, stride=2), :] = even[j]
        c32[j, pl.ds(1, 128, stride=2), :] = odd[j]
        code[:, 128 * j:128 * j + 128] = c32[j].astype(bf16)
    for j in range(2):
        wcode[:, 128 * j:128 * j + 128] = fb[pl.ds(640 + j, 256, stride=2), :].astype(bf16)

def contrast(weight, out_low, vec, place, placeT, allowed, choose, wproj, code, wcode, fb, p32, c32, tail, dctx, small):
    picked = mm(place[...], out_low[...]).astype(bf16)
    chosen = mm(picked, wproj[...]) + vec[0:1, BPROJ:BPROJ + 256]
    cv = jnp.concatenate([mm_nt(choose[g].astype(bf16), code[128 * g:128 * g + 128, :]) for g in range(2)], axis=1).astype(bf16)
    targets = mm(cv, wcode[...]) + vec[0:1, BCODE:BCODE + 256]
    n_l = lax.rsqrt(jnp.sum(chosen * chosen, axis=1, keepdims=True) + eps_cos)
    n_r = lax.rsqrt(jnp.sum(targets * targets, axis=1, keepdims=True) + eps_cos)
    left = chosen * n_l
    right = targets * n_r
    sim = mm_nt(left, right, lax.Precision.HIGHEST) / 0.1
    ok = allowed[...] > 0.5
    row = lax.broadcasted_iota(jnp.int32, (256, 256), 0)
    col = lax.broadcasted_iota(jnp.int32, (256, 256), 1)
    eye = jnp.where((row == col) & (row < MASKED), 1.0, 0.0)
    pos = jnp.sum(eye * sim, axis=1, keepdims=True)
    top = jnp.max(jnp.where(ok, sim, -1e30), axis=1, keepdims=True)
    parts = jnp.where(ok, jnp.exp(jnp.minimum(sim - top, 0.0)), 0.0)
    real = lax.broadcasted_iota(jnp.int32, (256, 1), 0) < MASKED
    total = jnp.where(real, jnp.sum(parts, axis=1, keepdims=True), 1.0)
    loss = jnp.sum(jnp.where(real, top + jnp.log(total) - pos, 0.0))
    dsim = (weight / 0.1) * (parts / total - eye)
    dl = hi(dsim, right)
    dr = hi(dsim.T, left)
    d_chosen = (n_l * dl - chosen * (n_l * n_l * n_l) * jnp.sum(chosen * dl, axis=1, keepdims=True)).astype(bf16)
    d_target = (n_r * dr - targets * (n_r * n_r * n_r) * jnp.sum(targets * dr, axis=1, keepdims=True)).astype(bf16)
    small[0:1, :] = jnp.sum(d_chosen.astype(f32), axis=0, keepdims=True)
    small[1:2, :] = jnp.sum(d_target.astype(f32), axis=0, keepdims=True)
    small[2:3, :] = jnp.broadcast_to(loss, (1, 256))
    dctx[...] = mm(placeT[...], d_chosen).astype(bf16)
    dproj = mm(picked.T, d_chosen)
    for j in range(2):
        p32[j] = dproj[:, 128 * j:128 * j + 128]
    for t in range(3):
        for j in range(2):
            tail[0:256, 256 * t + 128 * j:256 * t + 128 * j + 128] = p32[j, pl.ds(t, 256, stride=3), :].astype(bf16)
    dwcode = mm(cv.T, d_target)
    dcv = mm_nt(d_target, wcode[...])
    for g in range(2):
        dc = hi(dcv[:, 128 * g:128 * g + 128].T, choose[g])
        for j in range(3):
            c32[j, 128 * g:128 * g + 128, :] = dc[:, 128 * j:128 * j + 128]
    e = [c32[j, pl.ds(0, 128, stride=2), :] for j in range(3)]
    o = [pltpu.roll(c32[j, pl.ds(1, 128, stride=2), :], 64, 1) for j in range(3)]
    lo = lax.broadcasted_iota(jnp.int32, (128, 128), 1) < 64
    for j, v in enumerate((e[0], e[1], jnp.where(lo, e[2], o[0]), jnp.where(lo, o[0], o[1]), jnp.where(lo, o[1], o[2]))):
        fb[pl.ds(j, 128, stride=5), :] = v
    for j in range(2):
        fb[pl.ds(640 + j, 256, stride=2), :] = dwcode[:, 128 * j:128 * j + 128]
    for j in range(6):
        tail[256:448, 128 * j:128 * j + 128] = fb[pl.ds(j, 192, stride=6), :].astype(bf16)
STEP = 10


eps_norm = 1e-05
eps_cos = 1e-06
softness_divisor = 0.1
beta_one = 0.9
beta_two = 0.98
adam_eps = 1e-08
decay_rate = 0.01
rate_matrix = 0.03
rate_vector = 0.2
clip_level = 0.001


def sum8(v):
    r, n = v.shape
    return jnp.sum(v.reshape(r // 8, 8, n), axis=0)

def norm_back_first(dctx, wproj, gain, hat, rstd, low, acc):
    acc[...] = jnp.zeros((24, D), f32)
    def body(b, _):
        at = pl.multiple_of(b * 48, 16)
        dy = mm_nt(dctx[pl.ds(at, 48), :], wproj[...])
        norm_back_rows(dy, at, gain, hat, hat, rstd, low, acc)
        return 0
    lax.fori_loop(0, LT // 48, body, 0)

def norm_back_rows(dy, at, gain, hat, dst, rstd, low, acc):
    xh = hat[pl.ds(at, 48), :]
    inv = rstd[pl.ds(at, 48), 0:1]
    a = dy * gain
    m1 = jnp.mean(a, axis=-1, keepdims=True)
    m2 = jnp.mean(a * xh, axis=-1, keepdims=True)
    dr = inv * (a - m1 - xh * m2)
    lo = dr.astype(bf16)
    dst[pl.ds(at, 48), :] = dr
    low[pl.ds(at, 48), :] = lo
    acc[0:8, :] += sum8(dy * xh)
    acc[8:16, :] += sum8(dy)
    acc[16:24, :] += sum8(lo.astype(f32))

def norm_back(dy, gain, hat, rstd, low, acc):
    acc[...] = jnp.zeros((24, D), f32)
    def body(b, _):
        at = pl.multiple_of(b * 48, 16)
        norm_back_rows(dy[pl.ds(at, 48), :], at, gain, hat, hat, rstd, low, acc)
        return 0
    lax.fori_loop(0, LT // 48, body, 0)

def put_vec(vg, acc, offsets):
    for i, o in enumerate(offsets):
        vg[0:1, o:o + D] = jnp.sum(acc[8 * i:8 * i + 8, :], axis=0, keepdims=True)

def down_back(n, low2, gg, actT, gp, vg):
    at = pl.multiple_of(n * 256, 256)
    rows = pl.ds(pl.multiple_of(6144 + n * 256, 256), 256)
    d = mm_nt(low2[0:LT, :], gg[rows, :]) * gp[0:LT, pl.ds(at, 256)].astype(f32)
    d = d.astype(bf16)
    gp[0:LT, pl.ds(at, 256)] = d
    vg[0:1, pl.ds(pl.multiple_of(BUP + at, 128), 256)] = jnp.sum(d.astype(f32), axis=0, keepdims=True)
    gg[rows, :] = mm(actT[pl.ds(at, 256), :], low2[...]).astype(bf16)

def up_back_x(n, dh, gg, dr):
    cols = pl.ds(pl.multiple_of(n * 256, 256), 256)
    v = dr[:, cols]
    for c in range(4):
        w = gg[pl.ds(pl.multiple_of(3072 + c * D + n * 256, 256), 256), :]
        v = v + mm_nt(dh[0:LT, c * D:(c + 1) * D], w)
    dr[:, cols] = v

def weave(lhsT, rhs, parts, n, base, gg, tmp, stacked):
    def body(m, _):
        cols = pl.ds(pl.multiple_of(m * 256, 256), 256)
        for t in range(parts):
            r = rhs[t, :, cols] if stacked else rhs[:, pl.ds(pl.multiple_of(t * D + m * 256, 256), 256)]
            acc = mm(lhsT[pl.ds(pl.multiple_of(n * 256, 256), 256), :], r)
            for j in range(2):
                tmp[j, pl.ds(t, 256, stride=parts), :] = acc[:, 128 * j:128 * j + 128]
        for j in range(2):
            gg[pl.ds(pl.multiple_of(base + n * 256 * parts, 256), 256 * parts), pl.ds(pl.multiple_of(m * 256 + 128 * j, 128), 128)] = tmp[j, 0:256 * parts, :].astype(bf16)
        return 0
    lax.fori_loop(0, 3, body, 0)

def out_back(low1, gg, attT, da):
    for n in range(3):
        cols = slice(256 * n, 256 * n + 256)
        da[0:LT, cols] = mm_nt(low1[0:LT, :], gg[2304 + 256 * n:2304 + 256 * n + 256, :]).astype(bf16)
    for n in range(3):
        gg[2304 + 256 * n:2304 + 256 * n + 256, :] = mm(attT[256 * n:256 * n + 256, :], low1[...]).astype(bf16)

def attend_back(p, da, q, kT, vv, ring, dp, dqT):
    at = pl.multiple_of(128 * p, 128)
    lane = lax.broadcasted_iota(jnp.int32, (T, 128), 1)
    dap = da[:, pl.ds(at, 128)]
    qp = q[:, pl.ds(at, 128)]
    vp = vv[0:LT, pl.ds(at, 128)]
    dk = dv = None
    for h in range(2):
        half = (lane < 64) == (h == 0)
        dah = jnp.where(half, dap, jnp.zeros_like(dap))
        qh = jnp.where(half, qp, jnp.zeros_like(qp))
        pr = ring[pl.ds(pl.multiple_of(((2 * p + h) % 6) * T, T), LT), :]
        dpT = mm_nt(vp, dah)
        prf = pr.astype(f32)
        w = prf * dpT
        ds = (w - prf * jnp.sum(w, axis=0, keepdims=True)).astype(bf16)
        a = mm(pr, dah)
        b = mm(ds, qh)
        dv = a if dv is None else dv + a
        dk = b if dk is None else dk + b
        rows = pl.ds(pl.multiple_of(128 * p + 64 * h, 64), 64)
        dqT[rows, :] = (mm(kT[rows, 0:LT], ds) * 0.125).astype(bf16)
    dp[1, 0:LT, pl.ds(at, 128)] = (dk * 0.125).astype(bf16)
    dp[2, 0:LT, pl.ds(at, 128)] = dv.astype(bf16)
    dp[0, :, pl.ds(at, 128)] = dqT[pl.ds(at, 128), :].T

def input_back(n, dp, wq, dr, out):
    cols = slice(256 * n, 256 * n + 256)
    v = dr[:, cols]
    for t in range(3):
        v = v + mm_nt(dp[t, 0:LT, :], wq[t * D + 256 * n:t * D + 256 * n + 256, :])
    out[0, :, cols] = v[0:LEN]
MESH = pl.DeviceIdType.MESH
UP, DOWN, U, V_AXIS, CORE, HERE = range(6)
PLANES = 4
MAIN = 288
EXTRA = 16
HALF = MAIN + EXTRA
PLANE = 2416
UNIT = 608

class Place:
    def __init__(self):
        self.z = lax.axis_index("dp")
        self.f = f = lax.axis_index("fsdp")
        self.c = c = f % 2
        self.k = k = f // 2
        x = k % 2
        y = k // 2
        self.fc = f + 1 - 2 * c
        self.fx = f + 2 - 4 * x
        self.fy = f + 4 - 8 * y
        self.uf = self.fx * (1 - c) + self.fy * c
        self.vf = self.fy * (1 - c) + self.fx * c
        self.roles = (k, self.uf // 2, self.vf // 2, 3 - k)

    def greet(self):
        z = self.z
        bar = pltpu.get_barrier_semaphore()
        for t in (self.fc, self.fx, self.fy):
            pl.semaphore_signal(bar, inc=1, device_id=(z, t), device_id_type=MESH)
        @pl.when(z > 0)
        def _(): pl.semaphore_signal(bar, inc=1, device_id=(z - 1, self.f), device_id_type=MESH)
        @pl.when(z < PLANES - 1)
        def _(): pl.semaphore_signal(bar, inc=1, device_id=(z + 1, self.f), device_id_type=MESH)
        pl.semaphore_wait(bar, 3 + (z + PLANES - 1) // PLANES + (2 * PLANES - 2 - z) // PLANES)

    def greet_all(self, count):
        bar = pltpu.get_barrier_semaphore()
        for j in range(1, count):
            pl.semaphore_signal(bar, inc=1, device_id=(self.z, lax.rem(self.f + j, count)), device_id_type=MESH)
        for j in range(1, PLANES):
            pl.semaphore_signal(bar, inc=1, device_id=(lax.rem(self.z + j, PLANES), self.f), device_id_type=MESH)
        pl.semaphore_wait(bar, count + PLANES - 2)

    def span(self, p, r, c, first):
        kk = self.roles[r]
        m = PLANE * p + UNIT * kk
        return (pl.multiple_of(m + HALF * c + first, 16),
                pl.multiple_of((m + MAIN) * (1 - c) + (NROW + EXTRA * (4 * p + kk)) * c, 16))

def remote(src, dst, ssem, rsem, dev):
    return pltpu.make_async_remote_copy(src_ref=src, dst_ref=dst, send_sem=ssem, recv_sem=rsem, device_id=dev, device_id_type=MESH)

def shared_blocks(g, p, out):
    row = lax.broadcasted_iota(jnp.int32, (16, D), 0)
    if out:
        b = [g[PLANE * p + 16 * q:PLANE * p + 16 * q + 16, :].astype(f32) for q in (37, 75, 113)]
        for q, v in enumerate((b[0], jnp.where(row < 8, b[1], b[0]), jnp.where(row < 4, b[2], b[1]), b[2])):
            g[NROW + 16 * (4 * p + q):NROW + 16 * (4 * p + q) + 16, :] = v.astype(bf16)
    else:
        e = [g[NROW + 16 * (4 * p + q):NROW + 16 * (4 * p + q) + 16, :].astype(f32) for q in range(4)]
        for q, bound in enumerate((12, 8, 4)):
            at = PLANE * p + UNIT * q + 592
            g[at:at + 16, :] = jnp.where(row < bound, e[q], e[q + 1]).astype(bf16)

class Gather:
    def __init__(self, at, g, pieces, R, O, S):
        self.at, self.g, self.pieces, self.R, self.O, self.S = at, g, pieces, R, O, S
        self.index = {}
        self.made = {z: [] for z in range(PLANES)}
        self.seen = set()

    def sem(self, key):
        return self.S.at[self.index.setdefault(key, len(self.index))]

    def copies(self, i, p, r, dev, kind, c):
        _, first, rows, extra = self.pieces[p][i]
        a, e = self.at.span(p, r, c, first)
        unit = 4 * p + self.at.roles[r]
        got = self.O if kind == CORE else self.R
        out = []
        for j, (s, n) in enumerate([(a, rows)] + [(e, EXTRA)] * extra):
            ref = self.g.at[pl.ds(s, n)]
            out.append(remote(ref, ref, self.sem((HERE, j) if kind == HERE else (kind, i, p, r, j)), got.at[unit, i + j], dev))
        return out

    def op(self, zs, kind, i, p, r):
        at = self.at
        if not (p == zs and r == 0) and (zs, i, p, r) not in self.seen:
            self.seen.add((zs, i, p, r))
            for q in self.copies(i, p, r, (zs, at.fc), HERE, at.c): q.wait_recv()
        dev = ((zs + 1, at.f), (zs - 1, at.f), (zs, at.uf), (zs, at.vf), (zs, at.fc))[kind]
        for q in self.copies(i, p, r, dev, kind, at.c): q.start()
        self.made[zs].append((kind, i, p, r))

    def other_core(self, zs, p):
        for r in range(4):
            if p == zs and r == 0: continue
            for i in range(len(self.pieces[p])):
                for q in self.copies(i, p, r, (zs, self.at.fc), CORE, 1 - self.at.c): q.wait_recv()

    def drain(self):
        for zs in range(PLANES):
            @pl.when(self.at.z == zs)
            def _():
                for kind, i, p, r in self.made[zs]:
                    for q in self.copies(i, p, r, (zs, self.at.fc), kind, self.at.c): q.wait_send()

def own_rows(at, g, p_ref, raw, land, sem):
    n = p_ref.shape[0]
    copy = remote(p_ref.at[pl.ds(0, n)], land.at[pl.ds(0, n)], sem.at[0], sem.at[1], (at.z, at.fc))
    copy.start()
    @pl.when(at.c == 0)
    def _(): raw[96:96 + n, :] = p_ref[...]
    @pl.when(at.c == 1)
    def _(): raw[96 + n:96 + 2 * n, :] = p_ref[...]
    copy.wait()
    @pl.when(at.c == 1)
    def _(): raw[96:96 + n, :] = land[0:n]
    @pl.when(at.c == 0)
    def _(): raw[96 + n:96 + 2 * n, :] = land[0:n]
    k = at.k
    own = pl.multiple_of(PLANE * at.z + UNIT * k, 16)
    extra = pl.multiple_of(NROW + EXTRA * (4 * at.z + k), 16)
    row = lax.broadcasted_iota(jnp.int32, (16, 128), 0)
    for j in range(6):
        cols = slice(128 * j, 128 * j + 128)
        g[pl.ds(own, 592), cols] = raw[pl.ds(96 + 24 * k + j, 592, stride=6), :].astype(bf16)
        last = raw[pl.ds(96 + (592 + 4 * k) * 6 + j, 16, stride=6), :]
        first = raw[pl.ds(24 * k + j, 16, stride=6), :]
        g[pl.ds(extra, 16), cols] = jnp.where(row < 12 - 4 * k, last, first).astype(bf16)

K1_OUT = ("w", "wproj", "tail", "dctx", "small", "hat1", "r1", "hat2", "r2", "gp", "actT", "normT", "attT", "q", "kT", "vv", "xT", "pT")
K1_SHAPE = {"w": ((NROW, D), bf16), "wproj": ((D, 256), bf16), "tail": ((448, D), bf16), "dctx": ((T, 256), bf16), "small": ((8, 256), f32),
            "hat1": ((LT, D), f32), "r1": ((LT, 128), f32), "hat2": ((LT, D), f32), "r2": ((LT, 128), f32), "gp": ((T, FF), bf16), "actT": ((FF, T), bf16),
            "normT": ((D, T), bf16), "attT": ((D, T), bf16), "q": ((T, D), bf16), "kT": ((D, T), bf16), "vv": ((T, D), bf16), "xT": ((D, T), bf16),
            "pT": ((H * T, T), bf16)}

def forward_kernel(pieces, events, weight, p_ref, x, mask, dis, cho, vec_ref, *rest):
    n_out = len(K1_OUT)
    hbm = dict(zip(K1_OUT, rest[:n_out]))
    (out, vec, g, raw, land, nice, tmp, wproj, tail, dctx, small, hat1, r1, hat2, r2, gp, actT, normT, attT, q, kT, vv, xT, pT,
     xp, kk, vT, act, res, wide, low1, low2, place, placeT, allowed, choose, fb, p32, c32, code, wcode,
     sem_raw, R, O, S, OS, PS) = rest[n_out:]
    here = dict(wproj=wproj, tail=tail, dctx=dctx, small=small, hat1=hat1, r1=r1, hat2=hat2, r2=r2, gp=gp, actT=actT, normT=normT, attT=attT, q=q, kT=kT, vv=vv, xT=xT, pT=pT)
    outs = []
    count = iter(range(32))
    def put(src, dst):
        cp = pltpu.make_async_copy(src, dst, OS.at[next(count)])
        cp.start()
        outs.append(cp)
    def save(*names):
        for n in names: put(here[n], hbm[n])
    at = Place()
    ga = Gather(at, g, pieces, R, O, S)
    at.greet()
    own_rows(at, g, p_ref, raw, land, sem_raw)
    def slot(i, cond=None):
        for zs in range(PLANES):
            if events[zs][i]:
                @pl.when((at.z == zs) if cond is None else ((at.z == zs) & cond))
                def _():
                    for e in events[zs][i]: ga.op(zs, *e)
    def plane(p):
        for zs in range(PLANES):
            @pl.when(at.z == zs)
            def _(): ga.other_core(zs, p)
        shared_blocks(g, p, False)
    slot(0)
    prepare(x, xp, xT, mask, dis, cho, vec_ref, vec, place, placeT, allowed, choose)
    act[LT:T, :] = jnp.zeros((T - LT, FF), bf16)
    gp[LT:T, :] = jnp.zeros((T - LT, FF), bf16)
    low1[...] = jnp.zeros((T, D), bf16)
    low2[...] = jnp.zeros((T, D), bf16)
    small[...] = jnp.zeros((8, 256), f32)
    save("xT")
    slot(1)
    plane(0)
    split_rows(g, 0, 3, nice, 0, tmp)
    slot(2)
    project(xp, nice, vec, q, kk, kT, vv, vT)
    save("q", "kT", "vv")
    put(nice.at[pl.ds(0, 2304)], hbm["w"].at[pl.ds(0, 2304)])
    nice_out = outs.pop()
    slot(3)
    slot(4)
    def pair_out(p):
        b = p % 2
        return pltpu.make_async_copy(pT.at[pl.ds(pl.multiple_of(2 * T * b, T), 2 * T)], hbm["pT"].at[pl.ds(pl.multiple_of(2 * T * p, T), 2 * T)], PS.at[b])
    def pair(p, _):
        @pl.when(p >= 2)
        def _(): pair_out(p - 2).wait()
        attend(p, q, kk, vT, pT, attT)
        pair_out(p).start()
        for i in range(6): slot(5 + i, p == i)
        return 0
    lax.fori_loop(0, H // 2, pair, 0)
    pair_out(H // 2 - 2).wait()
    pair_out(H // 2 - 1).wait()
    save("attT")
    plane(1)
    out_project(attT, kk, xp, g.at[2304:3072], vec, res)
    put(g.at[pl.ds(2304, 768)], hbm["w"].at[pl.ds(2304, 768)])
    norm_rows(res, vec[0:1, G1:G1 + D], vec[0:1, S1:S1 + D], low1, wide, hat1, r1)
    save("hat1", "r1")
    transpose_to(low1, normT, T, D)
    save("normT")
    slot(11)
    plane(2)
    nice_out.wait()
    split_rows(g, 3072, 4, nice, 0, tmp)
    put(nice, hbm["w"].at[pl.ds(3072, 3072)])
    slot(12)
    def tile(n, _):
        up(n, low1, nice, vec, act, gp)
        for i in range(3): slot(13 + i, n == 3 * i + 2)
        return 0
    lax.fori_loop(0, 12, tile, 0)
    slot(16)
    save("gp")
    transpose_to(act, actT, T, FF)
    save("actT")
    slot(17)
    plane(3)
    put(g.at[pl.ds(6144, 3072)], hbm["w"].at[pl.ds(6144, 3072)])
    down(act, g, vec, res, wide)
    norm_rows(res, vec[0:1, G2:G2 + D], vec[0:1, S2:S2 + D], low2, None, hat2, r2)
    save("hat2", "r2")
    out[0] = low2[0:LEN, :]
    small_weights(g, fb, p32, c32, wproj, code, wcode)
    save("wproj")
    slot(18)
    contrast(weight, low2, vec, place, placeT, allowed, choose, wproj, code, wcode, fb, p32, c32, tail, dctx, small)
    save("tail", "dctx", "small")
    slot(19)
    ga.drain()
    for cp in outs: cp.wait()

def forward(pieces, events, weight, params, x, mask, dis, cho, vec):
    V_ = pl.BlockSpec(memory_space=pltpu.VMEM)
    A_ = pl.BlockSpec(memory_space=pl.ANY)
    VM = pltpu.VMEM
    DMA = pltpu.SemaphoreType.DMA
    sds = jax.ShapeDtypeStruct
    n = params.shape[0] // 128
    most = max(len(ps) for ps in pieces) + 1
    keys = len({e + (j,) for z in events for s in z for e in s for j in range(1 + pieces[e[2]][e[1]][3])})
    here = [VM(*K1_SHAPE[k]) for k in K1_OUT[1:-1]] + [VM((4 * T, T), bf16)]
    outs = pl.pallas_call(functools.partial(forward_kernel, pieces, events, weight),
        out_shape=[sds(*K1_SHAPE[k]) for k in K1_OUT] + [sds((1, LEN, D), bf16)],
        in_specs=[V_] * 6, out_specs=[A_] * len(K1_OUT) + [V_],
        scratch_shapes=[VM((1, vec.shape[0]), f32), VM((GROW, D), bf16), VM((96 + 2 * n + 96, 128), f32), VM((n + 4, 128), f32), VM((4 * D, D), bf16), VM((6, 256, 128), f32)] + here
            + [VM((T, D), bf16), VM((T, D), bf16), VM((D, T), bf16), VM((T, FF), bf16), VM((LT, D), f32), VM((LT, D), f32), VM((T, D), bf16), VM((T, D), bf16),
               VM((256, T), bf16), VM((T, 256), bf16), VM((256, 256), f32), VM((2, 256, 384), f32), VM((1152, 128), f32), VM((2, 768, 128), f32), VM((3, 256, 128), f32),
               VM((256, 384), bf16), VM((256, 256), bf16),
               DMA((2,)), DMA((16, most)), DMA((16, most)), DMA((keys + 2,)), DMA((24,)), DMA((2,))],
        compiler_params=pltpu.CompilerParams(collective_id=0, has_side_effects=True, vmem_limit_bytes=63 * 2**20),
    )(params.reshape(n, 128), x, mask, jnp.transpose(dis, (2, 0, 1)), jnp.swapaxes(cho, 1, 2), vec.reshape(-1, 128))
    return dict(zip(K1_OUT, outs)), outs[-1]
TO_CORE, TO_V, TO_U, TO_Z, KEEP, SMALL = range(6)

class Reduce:
    def __init__(self, at, g, pieces, LD, LV, LZ, LU, total, RD, RV, RZ, RU, S):
        self.at, self.g, self.pieces, self.total = at, g, pieces, total
        self.LD, self.LV, self.LZ, self.LU = LD, LV, LZ, LU
        self.RD, self.RV, self.RZ, self.RU, self.S = RD, RV, RZ, RU, S
        self.index = {}
        self.made = {z: [] for z in range(PLANES)}
        self.seen = set()

    def sem(self, key):
        return self.S.at[self.index.setdefault(key, len(self.index))]

    def copies(self, key, p, r, c, first, rows, extra, land, got, dev):
        a, e = self.at.span(p, r, c, first)
        out = []
        for j, (s, n, to) in enumerate([(a, rows, first)] + [(e, EXTRA, MAIN)] * extra):
            out.append(remote(self.g.at[pl.ds(s, n)], land.at[pl.ds(to, n)], self.sem(key + (j,)), got.at[j], dev))
        return out

    def build(self, zs, op):
        at = self.at
        kind, i, p, r = op
        unit = 4 * p + at.roles[r]
        if kind == TO_CORE:
            return self.copies(op, p, r, 1 - at.c, 0, MAIN, True, self.LD.at[unit], self.RD.at[unit], (zs, at.fc))
        _, first, rows, extra = self.pieces[p][i]
        if kind == TO_V:
            n = 2 * p + r - 2
            return self.copies(op, p, r, at.c, first, rows, extra, self.LV.at[n], self.RV.at[n, i], (zs, at.vf))
        if kind == TO_U:
            return self.copies(op, p, r, at.c, first, rows, extra, self.LU.at[p], self.RU.at[p, i], (zs, at.uf))
        up = p > zs
        to = zs + 1 if up else zs - 1
        n = 8 + r if (not up and to == p) else 2 * p + r
        return self.copies(op, p, r, at.c, first, rows, extra, self.LZ.at[n], self.RZ.at[n, i], (to, at.f))

    def once(self, zs, key, cs):
        if (zs, key) not in self.seen:
            self.seen.add((zs, key))
            for q in cs: q.wait_recv()

    def send(self, zs, op):
        for q in self.build(zs, op): q.start()
        self.made[zs].append(op)

    def add(self, p, r, first, rows, extra, lands, final):
        a, e = self.at.span(p, r, self.at.c, first)
        g, total = self.g, self.total
        def one(s, i):
            v = g[pl.ds(s, 16), :].astype(f32)
            for land in lands:
                v = v + land[pl.ds(i, 16), :].astype(f32)
            if final:
                total[pl.ds(16 + i, 16), :] = v
            else:
                g[pl.ds(s, 16), :] = v.astype(bf16)
        def body(b, _):
            one(pl.multiple_of(a + 16 * b, 16), pl.multiple_of(first + 16 * b, 16))
            return 0
        lax.fori_loop(0, rows // 16, body, 0)
        if extra: one(e, MAIN)

    def op(self, zs, op):
        at = self.at
        kind, i, p, r = op
        if kind == TO_CORE:
            for rr in (2, 3, 0, 1): self.send(zs, (TO_CORE, 0, p, rr))
            return
        unit = 4 * p + at.roles[r]
        self.once(zs, (TO_CORE, p, r), self.copies((HERE,), p, r, at.c, 0, MAIN, True, self.LD.at[unit], self.RD.at[unit], (zs, at.fc)))
        path, first, rows, extra = self.pieces[p][i]
        if kind == TO_V:
            self.add(p, r, first, rows, extra, [self.LD.at[unit]], False)
            self.send(zs, op)
            return
        n = 2 * p + r
        self.once(zs, ("v", i, p, r), self.copies((HERE,), p, r, at.c, first, rows, extra, self.LV.at[n], self.RV.at[n, i], (zs, at.fc)))
        lands = [self.LD.at[unit], self.LV.at[n]]
        def arrived(land, got, key):
            self.once(zs, key, self.copies((HERE,), p, r, at.c, first, rows, extra, land, got, (zs, at.fc)))
            lands.append(land)
        if path == 0 or r == 0:
            if p >= zs and zs > 0: arrived(self.LZ.at[n], self.RZ.at[n, i], (UP, i, p, r))
            if p <= zs and zs < PLANES - 1:
                m = 8 + r if p == zs else n
                arrived(self.LZ.at[m], self.RZ.at[m, i], (DOWN, i, p, r))
        if r == 0 and (path == 1 or p == zs):
            arrived(self.LU.at[p], self.RU.at[p, i], (TO_U, i, p))
        self.add(p, r, first, rows, extra, lands, kind == KEEP)
        if kind != KEEP: self.send(zs, op)

    def drain(self):
        for zs in range(PLANES):
            @pl.when(self.at.z == zs)
            def _():
                for op in self.made[zs]:
                    for q in self.build(zs, op): q.wait_send()

class Spread:
    def __init__(self, at, own, land, zland, S, count):
        self.at, self.own, self.land, self.zland, self.S, self.count = at, own, land, zland, S, count

    def round(self, n, me, land, base, dev):
        return [remote(self.own, land.at[me], self.S.at[0, base + j], self.S.at[1, base + j], dev(lax.rem(me + j, n))) for j in range(1, n)]

    def plane(self):
        return self.round(self.count, self.at.f, self.land, 0, lambda t: (self.at.z, t))

    def planes(self):
        return self.round(PLANES, self.at.z, self.zland, self.count, lambda t: (t, self.at.f))

    def first(self):
        for q in self.plane(): q.start()

    def total(self, land, n, me):
        land[me] = self.own[...]
        v = land[0]
        for j in range(1, n): v = v + land[j]
        return v

    def second(self):
        for q in self.plane(): q.wait()
        self.own[...] = self.total(self.land, self.count, self.at.f)
        for q in self.planes(): q.start()

    def last(self):
        for q in self.planes(): q.wait()
        self.own[...] = self.total(self.zland, PLANES, self.at.z)

K2_IN = K1_OUT
K2_HERE = ("wproj", "dctx", "small", "hat1", "r1", "hat2", "r2", "gp", "ring", "normT", "attT", "q", "kT", "vv", "xT", "wq")

def backward_kernel(pieces, events, vec_ref, *rest):
    n_in = len(K2_IN)
    hbm = dict(zip(K2_IN, rest[:n_in]))
    (grad, vsum, sq, ig, g, vec, wproj, dctx, small, hat1, r1, hat2, r2, gp, ring, normT, attT, q, kT, vv, xT, wq,
     low1, low2, acc, tmp, dp, LD, LV, LZ, LU, total, flat, vg, vland, vzland, sqv, sland, szland,
     IS, RD, RV, RZ, RU, S, TS, VS, SS) = rest[n_in:]
    here = dict(wproj=wproj, dctx=dctx, small=small, hat1=hat1, r1=r1, hat2=hat2, r2=r2, gp=gp, normT=normT, attT=attT, q=q, kT=kT, vv=vv, xT=xT)
    loads = {}
    def load(name, src=None, dst=None):
        cp = pltpu.make_async_copy(hbm[name] if src is None else src, here[name] if dst is None else dst, IS.at[len(loads)])
        cp.start()
        loads[name if src is None else (name, len(loads))] = cp
        return cp
    w = hbm["w"]
    first = [load(n) for n in ("dctx", "wproj", "hat2", "r2")]
    second = [load("w", w.at[pl.ds(6144, 3072)], g.at[pl.ds(6144, 3072)]), load("gp"), load("actT", hbm["actT"], ring)]
    tail = load("tail", hbm["tail"], g.at[pl.ds(9216, 448)])
    third = [load("w", w.at[pl.ds(3072, 3072)], g.at[pl.ds(3072, 3072)]), load("normT")]
    fifth = [load("w", w.at[pl.ds(2304, 768)], g.at[pl.ds(2304, 768)]), load("attT")]
    sixth = [load("q"), load("kT"), load("vv")]
    seventh = [load("xT"), load("w", w.at[pl.ds(0, 2304)], wq)]
    def ready(cs):
        for cp in cs: cp.wait()
    at = Place()
    at.greet_all(vland.shape[0])
    re = Reduce(at, g, pieces, LD, LV, LZ, LU, total, RD, RV, RZ, RU, S)
    vs = Spread(at, vg, vland, vzland, VS, vland.shape[0])
    ss = Spread(at, sqv, sland, szland, SS, vland.shape[0])
    def slot(i, cond=None):
        for zs in range(PLANES):
            if events[zs][i]:
                @pl.when((at.z == zs) if cond is None else ((at.z == zs) & cond))
                def _():
                    for e in events[zs][i]:
                        if e[0] == SMALL: (vs.first, vs.second, vs.last)[e[1]]()
                        else: re.op(zs, e)
    for i in range(vec_ref.shape[0]):
        vec[0:1, 128 * i:128 * i + 128] = vec_ref[i:i + 1, :]
    low2[...] = jnp.zeros((T, D), bf16)
    low1[...] = jnp.zeros((T, D), bf16)
    for t in range(3):
        dp[t] = jnp.zeros((T, D), bf16)
    ready(first)
    for n in range(3):
        hat1[:, 256 * n:256 * n + 256] = mm_nt(dctx[0:LT, :], wproj[256 * n:256 * n + 256, :])
    norm_back(hat1, vec[0:1, G2:G2 + D], hat2, r2, low2, acc)
    fourth = [load("hat1"), load("r1"), load("small")]
    put_vec(vg, acc, (G2, S2, BDOWN))
    ready(second)
    lax.fori_loop(0, 8, lambda n, _: (down_back(11 - n, low2, g, ring, gp, vg), 0)[1], 0)
    ready([tail])
    shared_blocks(g, 3, True)
    slot(0)
    slot(1)
    lax.fori_loop(8, 12, lambda n, _: (down_back(11 - n, low2, g, ring, gp, vg), 0)[1], 0)
    def head(h):
        return pltpu.make_async_copy(hbm["pT"].at[pl.ds(pl.multiple_of(h * T, T), T)], ring.at[pl.ds(pl.multiple_of((h % 6) * T, T), T)], TS.at[h % 6])
    for h in range(6): head(h).start()
    slot(2)
    ready(third)
    lax.fori_loop(0, 3, lambda n, _: (up_back_x(n, gp, g, hat2), 0)[1], 0)
    slot(3)
    def woven(n, _):
        weave(normT, gp, 4, 2 - n, 3072, g, tmp, False)
        slot(4, n == 0)
        slot(5, n == 1)
        return 0
    lax.fori_loop(0, 2, woven, 0)
    shared_blocks(g, 2, True)
    slot(6)
    lax.fori_loop(2, 3, woven, 0)
    slot(7)
    ready(fourth)
    norm_back(hat2, vec[0:1, G1:G1 + D], hat1, r1, low1, acc)
    put_vec(vg, acc, (G1, S1, BO))
    ready(fifth)
    da, dqT = low2, normT
    out_back(low1, g, attT, da)
    shared_blocks(g, 1, True)
    slot(8)
    slot(9)
    ready(sixth)
    def pair(p, _):
        head(2 * p).wait()
        head(2 * p + 1).wait()
        attend_back(p, da, q, kT, vv, ring, dp, dqT)
        @pl.when(p < 3)
        def _():
            head(2 * p + 6).start()
            head(2 * p + 7).start()
        for i in range(6): slot(10 + i, p == i)
        return 0
    lax.fori_loop(0, 6, pair, 0)
    ready(seventh)
    def wove(n, _):
        weave(xT, dp, 3, n, 0, g, tmp, True)
        for i in range(3): slot(16 + i, n == i)
        return 0
    lax.fori_loop(0, 3, wove, 0)
    shared_blocks(g, 0, True)
    slot(19)
    vg[0:1, BQ:BQ + D] = jnp.sum(dp[0].astype(f32), axis=0, keepdims=True)
    vg[0:1, BV:BV + D] = jnp.sum(dp[2].astype(f32), axis=0, keepdims=True)
    vg[0:1, BPROJ:BPROJ + 256] = small[0:1, :]
    vg[0:1, BCODE:BCODE + 256] = small[1:2, :]
    vg[0:1, BCODE + 256:BCODE + 512] = small[2:3, :]
    slot(20)
    slot(21)
    for n in range(3):
        input_back(n, dp, wq, hat1, ig)
    slot(22)
    z, c, k = at.z, at.c, at.k
    edge = remote(total.at[pl.ds(HALF, 16)], total.at[pl.ds(0, 16)], TS.at[6], TS.at[7], (z, at.fc))
    edge.start()
    for i in range(vsum.shape[0]):
        vsum[i:i + 1, :] = vg[0:1, 128 * i:128 * i + 128]
    edge.wait()
    part = jnp.zeros((8, 128), f32)
    n = grad.shape[0] // 6
    for j in range(6):
        flat[pl.ds(j, 320, stride=6), :] = total[:, 128 * j:128 * j + 128]
    for j in range(6):
        v = flat[pl.ds(6 * (16 - 2 * c - 4 * k) + j, n, stride=6), :]
        grad[pl.ds(j, n, stride=6), :] = v
        v = v * v
        part = part + sum8(v[0:n // 8 * 8])
        if n % 8: part = part + jnp.concatenate([v[n // 8 * 8:], jnp.zeros((8 - n % 8, 128), f32)], axis=0)
    sqv[...] = part
    ss.first()
    ss.second()
    ss.last()
    sq[...] = sqv[...]
    re.drain()

def backward(pieces, events, vec, hbm, count, n):
    V_ = pl.BlockSpec(memory_space=pltpu.VMEM)
    A_ = pl.BlockSpec(memory_space=pl.ANY)
    VM = pltpu.VMEM
    DMA = pltpu.SemaphoreType.DMA
    sds = jax.ShapeDtypeStruct
    most = max(len(ps) for ps in pieces)
    keys = 32 + len({e + (j,) for z in events for s in z for e in s if e[0] in (TO_V, TO_U, TO_Z) for j in range(1 + pieces[e[2]][e[1]][3])})
    nv = vec.shape[0] + 256
    shape = dict(K1_SHAPE, ring=((FF, T), bf16), wq=((3 * D, D), bf16))
    return pl.pallas_call(functools.partial(backward_kernel, pieces, events),
        out_shape=[sds((n, 128), f32), sds((nv // 128, 128), f32), sds((8, 128), f32), sds((1, LEN, D), f32)],
        in_specs=[V_] + [A_] * len(K2_IN), out_specs=[V_] * 4,
        scratch_shapes=[VM((GROW, D), bf16), VM((1, vec.shape[0]), f32)] + [VM(*shape[k]) for k in K2_HERE]
            + [VM((T, D), bf16), VM((T, D), bf16), VM((24, D), f32), VM((2, 1024, 128), f32), VM((3, T, D), bf16),
               VM((16, HALF, D), bf16), VM((8, HALF, D), bf16), VM((10, HALF, D), bf16), VM((4, HALF, D), bf16), VM((HALF + 16, D), f32), VM((6 * (HALF + 16), 128), f32),
               VM((1, nv), f32), VM((count, 1, nv), f32), VM((PLANES, 1, nv), f32), VM((8, 128), f32), VM((count, 8, 128), f32), VM((PLANES, 8, 128), f32),
               DMA((24,)), DMA((16, 2)), DMA((8, most, 2)), DMA((10, most, 2)), DMA((4, most, 2)), DMA((keys + 2,)), DMA((8,)), DMA((2, count + PLANES)), DMA((2, count + PLANES))],
        compiler_params=pltpu.CompilerParams(collective_id=1, has_side_effects=True, vmem_limit_bytes=63 * 2**20),
    )(vec.reshape(-1, 128), *[hbm[k] for k in K2_IN])

def update_kernel(total, g, p, m1, m2, vg, v, v1, v2, sq, np_, low, n1, n2, nv, nv1, nv2, loss, norm, scale):
    @pl.when(pl.program_id(0) == 0)
    def _():
        n = v.shape[0]
        gv = vg[0:n, :]
        s = jnp.sum(jnp.sum(sq[...], axis=0, keepdims=True), axis=1, keepdims=True)
        s = s + jnp.sum(jnp.sum(gv * gv, axis=0, keepdims=True), axis=1, keepdims=True)
        s = jnp.sqrt(s)
        f = jnp.minimum(1.0, clip_level / (s + 1e-06))
        norm[...] = s
        loss[...] = vg[n:n + 1, 0:1] / total
        scale[...] = jnp.broadcast_to(f, (8, 128))
        nv[...], nv1[...], nv2[...] = adamw_update(v[...], v1[...], v2[...], gv * f, rate_vector)
    new, first, second = adamw_update(p[...], m1[...], m2[...], g[...] * scale[0:1, 0:1], rate_matrix)
    np_[...] = new
    low[...] = new.astype(bf16)
    n1[...] = first
    n2[...] = second

def update(total, g, p, m1, m2, vg, v, v1, v2, sq):
    n, nv = g.shape[0], v.shape[0] // 128
    sds = jax.ShapeDtypeStruct
    rows = 608
    part = pl.BlockSpec((rows, 128), lambda i: (i, 0))
    def whole(*shape): return pl.BlockSpec(shape, lambda i: (0, 0))
    flat = lambda a: a.reshape(-1, 128)
    out = pl.pallas_call(functools.partial(update_kernel, total), grid=(pl.cdiv(n, rows),),
        out_shape=[sds((n, 128), f32), sds((n, 128), bf16), sds((n, 128), f32), sds((n, 128), f32)] + [sds((nv, 128), f32)] * 3 + [sds((1, 1), f32)] * 2,
        in_specs=[part] * 4 + [whole(*vg.shape)] + [whole(nv, 128)] * 3 + [whole(8, 128)],
        out_specs=[part] * 4 + [whole(nv, 128)] * 3 + [whole(1, 1)] * 2,
        scratch_shapes=[pltpu.VMEM((8, 128), f32)],
    )(g, flat(p), flat(m1), flat(m2), vg, flat(v), flat(v1), flat(v2), sq)
    return [a.reshape(-1) for a in out[:7]] + [a.reshape(()) for a in out[7:]]

PIECES_OUT = (((0, 0, 48, False), (0, 48, 48, False), (0, 96, 48, False), (1, 144, 48, False), (1, 192, 48, False), (1, 240, 48, True)),
 ((0, 0, 96, False), (0, 96, 96, False), (1, 192, 96, True)), ((1, 0, 96, False), (1, 96, 96, False), (1, 192, 96, True)),
 ((0, 0, 144, False), (0, 144, 144, True)))
PIECES_BACK = (((0, 0, 80, False), (0, 80, 64, False), (1, 144, 48, False), (1, 192, 48, False), (1, 240, 48, True)),
 ((0, 0, 80, False), (0, 80, 64, False), (1, 144, 48, False), (1, 192, 48, False), (1, 240, 48, True)),
 ((0, 0, 80, False), (0, 80, 64, False), (1, 144, 48, False), (1, 192, 48, False), (1, 240, 48, True)),
 ((0, 0, 96, False), (0, 96, 96, False), (0, 192, 96, True)))
SENDS_OUT = ((((0, 0, 0, 0), (0, 1, 0, 0), (2, 0, 0, 0), (2, 1, 0, 0), (2, 2, 0, 0)),
  ((0, 2, 0, 0), (0, 3, 0, 0), (2, 3, 0, 0), (2, 4, 0, 0), (2, 5, 0, 0), (4, 0, 0, 1), (4, 1, 0, 1), (0, 4, 0, 0), (4, 2, 0, 1), (3, 0, 0, 0),
   (3, 1, 0, 0), (4, 0, 1, 0), (4, 3, 0, 1), (0, 5, 0, 0), (3, 2, 0, 0), (4, 4, 0, 1), (3, 3, 0, 0), (3, 4, 0, 0), (4, 5, 0, 1), (0, 0, 0, 1),
   (3, 5, 0, 0), (4, 0, 0, 2), (4, 1, 1, 0), (4, 1, 0, 2), (3, 0, 0, 1), (0, 1, 0, 1), (4, 2, 0, 2), (3, 1, 0, 1), (4, 3, 0, 2), (3, 2, 0, 1),
   (0, 2, 0, 1), (4, 4, 0, 2), (3, 3, 0, 1), (4, 2, 1, 0), (3, 4, 0, 1), (4, 5, 0, 2), (3, 5, 0, 1), (4, 0, 0, 3), (4, 1, 0, 3), (2, 2, 1, 0),
   (4, 2, 0, 3), (4, 0, 1, 1), (4, 3, 0, 3), (3, 0, 1, 0), (4, 4, 0, 3), (4, 5, 0, 3), (3, 1, 1, 0), (4, 1, 1, 1), (3, 2, 1, 0), (4, 2, 1, 1)),
  (), ((4, 0, 1, 2), (4, 1, 1, 2), (3, 0, 1, 1), (3, 1, 1, 1), (4, 0, 2, 0), (4, 2, 1, 2)), (), ((3, 2, 1, 1), (4, 1, 2, 0)),
  ((4, 0, 1, 3), (2, 0, 2, 0)), ((4, 1, 1, 3), (2, 1, 2, 0), (4, 2, 2, 0)), ((4, 2, 1, 3), (2, 2, 2, 0)),
  ((4, 0, 2, 1), (3, 0, 2, 0), (4, 0, 3, 0), (4, 1, 2, 1), (3, 1, 2, 0)), ((3, 2, 2, 0), (4, 2, 2, 1)),
  ((4, 0, 2, 2), (4, 1, 2, 2), (3, 0, 2, 1), (3, 1, 2, 1), (4, 1, 3, 0), (4, 2, 2, 2), (3, 2, 2, 1), (4, 0, 2, 3), (3, 0, 3, 0), (4, 0, 3, 1),
   (4, 1, 2, 3), (3, 1, 3, 0), (4, 2, 2, 3), (3, 0, 3, 1), (4, 1, 3, 1), (4, 0, 3, 2)),
  (), ((3, 1, 3, 1),), ((4, 1, 3, 2),), (), ((4, 0, 3, 3),), ((4, 1, 3, 3),), (), ()),
 (((0, 0, 1, 0), (2, 0, 1, 0), (2, 1, 1, 0), (1, 0, 1, 0)),
  ((0, 1, 1, 0), (4, 0, 0, 0), (3, 0, 0, 0), (2, 2, 1, 0), (4, 0, 1, 1), (1, 1, 1, 0), (0, 0, 0, 0), (4, 1, 0, 0), (3, 1, 0, 0), (4, 1, 1, 1),
   (3, 0, 1, 0), (1, 2, 1, 0), (0, 1, 0, 0), (4, 0, 0, 2), (4, 2, 0, 0), (4, 0, 2, 0), (3, 2, 0, 0), (0, 2, 0, 0), (4, 2, 1, 1), (2, 3, 0, 0),
   (4, 3, 0, 0), (4, 1, 0, 2), (3, 3, 0, 0), (0, 3, 0, 0), (3, 1, 1, 0), (4, 4, 0, 0), (1, 0, 1, 1), (4, 0, 1, 2), (4, 1, 2, 0), (0, 4, 0, 0),
   (2, 4, 0, 0), (4, 2, 0, 2), (3, 4, 0, 0), (4, 5, 0, 0), (4, 3, 0, 1), (0, 5, 0, 0), (2, 5, 0, 0), (4, 3, 0, 2), (1, 1, 1, 1), (4, 0, 0, 1),
   (3, 5, 0, 0), (4, 2, 2, 0), (4, 1, 1, 2), (0, 0, 0, 1), (3, 3, 0, 1), (4, 1, 0, 1), (4, 4, 0, 1), (3, 0, 0, 1), (4, 4, 0, 2), (0, 1, 0, 1),
   (3, 1, 0, 1), (4, 2, 0, 1), (4, 5, 0, 1), (3, 4, 0, 1), (1, 0, 2, 0), (0, 2, 0, 1), (4, 5, 0, 2), (3, 2, 0, 1), (4, 0, 3, 0), (4, 3, 0, 3),
   (3, 5, 0, 1), (0, 2, 1, 0), (4, 0, 0, 3), (3, 2, 1, 0), (1, 1, 2, 0), (4, 1, 0, 3), (4, 4, 0, 3), (3, 0, 1, 1), (4, 2, 0, 3), (1, 2, 2, 0),
   (4, 1, 3, 0), (0, 0, 1, 1), (4, 5, 0, 3), (3, 1, 1, 1), (3, 2, 1, 1), (4, 2, 1, 2)),
  ((0, 1, 1, 1), (4, 0, 1, 3), (2, 0, 2, 0), (1, 0, 3, 0), (4, 0, 3, 1)),
  ((4, 1, 1, 3), (4, 2, 1, 3), (2, 1, 2, 0), (2, 2, 2, 0), (1, 1, 3, 0), (4, 0, 2, 1)), (), ((3, 0, 2, 0), (4, 1, 3, 1)),
  ((4, 1, 2, 1), (3, 1, 2, 0)), ((4, 2, 2, 1), (3, 2, 2, 0), (1, 0, 3, 1)), ((4, 0, 2, 2), (3, 0, 2, 1)),
  ((4, 1, 2, 2), (3, 1, 2, 1), (1, 1, 3, 1), (3, 2, 2, 1), (4, 2, 2, 2)), (), ((4, 0, 2, 3), (4, 1, 2, 3), (3, 0, 3, 0), (4, 2, 2, 3), (3, 1, 3, 0)),
  ((3, 0, 3, 1),), ((4, 0, 3, 2),), ((3, 1, 3, 1),), ((4, 1, 3, 2),), ((4, 0, 3, 3),), ((4, 1, 3, 3),), (), ()),
 (((0, 0, 2, 0), (2, 0, 2, 0), (2, 1, 2, 0), (1, 0, 2, 0)),
  ((0, 1, 2, 0), (2, 2, 2, 0), (4, 0, 2, 1), (3, 0, 2, 0), (1, 1, 2, 0), (0, 2, 2, 0), (4, 0, 1, 0), (4, 1, 2, 1), (3, 0, 1, 0), (1, 2, 2, 0),
   (4, 0, 3, 0), (3, 1, 2, 0), (4, 2, 2, 1), (4, 1, 1, 0), (0, 0, 1, 0), (3, 1, 1, 0), (4, 0, 2, 2), (1, 0, 3, 0), (4, 0, 0, 0), (3, 0, 0, 0),
   (4, 0, 1, 2), (3, 2, 2, 0), (4, 1, 0, 0), (0, 0, 0, 0), (4, 1, 2, 2), (4, 1, 3, 0), (3, 1, 0, 0), (4, 2, 0, 0), (0, 1, 0, 0), (4, 1, 1, 2),
   (3, 2, 0, 0), (1, 1, 3, 0), (2, 3, 0, 0), (0, 2, 0, 0), (4, 0, 0, 2), (4, 3, 0, 0), (3, 3, 0, 0), (3, 0, 2, 1), (4, 4, 0, 0), (0, 3, 0, 0),
   (4, 2, 2, 2), (4, 1, 0, 2), (4, 0, 3, 1), (2, 4, 0, 0), (4, 2, 0, 2), (0, 4, 0, 0), (4, 5, 0, 0), (2, 5, 0, 0), (4, 3, 0, 1), (4, 3, 0, 2),
   (0, 5, 0, 0), (4, 0, 0, 1), (3, 4, 0, 0), (3, 5, 0, 0), (1, 0, 3, 1), (4, 0, 2, 3), (4, 1, 0, 1), (3, 3, 0, 1), (0, 0, 0, 1), (4, 4, 0, 1),
   (3, 0, 0, 1), (4, 1, 3, 1), (4, 5, 0, 1), (4, 2, 0, 1), (0, 1, 0, 1), (4, 4, 0, 2), (3, 1, 0, 1), (3, 4, 0, 1), (1, 1, 3, 1), (4, 5, 0, 2),
   (0, 2, 0, 1), (3, 5, 0, 1), (4, 3, 0, 3), (3, 2, 0, 1), (4, 0, 0, 3), (0, 1, 1, 0), (2, 2, 1, 0), (4, 2, 1, 0), (4, 1, 0, 3), (4, 4, 0, 3),
   (3, 2, 1, 0), (4, 5, 0, 3), (0, 2, 1, 0), (4, 2, 0, 3), (4, 0, 1, 1), (3, 0, 1, 1), (4, 2, 1, 1), (3, 2, 1, 1)),
  (), ((0, 0, 1, 1), (4, 1, 1, 1), (4, 2, 1, 2), (4, 0, 1, 3), (3, 1, 1, 1), (3, 1, 2, 1), (4, 2, 1, 3), (0, 1, 1, 1)), (), ((3, 2, 2, 1),),
  ((4, 1, 1, 3), (3, 0, 3, 0)), ((4, 1, 2, 3),), ((4, 2, 2, 3), (3, 1, 3, 0)), ((3, 0, 3, 1),), ((4, 0, 3, 2),), ((4, 1, 3, 2), (3, 1, 3, 1)),
  ((4, 0, 3, 3),), (), (), ((4, 1, 3, 3),), (), (), (), ()),
 (((2, 0, 3, 0), (1, 0, 3, 0)),
  ((2, 1, 3, 0), (1, 1, 3, 0), (3, 0, 3, 0), (4, 0, 3, 1), (4, 0, 2, 0), (2, 0, 2, 0), (4, 1, 3, 1), (3, 0, 2, 0), (4, 1, 2, 0), (1, 0, 3, 1),
   (2, 1, 2, 0), (4, 0, 3, 2), (3, 1, 2, 0), (4, 0, 2, 1), (4, 2, 2, 0), (2, 2, 2, 0), (4, 0, 2, 2), (1, 1, 3, 1), (4, 1, 2, 1), (3, 0, 2, 1),
   (4, 0, 1, 0), (4, 1, 2, 2), (3, 0, 1, 0), (4, 0, 0, 0), (3, 0, 0, 0), (4, 2, 2, 1), (4, 1, 0, 0), (3, 1, 0, 0), (3, 2, 2, 0), (4, 0, 2, 3),
   (4, 2, 0, 0), (4, 0, 1, 2), (3, 2, 0, 0), (4, 3, 0, 0), (4, 0, 0, 2), (2, 3, 0, 0), (4, 1, 0, 2), (3, 3, 0, 0), (4, 4, 0, 0), (2, 4, 0, 0),
   (3, 4, 0, 0), (4, 2, 2, 2), (4, 5, 0, 0), (2, 5, 0, 0), (4, 2, 0, 2), (4, 3, 0, 1), (3, 5, 0, 0), (4, 0, 0, 1), (4, 3, 0, 2), (3, 3, 0, 1),
   (4, 4, 0, 1), (3, 0, 0, 1), (4, 1, 0, 1), (4, 4, 0, 2), (3, 4, 0, 1), (4, 5, 0, 1), (4, 2, 0, 1), (3, 1, 0, 1), (3, 5, 0, 1), (4, 5, 0, 2),
   (4, 3, 0, 3), (3, 2, 0, 1), (4, 0, 0, 3), (3, 1, 2, 1), (4, 1, 1, 0), (4, 4, 0, 3), (4, 1, 0, 3), (3, 1, 1, 0), (4, 5, 0, 3), (3, 2, 2, 1),
   (4, 2, 0, 3), (4, 2, 1, 0), (4, 1, 2, 3), (2, 2, 1, 0)),
  (), ((4, 1, 1, 2), (4, 0, 1, 1), (3, 2, 1, 0), (4, 2, 2, 3), (3, 0, 1, 1), (4, 2, 1, 1)), (), ((4, 1, 1, 1), (3, 2, 1, 1)),
  ((4, 2, 1, 2), (3, 1, 1, 1)), ((4, 0, 1, 3), (3, 1, 3, 0)), ((4, 2, 1, 3),), ((4, 1, 1, 3), (3, 0, 3, 1)), ((3, 1, 3, 1),),
  ((4, 1, 3, 2), (4, 0, 3, 3)), (), ((4, 1, 3, 3),), (), (), (), (), (), ()))
SENDS_BACK = (((), ((0, 0, 3, 0),), (), ((1, 0, 3, 2), (1, 1, 3, 2)), ((1, 2, 3, 2),), ((1, 0, 3, 3),), ((0, 0, 2, 0), (3, 0, 3, 0)), ((1, 1, 3, 3), (3, 1, 3, 0)),
  ((1, 2, 3, 3), (3, 2, 3, 0), (1, 0, 2, 2)), ((0, 0, 1, 0), (1, 1, 2, 2)), ((1, 2, 2, 2), (1, 3, 2, 2)), ((3, 0, 3, 1), (1, 4, 2, 2), (1, 0, 2, 3)),
  ((3, 1, 3, 1), (1, 0, 1, 2)), ((1, 1, 1, 2),), ((3, 2, 3, 1), (1, 2, 1, 2), (1, 3, 1, 2), (1, 4, 1, 2)), ((1, 0, 1, 3),),
  ((1, 1, 1, 3), (3, 0, 1, 0)), ((1, 2, 1, 3), (1, 3, 1, 3)), ((1, 4, 1, 3), (3, 1, 1, 0), (1, 1, 2, 3)), ((0, 0, 0, 0),), (),
  ((5, 0, 0, 0), (1, 2, 2, 3)),
  ((2, 2, 1, 1), (2, 3, 1, 1), (3, 0, 1, 1), (1, 0, 0, 2), (3, 1, 1, 1), (1, 1, 0, 2), (1, 2, 0, 2), (3, 0, 2, 0), (1, 3, 0, 2), (1, 4, 0, 2),
   (1, 0, 0, 3), (3, 2, 1, 0), (1, 1, 0, 3), (5, 1, 0, 0), (3, 3, 1, 0), (1, 2, 0, 3), (1, 3, 0, 3), (3, 1, 2, 0), (1, 4, 0, 3), (2, 4, 1, 1),
   (3, 0, 2, 1), (1, 3, 2, 3), (1, 4, 2, 3), (2, 2, 0, 1), (3, 1, 2, 1), (2, 3, 0, 1), (2, 4, 0, 1), (3, 4, 1, 0), (5, 2, 0, 0), (2, 2, 2, 1),
   (2, 3, 2, 1), (2, 4, 2, 1), (3, 2, 2, 0), (3, 3, 2, 0), (3, 4, 2, 0), (2, 0, 0, 1), (2, 1, 0, 1), (4, 0, 0, 0), (4, 2, 0, 0), (4, 1, 0, 0),
   (4, 3, 0, 0), (4, 4, 0, 0))),
 ((), ((0, 0, 3, 0),), (), ((1, 0, 3, 2), (1, 1, 3, 2)), ((1, 2, 3, 2),), ((1, 0, 3, 3),), ((0, 0, 2, 0),), ((1, 1, 3, 3),),
  ((1, 2, 3, 3), (1, 0, 2, 2)), ((0, 0, 1, 0), (3, 0, 3, 0)), ((1, 1, 2, 2), (1, 2, 2, 2)), ((3, 1, 3, 0), (1, 3, 2, 2), (1, 4, 2, 2)),
  ((1, 0, 1, 2), (1, 1, 1, 2)), ((3, 2, 3, 0), (1, 2, 1, 2), (1, 3, 1, 2)), ((1, 4, 1, 2),), ((3, 0, 3, 1), (1, 0, 1, 3), (1, 1, 1, 3)),
  ((1, 2, 1, 3),), ((3, 1, 3, 1), (1, 3, 1, 3), (1, 4, 1, 3)), ((1, 0, 2, 3),), ((0, 0, 0, 0),), ((1, 1, 2, 3),), ((5, 0, 0, 0),),
  ((3, 2, 3, 1), (2, 2, 1, 1), (1, 0, 0, 2), (1, 1, 0, 2), (1, 2, 0, 2), (1, 3, 0, 2), (1, 4, 0, 2), (1, 0, 0, 3), (1, 1, 0, 3), (1, 2, 0, 3),
   (1, 3, 0, 3), (1, 4, 0, 3), (2, 3, 1, 1), (2, 4, 1, 1), (5, 1, 0, 0), (3, 0, 2, 0), (2, 0, 1, 1), (2, 2, 0, 1), (4, 2, 1, 0), (2, 3, 0, 1),
   (2, 4, 0, 1), (2, 1, 1, 1), (3, 1, 2, 0), (1, 2, 2, 3), (4, 0, 1, 0), (3, 0, 0, 0), (1, 3, 2, 3), (1, 4, 2, 3), (3, 0, 2, 1), (3, 1, 0, 0),
   (4, 1, 1, 0), (5, 2, 0, 0), (3, 1, 2, 1), (2, 2, 2, 1), (3, 0, 0, 1), (2, 3, 2, 1), (2, 4, 2, 1), (3, 1, 0, 1), (3, 2, 2, 0), (3, 2, 0, 0),
   (3, 3, 2, 0), (3, 3, 0, 0), (3, 4, 2, 0), (3, 4, 0, 0), (4, 3, 1, 0), (4, 4, 1, 0))),
 ((), ((0, 0, 3, 0),), (), ((1, 0, 3, 2), (1, 1, 3, 2)), ((1, 2, 3, 2),), ((1, 0, 3, 3),), ((0, 0, 2, 0),), ((1, 1, 3, 3),),
  ((1, 2, 3, 3), (1, 0, 2, 2)), ((0, 0, 1, 0),), ((1, 1, 2, 2), (1, 2, 2, 2)), ((1, 3, 2, 2), (1, 4, 2, 2)), ((1, 0, 2, 3), (3, 0, 3, 0)),
  ((1, 0, 1, 2), (1, 1, 1, 2)), ((3, 1, 3, 0), (1, 2, 1, 2), (1, 3, 1, 2)), ((1, 4, 1, 2),), ((1, 0, 1, 3),),
  ((3, 2, 3, 0), (1, 1, 1, 3), (1, 2, 1, 3)), ((1, 3, 1, 3),), ((0, 0, 0, 0), (1, 4, 1, 3)), (), ((5, 0, 0, 0), (3, 0, 3, 1), (1, 1, 2, 3)),
  ((2, 2, 1, 1), (1, 0, 0, 2), (3, 0, 1, 0), (1, 1, 0, 2), (3, 1, 3, 1), (3, 1, 1, 0), (1, 2, 0, 2), (1, 3, 0, 2), (1, 4, 0, 2), (3, 0, 1, 1),
   (1, 0, 0, 3), (3, 2, 3, 1), (1, 1, 0, 3), (3, 1, 1, 1), (1, 2, 0, 3), (5, 1, 0, 0), (1, 3, 0, 3), (1, 4, 0, 3), (2, 3, 1, 1), (3, 2, 1, 0),
   (2, 4, 1, 1), (1, 2, 2, 3), (2, 2, 0, 1), (3, 0, 0, 0), (2, 3, 0, 1), (2, 4, 0, 1), (3, 1, 0, 0), (1, 3, 2, 3), (1, 4, 2, 3), (2, 2, 2, 1),
   (3, 0, 0, 1), (5, 2, 0, 0), (3, 1, 0, 1), (2, 3, 2, 1), (2, 4, 2, 1), (3, 2, 0, 0), (3, 3, 0, 0), (2, 0, 2, 1), (3, 4, 0, 0), (2, 1, 2, 1),
   (3, 3, 1, 0), (4, 0, 2, 0), (4, 1, 2, 0), (3, 4, 1, 0), (4, 2, 2, 0), (4, 3, 2, 0), (4, 4, 2, 0))),
 ((), ((0, 0, 3, 0),), (), ((1, 0, 3, 2), (1, 1, 3, 2)), ((1, 2, 3, 2),), ((1, 0, 3, 3),), ((0, 0, 2, 0),), ((1, 1, 3, 3),),
  ((1, 2, 3, 3), (1, 0, 2, 2)), ((0, 0, 1, 0),), ((1, 1, 2, 2), (1, 2, 2, 2)), ((1, 3, 2, 2), (1, 4, 2, 2)), ((1, 0, 2, 3), (3, 0, 2, 0)),
  ((1, 0, 1, 2), (1, 1, 1, 2), (3, 1, 2, 0)), ((1, 2, 1, 2), (1, 3, 1, 2)), ((1, 4, 1, 2), (3, 0, 2, 1), (1, 0, 1, 3)), ((3, 0, 1, 0), (1, 1, 1, 3)),
  ((1, 2, 1, 3), (3, 1, 1, 0)), ((1, 3, 1, 3), (1, 4, 1, 3)), ((0, 0, 0, 0),), ((1, 1, 2, 3),), ((5, 0, 0, 0), (3, 0, 1, 1)),
  ((2, 2, 1, 1), (3, 1, 1, 1), (1, 0, 0, 2), (1, 1, 0, 2), (1, 2, 0, 2), (1, 3, 0, 2), (3, 1, 2, 1), (1, 4, 0, 2), (3, 2, 1, 0), (1, 0, 0, 3),
   (3, 0, 0, 0), (1, 1, 0, 3), (1, 2, 0, 3), (1, 3, 0, 3), (5, 1, 0, 0), (3, 1, 0, 0), (1, 4, 0, 3), (2, 0, 3, 1), (3, 0, 0, 1), (2, 1, 3, 1),
   (2, 2, 0, 1), (3, 1, 0, 1), (2, 3, 0, 1), (2, 4, 0, 1), (4, 0, 3, 0), (2, 2, 3, 1), (4, 1, 3, 0), (2, 3, 1, 1), (3, 2, 0, 0), (2, 4, 1, 1),
   (5, 2, 0, 0), (3, 3, 0, 0), (1, 2, 2, 3), (3, 4, 0, 0), (1, 3, 2, 3), (1, 4, 2, 3), (4, 2, 3, 0), (3, 3, 1, 0), (3, 4, 1, 0), (2, 2, 2, 1),
   (2, 3, 2, 1), (2, 4, 2, 1), (3, 2, 2, 0), (3, 3, 2, 0), (3, 4, 2, 0))))

def unpack(flat_values):
    shapes = [(D, 3 * D), (D, D), (D, FF), (FF, D), (D, FINAL), (G * CD, V), (G * CD, FINAL)]
    pieces = []
    offset = 0
    for height, width in shapes:
        pieces.append(flat_values[offset : offset + height * width].reshape(height, width))
        offset = offset + height * width
    return pieces


def split_vectors(vector_all):
    lengths = [D, D, D, D, D, FF, D, D, D, FINAL, FINAL]
    pieces = []
    offset = 0
    for length in lengths:
        pieces.append(vector_all[offset : offset + length])
        offset = offset + length
    return pieces


def layer_norm(values, scale_gain, shift_bias):
    centered = values - jnp.mean(values, axis=-1, keepdims=True)
    variance = jnp.mean(centered * centered, axis=-1, keepdims=True)
    return centered * lax.rsqrt(variance + eps_norm) * scale_gain + shift_bias


def contrast_dense(chosen, targets, distract, weight):
    hi = dict(precision=lax.Precision.HIGHEST)
    frames = jnp.arange(MASKED, dtype=jnp.int32)
    allowed = jnp.any(distract[:, :, None] == frames, axis=1) | (frames[:, None] == frames)

    def agreement(chosen, targets):
        left = chosen * lax.rsqrt(jnp.sum(chosen * chosen, axis=-1, keepdims=True) + eps_cos)
        right = targets * lax.rsqrt(jnp.sum(targets * targets, axis=-1, keepdims=True) + eps_cos)
        return jnp.einsum("by,oy->bo", left, right, **hi) / softness_divisor

    similar, back = jax.vjp(agreement, chosen, targets)
    same = frames[:, None] == frames
    positive = jnp.sum(jnp.where(same, similar, 0.0), axis=1)
    top = jnp.max(jnp.where(allowed, similar, -jnp.inf), axis=1)
    parts = jnp.where(allowed, jnp.exp(similar - top[:, None]), 0.0)
    total = jnp.sum(parts, axis=1)
    loss = jnp.sum(top + jnp.log(total) - positive)
    d_similar = weight * (parts / total[:, None] - same.astype(jnp.float32))
    return (loss,) + back(d_similar)


def adamw_update(master, first_moment, second, gradient, step_rate):
    first_new = beta_one * first_moment + (1.0 - beta_one) * gradient
    second_new = beta_two * second + (1.0 - beta_two) * gradient * gradient
    first_hat = first_new / (1.0 - beta_one**STEP)
    second_hat = second_new / (1.0 - beta_two**STEP)
    master_new = master * (1.0 - step_rate * decay_rate) - step_rate * first_hat / (
        jnp.sqrt(second_hat) + adam_eps
    )
    return (master_new, first_new, second_new)


def column_sum(values):
    return jnp.sum(values.astype(jnp.float32), axis=tuple(range(values.ndim - 1)))


def finish(total_masked, square_sum, vector_sum, loss_sum, grad_shard, output, input_grad, params, moment_one, moment_two, vectors, vector_one, vector_two):
    grad_norm = jnp.sqrt(square_sum + jnp.sum(vector_sum * vector_sum))
    factor = jnp.minimum(1.0, clip_level / (grad_norm + 1e-06))
    refreshed_weights, new_one, new_two = adamw_update(params, moment_one, moment_two, grad_shard * factor, rate_matrix)
    new_vectors, new_vector_first, new_vector_second = adamw_update(vectors, vector_one, vector_two, vector_sum * factor, rate_vector)
    return (
        loss_sum / total_masked,
        grad_norm,
        output,
        input_grad,
        refreshed_weights,
        refreshed_weights.astype(bf16),
        new_one,
        new_two,
        new_vectors,
        new_vector_first,
        new_vector_second,
    )


def by_collectives(
    layer_input,
    mask_index,
    distract,
    code_choice,
    params,
    moment_one,
    moment_two,
    vectors,
    vector_one,
    vector_two,
):
    bf16 = jnp.bfloat16
    f32 = jnp.float32
    count_utts = layer_input.shape[0]
    total_masked = count_utts * lax.axis_size(("dp", "fsdp")) * MASKED
    token_rows = count_utts * LEN
    gathered = lax.all_gather(params.astype(bf16), ("dp", "fsdp"), axis=0, tiled=True)
    qkv_weight, out_weight, up_weight, down_weight, proj_weight, codebook, code_weight = unpack(
        gathered
    )
    (
        bias_query,
        bias_value,
        bias_out,
        gain_one,
        shift_one,
        bias_up,
        bias_down,
        gain_two,
        shift_two,
        bias_proj,
        bias_code,
    ) = split_vectors(vectors)
    inputs = layer_input.reshape(token_rows, D)
    projected = jnp.dot(inputs, qkv_weight, preferred_element_type=f32)
    query_heads = (projected[:, :D] + bias_query).astype(bf16).reshape(count_utts, LEN, H, HD)
    key_heads = projected[:, D : 2 * D].astype(bf16).reshape(count_utts, LEN, H, HD)
    value_heads = (projected[:, 2 * D :] + bias_value).astype(bf16).reshape(count_utts, LEN, H, HD)
    scores = (
        jnp.einsum("blhe,bmhe->bhlm", query_heads, key_heads, preferred_element_type=f32) * 0.125
    )
    attn_probs = jax.nn.softmax(scores, axis=-1)
    probs_low = attn_probs.astype(bf16)
    attended = jnp.einsum("bhlm,bmhe->blhe", probs_low, value_heads, preferred_element_type=f32)
    attended = attended.astype(bf16).reshape(token_rows, D)
    residual_one = (
        inputs.astype(f32) + jnp.dot(attended, out_weight, preferred_element_type=f32) + bias_out
    )
    normed, back_one = jax.vjp(layer_norm, residual_one, gain_one, shift_one)
    normed_low = normed.astype(bf16)
    hidden = jnp.dot(normed_low, up_weight, preferred_element_type=f32) + bias_up
    active, gelu_back = jax.vjp(functools.partial(jax.nn.gelu, approximate=False), hidden)
    active_low = active.astype(bf16)
    residual_two = normed + jnp.dot(active_low, down_weight, preferred_element_type=f32) + bias_down
    output, back_two = jax.vjp(layer_norm, residual_two, gain_two, shift_two)
    output_low = output.astype(bf16)
    place = (mask_index[0][:, None] == jnp.arange(LEN, dtype=jnp.int32)).astype(bf16)
    picked = jnp.dot(place, output_low, preferred_element_type=f32).astype(bf16)
    chosen = jnp.dot(picked, proj_weight, preferred_element_type=f32) + bias_proj
    choose = (code_choice[..., None] == jnp.arange(V, dtype=jnp.int32)).astype(bf16)
    code_vectors = jnp.einsum(
        "bmgv,gcv->bmgc", choose, codebook.reshape(G, CD, V), preferred_element_type=f32
    )
    code_vectors = code_vectors.astype(bf16).reshape(count_utts, MASKED, G * CD)
    targets = (
        jnp.einsum("bmc,cf->bmf", code_vectors, code_weight, preferred_element_type=f32) + bias_code
    )
    loss_local, d_chosen, d_targets = contrast_dense(chosen, targets[0], distract[0], 1.0 / total_masked)
    d_targets = d_targets[None]
    d_targets_low = d_targets.astype(bf16)
    quantized_offset_slope = column_sum(d_targets_low)
    d_code_weight = jnp.einsum(
        "bmc,bmf->cf", code_vectors, d_targets_low, preferred_element_type=f32
    )
    d_code_vectors = jnp.einsum(
        "bmf,cf->bmc", d_targets_low, code_weight, preferred_element_type=f32
    )
    d_codebook = jnp.einsum(
        "bmgc,bmgv->gcv",
        d_code_vectors.reshape(count_utts, MASKED, G, CD),
        choose.astype(f32),
        precision=lax.Precision.HIGHEST,
    ).reshape(G * CD, V)
    d_chosen_low = d_chosen.astype(bf16)
    d_bias_proj = column_sum(d_chosen_low)
    d_proj_weight = jnp.einsum("td,tf->df", picked, d_chosen_low, preferred_element_type=f32)
    d_context_low = jnp.einsum("mt,mf->tf", place, d_chosen_low, preferred_element_type=f32).astype(bf16)
    result_sensitivity = jnp.einsum(
        "tf,df->td", d_context_low, proj_weight, preferred_element_type=f32
    )
    d_residual_two, d_gain_two, d_shift_two = back_two(result_sensitivity)
    d_second_low = d_residual_two.astype(bf16)
    d_bias_down = column_sum(d_second_low)
    d_down_weight = jnp.einsum("th,td->hd", active_low, d_second_low, preferred_element_type=f32)
    d_active = jnp.einsum("td,hd->th", d_second_low, down_weight, preferred_element_type=f32)
    (d_hidden,) = gelu_back(d_active)
    d_hidden_low = d_hidden.astype(bf16)
    d_bias_up = column_sum(d_hidden_low)
    d_up_weight = jnp.einsum("td,th->dh", normed_low, d_hidden_low, preferred_element_type=f32)
    d_normed = d_residual_two + jnp.einsum(
        "th,dh->td", d_hidden_low, up_weight, preferred_element_type=f32
    )
    d_residual_one, d_gain_one, d_shift_one = back_one(d_normed)
    d_branch_low = d_residual_one.astype(bf16)
    d_bias_out = column_sum(d_branch_low)
    d_out_weight = jnp.einsum("td,te->de", attended, d_branch_low, preferred_element_type=f32)
    d_attended = jnp.einsum("te,de->td", d_branch_low, out_weight, preferred_element_type=f32)
    d_attended = d_attended.astype(bf16).reshape(count_utts, LEN, H, HD)
    d_value = jnp.einsum("bhlm,blhe->bmhe", probs_low, d_attended, preferred_element_type=f32)
    d_probs = jnp.einsum("blhe,bmhe->bhlm", d_attended, value_heads, preferred_element_type=f32)
    d_scores = (
        attn_probs * (d_probs - jnp.sum(attn_probs * d_probs, axis=-1, keepdims=True))
    ).astype(bf16)
    d_query = jnp.einsum("bhlm,bmhe->blhe", d_scores, key_heads, preferred_element_type=f32) * 0.125
    d_key = jnp.einsum("bhlm,blhe->bmhe", d_scores, query_heads, preferred_element_type=f32) * 0.125
    d_projected = jnp.concatenate(
        [
            d_query.reshape(token_rows, D),
            d_key.reshape(token_rows, D),
            d_value.reshape(token_rows, D),
        ],
        axis=1,
    ).astype(bf16)
    d_sums = column_sum(d_projected)
    d_qkv_weight = jnp.einsum("td,te->de", inputs, d_projected, preferred_element_type=f32)
    input_grad = d_residual_one + jnp.einsum(
        "te,de->td", d_projected, qkv_weight, preferred_element_type=f32
    )
    flat_grad = jnp.concatenate(
        [
            matrix_grad.reshape(-1)
            for matrix_grad in (
                d_qkv_weight,
                d_out_weight,
                d_up_weight,
                d_down_weight,
                d_proj_weight,
                d_codebook,
                d_code_weight,
            )
        ]
    )
    vector_gradient = jnp.concatenate(
        [
            d_sums[:D],
            d_sums[2 * D :],
            d_bias_out,
            d_gain_one,
            d_shift_one,
            d_bias_up,
            d_bias_down,
            d_gain_two,
            d_shift_two,
            d_bias_proj,
            quantized_offset_slope,
        ]
    )
    vector_sum, loss_sum = lax.psum((vector_gradient, loss_local), ("dp", "fsdp"))
    grad_shard = lax.psum_scatter(flat_grad, ("dp", "fsdp"), scatter_dimension=0, tiled=True)
    square_sum = lax.psum(jnp.sum(grad_shard * grad_shard), ("dp", "fsdp"))
    return finish(
        total_masked, square_sum, vector_sum, loss_sum, grad_shard, output_low.reshape(count_utts, LEN, D),
        input_grad.reshape(count_utts, LEN, D), params, moment_one, moment_two, vectors, vector_one, vector_two,
    )


def by_kernels(layer_input, mask_index, distract, code_choice, params, moment_one, moment_two, vectors, vector_one, vector_two):
    total_masked = layer_input.shape[0] * lax.axis_size(("dp", "fsdp")) * MASKED
    kept, output = forward(PIECES_OUT, SENDS_OUT, 1.0 / total_masked, params, layer_input, mask_index, distract, code_choice, vectors)
    grads, sums, squares, input_grad = backward(PIECES_BACK, SENDS_BACK, vectors, kept, lax.axis_size("fsdp"), params.shape[0] // 128)
    new, low, first, second, new_v, first_v, second_v, loss, norm = update(
        total_masked, grads, params, moment_one, moment_two, sums, vectors, vector_one, vector_two, squares
    )
    return loss, norm, output, input_grad, new, low, first, second, new_v, first_v, second_v


def solution(mesh):
    in_specs = (
        P(("dp", "fsdp"), None, None),
        P(("dp", "fsdp"), None),
        P(("dp", "fsdp"), None, None),
        P(("dp", "fsdp"), None, None),
        P(("dp", "fsdp")),
        P(("dp", "fsdp")),
        P(("dp", "fsdp")),
        P(),
        P(),
        P(),
    )
    out_specs = (
        P(),
        P(),
        P(("dp", "fsdp"), None, None),
        P(("dp", "fsdp"), None, None),
        P(("dp", "fsdp")),
        P(("dp", "fsdp")),
        P(("dp", "fsdp")),
        P(("dp", "fsdp")),
        P(),
        P(),
        P(),
    )
    fits = mesh.shape["dp"] == PLANES and mesh.shape["fsdp"] == 8
    return jax.shard_map(
        by_kernels if fits else by_collectives, mesh=mesh, in_specs=in_specs, out_specs=out_specs, check_vma=False
    )
```

```python
import functools

import jax
import jax.numpy as jnp
from jax import lax
from jax.experimental import pallas as pl
from jax.experimental.pallas import tpu as pltpu
from jax.sharding import PartitionSpec as P
D = 768; H = 12; HD = 64; FF = 3072; FINAL = 256; G = 2; V = 320; CD = 128; LEN = 472; MASKED = 232
NROW = 9664; GROW = NROW + 256
T = 512
LT = 480
NB = 240
TILE = 768
STEP_T = 512
bf16 = jnp.bfloat16
f32 = jnp.float32
NT = (((1,), (1,)), ((), ()))
BQ, BV, BO, G1, S1, BUP, BDOWN, G2, S2, BPROJ, BCODE = [768 * i for i in range(6)] + [3840 + 3072 + 768 * i for i in range(3)] + [9216, 9472]

def mm(a, b):
    return jnp.dot(a, b, preferred_element_type=f32)

def mm_nt(a, b, precision=None):
    return lax.dot_general(a, b, NT, preferred_element_type=f32, precision=precision)

def hi(a, b):
    return jnp.dot(a, b, preferred_element_type=f32, precision=lax.Precision.HIGHEST)

def split_rows(g, base, parts, nice, first, tmp):
    def body(b, _):
        src = pl.multiple_of(base + b * 64 * parts, 64)
        for j in range(6):
            tmp[j, 0:64 * parts, :] = g[pl.ds(src, 64 * parts), 128 * j:128 * j + 128].astype(f32)
        for t in range(parts):
            at = pl.multiple_of((first + t) * D + b * 64, 64)
            for j in range(6):
                nice[pl.ds(at, 64), 128 * j:128 * j + 128] = tmp[j, pl.ds(t, 64, stride=parts), :].astype(bf16)
        return 0
    lax.fori_loop(0, D // 64, body, 0)

def norm_rows(r, gain, shift, low, wide, hat, rstd):
    def body(b, _):
        at = pl.multiple_of(b * NB, 16)
        v = r[pl.ds(at, NB), :]
        m = jnp.mean(v, axis=-1, keepdims=True)
        c = v - m
        var = jnp.mean(c * c, axis=-1, keepdims=True)
        inv = lax.rsqrt(var + eps_norm)
        xh = c * inv
        o = xh * gain + shift
        hat[pl.ds(at, NB), :] = xh
        rstd[pl.ds(at, NB), :] = jnp.broadcast_to(inv, (NB, 128))
        if wide is not None:
            wide[pl.ds(at, NB), :] = o
        low[pl.ds(at, NB), :] = o.astype(bf16)
        return 0
    lax.fori_loop(0, LT // NB, body, 0)

def transpose_to(src, dst, rows, cols):
    step = min(STEP_T, cols // 3)
    def body(n, _):
        at = pl.multiple_of(n * step, step)
        dst[pl.ds(at, step), :] = src[:, pl.ds(at, step)].T
        return 0
    lax.fori_loop(0, cols // step, body, 0)

def prepare(x_ref, xp, xT, mask_ref, distract_ref, choice_ref, vec_ref, vec, place, placeT, allowed, choose):
    for i in range(vec_ref.shape[0]):
        vec[0:1, 128 * i:128 * i + 128] = vec_ref[i:i + 1, :]
    xp[...] = jnp.zeros((T, D), bf16)
    xp[0:LEN, :] = x_ref[0]
    transpose_to(xp, xT, T, D)
    zero = jnp.zeros((1, 256 - MASKED), jnp.int32) - 1
    def wide(row):
        return jnp.concatenate([row, zero], axis=1)
    hot = jnp.where(lax.broadcasted_iota(jnp.int32, (T, 256), 0) == wide(mask_ref[...]), 1.0, 0.0)
    placeT[...] = hot.astype(bf16)
    place[...] = hot.T.astype(bf16)
    row = lax.broadcasted_iota(jnp.int32, (256, 256), 0)
    col = lax.broadcasted_iota(jnp.int32, (256, 256), 1)
    allowed[...] = jnp.where((row == col) & (col < MASKED), 1.0, 0.0)
    rows = [wide(distract_ref[i]) for i in range(distract_ref.shape[0])]
    def body(b, _):
        at = pl.multiple_of(8 * b, 8)
        acc = allowed[pl.ds(at, 8), :]
        n = lax.broadcasted_iota(jnp.int32, (8, 256), 0) + at
        for r in rows:
            acc = jnp.where(n == r, 1.0, acc)
        allowed[pl.ds(at, 8), :] = acc
        return 0
    lax.fori_loop(0, MASKED // 8, body, 0)
    allowed[...] = allowed[...].T
    for g in range(2):
        v = jnp.where(lax.broadcasted_iota(jnp.int32, (384, 256), 0) == wide(choice_ref[0, g:g + 1, :]), 1.0, 0.0)
        choose[g] = v.T

def project(xp, nice, vec, q, kk, kT, vv, vT):
    for t, (dst, bias) in enumerate(((q, BQ), (kk, None), (vv, BV))):
        for n in range(3):
            acc = mm(xp[...], nice[t * D:(t + 1) * D, 256 * n:256 * n + 256])
            if bias is not None:
                acc = acc + vec[0:1, bias + 256 * n:bias + 256 * n + 256]
            dst[:, 256 * n:256 * n + 256] = acc.astype(bf16)
    transpose_to(kk, kT, T, D)
    transpose_to(vv, vT, T, D)

def attend(p, q, kk, vT, pT, attT):
    at = pl.multiple_of(128 * p, 128)
    qp = q[:, pl.ds(at, 128)]
    kp = kk[0:LT, pl.ds(at, 128)]
    lane = lax.broadcasted_iota(jnp.int32, (LT, 128), 1)
    for h in range(2):
        kh = jnp.where((lane < 64) == (h == 0), kp, jnp.zeros_like(kp))
        s = mm_nt(kh, qp)[0:LEN] * 0.125
        e = jnp.exp(s - jnp.max(s, axis=0, keepdims=True))
        pr = e * (1.0 / jnp.sum(e, axis=0, keepdims=True))
        pr = jnp.concatenate([pr, jnp.zeros((T - LEN, T), f32)], axis=0).astype(bf16)
        pT[pl.ds(pl.multiple_of((2 * (p % 2) + h) * T, T), T), :] = pr
        rows = pl.ds(pl.multiple_of(128 * p + 64 * h, 64), 64)
        attT[rows, :] = mm(vT[rows, :], pr).astype(bf16)

def out_project(attT, att, xp, wo, vec, res):
    for n in range(6):
        att[:, 128 * n:128 * n + 128] = attT[128 * n:128 * n + 128, :].T
    for n in range(3):
        cols = slice(256 * n, 256 * n + 256)
        acc = mm(att[0:LT, :], wo[:, cols])
        res[:, cols] = xp[0:LT, cols].astype(f32) + acc + vec[0:1, BO + 256 * n:BO + 256 * n + 256]

def up(n, norm_low, nice, vec, act, gp):
    root = 0.7071067811865476
    scale = 0.3989422804014327
    c = n * TILE // D
    at = pl.multiple_of(n * TILE, TILE)
    w = nice[pl.ds(pl.multiple_of(c * D, D), D), pl.ds(pl.multiple_of(at - c * D, TILE), TILE)]
    h = mm(norm_low[0:LT, :], w) + vec[0:1, pl.ds(pl.multiple_of(BUP + at, 256), TILE)]
    cdf = 0.5 * (1.0 + lax.erf(h * root))
    act[0:LT, pl.ds(at, TILE)] = (h * cdf).astype(bf16)
    gp[0:LT, pl.ds(at, TILE)] = (cdf + h * (scale * jnp.exp(-0.5 * h * h))).astype(bf16)

def down(act, g, vec, res, wide):
    for n in range(3):
        cols = slice(256 * n, 256 * n + 256)
        acc = mm(act[0:LT, :], g[6144:9216, cols])
        res[:, cols] = wide[:, cols] + acc + vec[0:1, BDOWN + 256 * n:BDOWN + 256 * n + 256]

def small_weights(g, fb, p32, c32, wproj, code, wcode):
    for t in range(3):
        for j in range(2):
            p32[j, pl.ds(t, 256, stride=3), :] = g[9216:9472, 256 * t + 128 * j:256 * t + 128 * j + 128].astype(f32)
    for j in range(2):
        wproj[:, 128 * j:128 * j + 128] = p32[j].astype(bf16)
    for j in range(6):
        fb[pl.ds(j, 192, stride=6), :] = g[9472:9664, 128 * j:128 * j + 128].astype(f32)
    a = [fb[pl.ds(j, 128, stride=5), :] for j in range(5)]
    lo = lax.broadcasted_iota(jnp.int32, (128, 128), 1) < 64
    r2, r3, r4 = [pltpu.roll(v, 64, 1) for v in a[2:]]
    zero = jnp.zeros((128, 128), f32)
    even = [a[0], a[1], jnp.where(lo, a[2], zero)]
    odd = [jnp.where(lo, r2, r3), jnp.where(lo, r3, r4), jnp.where(lo, r4, zero)]
    for j in range(3):
        c32[j, pl.ds(0, 128, stride=2), :] = even[j]
        c32[j, pl.ds(1, 128, stride=2), :] = odd[j]
        code[:, 128 * j:128 * j + 128] = c32[j].astype(bf16)
    for j in range(2):
        wcode[:, 128 * j:128 * j + 128] = fb[pl.ds(640 + j, 256, stride=2), :].astype(bf16)

def contrast(weight, out_low, vec, place, placeT, allowed, choose, wproj, code, wcode, fb, p32, c32, tail, dctx, small):
    picked = mm(place[...], out_low[...]).astype(bf16)
    chosen = mm(picked, wproj[...]) + vec[0:1, BPROJ:BPROJ + 256]
    cv = jnp.concatenate([mm_nt(choose[g].astype(bf16), code[128 * g:128 * g + 128, :]) for g in range(2)], axis=1).astype(bf16)
    targets = mm(cv, wcode[...]) + vec[0:1, BCODE:BCODE + 256]
    n_l = lax.rsqrt(jnp.sum(chosen * chosen, axis=1, keepdims=True) + eps_cos)
    n_r = lax.rsqrt(jnp.sum(targets * targets, axis=1, keepdims=True) + eps_cos)
    left = chosen * n_l
    right = targets * n_r
    sim = mm_nt(left, right, lax.Precision.HIGHEST) / 0.1
    ok = allowed[...] > 0.5
    row = lax.broadcasted_iota(jnp.int32, (256, 256), 0)
    col = lax.broadcasted_iota(jnp.int32, (256, 256), 1)
    eye = jnp.where((row == col) & (row < MASKED), 1.0, 0.0)
    pos = jnp.sum(eye * sim, axis=1, keepdims=True)
    top = jnp.max(jnp.where(ok, sim, -1e30), axis=1, keepdims=True)
    parts = jnp.where(ok, jnp.exp(jnp.minimum(sim - top, 0.0)), 0.0)
    real = lax.broadcasted_iota(jnp.int32, (256, 1), 0) < MASKED
    total = jnp.where(real, jnp.sum(parts, axis=1, keepdims=True), 1.0)
    loss = jnp.sum(jnp.where(real, top + jnp.log(total) - pos, 0.0))
    dsim = (weight / 0.1) * (parts / total - eye)
    dl = hi(dsim, right)
    dr = hi(dsim.T, left)
    d_chosen = (n_l * dl - chosen * (n_l * n_l * n_l) * jnp.sum(chosen * dl, axis=1, keepdims=True)).astype(bf16)
    d_target = (n_r * dr - targets * (n_r * n_r * n_r) * jnp.sum(targets * dr, axis=1, keepdims=True)).astype(bf16)
    small[0:1, :] = jnp.sum(d_chosen.astype(f32), axis=0, keepdims=True)
    small[1:2, :] = jnp.sum(d_target.astype(f32), axis=0, keepdims=True)
    small[2:3, :] = jnp.broadcast_to(loss, (1, 256))
    dctx[...] = mm(placeT[...], d_chosen).astype(bf16)
    dproj = mm(picked.T, d_chosen)
    for j in range(2):
        p32[j] = dproj[:, 128 * j:128 * j + 128]
    for t in range(3):
        for j in range(2):
            tail[0:256, 256 * t + 128 * j:256 * t + 128 * j + 128] = p32[j, pl.ds(t, 256, stride=3), :].astype(bf16)
    dwcode = mm(cv.T, d_target)
    dcv = mm_nt(d_target, wcode[...])
    for g in range(2):
        dc = hi(dcv[:, 128 * g:128 * g + 128].T, choose[g])
        for j in range(3):
            c32[j, 128 * g:128 * g + 128, :] = dc[:, 128 * j:128 * j + 128]
    e = [c32[j, pl.ds(0, 128, stride=2), :] for j in range(3)]
    o = [pltpu.roll(c32[j, pl.ds(1, 128, stride=2), :], 64, 1) for j in range(3)]
    lo = lax.broadcasted_iota(jnp.int32, (128, 128), 1) < 64
    for j, v in enumerate((e[0], e[1], jnp.where(lo, e[2], o[0]), jnp.where(lo, o[0], o[1]), jnp.where(lo, o[1], o[2]))):
        fb[pl.ds(j, 128, stride=5), :] = v
    for j in range(2):
        fb[pl.ds(640 + j, 256, stride=2), :] = dwcode[:, 128 * j:128 * j + 128]
    for j in range(6):
        tail[256:448, 128 * j:128 * j + 128] = fb[pl.ds(j, 192, stride=6), :].astype(bf16)
STEP = 10


eps_norm = 1e-05
eps_cos = 1e-06
softness_divisor = 0.1
beta_one = 0.9
beta_two = 0.98
adam_eps = 1e-08
decay_rate = 0.01
rate_matrix = 0.03
rate_vector = 0.2
clip_level = 0.001


def sum8(v):
    r, n = v.shape
    return jnp.sum(v.reshape(r // 8, 8, n), axis=0)

def norm_back_first(dctx, wproj, gain, hat, rstd, low, acc):
    acc[...] = jnp.zeros((24, D), f32)
    def body(b, _):
        at = pl.multiple_of(b * 48, 16)
        dy = mm_nt(dctx[pl.ds(at, 48), :], wproj[...])
        norm_back_rows(dy, at, gain, hat, hat, rstd, low, acc)
        return 0
    lax.fori_loop(0, LT // 48, body, 0)

def norm_back_rows(dy, at, gain, hat, dst, rstd, low, acc):
    xh = hat[pl.ds(at, NB), :]
    inv = rstd[pl.ds(at, NB), 0:1]
    a = dy * gain
    m1 = jnp.mean(a, axis=-1, keepdims=True)
    m2 = jnp.mean(a * xh, axis=-1, keepdims=True)
    dr = inv * (a - m1 - xh * m2)
    lo = dr.astype(bf16)
    dst[pl.ds(at, NB), :] = dr
    low[pl.ds(at, NB), :] = lo
    acc[0:8, :] += sum8(dy * xh)
    acc[8:16, :] += sum8(dy)
    acc[16:24, :] += sum8(lo.astype(f32))

def norm_back(dy, gain, hat, rstd, low, acc):
    acc[...] = jnp.zeros((24, D), f32)
    def body(b, _):
        at = pl.multiple_of(b * NB, 16)
        norm_back_rows(dy[pl.ds(at, NB), :], at, gain, hat, hat, rstd, low, acc)
        return 0
    lax.fori_loop(0, LT // NB, body, 0)

def put_vec(vg, acc, offsets):
    for i, o in enumerate(offsets):
        vg[0:1, o:o + D] = jnp.sum(acc[8 * i:8 * i + 8, :], axis=0, keepdims=True)

def down_back(n, low2, gg, actT, gp, vg):
    at = pl.multiple_of(n * TILE, TILE)
    rows = pl.ds(pl.multiple_of(6144 + n * TILE, 256), TILE)
    d = mm_nt(low2[0:LT, :], gg[rows, :]) * gp[0:LT, pl.ds(at, TILE)].astype(f32)
    d = d.astype(bf16)
    gp[0:LT, pl.ds(at, TILE)] = d
    vg[0:1, pl.ds(pl.multiple_of(BUP + at, 128), TILE)] = jnp.sum(d.astype(f32), axis=0, keepdims=True)
    gg[rows, :] = mm(actT[pl.ds(at, TILE), :], low2[...]).astype(bf16)

def up_back_x(n, dh, gg, dr):
    cols = pl.ds(pl.multiple_of(n * 256, 256), 256)
    v = dr[:, cols]
    for c in range(4):
        w = gg[pl.ds(pl.multiple_of(3072 + c * D + n * 256, 256), 256), :]
        v = v + mm_nt(dh[0:LT, c * D:(c + 1) * D], w)
    dr[:, cols] = v

def weave(lhsT, rhs, parts, n, base, gg, tmp, stacked):
    def body(m, _):
        cols = pl.ds(pl.multiple_of(m * 256, 256), 256)
        for t in range(parts):
            r = rhs[t, :, cols] if stacked else rhs[:, pl.ds(pl.multiple_of(t * D + m * 256, 256), 256)]
            acc = mm(lhsT[pl.ds(pl.multiple_of(n * 256, 256), 256), :], r)
            for j in range(2):
                tmp[j, pl.ds(t, 256, stride=parts), :] = acc[:, 128 * j:128 * j + 128]
        for j in range(2):
            gg[pl.ds(pl.multiple_of(base + n * 256 * parts, 256), 256 * parts), pl.ds(pl.multiple_of(m * 256 + 128 * j, 128), 128)] = tmp[j, 0:256 * parts, :].astype(bf16)
        return 0
    lax.fori_loop(0, 3, body, 0)

def out_back(low1, gg, attT, da):
    for n in range(3):
        cols = slice(256 * n, 256 * n + 256)
        da[0:LT, cols] = mm_nt(low1[0:LT, :], gg[2304 + 256 * n:2304 + 256 * n + 256, :]).astype(bf16)
    for n in range(3):
        gg[2304 + 256 * n:2304 + 256 * n + 256, :] = mm(attT[256 * n:256 * n + 256, :], low1[...]).astype(bf16)

def attend_back(p, da, q, kT, vv, ring, dp, dqT):
    at = pl.multiple_of(128 * p, 128)
    lane = lax.broadcasted_iota(jnp.int32, (T, 128), 1)
    dap = da[:, pl.ds(at, 128)]
    qp = q[:, pl.ds(at, 128)]
    vp = vv[0:LT, pl.ds(at, 128)]
    dk = dv = None
    for h in range(2):
        half = (lane < 64) == (h == 0)
        dah = jnp.where(half, dap, jnp.zeros_like(dap))
        qh = jnp.where(half, qp, jnp.zeros_like(qp))
        pr = ring[pl.ds(pl.multiple_of(((2 * p + h) % 6) * T, T), LT), :]
        dpT = mm_nt(vp, dah)
        prf = pr.astype(f32)
        w = prf * dpT
        ds = (w - prf * jnp.sum(w, axis=0, keepdims=True)).astype(bf16)
        a = mm(pr, dah)
        b = mm(ds, qh)
        dv = a if dv is None else dv + a
        dk = b if dk is None else dk + b
        rows = pl.ds(pl.multiple_of(128 * p + 64 * h, 64), 64)
        dqT[rows, :] = (mm(kT[rows, 0:LT], ds) * 0.125).astype(bf16)
    dp[1, 0:LT, pl.ds(at, 128)] = (dk * 0.125).astype(bf16)
    dp[2, 0:LT, pl.ds(at, 128)] = dv.astype(bf16)
    dp[0, :, pl.ds(at, 128)] = dqT[pl.ds(at, 128), :].T

def input_back(n, dp, wq, dr, out):
    cols = slice(256 * n, 256 * n + 256)
    v = dr[:, cols]
    for t in range(3):
        v = v + mm_nt(dp[t, 0:LT, :], wq[t * D + 256 * n:t * D + 256 * n + 256, :])
    out[0, :, cols] = v[0:LEN]
MESH = pl.DeviceIdType.MESH
UP, DOWN, U, V_AXIS, CORE, HERE = range(6)
PLANES = 4
MAIN = 288
EXTRA = 16
HALF = MAIN + EXTRA
RAW = 96
PLANE = 2416
UNIT = 608

class Place:
    def __init__(self):
        self.z = lax.axis_index("dp")
        self.f = f = lax.axis_index("fsdp")
        self.c = c = f % 2
        self.k = k = f // 2
        x = k % 2
        y = k // 2
        self.fc = f + 1 - 2 * c
        self.fx = f + 2 - 4 * x
        self.fy = f + 4 - 8 * y
        self.uf = self.fx * (1 - c) + self.fy * c
        self.vf = self.fy * (1 - c) + self.fx * c
        self.roles = (k, self.uf // 2, self.vf // 2, 3 - k)

    def greet(self):
        z = self.z
        bar = pltpu.get_barrier_semaphore()
        for t in (self.fc, self.fx, self.fy):
            pl.semaphore_signal(bar, inc=1, device_id=(z, t), device_id_type=MESH)
        @pl.when(z > 0)
        def _(): pl.semaphore_signal(bar, inc=1, device_id=(z - 1, self.f), device_id_type=MESH)
        @pl.when(z < PLANES - 1)
        def _(): pl.semaphore_signal(bar, inc=1, device_id=(z + 1, self.f), device_id_type=MESH)
        pl.semaphore_wait(bar, 3 + (z + PLANES - 1) // PLANES + (2 * PLANES - 2 - z) // PLANES)

    def greet_all(self, count):
        bar = pltpu.get_barrier_semaphore()
        for j in range(1, count):
            pl.semaphore_signal(bar, inc=1, device_id=(self.z, lax.rem(self.f + j, count)), device_id_type=MESH)
        for j in range(1, PLANES):
            pl.semaphore_signal(bar, inc=1, device_id=(lax.rem(self.z + j, PLANES), self.f), device_id_type=MESH)
        pl.semaphore_wait(bar, count + PLANES - 2)

    def span_of(self, p, kk, c, first):
        m = PLANE * p + UNIT * kk
        return (pl.multiple_of(m + HALF * c + first, 16),
                pl.multiple_of((m + MAIN) * (1 - c) + (NROW + EXTRA * (4 * p + kk)) * c, 16))

    def span(self, p, r, c, first):
        return self.span_of(p, self.roles[r], c, first)

def remote(src, dst, ssem, rsem, dev):
    return pltpu.make_async_remote_copy(src_ref=src, dst_ref=dst, send_sem=ssem, recv_sem=rsem, device_id=dev, device_id_type=MESH)

def shared_blocks(g, p):
    row = lax.broadcasted_iota(jnp.int32, (16, D), 0)
    e = [g[NROW + 16 * (4 * p + q):NROW + 16 * (4 * p + q) + 16, :].astype(f32) for q in range(4)]
    for q, bound in enumerate((12, 8, 4)):
        at = PLANE * p + UNIT * q + 592
        g[at:at + 16, :] = jnp.where(row < bound, e[q], e[q + 1]).astype(bf16)

def extra_rows(g, p, q):
    row = lax.broadcasted_iota(jnp.int32, (16, D), 0)
    b = [g[PLANE * p + UNIT * i + 592:PLANE * p + UNIT * i + 608, :].astype(f32) for i in range(max(q - 1, 0), min(q, 2) + 1)]
    v = b[0] if len(b) == 1 else jnp.where(row < 12 - 4 * q, b[1], b[0])
    g[NROW + 16 * (4 * p + q):NROW + 16 * (4 * p + q) + 16, :] = v.astype(bf16)

class Gather:
    def __init__(self, at, g, pieces, R, O, S):
        self.at, self.g, self.pieces, self.R, self.O, self.S = at, g, pieces, R, O, S
        self.index = {}
        self.made = {z: [] for z in range(PLANES)}
        self.seen = set()

    def sem(self, key):
        return self.S.at[self.index.setdefault(key, len(self.index))]

    def copies(self, i, p, r, dev, kind, c):
        _, first, rows, extra = self.pieces[p][i]
        a, e = self.at.span(p, r, c, first)
        unit = 4 * p + self.at.roles[r]
        got = self.O if kind == CORE else self.R
        out = []
        for j, (s, n) in enumerate([(a, rows)] + [(e, EXTRA)] * extra):
            ref = self.g.at[pl.ds(s, n)]
            out.append(remote(ref, ref, self.sem((HERE, j) if kind == HERE else (kind, i, p, r, j)), got.at[unit, i + j], dev))
        return out

    def op(self, zs, kind, i, p, r):
        at = self.at
        if not (p == zs and r == 0) and (zs, i, p, r) not in self.seen:
            self.seen.add((zs, i, p, r))
            for q in self.copies(i, p, r, (zs, at.fc), HERE, at.c): q.wait_recv()
        dev = ((zs + 1, at.f), (zs - 1, at.f), (zs, at.uf), (zs, at.vf), (zs, at.fc))[kind]
        for q in self.copies(i, p, r, dev, kind, at.c): q.start()
        self.made[zs].append((kind, i, p, r))

    def other_core(self, zs, p):
        for r in range(4):
            if p == zs and r == 0: continue
            for i in range(len(self.pieces[p])):
                for q in self.copies(i, p, r, (zs, self.at.fc), CORE, 1 - self.at.c): q.wait_recv()

    def drain(self):
        for zs in range(PLANES):
            @pl.when(self.at.z == zs)
            def _():
                for kind, i, p, r in self.made[zs]:
                    for q in self.copies(i, p, r, (zs, self.at.fc), kind, self.at.c): q.wait_send()

def own_rows(at, g, p_ref, raw, sem):
    n = p_ref.shape[0]
    gap = -n % 8
    base = pl.multiple_of(RAW + (n + gap) * at.c, 8)
    mine = pltpu.make_async_copy(p_ref.at[pl.ds(0, n)], raw.at[pl.ds(base, n)], sem.at[2])
    mine.start()
    both = remote(p_ref.at[pl.ds(0, n)], raw.at[pl.ds(base, n)], sem.at[0], sem.at[1], (at.z, at.fc))
    both.start()
    mine.wait()
    both.wait()
    k = at.k
    own = pl.multiple_of(PLANE * at.z + UNIT * k, 16)
    extra = pl.multiple_of(NROW + EXTRA * (4 * at.z + k), 16)
    row = lax.broadcasted_iota(jnp.int32, (16, 128), 0)
    first_core = lax.broadcasted_iota(jnp.int32, (592, 128), 0) + 4 * k < n // 6
    for j in range(6):
        cols = slice(128 * j, 128 * j + 128)
        v = [raw[pl.ds(RAW + gap * i + 24 * k + j, 592, stride=6), :] for i in range(2)]
        g[pl.ds(own, 592), cols] = jnp.where(first_core, v[0], v[1]).astype(bf16)
        last = raw[pl.ds(RAW + gap + (592 + 4 * k) * 6 + j, 16, stride=6), :]
        first = raw[pl.ds(RAW - 96 + 24 * k + j, 16, stride=6), :]
        g[pl.ds(extra, 16), cols] = jnp.where(row < 12 - 4 * k, last, first).astype(bf16)

K1_OUT = ("w", "wproj", "tail", "dctx", "small", "hat1", "r1", "hat2", "r2", "gp", "actT", "normT", "attT", "q", "kT", "vv", "xT", "pT")
K1_SHAPE = {"w": ((NROW, D), bf16), "wproj": ((D, 256), bf16), "tail": ((448, D), bf16), "dctx": ((T, 256), bf16), "small": ((8, 256), f32),
            "hat1": ((LT, D), f32), "r1": ((LT, 128), f32), "hat2": ((LT, D), f32), "r2": ((LT, 128), f32), "gp": ((T, FF), bf16), "actT": ((FF, T), bf16),
            "normT": ((D, T), bf16), "attT": ((D, T), bf16), "q": ((T, D), bf16), "kT": ((D, T), bf16), "vv": ((T, D), bf16), "xT": ((D, T), bf16),
            "pT": ((H * T, T), bf16)}

def forward_kernel(pieces, events, weight, p_ref, x, mask, dis, cho, vec_ref, *rest):
    n_out = len(K1_OUT)
    hbm = dict(zip(K1_OUT, rest[:n_out]))
    (out, vec, g, raw, nice, tmp, wproj, tail, dctx, small, hat1, r1, hat2, r2, gp, actT, normT, attT, q, kT, vv, xT, pT,
     xp, kk, vT, act, res, wide, low1, low2, place, placeT, allowed, choose, fb, p32, c32, code, wcode,
     sem_raw, R, O, S, OS, PS) = rest[n_out:]
    here = dict(wproj=wproj, tail=tail, dctx=dctx, small=small, hat1=hat1, r1=r1, hat2=hat2, r2=r2, gp=gp, actT=actT, normT=normT, attT=attT, q=q, kT=kT, vv=vv, xT=xT, pT=pT)
    outs = []
    count = iter(range(32))
    def put(src, dst):
        cp = pltpu.make_async_copy(src, dst, OS.at[next(count)])
        cp.start()
        outs.append(cp)
    def save(*names):
        for n in names: put(here[n], hbm[n])
    at = Place()
    ga = Gather(at, g, pieces, R, O, S)
    at.greet()
    own_rows(at, g, p_ref, raw, sem_raw)
    def slot(i, cond=None):
        for zs in range(PLANES):
            if events[zs][i]:
                @pl.when((at.z == zs) if cond is None else ((at.z == zs) & cond))
                def _():
                    for e in events[zs][i]: ga.op(zs, *e)
    def plane(p):
        for zs in range(PLANES):
            @pl.when(at.z == zs)
            def _(): ga.other_core(zs, p)
        shared_blocks(g, p)
    slot(0)
    prepare(x, xp, xT, mask, dis, cho, vec_ref, vec, place, placeT, allowed, choose)
    act[LT:T, :] = jnp.zeros((T - LT, FF), bf16)
    gp[LT:T, :] = jnp.zeros((T - LT, FF), bf16)
    low1[...] = jnp.zeros((T, D), bf16)
    low2[...] = jnp.zeros((T, D), bf16)
    small[...] = jnp.zeros((8, 256), f32)
    save("xT")
    slot(1)
    plane(0)
    split_rows(g, 0, 3, nice, 0, tmp)
    slot(2)
    project(xp, nice, vec, q, kk, kT, vv, vT)
    save("q", "kT", "vv")
    put(nice.at[pl.ds(0, 2304)], hbm["w"].at[pl.ds(0, 2304)])
    nice_out = outs.pop()
    slot(3)
    slot(4)
    def pair_out(p):
        b = p % 2
        return pltpu.make_async_copy(pT.at[pl.ds(pl.multiple_of(2 * T * b, T), 2 * T)], hbm["pT"].at[pl.ds(pl.multiple_of(2 * T * p, T), 2 * T)], PS.at[b])
    def pairs(b, _):
        p = 2 * b
        @pl.when(b > 0)
        def _():
            pair_out(p - 2).wait()
            pair_out(p - 1).wait()
        attend(p, q, kk, vT, pT, attT)
        attend(p + 1, q, kk, vT, pT, attT)
        pair_out(p).start()
        pair_out(p + 1).start()
        for i in range(3): slot(5 + i, b == i)
        return 0
    lax.fori_loop(0, H // 4, pairs, 0)
    pair_out(H // 2 - 2).wait()
    pair_out(H // 2 - 1).wait()
    save("attT")
    plane(1)
    out_project(attT, kk, xp, g.at[2304:3072], vec, res)
    put(g.at[pl.ds(2304, 768)], hbm["w"].at[pl.ds(2304, 768)])
    norm_rows(res, vec[0:1, G1:G1 + D], vec[0:1, S1:S1 + D], low1, wide, hat1, r1)
    save("hat1", "r1")
    transpose_to(low1, normT, T, D)
    save("normT")
    slot(8)
    plane(2)
    nice_out.wait()
    split_rows(g, 3072, 4, nice, 0, tmp)
    put(nice, hbm["w"].at[pl.ds(3072, 3072)])
    slot(9)
    def tile(n, _):
        up(n, low1, nice, vec, act, gp)
        for i in range(3): slot(10 + i, n == i)
        return 0
    lax.fori_loop(0, FF // TILE, tile, 0)
    slot(13)
    save("gp")
    transpose_to(act, actT, T, FF)
    save("actT")
    slot(14)
    plane(3)
    put(g.at[pl.ds(6144, 3072)], hbm["w"].at[pl.ds(6144, 3072)])
    down(act, g, vec, res, wide)
    norm_rows(res, vec[0:1, G2:G2 + D], vec[0:1, S2:S2 + D], low2, None, hat2, r2)
    save("hat2", "r2")
    out[0] = low2[0:LEN, :]
    small_weights(g, fb, p32, c32, wproj, code, wcode)
    save("wproj")
    slot(15)
    contrast(weight, low2, vec, place, placeT, allowed, choose, wproj, code, wcode, fb, p32, c32, tail, dctx, small)
    save("tail", "dctx", "small")
    slot(16)
    ga.drain()
    for cp in outs: cp.wait()

def forward(pieces, events, weight, params, x, mask, dis, cho, vec):
    V_ = pl.BlockSpec(memory_space=pltpu.VMEM)
    A_ = pl.BlockSpec(memory_space=pl.ANY)
    VM = pltpu.VMEM
    DMA = pltpu.SemaphoreType.DMA
    sds = jax.ShapeDtypeStruct
    n = params.shape[0] // 128
    most = max(len(ps) for ps in pieces) + 1
    keys = len({e + (j,) for z in events for s in z for e in s for j in range(1 + pieces[e[2]][e[1]][3])})
    here = [VM(*K1_SHAPE[k]) for k in K1_OUT[1:-1]] + [VM((4 * T, T), bf16)]
    outs = pl.pallas_call(functools.partial(forward_kernel, pieces, events, weight),
        out_shape=[sds(*K1_SHAPE[k]) for k in K1_OUT] + [sds((1, LEN, D), bf16)],
        in_specs=[A_] + [V_] * 5, out_specs=[A_] * len(K1_OUT) + [V_],
        scratch_shapes=[VM((1, vec.shape[0]), f32), VM((GROW, D), bf16), VM((RAW + 2 * (n + 4) + 96, 128), f32), VM((4 * D, D), bf16), VM((6, 256, 128), f32)] + here
            + [VM((T, D), bf16), VM((T, D), bf16), VM((D, T), bf16), VM((T, FF), bf16), VM((LT, D), f32), VM((LT, D), f32), VM((T, D), bf16), VM((T, D), bf16),
               VM((256, T), bf16), VM((T, 256), bf16), VM((256, 256), f32), VM((2, 256, 384), f32), VM((1152, 128), f32), VM((2, 768, 128), f32), VM((3, 256, 128), f32),
               VM((256, 384), bf16), VM((256, 256), bf16),
               DMA((3,)), DMA((16, most)), DMA((16, most)), DMA((keys + 2,)), DMA((24,)), DMA((2,))],
        compiler_params=pltpu.CompilerParams(collective_id=0, has_side_effects=True, vmem_limit_bytes=63 * 2**20),
    )(params.reshape(n, 128), x, mask, jnp.transpose(dis, (2, 0, 1)), jnp.swapaxes(cho, 1, 2), vec.reshape(-1, 128))
    return dict(zip(K1_OUT, outs)), outs[-1]
TO_CORE, TO_V, TO_U, TO_Z, KEEP, SMALL = range(6)

class Reduce:
    def __init__(self, at, g, pieces, LD, LV, LZ, LU, total, RD, RV, RZ, RU, S, SD):
        self.at, self.g, self.pieces, self.total = at, g, pieces, total
        self.LD, self.LV, self.LZ, self.LU = LD, LV, LZ, LU
        self.RD, self.RV, self.RZ, self.RU, self.S, self.SD = RD, RV, RZ, RU, S, SD
        self.index = {}
        self.made = {z: [] for z in range(PLANES)}
        self.seen = set()

    def sem(self, key):
        return self.S.at[self.index.setdefault(key, len(self.index))]

    def copies(self, key, p, r, c, first, rows, extra, land, got, dev):
        a, e = self.at.span(p, r, c, first)
        out = []
        for j, (s, n, to) in enumerate([(a, rows, first)] + [(e, EXTRA, MAIN)] * extra):
            out.append(remote(self.g.at[pl.ds(s, n)], land.at[pl.ds(to, n)], self.sem(key + (j,)), got.at[j], dev))
        return out

    def build(self, zs, op):
        at = self.at
        kind, i, p, r = op
        unit = 4 * p + at.roles[r]
        _, first, rows, extra = self.pieces[p][i]
        if kind == TO_V:
            n = 2 * p + r - 2
            return self.copies(op, p, r, at.c, first, rows, extra, self.LV.at[n], self.RV.at[n, i], (zs, at.vf))
        if kind == TO_U:
            return self.copies(op, p, r, at.c, first, rows, extra, self.LU.at[p], self.RU.at[p, i], (zs, at.uf))
        up = p > zs
        to = zs + 1 if up else zs - 1
        n = 8 + r if (not up and to == p) else 2 * p + r
        return self.copies(op, p, r, at.c, first, rows, extra, self.LZ.at[n], self.RZ.at[n, i], (to, at.f))

    def once(self, zs, key, cs):
        if (zs, key) not in self.seen:
            self.seen.add((zs, key))
            for q in cs: q.wait_recv()

    def send(self, zs, op):
        for q in self.build(zs, op): q.start()
        self.made[zs].append(op)

    def add(self, p, r, first, rows, extra, lands, final):
        a, e = self.at.span(p, r, self.at.c, first)
        g, total = self.g, self.total
        def one(s, i):
            v = g[pl.ds(s, 16), :].astype(f32)
            for land in lands:
                v = v + land[pl.ds(i, 16), :].astype(f32)
            if final:
                total[pl.ds(16 + i, 16), :] = v
            else:
                g[pl.ds(s, 16), :] = v.astype(bf16)
        def body(b, _):
            one(pl.multiple_of(a + 16 * b, 16), pl.multiple_of(first + 16 * b, 16))
            return 0
        lax.fori_loop(0, rows // 16, body, 0)
        if extra: one(e, MAIN)

    def op(self, zs, op):
        at = self.at
        kind, i, p, r = op
        unit = 4 * p + at.roles[r]
        self.once(zs, (TO_CORE, p, r), self.copies((HERE,), p, r, at.c, 0, MAIN, True, self.LD.at[unit], self.RD.at[unit], (zs, at.fc)))
        path, first, rows, extra = self.pieces[p][i]
        if kind == TO_V:
            self.add(p, r, first, rows, extra, [self.LD.at[unit]], False)
            self.send(zs, op)
            return
        n = 2 * p + r
        self.once(zs, ("v", i, p, r), self.copies((HERE,), p, r, at.c, first, rows, extra, self.LV.at[n], self.RV.at[n, i], (zs, at.fc)))
        lands = [self.LD.at[unit], self.LV.at[n]]
        def arrived(land, got, key):
            self.once(zs, key, self.copies((HERE,), p, r, at.c, first, rows, extra, land, got, (zs, at.fc)))
            lands.append(land)
        if path == 0 or r == 0:
            if p >= zs and zs > 0: arrived(self.LZ.at[n], self.RZ.at[n, i], (UP, i, p, r))
            if p <= zs and zs < PLANES - 1:
                m = 8 + r if p == zs else n
                arrived(self.LZ.at[m], self.RZ.at[m, i], (DOWN, i, p, r))
        if r == 0 and (path == 1 or p == zs):
            arrived(self.LU.at[p], self.RU.at[p, i], (TO_U, i, p))
        self.add(p, r, first, rows, extra, lands, kind == KEEP)
        if kind != KEEP: self.send(zs, op)

    def core_copies(self, p, kk):
        a, e = self.at.span_of(p, kk, 1 - self.at.c, 0)
        land = self.LD.at[4 * p + kk]
        dev = (self.at.z, self.at.fc)
        return [remote(self.g.at[pl.ds(s, n)], land.at[pl.ds(to, n)], self.SD.at[4 * p + kk, j], self.RD.at[4 * p + kk, j], dev)
                for j, (s, n, to) in enumerate(((a, MAIN, 0), (e, EXTRA, MAIN)))]

    def to_core(self, p, kk):
        extra_rows(self.g, p, kk)
        for q in self.core_copies(p, kk): q.start()

    def drain(self):
        for zs in range(PLANES):
            @pl.when(self.at.z == zs)
            def _():
                for op in self.made[zs]:
                    for q in self.build(zs, op): q.wait_send()
        for p in range(PLANES):
            for kk in range(4):
                for q in self.core_copies(p, kk): q.wait_send()

class Spread:
    def __init__(self, at, own, land, zland, S, count):
        self.at, self.own, self.land, self.zland, self.S, self.count = at, own, land, zland, S, count

    def round(self, n, me, land, base, dev):
        return [remote(self.own, land.at[me], self.S.at[0, base + j], self.S.at[1, base + j], dev(lax.rem(me + j, n))) for j in range(1, n)]

    def plane(self):
        return self.round(self.count, self.at.f, self.land, 0, lambda t: (self.at.z, t))

    def planes(self):
        return self.round(PLANES, self.at.z, self.zland, self.count, lambda t: (t, self.at.f))

    def first(self):
        for q in self.plane(): q.start()

    def total(self, land, n, me):
        land[me] = self.own[...]
        v = land[0]
        for j in range(1, n): v = v + land[j]
        return v

    def second(self):
        for q in self.plane(): q.wait()
        self.own[...] = self.total(self.land, self.count, self.at.f)
        for q in self.planes(): q.start()

    def last(self):
        for q in self.planes(): q.wait()
        self.own[...] = self.total(self.zland, PLANES, self.at.z)

K2_IN = K1_OUT
K2_HERE = ("wproj", "dctx", "small", "hat1", "r1", "hat2", "r2", "gp", "ring", "normT", "attT", "q", "kT", "vv", "xT", "wq")

def backward_kernel(pieces, events, vec_ref, *rest):
    n_in = len(K2_IN)
    hbm = dict(zip(K2_IN, rest[:n_in]))
    (grad, vsum, sq, ig_out, ig, g, vec, wproj, dctx, small, hat1, r1, hat2, r2, gp, ring, normT, attT, q, kT, vv, xT, wq,
     low1, low2, acc, tmp, dp, LD, LV, LZ, LU, total, flat, vg, vland, vzland, sqv, sland, szland,
     IS, RD, RV, RZ, RU, S, SD, TS, TL, VS, SS) = rest[n_in:]
    here = dict(wproj=wproj, dctx=dctx, small=small, hat1=hat1, r1=r1, hat2=hat2, r2=r2, gp=gp, normT=normT, attT=attT, q=q, kT=kT, vv=vv, xT=xT)
    loads = {}
    def load(name, src=None, dst=None):
        cp = pltpu.make_async_copy(hbm[name] if src is None else src, here[name] if dst is None else dst, IS.at[len(loads)])
        cp.start()
        loads[name if src is None else (name, len(loads))] = cp
        return cp
    w = hbm["w"]
    first = [load(n) for n in ("dctx", "wproj", "hat2", "r2")]
    def second(n):
        rows = pl.ds(pl.multiple_of(6144 + n * TILE, 256), TILE)
        own = pl.ds(pl.multiple_of(n * TILE, TILE), TILE)
        pairs = ((w.at[rows], g.at[rows]), (hbm["actT"].at[own], ring.at[own]), (hbm["gp"].at[:, own], gp.at[:, own]))
        return [pltpu.make_async_copy(s, d, TL.at[3 * n + i]) for i, (s, d) in enumerate(pairs)]
    for n in range(FF // TILE - 1, -1, -1):
        for cp in second(n): cp.start()
    tail = load("tail", hbm["tail"], g.at[pl.ds(9216, 448)])
    third = [load("w", w.at[pl.ds(3072, 3072)], g.at[pl.ds(3072, 3072)]), load("normT")]
    fifth = [load("w", w.at[pl.ds(2304, 768)], g.at[pl.ds(2304, 768)]), load("attT")]
    sixth = [load("q"), load("kT"), load("vv")]
    seventh = [load("xT"), load("w", w.at[pl.ds(0, 2304)], wq)]
    def ready(cs):
        for cp in cs: cp.wait()
    at = Place()
    at.greet_all(vland.shape[0])
    re = Reduce(at, g, pieces, LD, LV, LZ, LU, total, RD, RV, RZ, RU, S, SD)
    vs = Spread(at, vg, vland, vzland, VS, vland.shape[0])
    ss = Spread(at, sqv, sland, szland, SS, vland.shape[0])
    def slot(i, cond=None):
        for zs in range(PLANES):
            if events[zs][i]:
                @pl.when((at.z == zs) if cond is None else ((at.z == zs) & cond))
                def _():
                    for e in events[zs][i]:
                        if e[0] == SMALL: (vs.first, vs.second, vs.last)[e[1]]()
                        else: re.op(zs, e)
    for i in range(vec_ref.shape[0]):
        vec[0:1, 128 * i:128 * i + 128] = vec_ref[i:i + 1, :]
    low2[...] = jnp.zeros((T, D), bf16)
    low1[...] = jnp.zeros((T, D), bf16)
    for t in range(3):
        dp[t] = jnp.zeros((T, D), bf16)
    ready(first)
    for n in range(3):
        hat1[:, 256 * n:256 * n + 256] = mm_nt(dctx[0:LT, :], wproj[256 * n:256 * n + 256, :])
    norm_back(hat1, vec[0:1, G2:G2 + D], hat2, r2, low2, acc)
    fourth = [load("hat1"), load("r1"), load("small")]
    put_vec(vg, acc, (G2, S2, BDOWN))
    ready([tail])
    def downs(n, _):
        ready(second(3 - n))
        down_back(3 - n, low2, g, ring, gp, vg)
        for kk, last in ((3, 0), (2, 0), (1, 1), (0, 2)):
            @pl.when(n == last)
            def _(): re.to_core(3, kk)
        return 0
    lax.fori_loop(0, 3, downs, 0)
    slot(0)
    slot(1)
    ready(second(0))
    down_back(0, low2, g, ring, gp, vg)
    def head(h):
        return pltpu.make_async_copy(hbm["pT"].at[pl.ds(pl.multiple_of(h * T, T), T)], ring.at[pl.ds(pl.multiple_of((h % 6) * T, T), T)], TS.at[h % 6])
    for h in range(6): head(h).start()
    slot(2)
    ready(third)
    lax.fori_loop(0, 3, lambda n, _: (up_back_x(n, gp, g, hat2), 0)[1], 0)
    slot(3)
    def woven(n, _):
        weave(normT, gp, 4, 2 - n, 3072, g, tmp, False)
        for kk in range(4):
            @pl.when(n == int(kk == 0))
            def _(): re.to_core(2, kk)
        slot(4, n == 0)
        slot(5, n == 1)
        return 0
    lax.fori_loop(0, 2, woven, 0)
    slot(6)
    weave(normT, gp, 4, 0, 3072, g, tmp, False)
    re.to_core(1, 2)
    re.to_core(1, 3)
    slot(7)
    ready(fourth)
    norm_back(hat2, vec[0:1, G1:G1 + D], hat1, r1, low1, acc)
    put_vec(vg, acc, (G1, S1, BO))
    ready(fifth)
    da, dqT = low2, normT
    out_back(low1, g, attT, da)
    re.to_core(1, 0)
    re.to_core(1, 1)
    slot(8)
    slot(9)
    ready(sixth)
    def pairs(b, _):
        for p in (2 * b, 2 * b + 1):
            head(2 * p).wait()
            head(2 * p + 1).wait()
        attend_back(2 * b, da, q, kT, vv, ring, dp, dqT)
        attend_back(2 * b + 1, da, q, kT, vv, ring, dp, dqT)
        for p in (2 * b, 2 * b + 1):
            @pl.when(p < 3)
            def _():
                head(2 * p + 6).start()
                head(2 * p + 7).start()
        for i in range(3): slot(10 + i, b == i)
        return 0
    lax.fori_loop(0, H // 4, pairs, 0)
    ready(seventh)
    def wove(n, _):
        weave(xT, dp, 3, n, 0, g, tmp, True)
        for kk in range(4):
            @pl.when(n == min(kk, 2))
            def _(): re.to_core(0, kk)
        for i in range(3): slot(13 + i, n == i)
        return 0
    lax.fori_loop(0, 3, wove, 0)
    slot(16)
    vg[0:1, BQ:BQ + D] = jnp.sum(dp[0].astype(f32), axis=0, keepdims=True)
    vg[0:1, BV:BV + D] = jnp.sum(dp[2].astype(f32), axis=0, keepdims=True)
    vg[0:1, BPROJ:BPROJ + 256] = small[0:1, :]
    vg[0:1, BCODE:BCODE + 256] = small[1:2, :]
    vg[0:1, BCODE + 256:BCODE + 512] = small[2:3, :]
    slot(17)
    slot(18)
    for n in range(3):
        input_back(n, dp, wq, hat1, ig)
    put_ig = pltpu.make_async_copy(ig, ig_out, IS.at[len(loads)])
    put_ig.start()
    slot(19)
    z, c, k = at.z, at.c, at.k
    edge = remote(total.at[pl.ds(HALF, 16)], total.at[pl.ds(0, 16)], TS.at[6], TS.at[7], (z, at.fc))
    edge.start()
    row = lax.broadcasted_iota(jnp.int32, (16, D), 0)
    def square(b, acc):
        v = total[pl.ds(pl.multiple_of(16 + 16 * b, 16), 16), :]
        return acc + sum8(v * v)
    acc = lax.fori_loop(0, MAIN // 16, square, jnp.zeros((8, D), f32))
    v = jnp.where((c == 0) | (row < 12 - 4 * k) | (row >= 16 - 4 * k), total[16 + MAIN:16 + HALF, :], 0.0)
    acc = acc + sum8(v * v)
    sqv[...] = sum(acc[:, 128 * j:128 * j + 128] for j in range(6))
    ss.first()
    for i in range(vsum.shape[0]):
        vsum[i:i + 1, :] = vg[0:1, 128 * i:128 * i + 128]
    n = grad.shape[0] // 6
    edge.wait()
    for j in range(6):
        flat[pl.ds(j, 320, stride=6), :] = total[:, 128 * j:128 * j + 128]
    ss.second()
    for j in range(6):
        grad[pl.ds(j, n, stride=6), :] = flat[pl.ds(6 * (16 - 2 * c - 4 * k) + j, n, stride=6), :]
    ss.last()
    sq[...] = sqv[...]
    put_ig.wait()
    re.drain()

def backward(pieces, events, vec, hbm, count, n):
    V_ = pl.BlockSpec(memory_space=pltpu.VMEM)
    A_ = pl.BlockSpec(memory_space=pl.ANY)
    VM = pltpu.VMEM
    DMA = pltpu.SemaphoreType.DMA
    sds = jax.ShapeDtypeStruct
    most = max(len(ps) for ps in pieces)
    keys = len({e + (j,) for z in events for s in z for e in s if e[0] in (TO_V, TO_U, TO_Z) for j in range(1 + pieces[e[2]][e[1]][3])})
    nv = vec.shape[0] + 256
    shape = dict(K1_SHAPE, ring=((FF, T), bf16), wq=((3 * D, D), bf16))
    return pl.pallas_call(functools.partial(backward_kernel, pieces, events),
        out_shape=[sds((n, 128), f32), sds((nv // 128, 128), f32), sds((8, 128), f32), sds((1, LEN, D), f32)],
        in_specs=[V_] + [A_] * len(K2_IN), out_specs=[V_] * 3 + [A_],
        scratch_shapes=[VM((1, LEN, D), f32), VM((GROW, D), bf16), VM((1, vec.shape[0]), f32)] + [VM(*shape[k]) for k in K2_HERE]
            + [VM((T, D), bf16), VM((T, D), bf16), VM((24, D), f32), VM((2, 1024, 128), f32), VM((3, T, D), bf16),
               VM((16, HALF, D), bf16), VM((8, HALF, D), bf16), VM((10, HALF, D), bf16), VM((4, HALF, D), bf16), VM((HALF + 16, D), f32), VM((6 * (HALF + 16), 128), f32),
               VM((1, nv), f32), VM((count, 1, nv), f32), VM((PLANES, 1, nv), f32), VM((8, 128), f32), VM((count, 8, 128), f32), VM((PLANES, 8, 128), f32),
               DMA((24,)), DMA((16, 2)), DMA((8, most, 2)), DMA((10, most, 2)), DMA((4, most, 2)), DMA((keys + 2,)), DMA((16, 2)), DMA((8,)), DMA((12,)), DMA((2, count + PLANES)), DMA((2, count + PLANES))],
        compiler_params=pltpu.CompilerParams(collective_id=1, has_side_effects=True, vmem_limit_bytes=63 * 2**20),
    )(vec.reshape(-1, 128), *[hbm[k] for k in K2_IN])

def update_kernel(total, g, p, m1, m2, vg, v, v1, v2, sq, np_, low, n1, n2, nv, nv1, nv2, loss, norm, scale):
    @pl.when(pl.program_id(0) == 0)
    def _():
        n = v.shape[0]
        gv = vg[0:n, :]
        s = jnp.sum(jnp.sum(sq[...], axis=0, keepdims=True), axis=1, keepdims=True)
        s = s + jnp.sum(jnp.sum(gv * gv, axis=0, keepdims=True), axis=1, keepdims=True)
        s = jnp.sqrt(s)
        f = jnp.minimum(1.0, clip_level / (s + 1e-06))
        norm[...] = s
        loss[...] = vg[n:n + 1, 0:1] / total
        scale[...] = jnp.broadcast_to(f, (8, 128))
        nv[...], nv1[...], nv2[...] = adamw_update(v[...], v1[...], v2[...], gv * f, rate_vector)
    new, first, second = adamw_update(p[...], m1[...], m2[...], g[...] * scale[0:1, 0:1], rate_matrix)
    np_[...] = new
    low[...] = new.astype(bf16)
    n1[...] = first
    n2[...] = second

def update(total, g, p, m1, m2, vg, v, v1, v2, sq):
    n, nv = g.shape[0], v.shape[0] // 128
    sds = jax.ShapeDtypeStruct
    rows = 608
    part = pl.BlockSpec((rows, 128), lambda i: (i, 0))
    def whole(*shape): return pl.BlockSpec(shape, lambda i: (0, 0))
    flat = lambda a: a.reshape(-1, 128)
    out = pl.pallas_call(functools.partial(update_kernel, total), grid=(pl.cdiv(n, rows),),
        out_shape=[sds((n, 128), f32), sds((n, 128), bf16), sds((n, 128), f32), sds((n, 128), f32)] + [sds((nv, 128), f32)] * 3 + [sds((1, 1), f32)] * 2,
        in_specs=[part] * 4 + [whole(*vg.shape)] + [whole(nv, 128)] * 3 + [whole(8, 128)],
        out_specs=[part] * 4 + [whole(nv, 128)] * 3 + [whole(1, 1)] * 2,
        scratch_shapes=[pltpu.VMEM((8, 128), f32)],
    )(g, flat(p), flat(m1), flat(m2), vg, flat(v), flat(v1), flat(v2), sq)
    return [a.reshape(-1) for a in out[:7]] + [a.reshape(()) for a in out[7:]]

PIECES_OUT = (((0, 0, 48, False), (0, 48, 48, False), (0, 96, 48, False), (1, 144, 48, False), (1, 192, 32, False), (1, 224, 32, False), (1, 256, 32, True)),
 ((0, 0, 96, False), (0, 96, 96, False), (0, 192, 96, True)), ((1, 0, 144, False), (1, 144, 144, True)), ((0, 0, 192, False), (1, 192, 96, True)))
PIECES_BACK = (((0, 0, 48, False), (0, 48, 48, False), (0, 96, 48, False), (1, 144, 48, False), (1, 192, 32, False), (1, 224, 32, False), (1, 256, 32, True)),
 ((0, 0, 192, False), (1, 192, 48, False), (1, 240, 48, True)), ((1, 0, 96, False), (1, 96, 96, False), (1, 192, 96, True)),
 ((0, 0, 144, False), (0, 144, 144, True)))
SENDS_OUT = ((((0, 0, 0, 0), (0, 1, 0, 0), (3, 0, 0, 0), (3, 1, 0, 0), (3, 2, 0, 0)),
  ((0, 2, 0, 0), (0, 3, 0, 0), (4, 0, 0, 2), (3, 3, 0, 0), (3, 4, 0, 0), (4, 1, 0, 2), (0, 4, 0, 0), (3, 5, 0, 0), (4, 2, 0, 2), (3, 6, 0, 0),
   (0, 5, 0, 0), (4, 0, 1, 0), (2, 0, 0, 0), (2, 1, 0, 0), (0, 6, 0, 0), (2, 2, 0, 0), (4, 3, 0, 2), (2, 3, 0, 0), (4, 4, 0, 2), (2, 4, 0, 0),
   (4, 5, 0, 2), (4, 1, 1, 0), (2, 5, 0, 0), (4, 6, 0, 2), (2, 6, 0, 0), (3, 0, 1, 0), (0, 0, 0, 1), (4, 0, 0, 1), (0, 1, 0, 1), (4, 1, 0, 1),
   (3, 0, 0, 1), (0, 2, 0, 1), (4, 2, 0, 1), (4, 3, 0, 1), (3, 1, 0, 1), (4, 4, 0, 1), (3, 2, 0, 1), (4, 5, 0, 1), (4, 2, 1, 0), (3, 3, 0, 1),
   (4, 6, 0, 1), (3, 4, 0, 1), (3, 5, 0, 1), (3, 6, 0, 1), (4, 0, 1, 2), (3, 1, 1, 0), (4, 0, 0, 3), (4, 0, 2, 0), (4, 1, 0, 3), (3, 0, 2, 0),
   (4, 2, 0, 3), (4, 3, 0, 3), (4, 4, 0, 3), (4, 5, 0, 3), (2, 0, 2, 0), (4, 6, 0, 3), (4, 1, 2, 0), (4, 1, 1, 2), (3, 1, 2, 0)),
  (), ((3, 0, 2, 1), (4, 0, 1, 1), (4, 0, 2, 2), (4, 0, 2, 1), (4, 1, 1, 1), (2, 1, 2, 0)), (), ((3, 2, 1, 0), (4, 1, 2, 2)),
  ((4, 2, 1, 1), (3, 0, 1, 1), (3, 1, 1, 1), (4, 0, 2, 3), (4, 1, 2, 1)),
  ((3, 1, 2, 1), (4, 2, 1, 2), (4, 0, 3, 0), (4, 0, 1, 3), (3, 2, 1, 1), (4, 1, 1, 3), (3, 0, 3, 0), (4, 1, 3, 0), (4, 1, 2, 3), (2, 1, 3, 0),
   (4, 2, 1, 3), (3, 1, 3, 0), (4, 0, 3, 2), (4, 0, 3, 1), (3, 0, 3, 1)),
  ((4, 1, 3, 1), (3, 1, 3, 1)), ((4, 1, 3, 2),), (), (), (), ((4, 0, 3, 3),), ((4, 1, 3, 3),), (), ()),
 (((1, 0, 1, 0), (2, 0, 1, 0), (2, 1, 1, 0), (0, 0, 1, 0)),
  ((1, 1, 1, 0), (2, 2, 1, 0), (0, 1, 1, 0), (3, 0, 1, 0), (4, 0, 0, 0), (4, 0, 1, 1), (1, 2, 1, 0), (0, 0, 0, 0), (3, 0, 0, 0), (4, 1, 0, 0),
   (4, 1, 1, 1), (3, 1, 0, 0), (0, 1, 0, 0), (3, 1, 1, 0), (4, 0, 2, 0), (4, 2, 0, 0), (4, 2, 1, 1), (1, 0, 2, 0), (0, 2, 0, 0), (3, 2, 0, 0),
   (4, 3, 0, 0), (2, 3, 0, 0), (4, 0, 1, 2), (0, 3, 0, 0), (4, 4, 0, 0), (4, 0, 0, 2), (2, 4, 0, 0), (3, 3, 0, 0), (4, 1, 0, 2), (0, 4, 0, 0),
   (4, 5, 0, 0), (2, 5, 0, 0), (3, 4, 0, 0), (0, 5, 0, 0), (1, 1, 2, 0), (4, 6, 0, 0), (0, 6, 0, 0), (4, 2, 0, 2), (4, 1, 1, 2), (4, 3, 0, 1),
   (2, 6, 0, 0), (4, 4, 0, 1), (0, 0, 0, 1), (4, 0, 0, 1), (4, 3, 0, 2), (3, 5, 0, 0), (4, 5, 0, 1), (4, 1, 0, 1), (0, 1, 0, 1), (4, 4, 0, 2),
   (3, 6, 0, 0), (3, 3, 0, 1), (3, 4, 0, 1), (1, 0, 1, 1), (0, 2, 0, 1), (4, 2, 0, 1), (4, 0, 3, 0), (4, 6, 0, 1), (4, 5, 0, 2), (3, 0, 0, 1),
   (3, 5, 0, 1), (3, 1, 0, 1), (3, 2, 0, 1), (4, 6, 0, 2), (0, 2, 1, 0), (1, 1, 1, 1), (4, 3, 0, 3), (3, 6, 0, 1), (4, 4, 0, 3), (2, 1, 3, 0),
   (4, 1, 3, 0), (4, 1, 2, 0), (4, 0, 0, 3), (0, 0, 1, 1), (4, 5, 0, 3), (2, 0, 2, 0), (1, 2, 1, 1), (4, 1, 0, 3), (4, 2, 0, 3), (2, 1, 2, 0),
   (4, 6, 0, 3), (0, 1, 1, 1), (1, 0, 3, 0), (4, 1, 3, 1), (3, 0, 2, 0)),
  ((4, 0, 3, 1), (0, 2, 1, 1), (4, 0, 2, 1)), ((3, 1, 2, 0), (4, 1, 2, 1), (1, 1, 3, 0)), (), ((3, 0, 2, 1), (4, 0, 2, 2)),
  ((1, 0, 3, 1), (3, 1, 2, 1), (4, 1, 2, 2)),
  ((3, 2, 1, 0), (4, 0, 2, 3), (3, 0, 1, 1), (3, 1, 1, 1), (4, 1, 2, 3), (3, 2, 1, 1), (4, 2, 1, 2), (3, 0, 3, 0), (4, 0, 1, 3), (4, 1, 1, 3),
   (3, 1, 3, 0), (4, 2, 1, 3), (3, 1, 3, 1), (3, 0, 3, 1), (4, 0, 3, 2)),
  ((4, 1, 3, 2),), (), ((4, 1, 3, 3),), (), (), (), ((4, 0, 3, 3),), (), ()),
 (((0, 0, 2, 0), (1, 0, 2, 0), (3, 0, 2, 0)),
  ((3, 1, 2, 0), (0, 1, 2, 0), (1, 1, 2, 0), (2, 0, 2, 0), (4, 0, 2, 2), (2, 1, 2, 0), (4, 0, 1, 0), (0, 0, 1, 0), (4, 1, 2, 2), (4, 0, 3, 0),
   (3, 0, 3, 0), (4, 1, 1, 0), (1, 0, 3, 0), (4, 0, 2, 1), (4, 0, 0, 0), (0, 0, 0, 0), (3, 0, 0, 0), (4, 1, 3, 0), (0, 1, 0, 0), (3, 1, 0, 0),
   (4, 1, 2, 1), (4, 1, 0, 0), (3, 1, 3, 0), (4, 2, 0, 0), (0, 2, 0, 0), (1, 1, 3, 0), (3, 2, 0, 0), (0, 3, 0, 0), (4, 3, 0, 0), (3, 3, 0, 0),
   (4, 0, 3, 2), (4, 4, 0, 0), (3, 4, 0, 0), (0, 4, 0, 0), (4, 0, 0, 2), (3, 5, 0, 0), (4, 5, 0, 0), (0, 5, 0, 0), (3, 0, 3, 1), (4, 0, 3, 1),
   (4, 1, 0, 2), (0, 6, 0, 0), (4, 1, 3, 2), (4, 6, 0, 0), (1, 0, 3, 1), (4, 2, 0, 2), (0, 0, 0, 1), (4, 0, 0, 1), (3, 6, 0, 0), (4, 3, 0, 2),
   (4, 4, 0, 2), (3, 0, 0, 1), (0, 1, 0, 1), (4, 1, 0, 1), (3, 1, 0, 1), (4, 5, 0, 2), (2, 3, 0, 0), (4, 2, 0, 1), (0, 2, 0, 1), (3, 2, 0, 1),
   (2, 4, 0, 0), (0, 1, 1, 0), (4, 0, 3, 3), (2, 5, 0, 0), (4, 6, 0, 2), (2, 6, 0, 0), (3, 0, 2, 1), (4, 0, 0, 3), (4, 2, 1, 0), (4, 1, 0, 3),
   (0, 2, 1, 0), (4, 3, 0, 1), (3, 3, 0, 1), (4, 2, 0, 3), (4, 4, 0, 1), (3, 4, 0, 1), (4, 5, 0, 1), (3, 5, 0, 1), (4, 0, 1, 1), (3, 6, 0, 1),
   (4, 6, 0, 1), (3, 1, 2, 1), (0, 0, 1, 1), (4, 1, 1, 1), (4, 0, 2, 3), (4, 3, 0, 3), (3, 0, 1, 0), (4, 4, 0, 3), (0, 1, 1, 1), (4, 5, 0, 3),
   (3, 1, 1, 0), (4, 6, 0, 3), (4, 2, 1, 1), (3, 2, 1, 0), (0, 2, 1, 1), (4, 1, 2, 3)),
  ((3, 0, 1, 1),), ((4, 0, 1, 2), (4, 1, 1, 2), (3, 1, 1, 1), (4, 2, 1, 2), (3, 2, 1, 1)), (), ((4, 0, 1, 3), (2, 1, 3, 0)),
  ((4, 1, 1, 3), (4, 2, 1, 3)), ((3, 1, 3, 1), (4, 1, 3, 1)), (), (), (), ((4, 1, 3, 3),), (), (), (), (), ()),
 (((2, 0, 3, 0), (1, 0, 3, 0)),
  ((2, 1, 3, 0), (3, 0, 3, 0), (1, 1, 3, 0), (4, 0, 3, 1), (3, 1, 3, 0), (4, 0, 2, 0), (4, 1, 3, 1), (3, 0, 2, 0), (1, 0, 3, 1), (2, 0, 2, 0),
   (4, 0, 3, 2), (4, 1, 2, 0), (4, 1, 3, 2), (3, 1, 2, 0), (4, 0, 2, 2), (4, 0, 1, 0), (3, 0, 1, 0), (4, 0, 0, 0), (3, 0, 0, 0), (4, 0, 2, 1),
   (3, 0, 2, 1), (4, 1, 0, 0), (4, 1, 2, 2), (4, 2, 0, 0), (3, 1, 0, 0), (3, 2, 0, 0), (4, 0, 1, 2), (4, 3, 0, 0), (2, 3, 0, 0), (4, 0, 0, 2),
   (4, 4, 0, 0), (2, 4, 0, 0), (3, 3, 0, 0), (4, 5, 0, 0), (2, 5, 0, 0), (3, 4, 0, 0), (4, 0, 2, 3), (4, 6, 0, 0), (4, 1, 0, 2), (2, 6, 0, 0),
   (3, 5, 0, 0), (4, 2, 0, 2), (3, 6, 0, 0), (4, 0, 0, 1), (4, 3, 0, 1), (3, 0, 0, 1), (4, 4, 0, 1), (3, 3, 0, 1), (4, 1, 0, 1), (4, 3, 0, 2),
   (4, 5, 0, 1), (3, 4, 0, 1), (4, 4, 0, 2), (3, 1, 0, 1), (4, 2, 0, 1), (4, 6, 0, 1), (3, 5, 0, 1), (4, 5, 0, 2), (3, 2, 0, 1), (3, 6, 0, 1),
   (4, 6, 0, 2), (2, 1, 2, 0), (4, 0, 0, 3), (4, 1, 1, 0), (4, 3, 0, 3), (4, 4, 0, 3), (4, 1, 0, 3), (3, 1, 1, 0), (4, 5, 0, 3), (4, 2, 0, 3),
   (4, 2, 1, 0), (3, 2, 1, 0), (4, 6, 0, 3), (3, 0, 3, 1), (4, 1, 2, 1), (4, 0, 1, 1)),
  (), ((3, 0, 1, 1), (3, 1, 1, 1), (4, 1, 1, 2), (4, 2, 1, 2), (4, 1, 1, 1)), (),
  ((3, 2, 1, 1), (4, 2, 1, 1), (4, 0, 3, 3), (4, 0, 1, 3), (3, 1, 2, 1)), ((4, 1, 1, 3), (3, 1, 3, 1)), ((4, 2, 1, 3), (4, 1, 2, 3), (4, 1, 3, 3)),
  (), (), (), (), (), (), (), (), ()))
SENDS_BACK = (((), (), (), ((1, 0, 3, 2),), ((1, 0, 3, 3),), ((1, 1, 3, 2),), (), (), ((3, 0, 3, 0), (1, 1, 3, 3)), (), ((1, 0, 1, 2), (3, 0, 3, 1)),
  ((1, 0, 1, 3),), ((1, 1, 1, 2), (1, 1, 1, 3), (1, 2, 1, 2), (3, 1, 3, 0), (1, 2, 1, 3)), ((1, 0, 2, 2),), ((1, 0, 2, 3),),
  ((3, 1, 3, 1), (1, 1, 2, 2)), (), (), ((5, 0, 0, 0), (1, 1, 2, 3)),
  ((1, 2, 2, 2), (3, 0, 1, 0), (2, 0, 2, 1), (1, 2, 2, 3), (2, 1, 2, 1), (1, 0, 0, 2), (3, 0, 1, 1), (1, 0, 0, 3), (1, 1, 0, 2), (1, 1, 0, 3),
   (2, 2, 2, 1), (1, 2, 0, 2), (1, 2, 0, 3), (1, 3, 0, 2), (5, 1, 0, 0), (3, 0, 2, 0), (1, 3, 0, 3), (1, 4, 0, 2), (1, 4, 0, 3), (1, 5, 0, 2),
   (1, 5, 0, 3), (3, 1, 2, 0), (1, 6, 0, 2), (1, 6, 0, 3), (2, 1, 1, 1), (2, 3, 0, 1), (3, 2, 2, 0), (2, 2, 1, 1), (2, 4, 0, 1), (5, 2, 0, 0),
   (2, 5, 0, 1), (2, 0, 0, 1), (2, 6, 0, 1), (3, 1, 1, 0), (3, 2, 1, 0), (2, 1, 0, 1), (4, 0, 0, 0), (2, 2, 0, 1), (4, 1, 0, 0), (4, 3, 0, 0),
   (4, 4, 0, 0), (4, 2, 0, 0), (4, 5, 0, 0), (4, 6, 0, 0))),
 ((), (), (), ((1, 0, 3, 2),), ((1, 0, 3, 3),), ((1, 1, 3, 2),), (), (), ((1, 1, 3, 3),), (), ((1, 0, 2, 2), (1, 0, 2, 3)),
  ((1, 1, 2, 2), (1, 1, 2, 3)), ((3, 0, 3, 0), (2, 0, 2, 1), (1, 2, 2, 2)), (), ((3, 0, 3, 1), (2, 1, 2, 1), (1, 2, 2, 3)), (), (), ((1, 0, 1, 2),),
  ((5, 0, 0, 0),),
  ((1, 0, 0, 2), (3, 1, 3, 0), (1, 0, 0, 3), (2, 2, 2, 1), (1, 1, 0, 2), (1, 1, 0, 3), (1, 2, 0, 2), (3, 1, 3, 1), (1, 2, 0, 3), (1, 3, 0, 2),
   (1, 3, 0, 3), (1, 4, 0, 2), (1, 4, 0, 3), (1, 5, 0, 2), (1, 5, 0, 3), (5, 1, 0, 0), (1, 6, 0, 2), (1, 6, 0, 3), (1, 0, 1, 3), (2, 3, 0, 1),
   (2, 4, 0, 1), (2, 5, 0, 1), (3, 0, 0, 0), (2, 6, 0, 1), (1, 1, 1, 2), (3, 0, 0, 1), (1, 1, 1, 3), (1, 2, 1, 2), (3, 1, 0, 0), (2, 0, 1, 1),
   (3, 0, 2, 0), (5, 2, 0, 0), (3, 1, 0, 1), (3, 2, 0, 0), (1, 2, 1, 3), (3, 1, 2, 0), (3, 2, 0, 1), (2, 1, 1, 1), (3, 3, 0, 0), (3, 4, 0, 0),
   (3, 2, 2, 0), (4, 0, 1, 0), (3, 5, 0, 0), (2, 2, 1, 1), (3, 6, 0, 0), (4, 1, 1, 0), (4, 2, 1, 0))),
 ((), (), (), ((1, 0, 3, 2),), ((1, 0, 3, 3),), ((1, 1, 3, 2),), (), (), ((1, 1, 3, 3),), (), ((1, 0, 1, 2),), ((1, 0, 1, 3),),
  ((1, 1, 1, 2), (1, 1, 1, 3), (1, 2, 1, 2)), ((1, 2, 1, 3),), ((1, 0, 2, 2),), ((1, 0, 2, 3),), (), ((1, 1, 2, 2),), ((5, 0, 0, 0),),
  ((1, 0, 0, 2), (1, 0, 0, 3), (1, 1, 0, 2), (3, 0, 1, 0), (1, 1, 0, 3), (3, 0, 3, 0), (1, 2, 0, 2), (1, 2, 0, 3), (1, 3, 0, 2), (1, 3, 0, 3),
   (1, 4, 0, 2), (3, 0, 3, 1), (1, 4, 0, 3), (1, 5, 0, 2), (1, 5, 0, 3), (5, 1, 0, 0), (3, 0, 1, 1), (1, 6, 0, 2), (1, 6, 0, 3), (1, 1, 2, 3),
   (3, 1, 3, 0), (1, 2, 2, 2), (3, 0, 0, 0), (1, 2, 2, 3), (3, 0, 0, 1), (2, 0, 2, 1), (3, 1, 3, 1), (3, 1, 0, 0), (2, 1, 2, 1), (3, 1, 0, 1),
   (2, 3, 0, 1), (2, 4, 0, 1), (3, 2, 0, 0), (5, 2, 0, 0), (2, 2, 2, 1), (3, 2, 0, 1), (2, 5, 0, 1), (2, 6, 0, 1), (2, 1, 1, 1), (3, 3, 0, 0),
   (2, 2, 1, 1), (3, 4, 0, 0), (3, 5, 0, 0), (3, 6, 0, 0), (3, 1, 1, 0), (3, 2, 1, 0), (4, 0, 2, 0), (4, 1, 2, 0), (4, 2, 2, 0))),
 ((), (), (), ((1, 0, 3, 2),), ((1, 0, 3, 3),), ((1, 1, 3, 2),), (), (), ((1, 0, 2, 2), (1, 0, 2, 3)), (), ((1, 0, 1, 2),), ((1, 0, 1, 3),),
  ((3, 0, 1, 0), (1, 1, 1, 2), (1, 1, 1, 3), (1, 2, 1, 2)), ((1, 2, 1, 3), (1, 1, 2, 2)), ((1, 1, 2, 3),), ((3, 0, 1, 1), (2, 1, 1, 1)),
  ((1, 2, 2, 2),), (), ((5, 0, 0, 0),),
  ((1, 0, 0, 2), (1, 0, 0, 3), (1, 1, 0, 2), (1, 1, 0, 3), (3, 1, 1, 0), (1, 2, 0, 2), (1, 2, 0, 3), (1, 3, 0, 2), (3, 0, 0, 0), (1, 3, 0, 3),
   (3, 0, 0, 1), (1, 4, 0, 2), (1, 4, 0, 3), (3, 1, 0, 0), (5, 1, 0, 0), (1, 5, 0, 2), (1, 5, 0, 3), (1, 6, 0, 2), (3, 1, 0, 1), (1, 6, 0, 3),
   (2, 2, 1, 1), (3, 2, 0, 0), (2, 3, 0, 1), (3, 2, 0, 1), (2, 4, 0, 1), (1, 2, 2, 3), (2, 5, 0, 1), (2, 6, 0, 1), (3, 2, 1, 0), (2, 0, 2, 1),
   (5, 2, 0, 0), (3, 3, 0, 0), (2, 1, 2, 1), (3, 4, 0, 0), (2, 2, 2, 1), (3, 5, 0, 0), (3, 6, 0, 0), (1, 1, 3, 3), (3, 0, 2, 0), (2, 0, 3, 1),
   (3, 1, 2, 0), (3, 2, 2, 0), (2, 1, 3, 1), (4, 0, 3, 0), (4, 1, 3, 0))))

def unpack(flat_values):
    shapes = [(D, 3 * D), (D, D), (D, FF), (FF, D), (D, FINAL), (G * CD, V), (G * CD, FINAL)]
    pieces = []
    offset = 0
    for height, width in shapes:
        pieces.append(flat_values[offset : offset + height * width].reshape(height, width))
        offset = offset + height * width
    return pieces


def split_vectors(vector_all):
    lengths = [D, D, D, D, D, FF, D, D, D, FINAL, FINAL]
    pieces = []
    offset = 0
    for length in lengths:
        pieces.append(vector_all[offset : offset + length])
        offset = offset + length
    return pieces


def layer_norm(values, scale_gain, shift_bias):
    centered = values - jnp.mean(values, axis=-1, keepdims=True)
    variance = jnp.mean(centered * centered, axis=-1, keepdims=True)
    return centered * lax.rsqrt(variance + eps_norm) * scale_gain + shift_bias


def contrast_dense(chosen, targets, distract, weight):
    hi = dict(precision=lax.Precision.HIGHEST)
    frames = jnp.arange(MASKED, dtype=jnp.int32)
    allowed = jnp.any(distract[:, :, None] == frames, axis=1) | (frames[:, None] == frames)

    def agreement(chosen, targets):
        left = chosen * lax.rsqrt(jnp.sum(chosen * chosen, axis=-1, keepdims=True) + eps_cos)
        right = targets * lax.rsqrt(jnp.sum(targets * targets, axis=-1, keepdims=True) + eps_cos)
        return jnp.einsum("by,oy->bo", left, right, **hi) / softness_divisor

    similar, back = jax.vjp(agreement, chosen, targets)
    same = frames[:, None] == frames
    positive = jnp.sum(jnp.where(same, similar, 0.0), axis=1)
    top = jnp.max(jnp.where(allowed, similar, -jnp.inf), axis=1)
    parts = jnp.where(allowed, jnp.exp(similar - top[:, None]), 0.0)
    total = jnp.sum(parts, axis=1)
    loss = jnp.sum(top + jnp.log(total) - positive)
    d_similar = weight * (parts / total[:, None] - same.astype(jnp.float32))
    return (loss,) + back(d_similar)


def adamw_update(master, first_moment, second, gradient, step_rate):
    first_new = beta_one * first_moment + (1.0 - beta_one) * gradient
    second_new = beta_two * second + (1.0 - beta_two) * gradient * gradient
    first_hat = first_new / (1.0 - beta_one**STEP)
    second_hat = second_new / (1.0 - beta_two**STEP)
    master_new = master * (1.0 - step_rate * decay_rate) - step_rate * first_hat / (
        jnp.sqrt(second_hat) + adam_eps
    )
    return (master_new, first_new, second_new)


def column_sum(values):
    return jnp.sum(values.astype(jnp.float32), axis=tuple(range(values.ndim - 1)))


def finish(total_masked, square_sum, vector_sum, loss_sum, grad_shard, output, input_grad, params, moment_one, moment_two, vectors, vector_one, vector_two):
    grad_norm = jnp.sqrt(square_sum + jnp.sum(vector_sum * vector_sum))
    factor = jnp.minimum(1.0, clip_level / (grad_norm + 1e-06))
    refreshed_weights, new_one, new_two = adamw_update(params, moment_one, moment_two, grad_shard * factor, rate_matrix)
    new_vectors, new_vector_first, new_vector_second = adamw_update(vectors, vector_one, vector_two, vector_sum * factor, rate_vector)
    return (
        loss_sum / total_masked,
        grad_norm,
        output,
        input_grad,
        refreshed_weights,
        refreshed_weights.astype(bf16),
        new_one,
        new_two,
        new_vectors,
        new_vector_first,
        new_vector_second,
    )


def by_collectives(
    layer_input,
    mask_index,
    distract,
    code_choice,
    params,
    moment_one,
    moment_two,
    vectors,
    vector_one,
    vector_two,
):
    bf16 = jnp.bfloat16
    f32 = jnp.float32
    count_utts = layer_input.shape[0]
    total_masked = count_utts * lax.axis_size(("dp", "fsdp")) * MASKED
    token_rows = count_utts * LEN
    gathered = lax.all_gather(params.astype(bf16), ("dp", "fsdp"), axis=0, tiled=True)
    qkv_weight, out_weight, up_weight, down_weight, proj_weight, codebook, code_weight = unpack(
        gathered
    )
    (
        bias_query,
        bias_value,
        bias_out,
        gain_one,
        shift_one,
        bias_up,
        bias_down,
        gain_two,
        shift_two,
        bias_proj,
        bias_code,
    ) = split_vectors(vectors)
    inputs = layer_input.reshape(token_rows, D)
    projected = jnp.dot(inputs, qkv_weight, preferred_element_type=f32)
    query_heads = (projected[:, :D] + bias_query).astype(bf16).reshape(count_utts, LEN, H, HD)
    key_heads = projected[:, D : 2 * D].astype(bf16).reshape(count_utts, LEN, H, HD)
    value_heads = (projected[:, 2 * D :] + bias_value).astype(bf16).reshape(count_utts, LEN, H, HD)
    scores = (
        jnp.einsum("blhe,bmhe->bhlm", query_heads, key_heads, preferred_element_type=f32) * 0.125
    )
    attn_probs = jax.nn.softmax(scores, axis=-1)
    probs_low = attn_probs.astype(bf16)
    attended = jnp.einsum("bhlm,bmhe->blhe", probs_low, value_heads, preferred_element_type=f32)
    attended = attended.astype(bf16).reshape(token_rows, D)
    residual_one = (
        inputs.astype(f32) + jnp.dot(attended, out_weight, preferred_element_type=f32) + bias_out
    )
    normed, back_one = jax.vjp(layer_norm, residual_one, gain_one, shift_one)
    normed_low = normed.astype(bf16)
    hidden = jnp.dot(normed_low, up_weight, preferred_element_type=f32) + bias_up
    active, gelu_back = jax.vjp(functools.partial(jax.nn.gelu, approximate=False), hidden)
    active_low = active.astype(bf16)
    residual_two = normed + jnp.dot(active_low, down_weight, preferred_element_type=f32) + bias_down
    output, back_two = jax.vjp(layer_norm, residual_two, gain_two, shift_two)
    output_low = output.astype(bf16)
    place = (mask_index[0][:, None] == jnp.arange(LEN, dtype=jnp.int32)).astype(bf16)
    picked = jnp.dot(place, output_low, preferred_element_type=f32).astype(bf16)
    chosen = jnp.dot(picked, proj_weight, preferred_element_type=f32) + bias_proj
    choose = (code_choice[..., None] == jnp.arange(V, dtype=jnp.int32)).astype(bf16)
    code_vectors = jnp.einsum(
        "bmgv,gcv->bmgc", choose, codebook.reshape(G, CD, V), preferred_element_type=f32
    )
    code_vectors = code_vectors.astype(bf16).reshape(count_utts, MASKED, G * CD)
    targets = (
        jnp.einsum("bmc,cf->bmf", code_vectors, code_weight, preferred_element_type=f32) + bias_code
    )
    loss_local, d_chosen, d_targets = contrast_dense(chosen, targets[0], distract[0], 1.0 / total_masked)
    d_targets = d_targets[None]
    d_targets_low = d_targets.astype(bf16)
    quantized_offset_slope = column_sum(d_targets_low)
    d_code_weight = jnp.einsum(
        "bmc,bmf->cf", code_vectors, d_targets_low, preferred_element_type=f32
    )
    d_code_vectors = jnp.einsum(
        "bmf,cf->bmc", d_targets_low, code_weight, preferred_element_type=f32
    )
    d_codebook = jnp.einsum(
        "bmgc,bmgv->gcv",
        d_code_vectors.reshape(count_utts, MASKED, G, CD),
        choose.astype(f32),
        precision=lax.Precision.HIGHEST,
    ).reshape(G * CD, V)
    d_chosen_low = d_chosen.astype(bf16)
    d_bias_proj = column_sum(d_chosen_low)
    d_proj_weight = jnp.einsum("td,tf->df", picked, d_chosen_low, preferred_element_type=f32)
    d_context_low = jnp.einsum("mt,mf->tf", place, d_chosen_low, preferred_element_type=f32).astype(bf16)
    result_sensitivity = jnp.einsum(
        "tf,df->td", d_context_low, proj_weight, preferred_element_type=f32
    )
    d_residual_two, d_gain_two, d_shift_two = back_two(result_sensitivity)
    d_second_low = d_residual_two.astype(bf16)
    d_bias_down = column_sum(d_second_low)
    d_down_weight = jnp.einsum("th,td->hd", active_low, d_second_low, preferred_element_type=f32)
    d_active = jnp.einsum("td,hd->th", d_second_low, down_weight, preferred_element_type=f32)
    (d_hidden,) = gelu_back(d_active)
    d_hidden_low = d_hidden.astype(bf16)
    d_bias_up = column_sum(d_hidden_low)
    d_up_weight = jnp.einsum("td,th->dh", normed_low, d_hidden_low, preferred_element_type=f32)
    d_normed = d_residual_two + jnp.einsum(
        "th,dh->td", d_hidden_low, up_weight, preferred_element_type=f32
    )
    d_residual_one, d_gain_one, d_shift_one = back_one(d_normed)
    d_branch_low = d_residual_one.astype(bf16)
    d_bias_out = column_sum(d_branch_low)
    d_out_weight = jnp.einsum("td,te->de", attended, d_branch_low, preferred_element_type=f32)
    d_attended = jnp.einsum("te,de->td", d_branch_low, out_weight, preferred_element_type=f32)
    d_attended = d_attended.astype(bf16).reshape(count_utts, LEN, H, HD)
    d_value = jnp.einsum("bhlm,blhe->bmhe", probs_low, d_attended, preferred_element_type=f32)
    d_probs = jnp.einsum("blhe,bmhe->bhlm", d_attended, value_heads, preferred_element_type=f32)
    d_scores = (
        attn_probs * (d_probs - jnp.sum(attn_probs * d_probs, axis=-1, keepdims=True))
    ).astype(bf16)
    d_query = jnp.einsum("bhlm,bmhe->blhe", d_scores, key_heads, preferred_element_type=f32) * 0.125
    d_key = jnp.einsum("bhlm,blhe->bmhe", d_scores, query_heads, preferred_element_type=f32) * 0.125
    d_projected = jnp.concatenate(
        [
            d_query.reshape(token_rows, D),
            d_key.reshape(token_rows, D),
            d_value.reshape(token_rows, D),
        ],
        axis=1,
    ).astype(bf16)
    d_sums = column_sum(d_projected)
    d_qkv_weight = jnp.einsum("td,te->de", inputs, d_projected, preferred_element_type=f32)
    input_grad = d_residual_one + jnp.einsum(
        "te,de->td", d_projected, qkv_weight, preferred_element_type=f32
    )
    flat_grad = jnp.concatenate(
        [
            matrix_grad.reshape(-1)
            for matrix_grad in (
                d_qkv_weight,
                d_out_weight,
                d_up_weight,
                d_down_weight,
                d_proj_weight,
                d_codebook,
                d_code_weight,
            )
        ]
    )
    vector_gradient = jnp.concatenate(
        [
            d_sums[:D],
            d_sums[2 * D :],
            d_bias_out,
            d_gain_one,
            d_shift_one,
            d_bias_up,
            d_bias_down,
            d_gain_two,
            d_shift_two,
            d_bias_proj,
            quantized_offset_slope,
        ]
    )
    vector_sum, loss_sum = lax.psum((vector_gradient, loss_local), ("dp", "fsdp"))
    grad_shard = lax.psum_scatter(flat_grad, ("dp", "fsdp"), scatter_dimension=0, tiled=True)
    square_sum = lax.psum(jnp.sum(grad_shard * grad_shard), ("dp", "fsdp"))
    return finish(
        total_masked, square_sum, vector_sum, loss_sum, grad_shard, output_low.reshape(count_utts, LEN, D),
        input_grad.reshape(count_utts, LEN, D), params, moment_one, moment_two, vectors, vector_one, vector_two,
    )


def by_kernels(layer_input, mask_index, distract, code_choice, params, moment_one, moment_two, vectors, vector_one, vector_two):
    total_masked = layer_input.shape[0] * lax.axis_size(("dp", "fsdp")) * MASKED
    kept, output = forward(PIECES_OUT, SENDS_OUT, 1.0 / total_masked, params, layer_input, mask_index, distract, code_choice, vectors)
    grads, sums, squares, input_grad = backward(PIECES_BACK, SENDS_BACK, vectors, kept, lax.axis_size("fsdp"), params.shape[0] // 128)
    new, low, first, second, new_v, first_v, second_v, loss, norm = update(
        total_masked, grads, params, moment_one, moment_two, sums, vectors, vector_one, vector_two, squares
    )
    return loss, norm, output, input_grad, new, low, first, second, new_v, first_v, second_v


def solution(mesh):
    in_specs = (
        P(("dp", "fsdp"), None, None),
        P(("dp", "fsdp"), None),
        P(("dp", "fsdp"), None, None),
        P(("dp", "fsdp"), None, None),
        P(("dp", "fsdp")),
        P(("dp", "fsdp")),
        P(("dp", "fsdp")),
        P(),
        P(),
        P(),
    )
    out_specs = (
        P(),
        P(),
        P(("dp", "fsdp"), None, None),
        P(("dp", "fsdp"), None, None),
        P(("dp", "fsdp")),
        P(("dp", "fsdp")),
        P(("dp", "fsdp")),
        P(("dp", "fsdp")),
        P(),
        P(),
        P(),
    )
    fits = mesh.shape["dp"] == PLANES and mesh.shape["fsdp"] == 8
    return jax.shard_map(
        by_kernels if fits else by_collectives, mesh=mesh, in_specs=in_specs, out_specs=out_specs, check_vma=False
    )
```

```python
import functools

import jax
import jax.numpy as jnp
from jax import lax
from jax.experimental import pallas as pl
from jax.experimental.pallas import tpu as pltpu
from jax.sharding import PartitionSpec as P
D = 768; H = 12; HD = 64; FF = 3072; FINAL = 256; G = 2; V = 320; CD = 128; LEN = 472; MASKED = 232
NROW = 9664; GROW = NROW + 256
T = 512
LT = 480
NB = 240
TILE = 768
STEP_T = 512
bf16 = jnp.bfloat16
f32 = jnp.float32
NT = (((1,), (1,)), ((), ()))
BQ, BV, BO, G1, S1, BUP, BDOWN, G2, S2, BPROJ, BCODE = [768 * i for i in range(6)] + [3840 + 3072 + 768 * i for i in range(3)] + [9216, 9472]

def mm(a, b):
    return jnp.dot(a, b, preferred_element_type=f32)

def mm_nt(a, b, precision=None):
    return lax.dot_general(a, b, NT, preferred_element_type=f32, precision=precision)

def hi(a, b):
    return jnp.dot(a, b, preferred_element_type=f32, precision=lax.Precision.HIGHEST)

def split_rows(g, base, parts, nice, first, tmp):
    def body(b, _):
        src = pl.multiple_of(base + b * 64 * parts, 64)
        for j in range(6):
            tmp[j, 0:64 * parts, :] = g[pl.ds(src, 64 * parts), 128 * j:128 * j + 128].astype(f32)
        for t in range(parts):
            at = pl.multiple_of((first + t) * D + b * 64, 64)
            for j in range(6):
                nice[pl.ds(at, 64), 128 * j:128 * j + 128] = tmp[j, pl.ds(t, 64, stride=parts), :].astype(bf16)
        return 0
    lax.fori_loop(0, D // 64, body, 0)

def norm_rows(r, gain, shift, low, wide, hat, rstd):
    def body(b, _):
        at = pl.multiple_of(b * NB, 16)
        v = r[pl.ds(at, NB), :]
        m = jnp.mean(v, axis=-1, keepdims=True)
        c = v - m
        var = jnp.mean(c * c, axis=-1, keepdims=True)
        inv = lax.rsqrt(var + eps_norm)
        xh = c * inv
        o = xh * gain + shift
        hat[pl.ds(at, NB), :] = xh
        rstd[pl.ds(at, NB), :] = jnp.broadcast_to(inv, (NB, 128))
        if wide is not None:
            wide[pl.ds(at, NB), :] = o
        low[pl.ds(at, NB), :] = o.astype(bf16)
        return 0
    lax.fori_loop(0, LT // NB, body, 0)

def transpose_to(src, dst, rows, cols):
    step = min(STEP_T, cols // 3)
    def body(n, _):
        at = pl.multiple_of(n * step, step)
        dst[pl.ds(at, step), :] = src[:, pl.ds(at, step)].T
        return 0
    lax.fori_loop(0, cols // step, body, 0)

def prepare(x_ref, xp, xT, mask_ref, distract_ref, choice_ref, vec_ref, vec, place, placeT, allowed, choose):
    for i in range(vec_ref.shape[0]):
        vec[0:1, 128 * i:128 * i + 128] = vec_ref[i:i + 1, :]
    xp[...] = jnp.zeros((T, D), bf16)
    xp[0:LEN, :] = x_ref[0]
    transpose_to(xp, xT, T, D)
    zero = jnp.zeros((1, 256 - MASKED), jnp.int32) - 1
    def wide(row):
        return jnp.concatenate([row, zero], axis=1)
    hot = jnp.where(lax.broadcasted_iota(jnp.int32, (T, 256), 0) == wide(mask_ref[...]), 1.0, 0.0)
    placeT[...] = hot.astype(bf16)
    place[...] = hot.T.astype(bf16)
    row = lax.broadcasted_iota(jnp.int32, (256, 256), 0)
    col = lax.broadcasted_iota(jnp.int32, (256, 256), 1)
    allowed[...] = jnp.where((row == col) & (col < MASKED), 1.0, 0.0)
    rows = [wide(distract_ref[i]) for i in range(distract_ref.shape[0])]
    def body(b, _):
        at = pl.multiple_of(8 * b, 8)
        acc = allowed[pl.ds(at, 8), :]
        n = lax.broadcasted_iota(jnp.int32, (8, 256), 0) + at
        for r in rows:
            acc = jnp.where(n == r, 1.0, acc)
        allowed[pl.ds(at, 8), :] = acc
        return 0
    lax.fori_loop(0, MASKED // 8, body, 0)
    allowed[...] = allowed[...].T
    for g in range(2):
        v = jnp.where(lax.broadcasted_iota(jnp.int32, (384, 256), 0) == wide(choice_ref[0, g:g + 1, :]), 1.0, 0.0)
        choose[g] = v.T

def project(xp, nice, vec, q, kk, kT, vv, vT):
    for t, (dst, bias) in enumerate(((q, BQ), (kk, None), (vv, BV))):
        for n in range(3):
            acc = mm(xp[...], nice[t * D:(t + 1) * D, 256 * n:256 * n + 256])
            if bias is not None:
                acc = acc + vec[0:1, bias + 256 * n:bias + 256 * n + 256]
            dst[:, 256 * n:256 * n + 256] = acc.astype(bf16)
    transpose_to(kk, kT, T, D)
    transpose_to(vv, vT, T, D)

def attend(p, q, kk, vT, pT, attT):
    at = pl.multiple_of(128 * p, 128)
    qp = q[:, pl.ds(at, 128)]
    kp = kk[0:LT, pl.ds(at, 128)]
    lane = lax.broadcasted_iota(jnp.int32, (LT, 128), 1)
    for h in range(2):
        kh = jnp.where((lane < 64) == (h == 0), kp, jnp.zeros_like(kp))
        s = mm_nt(kh, qp)[0:LEN] * 0.125
        e = jnp.exp(s - jnp.max(s, axis=0, keepdims=True))
        pr = e * (1.0 / jnp.sum(e, axis=0, keepdims=True))
        pr = jnp.concatenate([pr, jnp.zeros((T - LEN, T), f32)], axis=0).astype(bf16)
        pT[pl.ds(pl.multiple_of((2 * (p % 2) + h) * T, T), T), :] = pr
        rows = pl.ds(pl.multiple_of(128 * p + 64 * h, 64), 64)
        attT[rows, :] = mm(vT[rows, :], pr).astype(bf16)

def out_project(attT, att, xp, wo, vec, res):
    for n in range(6):
        att[:, 128 * n:128 * n + 128] = attT[128 * n:128 * n + 128, :].T
    for n in range(3):
        cols = slice(256 * n, 256 * n + 256)
        acc = mm(att[0:LT, :], wo[:, cols])
        res[:, cols] = xp[0:LT, cols].astype(f32) + acc + vec[0:1, BO + 256 * n:BO + 256 * n + 256]

def up(n, norm_low, nice, vec, act, gp):
    root = 0.7071067811865476
    scale = 0.3989422804014327
    c = n * TILE // D
    at = pl.multiple_of(n * TILE, TILE)
    w = nice[pl.ds(pl.multiple_of(c * D, D), D), pl.ds(pl.multiple_of(at - c * D, TILE), TILE)]
    h = mm(norm_low[0:LT, :], w) + vec[0:1, pl.ds(pl.multiple_of(BUP + at, 256), TILE)]
    cdf = 0.5 * (1.0 + lax.erf(h * root))
    act[0:LT, pl.ds(at, TILE)] = (h * cdf).astype(bf16)
    gp[0:LT, pl.ds(at, TILE)] = (cdf + h * (scale * jnp.exp(-0.5 * h * h))).astype(bf16)

def down(act, g, vec, res, wide):
    for n in range(3):
        cols = slice(256 * n, 256 * n + 256)
        acc = mm(act[0:LT, :], g[6144:9216, cols])
        res[:, cols] = wide[:, cols] + acc + vec[0:1, BDOWN + 256 * n:BDOWN + 256 * n + 256]

def small_weights(g, fb, p32, c32, wproj, code, wcode):
    for t in range(3):
        for j in range(2):
            p32[j, pl.ds(t, 256, stride=3), :] = g[9216:9472, 256 * t + 128 * j:256 * t + 128 * j + 128].astype(f32)
    for j in range(2):
        wproj[:, 128 * j:128 * j + 128] = p32[j].astype(bf16)
    for j in range(6):
        fb[pl.ds(j, 192, stride=6), :] = g[9472:9664, 128 * j:128 * j + 128].astype(f32)
    a = [fb[pl.ds(j, 128, stride=5), :] for j in range(5)]
    lo = lax.broadcasted_iota(jnp.int32, (128, 128), 1) < 64
    r2, r3, r4 = [pltpu.roll(v, 64, 1) for v in a[2:]]
    zero = jnp.zeros((128, 128), f32)
    even = [a[0], a[1], jnp.where(lo, a[2], zero)]
    odd = [jnp.where(lo, r2, r3), jnp.where(lo, r3, r4), jnp.where(lo, r4, zero)]
    for j in range(3):
        c32[j, pl.ds(0, 128, stride=2), :] = even[j]
        c32[j, pl.ds(1, 128, stride=2), :] = odd[j]
        code[:, 128 * j:128 * j + 128] = c32[j].astype(bf16)
    for j in range(2):
        wcode[:, 128 * j:128 * j + 128] = fb[pl.ds(640 + j, 256, stride=2), :].astype(bf16)

def contrast(weight, out_low, vec, place, placeT, allowed, choose, wproj, code, wcode, fb, p32, c32, tail, dctx, small):
    picked = mm(place[...], out_low[...]).astype(bf16)
    chosen = mm(picked, wproj[...]) + vec[0:1, BPROJ:BPROJ + 256]
    cv = jnp.concatenate([mm_nt(choose[g].astype(bf16), code[128 * g:128 * g + 128, :]) for g in range(2)], axis=1).astype(bf16)
    targets = mm(cv, wcode[...]) + vec[0:1, BCODE:BCODE + 256]
    n_l = lax.rsqrt(jnp.sum(chosen * chosen, axis=1, keepdims=True) + eps_cos)
    n_r = lax.rsqrt(jnp.sum(targets * targets, axis=1, keepdims=True) + eps_cos)
    left = chosen * n_l
    right = targets * n_r
    sim = mm_nt(left, right, lax.Precision.HIGHEST) / 0.1
    ok = allowed[...] > 0.5
    row = lax.broadcasted_iota(jnp.int32, (256, 256), 0)
    col = lax.broadcasted_iota(jnp.int32, (256, 256), 1)
    eye = jnp.where((row == col) & (row < MASKED), 1.0, 0.0)
    pos = jnp.sum(eye * sim, axis=1, keepdims=True)
    top = jnp.max(jnp.where(ok, sim, -1e30), axis=1, keepdims=True)
    parts = jnp.where(ok, jnp.exp(jnp.minimum(sim - top, 0.0)), 0.0)
    real = lax.broadcasted_iota(jnp.int32, (256, 1), 0) < MASKED
    total = jnp.where(real, jnp.sum(parts, axis=1, keepdims=True), 1.0)
    loss = jnp.sum(jnp.where(real, top + jnp.log(total) - pos, 0.0))
    dsim = (weight / 0.1) * (parts / total - eye)
    dl = hi(dsim, right)
    dr = hi(dsim.T, left)
    d_chosen = (n_l * dl - chosen * (n_l * n_l * n_l) * jnp.sum(chosen * dl, axis=1, keepdims=True)).astype(bf16)
    d_target = (n_r * dr - targets * (n_r * n_r * n_r) * jnp.sum(targets * dr, axis=1, keepdims=True)).astype(bf16)
    small[0:1, :] = jnp.sum(d_chosen.astype(f32), axis=0, keepdims=True)
    small[1:2, :] = jnp.sum(d_target.astype(f32), axis=0, keepdims=True)
    small[2:3, :] = jnp.broadcast_to(loss, (1, 256))
    dctx[...] = mm(placeT[...], d_chosen).astype(bf16)
    dproj = mm(picked.T, d_chosen)
    for j in range(2):
        p32[j] = dproj[:, 128 * j:128 * j + 128]
    for t in range(3):
        for j in range(2):
            tail[0:256, 256 * t + 128 * j:256 * t + 128 * j + 128] = p32[j, pl.ds(t, 256, stride=3), :].astype(bf16)
    dwcode = mm(cv.T, d_target)
    dcv = mm_nt(d_target, wcode[...])
    for g in range(2):
        dc = hi(dcv[:, 128 * g:128 * g + 128].T, choose[g])
        for j in range(3):
            c32[j, 128 * g:128 * g + 128, :] = dc[:, 128 * j:128 * j + 128]
    e = [c32[j, pl.ds(0, 128, stride=2), :] for j in range(3)]
    o = [pltpu.roll(c32[j, pl.ds(1, 128, stride=2), :], 64, 1) for j in range(3)]
    lo = lax.broadcasted_iota(jnp.int32, (128, 128), 1) < 64
    for j, v in enumerate((e[0], e[1], jnp.where(lo, e[2], o[0]), jnp.where(lo, o[0], o[1]), jnp.where(lo, o[1], o[2]))):
        fb[pl.ds(j, 128, stride=5), :] = v
    for j in range(2):
        fb[pl.ds(640 + j, 256, stride=2), :] = dwcode[:, 128 * j:128 * j + 128]
    for j in range(6):
        tail[256:448, 128 * j:128 * j + 128] = fb[pl.ds(j, 192, stride=6), :].astype(bf16)
STEP = 10


eps_norm = 1e-05
eps_cos = 1e-06
softness_divisor = 0.1
beta_one = 0.9
beta_two = 0.98
adam_eps = 1e-08
decay_rate = 0.01
rate_matrix = 0.03
rate_vector = 0.2
clip_level = 0.001


def sum8(v):
    r, n = v.shape
    return jnp.sum(v.reshape(r // 8, 8, n), axis=0)

def norm_back_first(dctx, wproj, gain, hat, rstd, low, acc):
    acc[...] = jnp.zeros((24, D), f32)
    def body(b, _):
        at = pl.multiple_of(b * 48, 16)
        dy = mm_nt(dctx[pl.ds(at, 48), :], wproj[...])
        norm_back_rows(dy, at, gain, hat, hat, rstd, low, acc)
        return 0
    lax.fori_loop(0, LT // 48, body, 0)

def norm_back_rows(dy, at, gain, hat, dst, rstd, low, acc):
    xh = hat[pl.ds(at, NB), :]
    inv = rstd[pl.ds(at, NB), 0:1]
    a = dy * gain
    m1 = jnp.mean(a, axis=-1, keepdims=True)
    m2 = jnp.mean(a * xh, axis=-1, keepdims=True)
    dr = inv * (a - m1 - xh * m2)
    lo = dr.astype(bf16)
    dst[pl.ds(at, NB), :] = dr
    low[pl.ds(at, NB), :] = lo
    acc[0:8, :] += sum8(dy * xh)
    acc[8:16, :] += sum8(dy)
    acc[16:24, :] += sum8(lo.astype(f32))

def norm_back(dy, gain, hat, rstd, low, acc):
    acc[...] = jnp.zeros((24, D), f32)
    def body(b, _):
        at = pl.multiple_of(b * NB, 16)
        norm_back_rows(dy[pl.ds(at, NB), :], at, gain, hat, hat, rstd, low, acc)
        return 0
    lax.fori_loop(0, LT // NB, body, 0)

def put_vec(vg, acc, offsets):
    for i, o in enumerate(offsets):
        vg[0:1, o:o + D] = jnp.sum(acc[8 * i:8 * i + 8, :], axis=0, keepdims=True)

def down_back(n, low2, gg, actT, gp, vg):
    at = pl.multiple_of(n * TILE, TILE)
    rows = pl.ds(pl.multiple_of(6144 + n * TILE, 256), TILE)
    d = mm_nt(low2[0:LT, :], gg[rows, :]) * gp[0:LT, pl.ds(at, TILE)].astype(f32)
    d = d.astype(bf16)
    gp[0:LT, pl.ds(at, TILE)] = d
    vg[0:1, pl.ds(pl.multiple_of(BUP + at, 128), TILE)] = jnp.sum(d.astype(f32), axis=0, keepdims=True)
    gg[rows, :] = mm(actT[pl.ds(at, TILE), :], low2[...]).astype(bf16)

def up_back_x(n, dh, gg, dr):
    cols = pl.ds(pl.multiple_of(n * 256, 256), 256)
    v = dr[:, cols]
    for c in range(4):
        w = gg[pl.ds(pl.multiple_of(3072 + c * D + n * 256, 256), 256), :]
        v = v + mm_nt(dh[0:LT, c * D:(c + 1) * D], w)
    dr[:, cols] = v

def weave(lhsT, rhs, parts, n, base, gg, tmp, stacked):
    def body(m, _):
        cols = pl.ds(pl.multiple_of(m * 256, 256), 256)
        for t in range(parts):
            r = rhs[t, :, cols] if stacked else rhs[:, pl.ds(pl.multiple_of(t * D + m * 256, 256), 256)]
            acc = mm(lhsT[pl.ds(pl.multiple_of(n * 256, 256), 256), :], r)
            for j in range(2):
                tmp[j, pl.ds(t, 256, stride=parts), :] = acc[:, 128 * j:128 * j + 128]
        for j in range(2):
            gg[pl.ds(pl.multiple_of(base + n * 256 * parts, 256), 256 * parts), pl.ds(pl.multiple_of(m * 256 + 128 * j, 128), 128)] = tmp[j, 0:256 * parts, :].astype(bf16)
        return 0
    lax.fori_loop(0, 3, body, 0)

def out_back(low1, gg, attT, da):
    for n in range(3):
        cols = slice(256 * n, 256 * n + 256)
        da[0:LT, cols] = mm_nt(low1[0:LT, :], gg[2304 + 256 * n:2304 + 256 * n + 256, :]).astype(bf16)
    for n in range(3):
        gg[2304 + 256 * n:2304 + 256 * n + 256, :] = mm(attT[256 * n:256 * n + 256, :], low1[...]).astype(bf16)

def attend_back(p, da, q, kT, vv, ring, dp, dqT):
    at = pl.multiple_of(128 * p, 128)
    lane = lax.broadcasted_iota(jnp.int32, (T, 128), 1)
    dap = da[:, pl.ds(at, 128)]
    qp = q[:, pl.ds(at, 128)]
    vp = vv[0:LT, pl.ds(at, 128)]
    dk = dv = None
    for h in range(2):
        half = (lane < 64) == (h == 0)
        dah = jnp.where(half, dap, jnp.zeros_like(dap))
        qh = jnp.where(half, qp, jnp.zeros_like(qp))
        pr = ring[pl.ds(pl.multiple_of(((2 * p + h) % 6) * T, T), LT), :]
        dpT = mm_nt(vp, dah)
        prf = pr.astype(f32)
        w = prf * dpT
        ds = (w - prf * jnp.sum(w, axis=0, keepdims=True)).astype(bf16)
        a = mm(pr, dah)
        b = mm(ds, qh)
        dv = a if dv is None else dv + a
        dk = b if dk is None else dk + b
        rows = pl.ds(pl.multiple_of(128 * p + 64 * h, 64), 64)
        dqT[rows, :] = (mm(kT[rows, 0:LT], ds) * 0.125).astype(bf16)
    dp[1, 0:LT, pl.ds(at, 128)] = (dk * 0.125).astype(bf16)
    dp[2, 0:LT, pl.ds(at, 128)] = dv.astype(bf16)
    dp[0, :, pl.ds(at, 128)] = dqT[pl.ds(at, 128), :].T

def input_back(n, dp, wq, dr, out):
    cols = slice(256 * n, 256 * n + 256)
    v = dr[:, cols]
    for t in range(3):
        v = v + mm_nt(dp[t, 0:LT, :], wq[t * D + 256 * n:t * D + 256 * n + 256, :])
    out[0, :, cols] = v[0:LEN]
MESH = pl.DeviceIdType.MESH
UP, DOWN, U, V_AXIS, CORE, HERE = range(6)
PLANES = 4
MAIN = 288
EXTRA = 16
HALF = MAIN + EXTRA
RAW = 96
PLANE = 2416
UNIT = 608

class Place:
    def __init__(self):
        self.z = lax.axis_index("dp")
        self.f = f = lax.axis_index("fsdp")
        self.c = c = f % 2
        self.k = k = f // 2
        x = k % 2
        y = k // 2
        self.fc = f + 1 - 2 * c
        self.fx = f + 2 - 4 * x
        self.fy = f + 4 - 8 * y
        self.uf = self.fx * (1 - c) + self.fy * c
        self.vf = self.fy * (1 - c) + self.fx * c
        self.roles = (k, self.uf // 2, self.vf // 2, 3 - k)

    def greet(self):
        z = self.z
        bar = pltpu.get_barrier_semaphore()
        for t in (self.fc, self.fx, self.fy):
            pl.semaphore_signal(bar, inc=1, device_id=(z, t), device_id_type=MESH)
        @pl.when(z > 0)
        def _(): pl.semaphore_signal(bar, inc=1, device_id=(z - 1, self.f), device_id_type=MESH)
        @pl.when(z < PLANES - 1)
        def _(): pl.semaphore_signal(bar, inc=1, device_id=(z + 1, self.f), device_id_type=MESH)
        pl.semaphore_wait(bar, 3 + (z + PLANES - 1) // PLANES + (2 * PLANES - 2 - z) // PLANES)

    def greet_all(self, count):
        bar = pltpu.get_barrier_semaphore()
        for j in range(1, count):
            pl.semaphore_signal(bar, inc=1, device_id=(self.z, lax.rem(self.f + j, count)), device_id_type=MESH)
        for j in range(1, PLANES):
            pl.semaphore_signal(bar, inc=1, device_id=(lax.rem(self.z + j, PLANES), self.f), device_id_type=MESH)
        pl.semaphore_wait(bar, count + PLANES - 2)

    def span_of(self, p, kk, c, first):
        m = PLANE * p + UNIT * kk
        return (pl.multiple_of(m + HALF * c + first, 16),
                pl.multiple_of((m + MAIN) * (1 - c) + (NROW + EXTRA * (4 * p + kk)) * c, 16))

    def span(self, p, r, c, first):
        return self.span_of(p, self.roles[r], c, first)

def remote(src, dst, ssem, rsem, dev):
    return pltpu.make_async_remote_copy(src_ref=src, dst_ref=dst, send_sem=ssem, recv_sem=rsem, device_id=dev, device_id_type=MESH)

def shared_blocks(g, p):
    row = lax.broadcasted_iota(jnp.int32, (16, D), 0)
    e = [g[NROW + 16 * (4 * p + q):NROW + 16 * (4 * p + q) + 16, :].astype(f32) for q in range(4)]
    for q, bound in enumerate((12, 8, 4)):
        at = PLANE * p + UNIT * q + 592
        g[at:at + 16, :] = jnp.where(row < bound, e[q], e[q + 1]).astype(bf16)

def extra_rows(g, p, q):
    row = lax.broadcasted_iota(jnp.int32, (16, D), 0)
    b = [g[PLANE * p + UNIT * i + 592:PLANE * p + UNIT * i + 608, :].astype(f32) for i in range(max(q - 1, 0), min(q, 2) + 1)]
    v = b[0] if len(b) == 1 else jnp.where(row < 12 - 4 * q, b[1], b[0])
    g[NROW + 16 * (4 * p + q):NROW + 16 * (4 * p + q) + 16, :] = v.astype(bf16)

def wait_sent(g, rows, ssem, rsem, dev):
    if rows:
        ref = g.at[pl.ds(0, rows)]
        remote(ref, ref, ssem, rsem, dev).wait_send()

class Gather:
    def __init__(self, at, g, pieces, R, O, S):
        self.at, self.g, self.pieces, self.R, self.O, self.S = at, g, pieces, R, O, S
        self.sent = {z: [0, 0] for z in range(PLANES)}
        self.seen = set()

    def copies(self, i, p, r, dev, kind):
        _, first, rows, extra = self.pieces[p][i]
        a, e = self.at.span(p, r, self.at.c, first)
        unit = 4 * p + self.at.roles[r]
        out = []
        for j, (s, n) in enumerate([(a, rows)] + [(e, EXTRA)] * extra):
            ref = self.g.at[pl.ds(s, n)]
            out.append(remote(ref, ref, self.S.at[int(kind == CORE)], self.O.at[p] if kind == CORE else self.R.at[unit, i + j], dev))
        return out

    def op(self, zs, kind, i, p, r):
        at = self.at
        if not (p == zs and r == 0) and (zs, i, p, r) not in self.seen:
            self.seen.add((zs, i, p, r))
            for q in self.copies(i, p, r, (zs, at.fc), HERE): q.wait_recv()
        dev = ((zs + 1, at.f), (zs - 1, at.f), (zs, at.uf), (zs, at.vf), (zs, at.fc))[kind]
        for q in self.copies(i, p, r, dev, kind): q.start()
        _, _, rows, extra = self.pieces[p][i]
        self.sent[zs][int(kind == CORE)] += rows + EXTRA * extra

    def other_core(self, zs, p):
        ref = self.g.at[pl.ds(0, HALF * (3 if p == zs else 4))]
        remote(ref, ref, self.S.at[1], self.O.at[p], (zs, self.at.fc)).wait_recv()

    def drain(self):
        for zs in range(PLANES):
            @pl.when(self.at.z == zs)
            def _():
                for i in range(2): wait_sent(self.g, self.sent[zs][i], self.S.at[i], self.O.at[0], (zs, self.at.fc))

def own_rows(at, g, p_ref, raw, sem):
    n = p_ref.shape[0]
    gap = -n % 8
    base = pl.multiple_of(RAW + (n + gap) * at.c, 8)
    mine = pltpu.make_async_copy(p_ref.at[pl.ds(0, n)], raw.at[pl.ds(base, n)], sem.at[2])
    mine.start()
    both = remote(p_ref.at[pl.ds(0, n)], raw.at[pl.ds(base, n)], sem.at[0], sem.at[1], (at.z, at.fc))
    both.start()
    mine.wait()
    both.wait()
    k = at.k
    own = pl.multiple_of(PLANE * at.z + UNIT * k, 16)
    extra = pl.multiple_of(NROW + EXTRA * (4 * at.z + k), 16)
    row = lax.broadcasted_iota(jnp.int32, (16, 128), 0)
    first_core = lax.broadcasted_iota(jnp.int32, (592, 128), 0) + 4 * k < n // 6
    for j in range(6):
        cols = slice(128 * j, 128 * j + 128)
        v = [raw[pl.ds(RAW + gap * i + 24 * k + j, 592, stride=6), :] for i in range(2)]
        g[pl.ds(own, 592), cols] = jnp.where(first_core, v[0], v[1]).astype(bf16)
        last = raw[pl.ds(RAW + gap + (592 + 4 * k) * 6 + j, 16, stride=6), :]
        first = raw[pl.ds(RAW - 96 + 24 * k + j, 16, stride=6), :]
        g[pl.ds(extra, 16), cols] = jnp.where(row < 12 - 4 * k, last, first).astype(bf16)

K1_OUT = ("w", "wproj", "tail", "dctx", "small", "hat1", "r1", "hat2", "r2", "gp", "actT", "normT", "attT", "q", "kT", "vv", "xT", "pT")
K1_SHAPE = {"w": ((NROW, D), bf16), "wproj": ((D, 256), bf16), "tail": ((448, D), bf16), "dctx": ((T, 256), bf16), "small": ((8, 256), f32),
            "hat1": ((LT, D), f32), "r1": ((LT, 128), f32), "hat2": ((LT, D), f32), "r2": ((LT, 128), f32), "gp": ((T, FF), bf16), "actT": ((FF, T), bf16),
            "normT": ((D, T), bf16), "attT": ((D, T), bf16), "q": ((T, D), bf16), "kT": ((D, T), bf16), "vv": ((T, D), bf16), "xT": ((D, T), bf16),
            "pT": ((H * T, T), bf16)}

def forward_kernel(pieces, events, weight, p_ref, x, mask, dis, cho, vec_ref, *rest):
    n_out = len(K1_OUT)
    hbm = dict(zip(K1_OUT, rest[:n_out]))
    (out, vec, g, raw, nice, tmp, wproj, tail, dctx, small, hat1, r1, hat2, r2, gp, actT, normT, attT, q, kT, vv, xT, pT,
     xp, kk, vT, act, res, wide, low1, low2, place, placeT, allowed, choose, fb, p32, c32, code, wcode,
     sem_raw, R, O, S, OS, PS) = rest[n_out:]
    here = dict(wproj=wproj, tail=tail, dctx=dctx, small=small, hat1=hat1, r1=r1, hat2=hat2, r2=r2, gp=gp, actT=actT, normT=normT, attT=attT, q=q, kT=kT, vv=vv, xT=xT, pT=pT)
    outs = []
    count = iter(range(32))
    def put(src, dst):
        cp = pltpu.make_async_copy(src, dst, OS.at[next(count)])
        cp.start()
        outs.append(cp)
    def save(*names):
        for n in names: put(here[n], hbm[n])
    at = Place()
    ga = Gather(at, g, pieces, R, O, S)
    at.greet()
    own_rows(at, g, p_ref, raw, sem_raw)
    def slot(i, cond=None):
        for zs in range(PLANES):
            if events[zs][i]:
                @pl.when((at.z == zs) if cond is None else ((at.z == zs) & cond))
                def _():
                    for e in events[zs][i]: ga.op(zs, *e)
    def plane(p):
        for zs in range(PLANES):
            @pl.when(at.z == zs)
            def _(): ga.other_core(zs, p)
        shared_blocks(g, p)
    slot(0)
    prepare(x, xp, xT, mask, dis, cho, vec_ref, vec, place, placeT, allowed, choose)
    act[LT:T, :] = jnp.zeros((T - LT, FF), bf16)
    gp[LT:T, :] = jnp.zeros((T - LT, FF), bf16)
    low1[...] = jnp.zeros((T, D), bf16)
    low2[...] = jnp.zeros((T, D), bf16)
    small[...] = jnp.zeros((8, 256), f32)
    save("xT")
    slot(1)
    plane(0)
    split_rows(g, 0, 3, nice, 0, tmp)
    slot(2)
    project(xp, nice, vec, q, kk, kT, vv, vT)
    save("q", "kT", "vv")
    put(nice.at[pl.ds(0, 2304)], hbm["w"].at[pl.ds(0, 2304)])
    nice_out = outs.pop()
    slot(3)
    slot(4)
    def pair_out(p):
        b = p % 2
        return pltpu.make_async_copy(pT.at[pl.ds(pl.multiple_of(2 * T * b, T), 2 * T)], hbm["pT"].at[pl.ds(pl.multiple_of(2 * T * p, T), 2 * T)], PS.at[b])
    def pairs(b, _):
        p = 2 * b
        @pl.when(b > 0)
        def _():
            pair_out(p - 2).wait()
            pair_out(p - 1).wait()
        attend(p, q, kk, vT, pT, attT)
        attend(p + 1, q, kk, vT, pT, attT)
        pair_out(p).start()
        pair_out(p + 1).start()
        for i in range(3): slot(5 + i, b == i)
        return 0
    lax.fori_loop(0, H // 4, pairs, 0)
    pair_out(H // 2 - 2).wait()
    pair_out(H // 2 - 1).wait()
    save("attT")
    plane(1)
    out_project(attT, kk, xp, g.at[2304:3072], vec, res)
    put(g.at[pl.ds(2304, 768)], hbm["w"].at[pl.ds(2304, 768)])
    norm_rows(res, vec[0:1, G1:G1 + D], vec[0:1, S1:S1 + D], low1, wide, hat1, r1)
    save("hat1", "r1")
    transpose_to(low1, normT, T, D)
    save("normT")
    slot(8)
    plane(2)
    nice_out.wait()
    split_rows(g, 3072, 4, nice, 0, tmp)
    put(nice, hbm["w"].at[pl.ds(3072, 3072)])
    slot(9)
    def tile(n, _):
        up(n, low1, nice, vec, act, gp)
        for i in range(3): slot(10 + i, n == i)
        return 0
    lax.fori_loop(0, FF // TILE, tile, 0)
    slot(13)
    save("gp")
    transpose_to(act, actT, T, FF)
    save("actT")
    slot(14)
    plane(3)
    put(g.at[pl.ds(6144, 3072)], hbm["w"].at[pl.ds(6144, 3072)])
    down(act, g, vec, res, wide)
    norm_rows(res, vec[0:1, G2:G2 + D], vec[0:1, S2:S2 + D], low2, None, hat2, r2)
    save("hat2", "r2")
    out[0] = low2[0:LEN, :]
    small_weights(g, fb, p32, c32, wproj, code, wcode)
    save("wproj")
    slot(15)
    contrast(weight, low2, vec, place, placeT, allowed, choose, wproj, code, wcode, fb, p32, c32, tail, dctx, small)
    save("tail", "dctx", "small")
    slot(16)
    ga.drain()
    for cp in outs: cp.wait()

def forward(pieces, events, weight, params, x, mask, dis, cho, vec):
    V_ = pl.BlockSpec(memory_space=pltpu.VMEM)
    A_ = pl.BlockSpec(memory_space=pl.ANY)
    VM = pltpu.VMEM
    DMA = pltpu.SemaphoreType.DMA
    sds = jax.ShapeDtypeStruct
    n = params.shape[0] // 128
    most = max(len(ps) for ps in pieces) + 1
    here = [VM(*K1_SHAPE[k]) for k in K1_OUT[1:-1]] + [VM((4 * T, T), bf16)]
    outs = pl.pallas_call(functools.partial(forward_kernel, pieces, events, weight),
        out_shape=[sds(*K1_SHAPE[k]) for k in K1_OUT] + [sds((1, LEN, D), bf16)],
        in_specs=[A_] + [V_] * 5, out_specs=[A_] * len(K1_OUT) + [V_],
        scratch_shapes=[VM((1, vec.shape[0]), f32), VM((GROW, D), bf16), VM((RAW + 2 * (n + 4) + 96, 128), f32), VM((4 * D, D), bf16), VM((6, 256, 128), f32)] + here
            + [VM((T, D), bf16), VM((T, D), bf16), VM((D, T), bf16), VM((T, FF), bf16), VM((LT, D), f32), VM((LT, D), f32), VM((T, D), bf16), VM((T, D), bf16),
               VM((256, T), bf16), VM((T, 256), bf16), VM((256, 256), f32), VM((2, 256, 384), f32), VM((1152, 128), f32), VM((2, 768, 128), f32), VM((3, 256, 128), f32),
               VM((256, 384), bf16), VM((256, 256), bf16),
               DMA((3,)), DMA((16, most)), DMA((PLANES,)), DMA((2,)), DMA((24,)), DMA((2,))],
        compiler_params=pltpu.CompilerParams(collective_id=0, has_side_effects=True, vmem_limit_bytes=63 * 2**20),
    )(params.reshape(n, 128), x, mask, jnp.transpose(dis, (2, 0, 1)), jnp.swapaxes(cho, 1, 2), vec.reshape(-1, 128))
    return dict(zip(K1_OUT, outs)), outs[-1]
TO_CORE, TO_V, TO_U, TO_Z, KEEP, SMALL = range(6)

class Reduce:
    def __init__(self, at, g, pieces, LD, LV, LZ, LU, total, RD, RV, RZ, RU, S):
        self.at, self.g, self.pieces, self.total = at, g, pieces, total
        self.LD, self.LV, self.LZ, self.LU = LD, LV, LZ, LU
        self.RD, self.RV, self.RZ, self.RU, self.S = RD, RV, RZ, RU, S
        self.sent = {z: 0 for z in range(PLANES)}
        self.seen = set()

    def copies(self, p, r, c, first, rows, extra, land, got, dev):
        a, e = self.at.span(p, r, c, first)
        out = []
        for j, (s, n, to) in enumerate([(a, rows, first)] + [(e, EXTRA, MAIN)] * extra):
            out.append(remote(self.g.at[pl.ds(s, n)], land.at[pl.ds(to, n)], self.S.at[0], got.at[j], dev))
        return out

    def build(self, zs, op):
        at = self.at
        kind, i, p, r = op
        unit = 4 * p + at.roles[r]
        _, first, rows, extra = self.pieces[p][i]
        if kind == TO_V:
            n = 2 * p + r - 2
            return self.copies(p, r, at.c, first, rows, extra, self.LV.at[n], self.RV.at[n, i], (zs, at.vf))
        if kind == TO_U:
            return self.copies(p, r, at.c, first, rows, extra, self.LU.at[p], self.RU.at[p, i], (zs, at.uf))
        up = p > zs
        to = zs + 1 if up else zs - 1
        n = 8 + r if (not up and to == p) else 2 * p + r
        return self.copies(p, r, at.c, first, rows, extra, self.LZ.at[n], self.RZ.at[n, i], (to, at.f))

    def once(self, zs, key, cs):
        if (zs, key) not in self.seen:
            self.seen.add((zs, key))
            for q in cs: q.wait_recv()

    def send(self, zs, op):
        for q in self.build(zs, op): q.start()
        _, _, rows, extra = self.pieces[op[2]][op[1]]
        self.sent[zs] += rows + EXTRA * extra

    def add(self, p, r, first, rows, extra, lands, final):
        a, e = self.at.span(p, r, self.at.c, first)
        g, total = self.g, self.total
        def one(s, i):
            v = g[pl.ds(s, 16), :].astype(f32)
            for land in lands:
                v = v + land[pl.ds(i, 16), :].astype(f32)
            if final:
                total[pl.ds(16 + i, 16), :] = v
            else:
                g[pl.ds(s, 16), :] = v.astype(bf16)
        def body(b, _):
            one(pl.multiple_of(a + 16 * b, 16), pl.multiple_of(first + 16 * b, 16))
            return 0
        lax.fori_loop(0, rows // 16, body, 0)
        if extra: one(e, MAIN)

    def op(self, zs, op):
        at = self.at
        kind, i, p, r = op
        unit = 4 * p + at.roles[r]
        self.once(zs, (TO_CORE, p, r), self.copies(p, r, at.c, 0, MAIN, True, self.LD.at[unit], self.RD.at[unit], (zs, at.fc)))
        path, first, rows, extra = self.pieces[p][i]
        if kind == TO_V:
            self.add(p, r, first, rows, extra, [self.LD.at[unit]], False)
            self.send(zs, op)
            return
        n = 2 * p + r
        self.once(zs, ("v", i, p, r), self.copies(p, r, at.c, first, rows, extra, self.LV.at[n], self.RV.at[n, i], (zs, at.fc)))
        lands = [self.LD.at[unit], self.LV.at[n]]
        def arrived(land, got, key):
            self.once(zs, key, self.copies(p, r, at.c, first, rows, extra, land, got, (zs, at.fc)))
            lands.append(land)
        if path == 0 or r == 0:
            if p >= zs and zs > 0: arrived(self.LZ.at[n], self.RZ.at[n, i], (UP, i, p, r))
            if p <= zs and zs < PLANES - 1:
                m = 8 + r if p == zs else n
                arrived(self.LZ.at[m], self.RZ.at[m, i], (DOWN, i, p, r))
        if r == 0 and (path == 1 or p == zs):
            arrived(self.LU.at[p], self.RU.at[p, i], (TO_U, i, p))
        self.add(p, r, first, rows, extra, lands, kind == KEEP)
        if kind != KEEP: self.send(zs, op)

    def core_copies(self, p, kk):
        a, e = self.at.span_of(p, kk, 1 - self.at.c, 0)
        land = self.LD.at[4 * p + kk]
        dev = (self.at.z, self.at.fc)
        return [remote(self.g.at[pl.ds(s, n)], land.at[pl.ds(to, n)], self.S.at[1], self.RD.at[4 * p + kk, j], dev)
                for j, (s, n, to) in enumerate(((a, MAIN, 0), (e, EXTRA, MAIN)))]

    def to_core(self, p, kk):
        extra_rows(self.g, p, kk)
        for q in self.core_copies(p, kk): q.start()

    def drain(self):
        for zs in range(PLANES):
            @pl.when(self.at.z == zs)
            def _(): wait_sent(self.g, self.sent[zs], self.S.at[0], self.RD.at[0, 0], (zs, self.at.fc))
        wait_sent(self.g, 4 * PLANES * HALF, self.S.at[1], self.RD.at[0, 0], (self.at.z, self.at.fc))

class Spread:
    def __init__(self, at, own, land, zland, S, count):
        self.at, self.own, self.land, self.zland, self.S, self.count = at, own, land, zland, S, count

    def round(self, n, me, land, base, dev):
        return [remote(self.own, land.at[me], self.S.at[0, base + j], self.S.at[1, base + j], dev(lax.rem(me + j, n))) for j in range(1, n)]

    def plane(self):
        return self.round(self.count, self.at.f, self.land, 0, lambda t: (self.at.z, t))

    def planes(self):
        return self.round(PLANES, self.at.z, self.zland, self.count, lambda t: (t, self.at.f))

    def first(self):
        for q in self.plane(): q.start()

    def total(self, land, n, me):
        land[me] = self.own[...]
        v = land[0]
        for j in range(1, n): v = v + land[j]
        return v

    def second(self):
        for q in self.plane(): q.wait()
        self.own[...] = self.total(self.land, self.count, self.at.f)
        for q in self.planes(): q.start()

    def last(self):
        for q in self.planes(): q.wait()
        self.own[...] = self.total(self.zland, PLANES, self.at.z)

K2_IN = K1_OUT
K2_HERE = ("wproj", "dctx", "small", "hat1", "r1", "hat2", "r2", "gp", "ring", "normT", "attT", "q", "kT", "vv", "xT", "wq")

def backward_kernel(pieces, events, vec_ref, *rest):
    n_in = len(K2_IN)
    hbm = dict(zip(K2_IN, rest[:n_in]))
    (grad, vsum, sq, ig_out, ig, g, vec, wproj, dctx, small, hat1, r1, hat2, r2, gp, ring, normT, attT, q, kT, vv, xT, wq,
     low1, low2, acc, tmp, dp, LD, LV, LZ, LU, total, flat, vg, vland, vzland, sqv, sland, szland,
     IS, RD, RV, RZ, RU, S, TS, TL, VS, SS) = rest[n_in:]
    here = dict(wproj=wproj, dctx=dctx, small=small, hat1=hat1, r1=r1, hat2=hat2, r2=r2, gp=gp, normT=normT, attT=attT, q=q, kT=kT, vv=vv, xT=xT)
    loads = {}
    def load(name, src=None, dst=None):
        cp = pltpu.make_async_copy(hbm[name] if src is None else src, here[name] if dst is None else dst, IS.at[len(loads)])
        cp.start()
        loads[name if src is None else (name, len(loads))] = cp
        return cp
    w = hbm["w"]
    first = [load(n) for n in ("dctx", "wproj", "hat2", "r2")]
    def second(n):
        rows = pl.ds(pl.multiple_of(6144 + n * TILE, 256), TILE)
        own = pl.ds(pl.multiple_of(n * TILE, TILE), TILE)
        pairs = ((w.at[rows], g.at[rows]), (hbm["actT"].at[own], ring.at[own]), (hbm["gp"].at[:, own], gp.at[:, own]))
        return [pltpu.make_async_copy(s, d, TL.at[3 * n + i]) for i, (s, d) in enumerate(pairs)]
    for n in range(FF // TILE - 1, -1, -1):
        for cp in second(n): cp.start()
    tail = load("tail", hbm["tail"], g.at[pl.ds(9216, 448)])
    third = [load("w", w.at[pl.ds(3072, 3072)], g.at[pl.ds(3072, 3072)]), load("normT")]
    fifth = [load("w", w.at[pl.ds(2304, 768)], g.at[pl.ds(2304, 768)]), load("attT")]
    sixth = [load("q"), load("kT"), load("vv")]
    seventh = [load("xT"), load("w", w.at[pl.ds(0, 2304)], wq)]
    def ready(cs):
        for cp in cs: cp.wait()
    at = Place()
    at.greet_all(vland.shape[0])
    re = Reduce(at, g, pieces, LD, LV, LZ, LU, total, RD, RV, RZ, RU, S)
    vs = Spread(at, vg, vland, vzland, VS, vland.shape[0])
    ss = Spread(at, sqv, sland, szland, SS, vland.shape[0])
    def slot(i, cond=None):
        for zs in range(PLANES):
            if events[zs][i]:
                @pl.when((at.z == zs) if cond is None else ((at.z == zs) & cond))
                def _():
                    for e in events[zs][i]:
                        if e[0] == SMALL: (vs.first, vs.second, vs.last)[e[1]]()
                        else: re.op(zs, e)
    for i in range(vec_ref.shape[0]):
        vec[0:1, 128 * i:128 * i + 128] = vec_ref[i:i + 1, :]
    low2[...] = jnp.zeros((T, D), bf16)
    low1[...] = jnp.zeros((T, D), bf16)
    for t in range(3):
        dp[t] = jnp.zeros((T, D), bf16)
    ready(first)
    for n in range(3):
        hat1[:, 256 * n:256 * n + 256] = mm_nt(dctx[0:LT, :], wproj[256 * n:256 * n + 256, :])
    norm_back(hat1, vec[0:1, G2:G2 + D], hat2, r2, low2, acc)
    fourth = [load("hat1"), load("r1"), load("small")]
    put_vec(vg, acc, (G2, S2, BDOWN))
    ready([tail])
    def downs(n, _):
        ready(second(3 - n))
        down_back(3 - n, low2, g, ring, gp, vg)
        for kk, last in ((3, 0), (2, 0), (1, 1), (0, 2)):
            @pl.when(n == last)
            def _(): re.to_core(3, kk)
        return 0
    lax.fori_loop(0, 3, downs, 0)
    slot(0)
    slot(1)
    ready(second(0))
    down_back(0, low2, g, ring, gp, vg)
    def head(h):
        return pltpu.make_async_copy(hbm["pT"].at[pl.ds(pl.multiple_of(h * T, T), T)], ring.at[pl.ds(pl.multiple_of((h % 6) * T, T), T)], TS.at[h % 6])
    for h in range(6): head(h).start()
    slot(2)
    ready(third)
    lax.fori_loop(0, 3, lambda n, _: (up_back_x(n, gp, g, hat2), 0)[1], 0)
    slot(3)
    def woven(n, _):
        weave(normT, gp, 4, 2 - n, 3072, g, tmp, False)
        for kk in range(4):
            @pl.when(n == int(kk == 0))
            def _(): re.to_core(2, kk)
        slot(4, n == 0)
        slot(5, n == 1)
        return 0
    lax.fori_loop(0, 2, woven, 0)
    slot(6)
    weave(normT, gp, 4, 0, 3072, g, tmp, False)
    re.to_core(1, 2)
    re.to_core(1, 3)
    slot(7)
    ready(fourth)
    norm_back(hat2, vec[0:1, G1:G1 + D], hat1, r1, low1, acc)
    put_vec(vg, acc, (G1, S1, BO))
    ready(fifth)
    da, dqT = low2, normT
    out_back(low1, g, attT, da)
    re.to_core(1, 0)
    re.to_core(1, 1)
    slot(8)
    slot(9)
    ready(sixth)
    def pairs(b, _):
        for p in (2 * b, 2 * b + 1):
            head(2 * p).wait()
            head(2 * p + 1).wait()
        attend_back(2 * b, da, q, kT, vv, ring, dp, dqT)
        attend_back(2 * b + 1, da, q, kT, vv, ring, dp, dqT)
        for p in (2 * b, 2 * b + 1):
            @pl.when(p < 3)
            def _():
                head(2 * p + 6).start()
                head(2 * p + 7).start()
        for i in range(3): slot(10 + i, b == i)
        return 0
    lax.fori_loop(0, H // 4, pairs, 0)
    ready(seventh)
    def wove(n, _):
        weave(xT, dp, 3, n, 0, g, tmp, True)
        for kk in range(4):
            @pl.when(n == min(kk, 2))
            def _(): re.to_core(0, kk)
        for i in range(3): slot(13 + i, n == i)
        return 0
    lax.fori_loop(0, 3, wove, 0)
    slot(16)
    vg[0:1, BQ:BQ + D] = jnp.sum(dp[0].astype(f32), axis=0, keepdims=True)
    vg[0:1, BV:BV + D] = jnp.sum(dp[2].astype(f32), axis=0, keepdims=True)
    vg[0:1, BPROJ:BPROJ + 256] = small[0:1, :]
    vg[0:1, BCODE:BCODE + 256] = small[1:2, :]
    vg[0:1, BCODE + 256:BCODE + 512] = small[2:3, :]
    slot(17)
    slot(18)
    for n in range(3):
        input_back(n, dp, wq, hat1, ig)
    put_ig = pltpu.make_async_copy(ig, ig_out, IS.at[len(loads)])
    put_ig.start()
    slot(19)
    z, c, k = at.z, at.c, at.k
    edge = remote(total.at[pl.ds(HALF, 16)], total.at[pl.ds(0, 16)], TS.at[6], TS.at[7], (z, at.fc))
    edge.start()
    row = lax.broadcasted_iota(jnp.int32, (16, D), 0)
    def square(b, acc):
        v = total[pl.ds(pl.multiple_of(16 + 16 * b, 16), 16), :]
        return acc + sum8(v * v)
    acc = lax.fori_loop(0, MAIN // 16, square, jnp.zeros((8, D), f32))
    v = jnp.where((c == 0) | (row < 12 - 4 * k) | (row >= 16 - 4 * k), total[16 + MAIN:16 + HALF, :], 0.0)
    acc = acc + sum8(v * v)
    sqv[...] = sum(acc[:, 128 * j:128 * j + 128] for j in range(6))
    ss.first()
    for i in range(vsum.shape[0]):
        vsum[i:i + 1, :] = vg[0:1, 128 * i:128 * i + 128]
    n = grad.shape[0] // 6
    edge.wait()
    for j in range(6):
        flat[pl.ds(j, 320, stride=6), :] = total[:, 128 * j:128 * j + 128]
    ss.second()
    for j in range(6):
        grad[pl.ds(j, n, stride=6), :] = flat[pl.ds(6 * (16 - 2 * c - 4 * k) + j, n, stride=6), :]
    re.drain()
    ss.last()
    sq[...] = sqv[...]
    put_ig.wait()

def backward(pieces, events, vec, hbm, count, n):
    V_ = pl.BlockSpec(memory_space=pltpu.VMEM)
    A_ = pl.BlockSpec(memory_space=pl.ANY)
    VM = pltpu.VMEM
    DMA = pltpu.SemaphoreType.DMA
    sds = jax.ShapeDtypeStruct
    most = max(len(ps) for ps in pieces)
    nv = vec.shape[0] + 256
    shape = dict(K1_SHAPE, ring=((FF, T), bf16), wq=((3 * D, D), bf16))
    return pl.pallas_call(functools.partial(backward_kernel, pieces, events),
        out_shape=[sds((n, 128), f32), sds((nv // 128, 128), f32), sds((8, 128), f32), sds((1, LEN, D), f32)],
        in_specs=[V_] + [A_] * len(K2_IN), out_specs=[V_] * 3 + [A_],
        scratch_shapes=[VM((1, LEN, D), f32), VM((GROW, D), bf16), VM((1, vec.shape[0]), f32)] + [VM(*shape[k]) for k in K2_HERE]
            + [VM((T, D), bf16), VM((T, D), bf16), VM((24, D), f32), VM((2, 1024, 128), f32), VM((3, T, D), bf16),
               VM((16, HALF, D), bf16), VM((8, HALF, D), bf16), VM((10, HALF, D), bf16), VM((4, HALF, D), bf16), VM((HALF + 16, D), f32), VM((6 * (HALF + 16), 128), f32),
               VM((1, nv), f32), VM((count, 1, nv), f32), VM((PLANES, 1, nv), f32), VM((8, 128), f32), VM((count, 8, 128), f32), VM((PLANES, 8, 128), f32),
               DMA((24,)), DMA((16, 2)), DMA((8, most, 2)), DMA((10, most, 2)), DMA((4, most, 2)), DMA((2,)), DMA((8,)), DMA((12,)), DMA((2, count + PLANES)), DMA((2, count + PLANES))],
        compiler_params=pltpu.CompilerParams(collective_id=1, has_side_effects=True, vmem_limit_bytes=63 * 2**20),
    )(vec.reshape(-1, 128), *[hbm[k] for k in K2_IN])

def update_kernel(total, g, p, m1, m2, vg, v, v1, v2, sq, np_, low, n1, n2, nv, nv1, nv2, loss, norm, scale):
    @pl.when(pl.program_id(0) == 0)
    def _():
        n = v.shape[0]
        gv = vg[0:n, :]
        s = jnp.sum(jnp.sum(sq[...], axis=0, keepdims=True), axis=1, keepdims=True)
        s = s + jnp.sum(jnp.sum(gv * gv, axis=0, keepdims=True), axis=1, keepdims=True)
        s = jnp.sqrt(s)
        f = jnp.minimum(1.0, clip_level / (s + 1e-06))
        norm[...] = s
        loss[...] = vg[n:n + 1, 0:1] / total
        scale[...] = jnp.broadcast_to(f, (8, 128))
        nv[...], nv1[...], nv2[...] = adamw_update(v[...], v1[...], v2[...], gv * f, rate_vector)
    new, first, second = adamw_update(p[...], m1[...], m2[...], g[...] * scale[0:1, 0:1], rate_matrix)
    np_[...] = new
    low[...] = new.astype(bf16)
    n1[...] = first
    n2[...] = second

def update(total, g, p, m1, m2, vg, v, v1, v2, sq):
    n, nv = g.shape[0], v.shape[0] // 128
    sds = jax.ShapeDtypeStruct
    rows = 608
    part = pl.BlockSpec((rows, 128), lambda i: (i, 0))
    def whole(*shape): return pl.BlockSpec(shape, lambda i: (0, 0))
    flat = lambda a: a.reshape(-1, 128)
    out = pl.pallas_call(functools.partial(update_kernel, total), grid=(pl.cdiv(n, rows),),
        out_shape=[sds((n, 128), f32), sds((n, 128), bf16), sds((n, 128), f32), sds((n, 128), f32)] + [sds((nv, 128), f32)] * 3 + [sds((1, 1), f32)] * 2,
        in_specs=[part] * 4 + [whole(*vg.shape)] + [whole(nv, 128)] * 3 + [whole(8, 128)],
        out_specs=[part] * 4 + [whole(nv, 128)] * 3 + [whole(1, 1)] * 2,
        scratch_shapes=[pltpu.VMEM((8, 128), f32)],
    )(g, flat(p), flat(m1), flat(m2), vg, flat(v), flat(v1), flat(v2), sq)
    return [a.reshape(-1) for a in out[:7]] + [a.reshape(()) for a in out[7:]]

PIECES_OUT = (((0, 0, 48, False), (0, 48, 48, False), (0, 96, 48, False), (1, 144, 48, False), (1, 192, 32, False), (1, 224, 32, False), (1, 256, 32, True)),
 ((0, 0, 96, False), (0, 96, 96, False), (0, 192, 96, True)), ((1, 0, 144, False), (1, 144, 144, True)), ((0, 0, 192, False), (1, 192, 96, True)))
PIECES_BACK = (((0, 0, 48, False), (0, 48, 48, False), (0, 96, 48, False), (1, 144, 48, False), (1, 192, 32, False), (1, 224, 32, False), (1, 256, 32, True)),
 ((0, 0, 192, False), (1, 192, 48, False), (1, 240, 48, True)), ((1, 0, 96, False), (1, 96, 96, False), (1, 192, 96, True)),
 ((0, 0, 144, False), (0, 144, 144, True)))
SENDS_OUT = ((((0, 0, 0, 0), (0, 1, 0, 0), (3, 0, 0, 0), (3, 1, 0, 0), (3, 2, 0, 0)),
  ((0, 2, 0, 0), (0, 3, 0, 0), (4, 0, 0, 2), (3, 3, 0, 0), (3, 4, 0, 0), (4, 1, 0, 2), (0, 4, 0, 0), (3, 5, 0, 0), (4, 2, 0, 2), (3, 6, 0, 0),
   (0, 5, 0, 0), (4, 0, 1, 0), (2, 0, 0, 0), (2, 1, 0, 0), (0, 6, 0, 0), (2, 2, 0, 0), (4, 3, 0, 2), (2, 3, 0, 0), (4, 4, 0, 2), (2, 4, 0, 0),
   (4, 5, 0, 2), (4, 1, 1, 0), (2, 5, 0, 0), (4, 6, 0, 2), (2, 6, 0, 0), (3, 0, 1, 0), (0, 0, 0, 1), (4, 0, 0, 1), (0, 1, 0, 1), (4, 1, 0, 1),
   (3, 0, 0, 1), (0, 2, 0, 1), (4, 2, 0, 1), (4, 3, 0, 1), (3, 1, 0, 1), (4, 4, 0, 1), (3, 2, 0, 1), (4, 5, 0, 1), (4, 2, 1, 0), (3, 3, 0, 1),
   (4, 6, 0, 1), (3, 4, 0, 1), (3, 5, 0, 1), (3, 6, 0, 1), (4, 0, 1, 2), (3, 1, 1, 0), (4, 0, 0, 3), (4, 0, 2, 0), (4, 1, 0, 3), (3, 0, 2, 0),
   (4, 2, 0, 3), (4, 3, 0, 3), (4, 4, 0, 3), (4, 5, 0, 3), (2, 0, 2, 0), (4, 6, 0, 3), (4, 1, 2, 0), (4, 1, 1, 2), (3, 1, 2, 0)),
  (), ((3, 0, 2, 1), (4, 0, 1, 1), (4, 0, 2, 2), (4, 0, 2, 1), (4, 1, 1, 1), (2, 1, 2, 0)), (), ((3, 2, 1, 0), (4, 1, 2, 2)),
  ((4, 2, 1, 1), (3, 0, 1, 1), (3, 1, 1, 1), (4, 0, 2, 3), (4, 1, 2, 1)),
  ((3, 1, 2, 1), (4, 2, 1, 2), (4, 0, 3, 0), (4, 0, 1, 3), (3, 2, 1, 1), (4, 1, 1, 3), (3, 0, 3, 0), (4, 1, 3, 0), (4, 1, 2, 3), (2, 1, 3, 0),
   (4, 2, 1, 3), (3, 1, 3, 0), (4, 0, 3, 2), (4, 0, 3, 1), (3, 0, 3, 1)),
  ((4, 1, 3, 1), (3, 1, 3, 1)), ((4, 1, 3, 2),), (), (), (), ((4, 0, 3, 3),), ((4, 1, 3, 3),), (), ()),
 (((1, 0, 1, 0), (2, 0, 1, 0), (2, 1, 1, 0), (0, 0, 1, 0)),
  ((1, 1, 1, 0), (2, 2, 1, 0), (0, 1, 1, 0), (3, 0, 1, 0), (4, 0, 0, 0), (4, 0, 1, 1), (1, 2, 1, 0), (0, 0, 0, 0), (3, 0, 0, 0), (4, 1, 0, 0),
   (4, 1, 1, 1), (3, 1, 0, 0), (0, 1, 0, 0), (3, 1, 1, 0), (4, 0, 2, 0), (4, 2, 0, 0), (4, 2, 1, 1), (1, 0, 2, 0), (0, 2, 0, 0), (3, 2, 0, 0),
   (4, 3, 0, 0), (2, 3, 0, 0), (4, 0, 1, 2), (0, 3, 0, 0), (4, 4, 0, 0), (4, 0, 0, 2), (2, 4, 0, 0), (3, 3, 0, 0), (4, 1, 0, 2), (0, 4, 0, 0),
   (4, 5, 0, 0), (2, 5, 0, 0), (3, 4, 0, 0), (0, 5, 0, 0), (1, 1, 2, 0), (4, 6, 0, 0), (0, 6, 0, 0), (4, 2, 0, 2), (4, 1, 1, 2), (4, 3, 0, 1),
   (2, 6, 0, 0), (4, 4, 0, 1), (0, 0, 0, 1), (4, 0, 0, 1), (4, 3, 0, 2), (3, 5, 0, 0), (4, 5, 0, 1), (4, 1, 0, 1), (0, 1, 0, 1), (4, 4, 0, 2),
   (3, 6, 0, 0), (3, 3, 0, 1), (3, 4, 0, 1), (1, 0, 1, 1), (0, 2, 0, 1), (4, 2, 0, 1), (4, 0, 3, 0), (4, 6, 0, 1), (4, 5, 0, 2), (3, 0, 0, 1),
   (3, 5, 0, 1), (3, 1, 0, 1), (3, 2, 0, 1), (4, 6, 0, 2), (0, 2, 1, 0), (1, 1, 1, 1), (4, 3, 0, 3), (3, 6, 0, 1), (4, 4, 0, 3), (2, 1, 3, 0),
   (4, 1, 3, 0), (4, 1, 2, 0), (4, 0, 0, 3), (0, 0, 1, 1), (4, 5, 0, 3), (2, 0, 2, 0), (1, 2, 1, 1), (4, 1, 0, 3), (4, 2, 0, 3), (2, 1, 2, 0),
   (4, 6, 0, 3), (0, 1, 1, 1), (1, 0, 3, 0), (4, 1, 3, 1), (3, 0, 2, 0)),
  ((4, 0, 3, 1), (0, 2, 1, 1), (4, 0, 2, 1)), ((3, 1, 2, 0), (4, 1, 2, 1), (1, 1, 3, 0)), (), ((3, 0, 2, 1), (4, 0, 2, 2)),
  ((1, 0, 3, 1), (3, 1, 2, 1), (4, 1, 2, 2)),
  ((3, 2, 1, 0), (4, 0, 2, 3), (3, 0, 1, 1), (3, 1, 1, 1), (4, 1, 2, 3), (3, 2, 1, 1), (4, 2, 1, 2), (3, 0, 3, 0), (4, 0, 1, 3), (4, 1, 1, 3),
   (3, 1, 3, 0), (4, 2, 1, 3), (3, 1, 3, 1), (3, 0, 3, 1), (4, 0, 3, 2)),
  ((4, 1, 3, 2),), (), ((4, 1, 3, 3),), (), (), (), ((4, 0, 3, 3),), (), ()),
 (((0, 0, 2, 0), (1, 0, 2, 0), (3, 0, 2, 0)),
  ((3, 1, 2, 0), (0, 1, 2, 0), (1, 1, 2, 0), (2, 0, 2, 0), (4, 0, 2, 2), (2, 1, 2, 0), (4, 0, 1, 0), (0, 0, 1, 0), (4, 1, 2, 2), (4, 0, 3, 0),
   (3, 0, 3, 0), (4, 1, 1, 0), (1, 0, 3, 0), (4, 0, 2, 1), (4, 0, 0, 0), (0, 0, 0, 0), (3, 0, 0, 0), (4, 1, 3, 0), (0, 1, 0, 0), (3, 1, 0, 0),
   (4, 1, 2, 1), (4, 1, 0, 0), (3, 1, 3, 0), (4, 2, 0, 0), (0, 2, 0, 0), (1, 1, 3, 0), (3, 2, 0, 0), (0, 3, 0, 0), (4, 3, 0, 0), (3, 3, 0, 0),
   (4, 0, 3, 2), (4, 4, 0, 0), (3, 4, 0, 0), (0, 4, 0, 0), (4, 0, 0, 2), (3, 5, 0, 0), (4, 5, 0, 0), (0, 5, 0, 0), (3, 0, 3, 1), (4, 0, 3, 1),
   (4, 1, 0, 2), (0, 6, 0, 0), (4, 1, 3, 2), (4, 6, 0, 0), (1, 0, 3, 1), (4, 2, 0, 2), (0, 0, 0, 1), (4, 0, 0, 1), (3, 6, 0, 0), (4, 3, 0, 2),
   (4, 4, 0, 2), (3, 0, 0, 1), (0, 1, 0, 1), (4, 1, 0, 1), (3, 1, 0, 1), (4, 5, 0, 2), (2, 3, 0, 0), (4, 2, 0, 1), (0, 2, 0, 1), (3, 2, 0, 1),
   (2, 4, 0, 0), (0, 1, 1, 0), (4, 0, 3, 3), (2, 5, 0, 0), (4, 6, 0, 2), (2, 6, 0, 0), (3, 0, 2, 1), (4, 0, 0, 3), (4, 2, 1, 0), (4, 1, 0, 3),
   (0, 2, 1, 0), (4, 3, 0, 1), (3, 3, 0, 1), (4, 2, 0, 3), (4, 4, 0, 1), (3, 4, 0, 1), (4, 5, 0, 1), (3, 5, 0, 1), (4, 0, 1, 1), (3, 6, 0, 1),
   (4, 6, 0, 1), (3, 1, 2, 1), (0, 0, 1, 1), (4, 1, 1, 1), (4, 0, 2, 3), (4, 3, 0, 3), (3, 0, 1, 0), (4, 4, 0, 3), (0, 1, 1, 1), (4, 5, 0, 3),
   (3, 1, 1, 0), (4, 6, 0, 3), (4, 2, 1, 1), (3, 2, 1, 0), (0, 2, 1, 1), (4, 1, 2, 3)),
  ((3, 0, 1, 1),), ((4, 0, 1, 2), (4, 1, 1, 2), (3, 1, 1, 1), (4, 2, 1, 2), (3, 2, 1, 1)), (), ((4, 0, 1, 3), (2, 1, 3, 0)),
  ((4, 1, 1, 3), (4, 2, 1, 3)), ((3, 1, 3, 1), (4, 1, 3, 1)), (), (), (), ((4, 1, 3, 3),), (), (), (), (), ()),
 (((2, 0, 3, 0), (1, 0, 3, 0)),
  ((2, 1, 3, 0), (3, 0, 3, 0), (1, 1, 3, 0), (4, 0, 3, 1), (3, 1, 3, 0), (4, 0, 2, 0), (4, 1, 3, 1), (3, 0, 2, 0), (1, 0, 3, 1), (2, 0, 2, 0),
   (4, 0, 3, 2), (4, 1, 2, 0), (4, 1, 3, 2), (3, 1, 2, 0), (4, 0, 2, 2), (4, 0, 1, 0), (3, 0, 1, 0), (4, 0, 0, 0), (3, 0, 0, 0), (4, 0, 2, 1),
   (3, 0, 2, 1), (4, 1, 0, 0), (4, 1, 2, 2), (4, 2, 0, 0), (3, 1, 0, 0), (3, 2, 0, 0), (4, 0, 1, 2), (4, 3, 0, 0), (2, 3, 0, 0), (4, 0, 0, 2),
   (4, 4, 0, 0), (2, 4, 0, 0), (3, 3, 0, 0), (4, 5, 0, 0), (2, 5, 0, 0), (3, 4, 0, 0), (4, 0, 2, 3), (4, 6, 0, 0), (4, 1, 0, 2), (2, 6, 0, 0),
   (3, 5, 0, 0), (4, 2, 0, 2), (3, 6, 0, 0), (4, 0, 0, 1), (4, 3, 0, 1), (3, 0, 0, 1), (4, 4, 0, 1), (3, 3, 0, 1), (4, 1, 0, 1), (4, 3, 0, 2),
   (4, 5, 0, 1), (3, 4, 0, 1), (4, 4, 0, 2), (3, 1, 0, 1), (4, 2, 0, 1), (4, 6, 0, 1), (3, 5, 0, 1), (4, 5, 0, 2), (3, 2, 0, 1), (3, 6, 0, 1),
   (4, 6, 0, 2), (2, 1, 2, 0), (4, 0, 0, 3), (4, 1, 1, 0), (4, 3, 0, 3), (4, 4, 0, 3), (4, 1, 0, 3), (3, 1, 1, 0), (4, 5, 0, 3), (4, 2, 0, 3),
   (4, 2, 1, 0), (3, 2, 1, 0), (4, 6, 0, 3), (3, 0, 3, 1), (4, 1, 2, 1), (4, 0, 1, 1)),
  (), ((3, 0, 1, 1), (3, 1, 1, 1), (4, 1, 1, 2), (4, 2, 1, 2), (4, 1, 1, 1)), (),
  ((3, 2, 1, 1), (4, 2, 1, 1), (4, 0, 3, 3), (4, 0, 1, 3), (3, 1, 2, 1)), ((4, 1, 1, 3), (3, 1, 3, 1)), ((4, 2, 1, 3), (4, 1, 2, 3), (4, 1, 3, 3)),
  (), (), (), (), (), (), (), (), ()))
SENDS_BACK = (((), (), (), ((1, 0, 3, 2),), ((1, 0, 3, 3),), ((1, 1, 3, 2),), (), (), ((3, 0, 3, 0), (1, 1, 3, 3)), (), ((1, 0, 1, 2), (3, 0, 3, 1)),
  ((1, 0, 1, 3),), ((1, 1, 1, 2), (1, 1, 1, 3), (1, 2, 1, 2), (3, 1, 3, 0), (1, 2, 1, 3)), ((1, 0, 2, 2),), ((1, 0, 2, 3),),
  ((3, 1, 3, 1), (1, 1, 2, 2)), (), (), ((5, 0, 0, 0), (1, 1, 2, 3)),
  ((1, 2, 2, 2), (3, 0, 1, 0), (2, 0, 2, 1), (1, 2, 2, 3), (2, 1, 2, 1), (1, 0, 0, 2), (3, 0, 1, 1), (1, 0, 0, 3), (1, 1, 0, 2), (1, 1, 0, 3),
   (2, 2, 2, 1), (1, 2, 0, 2), (1, 2, 0, 3), (1, 3, 0, 2), (5, 1, 0, 0), (3, 0, 2, 0), (1, 3, 0, 3), (1, 4, 0, 2), (1, 4, 0, 3), (1, 5, 0, 2),
   (1, 5, 0, 3), (3, 1, 2, 0), (1, 6, 0, 2), (1, 6, 0, 3), (2, 1, 1, 1), (2, 3, 0, 1), (3, 2, 2, 0), (2, 2, 1, 1), (2, 4, 0, 1), (5, 2, 0, 0),
   (2, 5, 0, 1), (2, 0, 0, 1), (2, 6, 0, 1), (3, 1, 1, 0), (3, 2, 1, 0), (2, 1, 0, 1), (4, 0, 0, 0), (2, 2, 0, 1), (4, 1, 0, 0), (4, 3, 0, 0),
   (4, 4, 0, 0), (4, 2, 0, 0), (4, 5, 0, 0), (4, 6, 0, 0))),
 ((), (), (), ((1, 0, 3, 2),), ((1, 0, 3, 3),), ((1, 1, 3, 2),), (), (), ((1, 1, 3, 3),), (), ((1, 0, 2, 2), (1, 0, 2, 3)),
  ((1, 1, 2, 2), (1, 1, 2, 3)), ((3, 0, 3, 0), (2, 0, 2, 1), (1, 2, 2, 2)), (), ((3, 0, 3, 1), (2, 1, 2, 1), (1, 2, 2, 3)), (), (), ((1, 0, 1, 2),),
  ((5, 0, 0, 0),),
  ((1, 0, 0, 2), (3, 1, 3, 0), (1, 0, 0, 3), (2, 2, 2, 1), (1, 1, 0, 2), (1, 1, 0, 3), (1, 2, 0, 2), (3, 1, 3, 1), (1, 2, 0, 3), (1, 3, 0, 2),
   (1, 3, 0, 3), (1, 4, 0, 2), (1, 4, 0, 3), (1, 5, 0, 2), (1, 5, 0, 3), (5, 1, 0, 0), (1, 6, 0, 2), (1, 6, 0, 3), (1, 0, 1, 3), (2, 3, 0, 1),
   (2, 4, 0, 1), (2, 5, 0, 1), (3, 0, 0, 0), (2, 6, 0, 1), (1, 1, 1, 2), (3, 0, 0, 1), (1, 1, 1, 3), (1, 2, 1, 2), (3, 1, 0, 0), (2, 0, 1, 1),
   (3, 0, 2, 0), (5, 2, 0, 0), (3, 1, 0, 1), (3, 2, 0, 0), (1, 2, 1, 3), (3, 1, 2, 0), (3, 2, 0, 1), (2, 1, 1, 1), (3, 3, 0, 0), (3, 4, 0, 0),
   (3, 2, 2, 0), (4, 0, 1, 0), (3, 5, 0, 0), (2, 2, 1, 1), (3, 6, 0, 0), (4, 1, 1, 0), (4, 2, 1, 0))),
 ((), (), (), ((1, 0, 3, 2),), ((1, 0, 3, 3),), ((1, 1, 3, 2),), (), (), ((1, 1, 3, 3),), (), ((1, 0, 1, 2),), ((1, 0, 1, 3),),
  ((1, 1, 1, 2), (1, 1, 1, 3), (1, 2, 1, 2)), ((1, 2, 1, 3),), ((1, 0, 2, 2),), ((1, 0, 2, 3),), (), ((1, 1, 2, 2),), ((5, 0, 0, 0),),
  ((1, 0, 0, 2), (1, 0, 0, 3), (1, 1, 0, 2), (3, 0, 1, 0), (1, 1, 0, 3), (3, 0, 3, 0), (1, 2, 0, 2), (1, 2, 0, 3), (1, 3, 0, 2), (1, 3, 0, 3),
   (1, 4, 0, 2), (3, 0, 3, 1), (1, 4, 0, 3), (1, 5, 0, 2), (1, 5, 0, 3), (5, 1, 0, 0), (3, 0, 1, 1), (1, 6, 0, 2), (1, 6, 0, 3), (1, 1, 2, 3),
   (3, 1, 3, 0), (1, 2, 2, 2), (3, 0, 0, 0), (1, 2, 2, 3), (3, 0, 0, 1), (2, 0, 2, 1), (3, 1, 3, 1), (3, 1, 0, 0), (2, 1, 2, 1), (3, 1, 0, 1),
   (2, 3, 0, 1), (2, 4, 0, 1), (3, 2, 0, 0), (5, 2, 0, 0), (2, 2, 2, 1), (3, 2, 0, 1), (2, 5, 0, 1), (2, 6, 0, 1), (2, 1, 1, 1), (3, 3, 0, 0),
   (2, 2, 1, 1), (3, 4, 0, 0), (3, 5, 0, 0), (3, 6, 0, 0), (3, 1, 1, 0), (3, 2, 1, 0), (4, 0, 2, 0), (4, 1, 2, 0), (4, 2, 2, 0))),
 ((), (), (), ((1, 0, 3, 2),), ((1, 0, 3, 3),), ((1, 1, 3, 2),), (), (), ((1, 0, 2, 2), (1, 0, 2, 3)), (), ((1, 0, 1, 2),), ((1, 0, 1, 3),),
  ((3, 0, 1, 0), (1, 1, 1, 2), (1, 1, 1, 3), (1, 2, 1, 2)), ((1, 2, 1, 3), (1, 1, 2, 2)), ((1, 1, 2, 3),), ((3, 0, 1, 1), (2, 1, 1, 1)),
  ((1, 2, 2, 2),), (), ((5, 0, 0, 0),),
  ((1, 0, 0, 2), (1, 0, 0, 3), (1, 1, 0, 2), (1, 1, 0, 3), (3, 1, 1, 0), (1, 2, 0, 2), (1, 2, 0, 3), (1, 3, 0, 2), (3, 0, 0, 0), (1, 3, 0, 3),
   (3, 0, 0, 1), (1, 4, 0, 2), (1, 4, 0, 3), (3, 1, 0, 0), (5, 1, 0, 0), (1, 5, 0, 2), (1, 5, 0, 3), (1, 6, 0, 2), (3, 1, 0, 1), (1, 6, 0, 3),
   (2, 2, 1, 1), (3, 2, 0, 0), (2, 3, 0, 1), (3, 2, 0, 1), (2, 4, 0, 1), (1, 2, 2, 3), (2, 5, 0, 1), (2, 6, 0, 1), (3, 2, 1, 0), (2, 0, 2, 1),
   (5, 2, 0, 0), (3, 3, 0, 0), (2, 1, 2, 1), (3, 4, 0, 0), (2, 2, 2, 1), (3, 5, 0, 0), (3, 6, 0, 0), (1, 1, 3, 3), (3, 0, 2, 0), (2, 0, 3, 1),
   (3, 1, 2, 0), (3, 2, 2, 0), (2, 1, 3, 1), (4, 0, 3, 0), (4, 1, 3, 0))))

def unpack(flat_values):
    shapes = [(D, 3 * D), (D, D), (D, FF), (FF, D), (D, FINAL), (G * CD, V), (G * CD, FINAL)]
    pieces = []
    offset = 0
    for height, width in shapes:
        pieces.append(flat_values[offset : offset + height * width].reshape(height, width))
        offset = offset + height * width
    return pieces


def split_vectors(vector_all):
    lengths = [D, D, D, D, D, FF, D, D, D, FINAL, FINAL]
    pieces = []
    offset = 0
    for length in lengths:
        pieces.append(vector_all[offset : offset + length])
        offset = offset + length
    return pieces


def layer_norm(values, scale_gain, shift_bias):
    centered = values - jnp.mean(values, axis=-1, keepdims=True)
    variance = jnp.mean(centered * centered, axis=-1, keepdims=True)
    return centered * lax.rsqrt(variance + eps_norm) * scale_gain + shift_bias


def contrast_dense(chosen, targets, distract, weight):
    hi = dict(precision=lax.Precision.HIGHEST)
    frames = jnp.arange(MASKED, dtype=jnp.int32)
    allowed = jnp.any(distract[:, :, None] == frames, axis=1) | (frames[:, None] == frames)

    def agreement(chosen, targets):
        left = chosen * lax.rsqrt(jnp.sum(chosen * chosen, axis=-1, keepdims=True) + eps_cos)
        right = targets * lax.rsqrt(jnp.sum(targets * targets, axis=-1, keepdims=True) + eps_cos)
        return jnp.einsum("by,oy->bo", left, right, **hi) / softness_divisor

    similar, back = jax.vjp(agreement, chosen, targets)
    same = frames[:, None] == frames
    positive = jnp.sum(jnp.where(same, similar, 0.0), axis=1)
    top = jnp.max(jnp.where(allowed, similar, -jnp.inf), axis=1)
    parts = jnp.where(allowed, jnp.exp(similar - top[:, None]), 0.0)
    total = jnp.sum(parts, axis=1)
    loss = jnp.sum(top + jnp.log(total) - positive)
    d_similar = weight * (parts / total[:, None] - same.astype(jnp.float32))
    return (loss,) + back(d_similar)


def adamw_update(master, first_moment, second, gradient, step_rate):
    first_new = beta_one * first_moment + (1.0 - beta_one) * gradient
    second_new = beta_two * second + (1.0 - beta_two) * gradient * gradient
    first_hat = first_new / (1.0 - beta_one**STEP)
    second_hat = second_new / (1.0 - beta_two**STEP)
    master_new = master * (1.0 - step_rate * decay_rate) - step_rate * first_hat / (
        jnp.sqrt(second_hat) + adam_eps
    )
    return (master_new, first_new, second_new)


def column_sum(values):
    return jnp.sum(values.astype(jnp.float32), axis=tuple(range(values.ndim - 1)))


def finish(total_masked, square_sum, vector_sum, loss_sum, grad_shard, output, input_grad, params, moment_one, moment_two, vectors, vector_one, vector_two):
    grad_norm = jnp.sqrt(square_sum + jnp.sum(vector_sum * vector_sum))
    factor = jnp.minimum(1.0, clip_level / (grad_norm + 1e-06))
    refreshed_weights, new_one, new_two = adamw_update(params, moment_one, moment_two, grad_shard * factor, rate_matrix)
    new_vectors, new_vector_first, new_vector_second = adamw_update(vectors, vector_one, vector_two, vector_sum * factor, rate_vector)
    return (
        loss_sum / total_masked,
        grad_norm,
        output,
        input_grad,
        refreshed_weights,
        refreshed_weights.astype(bf16),
        new_one,
        new_two,
        new_vectors,
        new_vector_first,
        new_vector_second,
    )


def by_collectives(
    layer_input,
    mask_index,
    distract,
    code_choice,
    params,
    moment_one,
    moment_two,
    vectors,
    vector_one,
    vector_two,
):
    bf16 = jnp.bfloat16
    f32 = jnp.float32
    count_utts = layer_input.shape[0]
    total_masked = count_utts * lax.axis_size(("dp", "fsdp")) * MASKED
    token_rows = count_utts * LEN
    gathered = lax.all_gather(params.astype(bf16), ("dp", "fsdp"), axis=0, tiled=True)
    qkv_weight, out_weight, up_weight, down_weight, proj_weight, codebook, code_weight = unpack(
        gathered
    )
    (
        bias_query,
        bias_value,
        bias_out,
        gain_one,
        shift_one,
        bias_up,
        bias_down,
        gain_two,
        shift_two,
        bias_proj,
        bias_code,
    ) = split_vectors(vectors)
    inputs = layer_input.reshape(token_rows, D)
    projected = jnp.dot(inputs, qkv_weight, preferred_element_type=f32)
    query_heads = (projected[:, :D] + bias_query).astype(bf16).reshape(count_utts, LEN, H, HD)
    key_heads = projected[:, D : 2 * D].astype(bf16).reshape(count_utts, LEN, H, HD)
    value_heads = (projected[:, 2 * D :] + bias_value).astype(bf16).reshape(count_utts, LEN, H, HD)
    scores = (
        jnp.einsum("blhe,bmhe->bhlm", query_heads, key_heads, preferred_element_type=f32) * 0.125
    )
    attn_probs = jax.nn.softmax(scores, axis=-1)
    probs_low = attn_probs.astype(bf16)
    attended = jnp.einsum("bhlm,bmhe->blhe", probs_low, value_heads, preferred_element_type=f32)
    attended = attended.astype(bf16).reshape(token_rows, D)
    residual_one = (
        inputs.astype(f32) + jnp.dot(attended, out_weight, preferred_element_type=f32) + bias_out
    )
    normed, back_one = jax.vjp(layer_norm, residual_one, gain_one, shift_one)
    normed_low = normed.astype(bf16)
    hidden = jnp.dot(normed_low, up_weight, preferred_element_type=f32) + bias_up
    active, gelu_back = jax.vjp(functools.partial(jax.nn.gelu, approximate=False), hidden)
    active_low = active.astype(bf16)
    residual_two = normed + jnp.dot(active_low, down_weight, preferred_element_type=f32) + bias_down
    output, back_two = jax.vjp(layer_norm, residual_two, gain_two, shift_two)
    output_low = output.astype(bf16)
    place = (mask_index[0][:, None] == jnp.arange(LEN, dtype=jnp.int32)).astype(bf16)
    picked = jnp.dot(place, output_low, preferred_element_type=f32).astype(bf16)
    chosen = jnp.dot(picked, proj_weight, preferred_element_type=f32) + bias_proj
    choose = (code_choice[..., None] == jnp.arange(V, dtype=jnp.int32)).astype(bf16)
    code_vectors = jnp.einsum(
        "bmgv,gcv->bmgc", choose, codebook.reshape(G, CD, V), preferred_element_type=f32
    )
    code_vectors = code_vectors.astype(bf16).reshape(count_utts, MASKED, G * CD)
    targets = (
        jnp.einsum("bmc,cf->bmf", code_vectors, code_weight, preferred_element_type=f32) + bias_code
    )
    loss_local, d_chosen, d_targets = contrast_dense(chosen, targets[0], distract[0], 1.0 / total_masked)
    d_targets = d_targets[None]
    d_targets_low = d_targets.astype(bf16)
    quantized_offset_slope = column_sum(d_targets_low)
    d_code_weight = jnp.einsum(
        "bmc,bmf->cf", code_vectors, d_targets_low, preferred_element_type=f32
    )
    d_code_vectors = jnp.einsum(
        "bmf,cf->bmc", d_targets_low, code_weight, preferred_element_type=f32
    )
    d_codebook = jnp.einsum(
        "bmgc,bmgv->gcv",
        d_code_vectors.reshape(count_utts, MASKED, G, CD),
        choose.astype(f32),
        precision=lax.Precision.HIGHEST,
    ).reshape(G * CD, V)
    d_chosen_low = d_chosen.astype(bf16)
    d_bias_proj = column_sum(d_chosen_low)
    d_proj_weight = jnp.einsum("td,tf->df", picked, d_chosen_low, preferred_element_type=f32)
    d_context_low = jnp.einsum("mt,mf->tf", place, d_chosen_low, preferred_element_type=f32).astype(bf16)
    result_sensitivity = jnp.einsum(
        "tf,df->td", d_context_low, proj_weight, preferred_element_type=f32
    )
    d_residual_two, d_gain_two, d_shift_two = back_two(result_sensitivity)
    d_second_low = d_residual_two.astype(bf16)
    d_bias_down = column_sum(d_second_low)
    d_down_weight = jnp.einsum("th,td->hd", active_low, d_second_low, preferred_element_type=f32)
    d_active = jnp.einsum("td,hd->th", d_second_low, down_weight, preferred_element_type=f32)
    (d_hidden,) = gelu_back(d_active)
    d_hidden_low = d_hidden.astype(bf16)
    d_bias_up = column_sum(d_hidden_low)
    d_up_weight = jnp.einsum("td,th->dh", normed_low, d_hidden_low, preferred_element_type=f32)
    d_normed = d_residual_two + jnp.einsum(
        "th,dh->td", d_hidden_low, up_weight, preferred_element_type=f32
    )
    d_residual_one, d_gain_one, d_shift_one = back_one(d_normed)
    d_branch_low = d_residual_one.astype(bf16)
    d_bias_out = column_sum(d_branch_low)
    d_out_weight = jnp.einsum("td,te->de", attended, d_branch_low, preferred_element_type=f32)
    d_attended = jnp.einsum("te,de->td", d_branch_low, out_weight, preferred_element_type=f32)
    d_attended = d_attended.astype(bf16).reshape(count_utts, LEN, H, HD)
    d_value = jnp.einsum("bhlm,blhe->bmhe", probs_low, d_attended, preferred_element_type=f32)
    d_probs = jnp.einsum("blhe,bmhe->bhlm", d_attended, value_heads, preferred_element_type=f32)
    d_scores = (
        attn_probs * (d_probs - jnp.sum(attn_probs * d_probs, axis=-1, keepdims=True))
    ).astype(bf16)
    d_query = jnp.einsum("bhlm,bmhe->blhe", d_scores, key_heads, preferred_element_type=f32) * 0.125
    d_key = jnp.einsum("bhlm,blhe->bmhe", d_scores, query_heads, preferred_element_type=f32) * 0.125
    d_projected = jnp.concatenate(
        [
            d_query.reshape(token_rows, D),
            d_key.reshape(token_rows, D),
            d_value.reshape(token_rows, D),
        ],
        axis=1,
    ).astype(bf16)
    d_sums = column_sum(d_projected)
    d_qkv_weight = jnp.einsum("td,te->de", inputs, d_projected, preferred_element_type=f32)
    input_grad = d_residual_one + jnp.einsum(
        "te,de->td", d_projected, qkv_weight, preferred_element_type=f32
    )
    flat_grad = jnp.concatenate(
        [
            matrix_grad.reshape(-1)
            for matrix_grad in (
                d_qkv_weight,
                d_out_weight,
                d_up_weight,
                d_down_weight,
                d_proj_weight,
                d_codebook,
                d_code_weight,
            )
        ]
    )
    vector_gradient = jnp.concatenate(
        [
            d_sums[:D],
            d_sums[2 * D :],
            d_bias_out,
            d_gain_one,
            d_shift_one,
            d_bias_up,
            d_bias_down,
            d_gain_two,
            d_shift_two,
            d_bias_proj,
            quantized_offset_slope,
        ]
    )
    vector_sum, loss_sum = lax.psum((vector_gradient, loss_local), ("dp", "fsdp"))
    grad_shard = lax.psum_scatter(flat_grad, ("dp", "fsdp"), scatter_dimension=0, tiled=True)
    square_sum = lax.psum(jnp.sum(grad_shard * grad_shard), ("dp", "fsdp"))
    return finish(
        total_masked, square_sum, vector_sum, loss_sum, grad_shard, output_low.reshape(count_utts, LEN, D),
        input_grad.reshape(count_utts, LEN, D), params, moment_one, moment_two, vectors, vector_one, vector_two,
    )


def by_kernels(layer_input, mask_index, distract, code_choice, params, moment_one, moment_two, vectors, vector_one, vector_two):
    total_masked = layer_input.shape[0] * lax.axis_size(("dp", "fsdp")) * MASKED
    kept, output = forward(PIECES_OUT, SENDS_OUT, 1.0 / total_masked, params, layer_input, mask_index, distract, code_choice, vectors)
    grads, sums, squares, input_grad = backward(PIECES_BACK, SENDS_BACK, vectors, kept, lax.axis_size("fsdp"), params.shape[0] // 128)
    new, low, first, second, new_v, first_v, second_v, loss, norm = update(
        total_masked, grads, params, moment_one, moment_two, sums, vectors, vector_one, vector_two, squares
    )
    return loss, norm, output, input_grad, new, low, first, second, new_v, first_v, second_v


def solution(mesh):
    in_specs = (
        P(("dp", "fsdp"), None, None),
        P(("dp", "fsdp"), None),
        P(("dp", "fsdp"), None, None),
        P(("dp", "fsdp"), None, None),
        P(("dp", "fsdp")),
        P(("dp", "fsdp")),
        P(("dp", "fsdp")),
        P(),
        P(),
        P(),
    )
    out_specs = (
        P(),
        P(),
        P(("dp", "fsdp"), None, None),
        P(("dp", "fsdp"), None, None),
        P(("dp", "fsdp")),
        P(("dp", "fsdp")),
        P(("dp", "fsdp")),
        P(("dp", "fsdp")),
        P(),
        P(),
        P(),
    )
    fits = mesh.shape["dp"] == PLANES and mesh.shape["fsdp"] == 8
    return jax.shard_map(
        by_kernels if fits else by_collectives, mesh=mesh, in_specs=in_specs, out_specs=out_specs, check_vma=False
    )
```

```python
import functools

import jax
import jax.numpy as jnp
from jax import lax
from jax.experimental import pallas as pl
from jax.experimental.pallas import tpu as pltpu
from jax.sharding import PartitionSpec as P
D = 768; H = 12; HD = 64; FF = 3072; FINAL = 256; G = 2; V = 320; CD = 128; LEN = 472; MASKED = 232
NROW = 9664; GROW = NROW + 256
T = 512
LT = 480
NB = 240
TILE = 768
STEP_T = 512
bf16 = jnp.bfloat16
f32 = jnp.float32
NT = (((1,), (1,)), ((), ()))
BQ, BV, BO, G1, S1, BUP, BDOWN, G2, S2, BPROJ, BCODE = [768 * i for i in range(6)] + [3840 + 3072 + 768 * i for i in range(3)] + [9216, 9472]

def mm(a, b):
    return jnp.dot(a, b, preferred_element_type=f32)

def mm_nt(a, b, precision=None):
    return lax.dot_general(a, b, NT, preferred_element_type=f32, precision=precision)

def hi(a, b):
    return jnp.dot(a, b, preferred_element_type=f32, precision=lax.Precision.HIGHEST)

def split_rows(g, base, parts, nice, first, tmp):
    def body(b, _):
        src = pl.multiple_of(base + b * 64 * parts, 64)
        for j in range(6):
            tmp[j, 0:64 * parts, :] = g[pl.ds(src, 64 * parts), 128 * j:128 * j + 128].astype(f32)
        for t in range(parts):
            at = pl.multiple_of((first + t) * D + b * 64, 64)
            for j in range(6):
                nice[pl.ds(at, 64), 128 * j:128 * j + 128] = tmp[j, pl.ds(t, 64, stride=parts), :].astype(bf16)
        return 0
    lax.fori_loop(0, D // 64, body, 0)

def norm_rows(r, gain, shift, low, wide, hat, rstd):
    def body(b, _):
        at = pl.multiple_of(b * NB, 16)
        v = r[pl.ds(at, NB), :]
        m = jnp.mean(v, axis=-1, keepdims=True)
        c = v - m
        var = jnp.mean(c * c, axis=-1, keepdims=True)
        inv = lax.rsqrt(var + eps_norm)
        xh = c * inv
        o = xh * gain + shift
        hat[pl.ds(at, NB), :] = xh
        rstd[pl.ds(at, NB), :] = jnp.broadcast_to(inv, (NB, 128))
        if wide is not None:
            wide[pl.ds(at, NB), :] = o
        low[pl.ds(at, NB), :] = o.astype(bf16)
        return 0
    lax.fori_loop(0, LT // NB, body, 0)

def transpose_to(src, dst, rows, cols):
    step = min(STEP_T, cols // 3)
    def body(n, _):
        at = pl.multiple_of(n * step, step)
        dst[pl.ds(at, step), :] = src[:, pl.ds(at, step)].T
        return 0
    lax.fori_loop(0, cols // step, body, 0)

def prepare(x_ref, xp, xT, mask_ref, distract_ref, choice_ref, vec_ref, vec, place, placeT, allowed, choose):
    for i in range(vec_ref.shape[0]):
        vec[0:1, 128 * i:128 * i + 128] = vec_ref[i:i + 1, :]
    xp[...] = jnp.zeros((T, D), bf16)
    xp[0:LEN, :] = x_ref[0]
    transpose_to(xp, xT, T, D)
    zero = jnp.zeros((1, 256 - MASKED), jnp.int32) - 1
    def wide(row):
        return jnp.concatenate([row, zero], axis=1)
    hot = jnp.where(lax.broadcasted_iota(jnp.int32, (T, 256), 0) == wide(mask_ref[...]), 1.0, 0.0)
    placeT[...] = hot.astype(bf16)
    place[...] = hot.T.astype(bf16)
    row = lax.broadcasted_iota(jnp.int32, (256, 256), 0)
    col = lax.broadcasted_iota(jnp.int32, (256, 256), 1)
    allowed[...] = jnp.where((row == col) & (col < MASKED), 1.0, 0.0)
    rows = [wide(distract_ref[i]) for i in range(distract_ref.shape[0])]
    def body(b, _):
        at = pl.multiple_of(8 * b, 8)
        acc = allowed[pl.ds(at, 8), :]
        n = lax.broadcasted_iota(jnp.int32, (8, 256), 0) + at
        for r in rows:
            acc = jnp.where(n == r, 1.0, acc)
        allowed[pl.ds(at, 8), :] = acc
        return 0
    lax.fori_loop(0, MASKED // 8, body, 0)
    allowed[...] = allowed[...].T
    for g in range(2):
        v = jnp.where(lax.broadcasted_iota(jnp.int32, (384, 256), 0) == wide(choice_ref[0, g:g + 1, :]), 1.0, 0.0)
        choose[g] = v.T

def project(xp, nice, vec, q, kk, kT, vv, vT):
    for t, (dst, bias) in enumerate(((q, BQ), (kk, None), (vv, BV))):
        for n in range(3):
            acc = mm(xp[...], nice[t * D:(t + 1) * D, 256 * n:256 * n + 256])
            if bias is not None:
                acc = acc + vec[0:1, bias + 256 * n:bias + 256 * n + 256]
            dst[:, 256 * n:256 * n + 256] = acc.astype(bf16)
    transpose_to(kk, kT, T, D)
    transpose_to(vv, vT, T, D)

def attend(p, q, kk, vT, pT, attT):
    at = pl.multiple_of(128 * p, 128)
    qp = q[:, pl.ds(at, 128)]
    kp = kk[0:LT, pl.ds(at, 128)]
    lane = lax.broadcasted_iota(jnp.int32, (LT, 128), 1)
    for h in range(2):
        kh = jnp.where((lane < 64) == (h == 0), kp, jnp.zeros_like(kp))
        s = mm_nt(kh, qp)[0:LEN] * 0.125
        e = jnp.exp(s - jnp.max(s, axis=0, keepdims=True))
        pr = e * (1.0 / jnp.sum(e, axis=0, keepdims=True))
        pr = jnp.concatenate([pr, jnp.zeros((T - LEN, T), f32)], axis=0).astype(bf16)
        pT[pl.ds(pl.multiple_of((2 * (p % 2) + h) * T, T), T), :] = pr
        rows = pl.ds(pl.multiple_of(128 * p + 64 * h, 64), 64)
        attT[rows, :] = mm(vT[rows, :], pr).astype(bf16)

def out_project(attT, att, xp, wo, vec, res):
    for n in range(6):
        att[:, 128 * n:128 * n + 128] = attT[128 * n:128 * n + 128, :].T
    for n in range(3):
        cols = slice(256 * n, 256 * n + 256)
        acc = mm(att[0:LT, :], wo[:, cols])
        res[:, cols] = xp[0:LT, cols].astype(f32) + acc + vec[0:1, BO + 256 * n:BO + 256 * n + 256]

def up(n, norm_low, nice, vec, act, gp):
    root = 0.7071067811865476
    scale = 0.3989422804014327
    c = n * TILE // D
    at = pl.multiple_of(n * TILE, TILE)
    w = nice[pl.ds(pl.multiple_of(c * D, D), D), pl.ds(pl.multiple_of(at - c * D, TILE), TILE)]
    h = mm(norm_low[0:LT, :], w) + vec[0:1, pl.ds(pl.multiple_of(BUP + at, 256), TILE)]
    cdf = 0.5 * (1.0 + lax.erf(h * root))
    act[0:LT, pl.ds(at, TILE)] = (h * cdf).astype(bf16)
    gp[0:LT, pl.ds(at, TILE)] = (cdf + h * (scale * jnp.exp(-0.5 * h * h))).astype(bf16)

def down(act, g, vec, res, wide):
    for n in range(3):
        cols = slice(256 * n, 256 * n + 256)
        acc = mm(act[0:LT, :], g[6144:9216, cols])
        res[:, cols] = wide[:, cols] + acc + vec[0:1, BDOWN + 256 * n:BDOWN + 256 * n + 256]

def small_weights(g, fb, p32, c32, wproj, code, wcode):
    for t in range(3):
        for j in range(2):
            p32[j, pl.ds(t, 256, stride=3), :] = g[9216:9472, 256 * t + 128 * j:256 * t + 128 * j + 128].astype(f32)
    for j in range(2):
        wproj[:, 128 * j:128 * j + 128] = p32[j].astype(bf16)
    for j in range(6):
        fb[pl.ds(j, 192, stride=6), :] = g[9472:9664, 128 * j:128 * j + 128].astype(f32)
    a = [fb[pl.ds(j, 128, stride=5), :] for j in range(5)]
    lo = lax.broadcasted_iota(jnp.int32, (128, 128), 1) < 64
    r2, r3, r4 = [pltpu.roll(v, 64, 1) for v in a[2:]]
    zero = jnp.zeros((128, 128), f32)
    even = [a[0], a[1], jnp.where(lo, a[2], zero)]
    odd = [jnp.where(lo, r2, r3), jnp.where(lo, r3, r4), jnp.where(lo, r4, zero)]
    for j in range(3):
        c32[j, pl.ds(0, 128, stride=2), :] = even[j]
        c32[j, pl.ds(1, 128, stride=2), :] = odd[j]
        code[:, 128 * j:128 * j + 128] = c32[j].astype(bf16)
    for j in range(2):
        wcode[:, 128 * j:128 * j + 128] = fb[pl.ds(640 + j, 256, stride=2), :].astype(bf16)

def contrast(weight, out_low, vec, place, placeT, allowed, choose, wproj, code, wcode, fb, p32, c32, tail, dctx, small):
    picked = mm(place[...], out_low[...]).astype(bf16)
    chosen = mm(picked, wproj[...]) + vec[0:1, BPROJ:BPROJ + 256]
    cv = jnp.concatenate([mm_nt(choose[g].astype(bf16), code[128 * g:128 * g + 128, :]) for g in range(2)], axis=1).astype(bf16)
    targets = mm(cv, wcode[...]) + vec[0:1, BCODE:BCODE + 256]
    n_l = lax.rsqrt(jnp.sum(chosen * chosen, axis=1, keepdims=True) + eps_cos)
    n_r = lax.rsqrt(jnp.sum(targets * targets, axis=1, keepdims=True) + eps_cos)
    left = chosen * n_l
    right = targets * n_r
    sim = mm_nt(left, right, lax.Precision.HIGHEST) / 0.1
    ok = allowed[...] > 0.5
    row = lax.broadcasted_iota(jnp.int32, (256, 256), 0)
    col = lax.broadcasted_iota(jnp.int32, (256, 256), 1)
    eye = jnp.where((row == col) & (row < MASKED), 1.0, 0.0)
    pos = jnp.sum(eye * sim, axis=1, keepdims=True)
    top = jnp.max(jnp.where(ok, sim, -1e30), axis=1, keepdims=True)
    parts = jnp.where(ok, jnp.exp(jnp.minimum(sim - top, 0.0)), 0.0)
    real = lax.broadcasted_iota(jnp.int32, (256, 1), 0) < MASKED
    total = jnp.where(real, jnp.sum(parts, axis=1, keepdims=True), 1.0)
    loss = jnp.sum(jnp.where(real, top + jnp.log(total) - pos, 0.0))
    dsim = (weight / 0.1) * (parts / total - eye)
    dl = hi(dsim, right)
    dr = hi(dsim.T, left)
    d_chosen = (n_l * dl - chosen * (n_l * n_l * n_l) * jnp.sum(chosen * dl, axis=1, keepdims=True)).astype(bf16)
    d_target = (n_r * dr - targets * (n_r * n_r * n_r) * jnp.sum(targets * dr, axis=1, keepdims=True)).astype(bf16)
    small[0:1, :] = jnp.sum(d_chosen.astype(f32), axis=0, keepdims=True)
    small[1:2, :] = jnp.sum(d_target.astype(f32), axis=0, keepdims=True)
    small[2:3, :] = jnp.broadcast_to(loss, (1, 256))
    dctx[...] = mm(placeT[...], d_chosen).astype(bf16)
    dproj = mm(picked.T, d_chosen)
    for j in range(2):
        p32[j] = dproj[:, 128 * j:128 * j + 128]
    for t in range(3):
        for j in range(2):
            tail[0:256, 256 * t + 128 * j:256 * t + 128 * j + 128] = p32[j, pl.ds(t, 256, stride=3), :].astype(bf16)
    dwcode = mm(cv.T, d_target)
    dcv = mm_nt(d_target, wcode[...])
    for g in range(2):
        dc = hi(dcv[:, 128 * g:128 * g + 128].T, choose[g])
        for j in range(3):
            c32[j, 128 * g:128 * g + 128, :] = dc[:, 128 * j:128 * j + 128]
    e = [c32[j, pl.ds(0, 128, stride=2), :] for j in range(3)]
    o = [pltpu.roll(c32[j, pl.ds(1, 128, stride=2), :], 64, 1) for j in range(3)]
    lo = lax.broadcasted_iota(jnp.int32, (128, 128), 1) < 64
    for j, v in enumerate((e[0], e[1], jnp.where(lo, e[2], o[0]), jnp.where(lo, o[0], o[1]), jnp.where(lo, o[1], o[2]))):
        fb[pl.ds(j, 128, stride=5), :] = v
    for j in range(2):
        fb[pl.ds(640 + j, 256, stride=2), :] = dwcode[:, 128 * j:128 * j + 128]
    for j in range(6):
        tail[256:448, 128 * j:128 * j + 128] = fb[pl.ds(j, 192, stride=6), :].astype(bf16)
STEP = 10


eps_norm = 1e-05
eps_cos = 1e-06
softness_divisor = 0.1
beta_one = 0.9
beta_two = 0.98
adam_eps = 1e-08
decay_rate = 0.01
rate_matrix = 0.03
rate_vector = 0.2
clip_level = 0.001


def sum8(v):
    r, n = v.shape
    return jnp.sum(v.reshape(r // 8, 8, n), axis=0)

def norm_back_first(dctx, wproj, gain, hat, rstd, low, acc):
    acc[...] = jnp.zeros((24, D), f32)
    def body(b, _):
        at = pl.multiple_of(b * 48, 16)
        dy = mm_nt(dctx[pl.ds(at, 48), :], wproj[...])
        norm_back_rows(dy, at, gain, hat, hat, rstd, low, acc)
        return 0
    lax.fori_loop(0, LT // 48, body, 0)

def norm_back_rows(dy, at, gain, hat, dst, rstd, low, acc):
    xh = hat[pl.ds(at, NB), :]
    inv = rstd[pl.ds(at, NB), 0:1]
    a = dy * gain
    m1 = jnp.mean(a, axis=-1, keepdims=True)
    m2 = jnp.mean(a * xh, axis=-1, keepdims=True)
    dr = inv * (a - m1 - xh * m2)
    lo = dr.astype(bf16)
    dst[pl.ds(at, NB), :] = dr
    low[pl.ds(at, NB), :] = lo
    acc[0:8, :] += sum8(dy * xh)
    acc[8:16, :] += sum8(dy)
    acc[16:24, :] += sum8(lo.astype(f32))

def norm_back(dy, gain, hat, rstd, low, acc):
    acc[...] = jnp.zeros((24, D), f32)
    def body(b, _):
        at = pl.multiple_of(b * NB, 16)
        norm_back_rows(dy[pl.ds(at, NB), :], at, gain, hat, hat, rstd, low, acc)
        return 0
    lax.fori_loop(0, LT // NB, body, 0)

def put_vec(vg, acc, offsets):
    for i, o in enumerate(offsets):
        vg[0:1, o:o + D] = jnp.sum(acc[8 * i:8 * i + 8, :], axis=0, keepdims=True)

def down_back(n, low2, gg, actT, gp, vg):
    at = pl.multiple_of(n * TILE, TILE)
    rows = pl.ds(pl.multiple_of(6144 + n * TILE, 256), TILE)
    d = mm_nt(low2[0:LT, :], gg[rows, :]) * gp[0:LT, pl.ds(at, TILE)].astype(f32)
    d = d.astype(bf16)
    gp[0:LT, pl.ds(at, TILE)] = d
    vg[0:1, pl.ds(pl.multiple_of(BUP + at, 128), TILE)] = jnp.sum(d.astype(f32), axis=0, keepdims=True)
    gg[rows, :] = mm(actT[pl.ds(at, TILE), :], low2[...]).astype(bf16)

def up_back_x(n, dh, gg, dr):
    cols = pl.ds(pl.multiple_of(n * 256, 256), 256)
    v = dr[:, cols]
    for c in range(4):
        w = gg[pl.ds(pl.multiple_of(3072 + c * D + n * 256, 256), 256), :]
        v = v + mm_nt(dh[0:LT, c * D:(c + 1) * D], w)
    dr[:, cols] = v

WEAVE = 384

def weave(lhsT, rhs, parts, n, base, gg, tmp, stacked):
    def body(m, _):
        cols = pl.ds(pl.multiple_of(m * 256, 256), 256)
        for t in range(parts):
            r = rhs[t, :, cols] if stacked else rhs[:, pl.ds(pl.multiple_of(t * D + m * 256, 256), 256)]
            acc = mm(lhsT[pl.ds(pl.multiple_of(n * WEAVE, WEAVE), WEAVE), :], r)
            for j in range(2):
                tmp[j, pl.ds(t, WEAVE, stride=parts), :] = acc[:, 128 * j:128 * j + 128]
        for j in range(2):
            gg[pl.ds(pl.multiple_of(base + n * WEAVE * parts, 128), WEAVE * parts), pl.ds(pl.multiple_of(m * 256 + 128 * j, 128), 128)] = tmp[j, 0:WEAVE * parts, :].astype(bf16)
        return 0
    lax.fori_loop(0, 3, body, 0)

def out_back(low1, gg, attT, da):
    for n in range(3):
        cols = slice(256 * n, 256 * n + 256)
        da[0:LT, cols] = mm_nt(low1[0:LT, :], gg[2304 + 256 * n:2304 + 256 * n + 256, :]).astype(bf16)
    for n in range(3):
        gg[2304 + 256 * n:2304 + 256 * n + 256, :] = mm(attT[256 * n:256 * n + 256, :], low1[...]).astype(bf16)

def attend_back(p, da, q, kT, vv, ring, dp, dqT):
    at = pl.multiple_of(128 * p, 128)
    lane = lax.broadcasted_iota(jnp.int32, (T, 128), 1)
    dap = da[:, pl.ds(at, 128)]
    qp = q[:, pl.ds(at, 128)]
    vp = vv[0:LT, pl.ds(at, 128)]
    dk = dv = None
    for h in range(2):
        half = (lane < 64) == (h == 0)
        dah = jnp.where(half, dap, jnp.zeros_like(dap))
        qh = jnp.where(half, qp, jnp.zeros_like(qp))
        pr = ring[pl.ds(pl.multiple_of(((2 * p + h) % 6) * T, T), LT), :]
        dpT = mm_nt(vp, dah)
        prf = pr.astype(f32)
        w = prf * dpT
        ds = (w - prf * jnp.sum(w, axis=0, keepdims=True)).astype(bf16)
        a = mm(pr, dah)
        b = mm(ds, qh)
        dv = a if dv is None else dv + a
        dk = b if dk is None else dk + b
        rows = pl.ds(pl.multiple_of(128 * p + 64 * h, 64), 64)
        dqT[rows, :] = (mm(kT[rows, 0:LT], ds) * 0.125).astype(bf16)
    dp[1, 0:LT, pl.ds(at, 128)] = (dk * 0.125).astype(bf16)
    dp[2, 0:LT, pl.ds(at, 128)] = dv.astype(bf16)
    dp[0, :, pl.ds(at, 128)] = dqT[pl.ds(at, 128), :].T

def input_back(n, dp, wq, dr):
    cols = slice(256 * n, 256 * n + 256)
    v = dr[:, cols]
    for t in range(3):
        v = v + mm_nt(dp[t, 0:LT, :], wq[t * D + 256 * n:t * D + 256 * n + 256, :])
    dr[:, cols] = v
MESH = pl.DeviceIdType.MESH
UP, DOWN, U, V_AXIS, CORE = range(5)
PLANES = 4
MAIN = 288
EXTRA = 16
HALF = MAIN + EXTRA
RAW = 96
PLANE = 2416
UNIT = 608

class Place:
    def __init__(self):
        self.z = lax.axis_index("dp")
        self.f = f = lax.axis_index("fsdp")
        self.c = c = f % 2
        self.k = k = f // 2
        x = k % 2
        y = k // 2
        self.fc = f + 1 - 2 * c
        self.fx = f + 2 - 4 * x
        self.fy = f + 4 - 8 * y
        self.uf = self.fx * (1 - c) + self.fy * c
        self.vf = self.fy * (1 - c) + self.fx * c
        self.roles = (k, self.uf // 2, self.vf // 2, 3 - k)

    def greet(self):
        z = self.z
        bar = pltpu.get_barrier_semaphore()
        for t in (self.fc, self.fx, self.fy):
            pl.semaphore_signal(bar, inc=1, device_id=(z, t), device_id_type=MESH)
        @pl.when(z > 0)
        def _(): pl.semaphore_signal(bar, inc=1, device_id=(z - 1, self.f), device_id_type=MESH)
        @pl.when(z < PLANES - 1)
        def _(): pl.semaphore_signal(bar, inc=1, device_id=(z + 1, self.f), device_id_type=MESH)
        pl.semaphore_wait(bar, 3 + (z + PLANES - 1) // PLANES + (2 * PLANES - 2 - z) // PLANES)

    def greet_all(self, count):
        bar = pltpu.get_barrier_semaphore()
        for j in range(1, count):
            pl.semaphore_signal(bar, inc=1, device_id=(self.z, lax.rem(self.f + j, count)), device_id_type=MESH)
        for j in range(1, PLANES):
            pl.semaphore_signal(bar, inc=1, device_id=(lax.rem(self.z + j, PLANES), self.f), device_id_type=MESH)
        pl.semaphore_wait(bar, count + PLANES - 2)

    def span_of(self, p, kk, c, first):
        m = PLANE * p + UNIT * kk
        return (pl.multiple_of(m + HALF * c + first, 16),
                pl.multiple_of((m + MAIN) * (1 - c) + (NROW + EXTRA * (4 * p + kk)) * c, 16))

    def span(self, p, r, c, first):
        return self.span_of(p, self.roles[r], c, first)

def remote(src, dst, ssem, rsem, dev):
    return pltpu.make_async_remote_copy(src_ref=src, dst_ref=dst, send_sem=ssem, recv_sem=rsem, device_id=dev, device_id_type=MESH)

def shared_blocks(g, p):
    row = lax.broadcasted_iota(jnp.int32, (16, D), 0)
    e = [g[NROW + 16 * (4 * p + q):NROW + 16 * (4 * p + q) + 16, :].astype(f32) for q in range(4)]
    for q, bound in enumerate((12, 8, 4)):
        at = PLANE * p + UNIT * q + 592
        g[at:at + 16, :] = jnp.where(row < bound, e[q], e[q + 1]).astype(bf16)

def extra_rows(g, p, q):
    row = lax.broadcasted_iota(jnp.int32, (16, D), 0)
    b = [g[PLANE * p + UNIT * i + 592:PLANE * p + UNIT * i + 608, :].astype(f32) for i in range(max(q - 1, 0), min(q, 2) + 1)]
    v = b[0] if len(b) == 1 else jnp.where(row < 12 - 4 * q, b[1], b[0])
    g[NROW + 16 * (4 * p + q):NROW + 16 * (4 * p + q) + 16, :] = v.astype(bf16)

def wait_sent(g, rows, ssem, rsem, dev):
    if rows:
        ref = g.at[pl.ds(0, rows)]
        remote(ref, ref, ssem, rsem, dev).wait_send()

class Gather:
    def __init__(self, at, g, pieces, R, O, S):
        self.at, self.g, self.pieces, self.R, self.O, self.S = at, g, pieces, R, O, S
        self.sent = {z: [0, 0] for z in range(PLANES)}
        self.seen = set()

    def copies(self, i, p, r, dev, kind):
        _, first, rows, extra = self.pieces[p][i]
        a, e = self.at.span(p, r, self.at.c, first)
        unit = 4 * p + self.at.roles[r]
        out = []
        for s, n in [(a, rows)] + [(e, EXTRA)] * extra:
            ref = self.g.at[pl.ds(s, n)]
            out.append(remote(ref, ref, self.S.at[int(kind == CORE)], self.O.at[p] if kind == CORE else self.R.at[unit, i], dev))
        return out

    def op(self, zs, kind, i, p, r):
        at = self.at
        _, _, rows, extra = self.pieces[p][i]
        rows += EXTRA * extra
        if not (p == zs and r == 0) and (zs, i, p, r) not in self.seen:
            self.seen.add((zs, i, p, r))
            ref = self.g.at[pl.ds(0, rows)]
            remote(ref, ref, self.S.at[0], self.R.at[4 * p + at.roles[r], i], (zs, at.fc)).wait_recv()
        dev = ((zs + 1, at.f), (zs - 1, at.f), (zs, at.uf), (zs, at.vf), (zs, at.fc))[kind]
        for q in self.copies(i, p, r, dev, kind): q.start()
        self.sent[zs][int(kind == CORE)] += rows

    def other_core(self, zs, p):
        ref = self.g.at[pl.ds(0, HALF * (3 if p == zs else 4))]
        remote(ref, ref, self.S.at[1], self.O.at[p], (zs, self.at.fc)).wait_recv()

    def drain(self):
        for zs in range(PLANES):
            @pl.when(self.at.z == zs)
            def _():
                for i in range(2): wait_sent(self.g, self.sent[zs][i], self.S.at[i], self.O.at[0], (zs, self.at.fc))

def own_rows(at, g, p_ref, raw, sem):
    n = p_ref.shape[0]
    gap = -n % 8
    base = pl.multiple_of(RAW + (n + gap) * at.c, 8)
    mine = pltpu.make_async_copy(p_ref.at[pl.ds(0, n)], raw.at[pl.ds(base, n)], sem.at[2])
    mine.start()
    both = remote(p_ref.at[pl.ds(0, n)], raw.at[pl.ds(base, n)], sem.at[0], sem.at[1], (at.z, at.fc))
    both.start()
    mine.wait()
    both.wait()
    k = at.k
    own = pl.multiple_of(PLANE * at.z + UNIT * k, 16)
    extra = pl.multiple_of(NROW + EXTRA * (4 * at.z + k), 16)
    row = lax.broadcasted_iota(jnp.int32, (16, 128), 0)
    first_core = lax.broadcasted_iota(jnp.int32, (592, 128), 0) + 4 * k < n // 6
    for j in range(6):
        cols = slice(128 * j, 128 * j + 128)
        v = [raw[pl.ds(RAW + gap * i + 24 * k + j, 592, stride=6), :] for i in range(2)]
        g[pl.ds(own, 592), cols] = jnp.where(first_core, v[0], v[1]).astype(bf16)
        last = raw[pl.ds(RAW + gap + (592 + 4 * k) * 6 + j, 16, stride=6), :]
        first = raw[pl.ds(RAW - 96 + 24 * k + j, 16, stride=6), :]
        g[pl.ds(extra, 16), cols] = jnp.where(row < 12 - 4 * k, last, first).astype(bf16)

K1_OUT = ("w", "wproj", "tail", "dctx", "small", "hat1", "r1", "hat2", "r2", "gp", "actT", "normT", "attT", "q", "kT", "vv", "xT", "pT")
K1_SHAPE = {"w": ((NROW, D), bf16), "wproj": ((D, 256), bf16), "tail": ((448, D), bf16), "dctx": ((T, 256), bf16), "small": ((8, 256), f32),
            "hat1": ((LT, D), f32), "r1": ((LT, 128), f32), "hat2": ((LT, D), f32), "r2": ((LT, 128), f32), "gp": ((T, FF), bf16), "actT": ((FF, T), bf16),
            "normT": ((D, T), bf16), "attT": ((D, T), bf16), "q": ((T, D), bf16), "kT": ((D, T), bf16), "vv": ((T, D), bf16), "xT": ((D, T), bf16),
            "pT": ((H * T, T), bf16)}

def forward_kernel(pieces, events, weight, p_ref, x, mask, dis, cho, vec_ref, *rest):
    n_out = len(K1_OUT)
    hbm = dict(zip(K1_OUT, rest[:n_out]))
    (out, vec, g, raw, nice, tmp, wproj, tail, dctx, small, hat1, r1, hat2, r2, gp, actT, normT, attT, q, kT, vv, xT, pT,
     xp, kk, vT, act, res, wide, low1, low2, place, placeT, allowed, choose, fb, p32, c32, code, wcode,
     sem_raw, R, O, S, OS, PS) = rest[n_out:]
    here = dict(wproj=wproj, tail=tail, dctx=dctx, small=small, hat1=hat1, r1=r1, hat2=hat2, r2=r2, gp=gp, actT=actT, normT=normT, attT=attT, q=q, kT=kT, vv=vv, xT=xT, pT=pT)
    outs = []
    count = iter(range(32))
    def put(src, dst):
        cp = pltpu.make_async_copy(src, dst, OS.at[next(count)])
        cp.start()
        outs.append(cp)
    def save(*names):
        for n in names: put(here[n], hbm[n])
    at = Place()
    ga = Gather(at, g, pieces, R, O, S)
    at.greet()
    own_rows(at, g, p_ref, raw, sem_raw)
    def slot(i, cond=None):
        for zs in range(PLANES):
            if events[zs][i]:
                @pl.when((at.z == zs) if cond is None else ((at.z == zs) & cond))
                def _():
                    for e in events[zs][i]: ga.op(zs, *e)
    def plane(p):
        for zs in range(PLANES):
            @pl.when(at.z == zs)
            def _(): ga.other_core(zs, p)
        shared_blocks(g, p)
    slot(0)
    prepare(x, xp, xT, mask, dis, cho, vec_ref, vec, place, placeT, allowed, choose)
    act[LT:T, :] = jnp.zeros((T - LT, FF), bf16)
    gp[LT:T, :] = jnp.zeros((T - LT, FF), bf16)
    low1[...] = jnp.zeros((T, D), bf16)
    low2[...] = jnp.zeros((T, D), bf16)
    small[...] = jnp.zeros((8, 256), f32)
    save("xT")
    slot(1)
    plane(0)
    split_rows(g, 0, 3, nice, 0, tmp)
    slot(2)
    project(xp, nice, vec, q, kk, kT, vv, vT)
    save("q", "kT", "vv")
    put(nice.at[pl.ds(0, 2304)], hbm["w"].at[pl.ds(0, 2304)])
    nice_out = outs.pop()
    slot(3)
    slot(4)
    def pair_out(p):
        b = p % 2
        return pltpu.make_async_copy(pT.at[pl.ds(pl.multiple_of(2 * T * b, T), 2 * T)], hbm["pT"].at[pl.ds(pl.multiple_of(2 * T * p, T), 2 * T)], PS.at[b])
    def pairs(b, _):
        p = 2 * b
        @pl.when(b > 0)
        def _():
            pair_out(p - 2).wait()
            pair_out(p - 1).wait()
        attend(p, q, kk, vT, pT, attT)
        attend(p + 1, q, kk, vT, pT, attT)
        pair_out(p).start()
        pair_out(p + 1).start()
        for i in range(3): slot(5 + i, b == i)
        return 0
    lax.fori_loop(0, H // 4, pairs, 0)
    pair_out(H // 2 - 2).wait()
    pair_out(H // 2 - 1).wait()
    save("attT")
    plane(1)
    out_project(attT, kk, xp, g.at[2304:3072], vec, res)
    put(g.at[pl.ds(2304, 768)], hbm["w"].at[pl.ds(2304, 768)])
    norm_rows(res, vec[0:1, G1:G1 + D], vec[0:1, S1:S1 + D], low1, wide, hat1, r1)
    save("hat1", "r1")
    transpose_to(low1, normT, T, D)
    save("normT")
    slot(8)
    plane(2)
    nice_out.wait()
    split_rows(g, 3072, 4, nice, 0, tmp)
    put(nice, hbm["w"].at[pl.ds(3072, 3072)])
    slot(9)
    def tile(n, _):
        up(n, low1, nice, vec, act, gp)
        for i in range(3): slot(10 + i, n == i)
        return 0
    lax.fori_loop(0, FF // TILE, tile, 0)
    slot(13)
    save("gp")
    transpose_to(act, actT, T, FF)
    save("actT")
    slot(14)
    plane(3)
    put(g.at[pl.ds(6144, 3072)], hbm["w"].at[pl.ds(6144, 3072)])
    down(act, g, vec, res, wide)
    norm_rows(res, vec[0:1, G2:G2 + D], vec[0:1, S2:S2 + D], low2, None, hat2, r2)
    save("hat2", "r2")
    out[0] = low2[0:LEN, :]
    small_weights(g, fb, p32, c32, wproj, code, wcode)
    save("wproj")
    slot(15)
    contrast(weight, low2, vec, place, placeT, allowed, choose, wproj, code, wcode, fb, p32, c32, tail, dctx, small)
    save("tail", "dctx", "small")
    slot(16)
    ga.drain()
    for cp in outs: cp.wait()

def forward(pieces, events, weight, params, x, mask, dis, cho, vec):
    V_ = pl.BlockSpec(memory_space=pltpu.VMEM)
    A_ = pl.BlockSpec(memory_space=pl.ANY)
    VM = pltpu.VMEM
    DMA = pltpu.SemaphoreType.DMA
    sds = jax.ShapeDtypeStruct
    n = params.shape[0] // 128
    most = max(len(ps) for ps in pieces)
    here = [VM(*K1_SHAPE[k]) for k in K1_OUT[1:-1]] + [VM((4 * T, T), bf16)]
    outs = pl.pallas_call(functools.partial(forward_kernel, pieces, events, weight),
        out_shape=[sds(*K1_SHAPE[k]) for k in K1_OUT] + [sds((1, LEN, D), bf16)],
        in_specs=[A_] + [V_] * 5, out_specs=[A_] * len(K1_OUT) + [V_],
        scratch_shapes=[VM((1, vec.shape[0]), f32), VM((GROW, D), bf16), VM((RAW + 2 * (n + 4) + 96, 128), f32), VM((4 * D, D), bf16), VM((6, 256, 128), f32)] + here
            + [VM((T, D), bf16), VM((T, D), bf16), VM((D, T), bf16), VM((T, FF), bf16), VM((LT, D), f32), VM((LT, D), f32), VM((T, D), bf16), VM((T, D), bf16),
               VM((256, T), bf16), VM((T, 256), bf16), VM((256, 256), f32), VM((2, 256, 384), f32), VM((1152, 128), f32), VM((2, 768, 128), f32), VM((3, 256, 128), f32),
               VM((256, 384), bf16), VM((256, 256), bf16),
               DMA((3,)), DMA((16, most)), DMA((PLANES,)), DMA((2,)), DMA((24,)), DMA((2,))],
        compiler_params=pltpu.CompilerParams(collective_id=0, has_side_effects=True, vmem_limit_bytes=63 * 2**20),
    )(params.reshape(n, 128), x, mask, jnp.transpose(dis, (2, 0, 1)), jnp.swapaxes(cho, 1, 2), vec.reshape(-1, 128))
    return dict(zip(K1_OUT, outs)), outs[-1]
TO_CORE, TO_V, TO_U, TO_Z, KEEP, SMALL = range(6)

class Reduce:
    def __init__(self, at, g, pieces, LD, LV, LZ, LU, total, RD, RV, RZ, RU, S):
        self.at, self.g, self.pieces, self.total = at, g, pieces, total
        self.LD, self.LV, self.LZ, self.LU = LD, LV, LZ, LU
        self.RD, self.RV, self.RZ, self.RU, self.S = RD, RV, RZ, RU, S
        self.sent = {z: 0 for z in range(PLANES)}
        self.seen = set()

    def copies(self, p, r, c, first, rows, extra, land, got, dev):
        a, e = self.at.span(p, r, c, first)
        out = []
        for s, n, to in [(a, rows, first)] + [(e, EXTRA, MAIN)] * extra:
            out.append(remote(self.g.at[pl.ds(s, n)], land.at[pl.ds(to, n)], self.S.at[0], got, dev))
        return out

    def build(self, zs, op):
        at = self.at
        kind, i, p, r = op
        unit = 4 * p + at.roles[r]
        _, first, rows, extra = self.pieces[p][i]
        if kind == TO_V:
            n = 2 * p + r - 2
            return self.copies(p, r, at.c, first, rows, extra, self.LV.at[n], self.RV.at[n, i], (zs, at.vf))
        if kind == TO_U:
            return self.copies(p, r, at.c, first, rows, extra, self.LU.at[p], self.RU.at[p, i], (zs, at.uf))
        up = p > zs
        to = zs + 1 if up else zs - 1
        n = 8 + r if (not up and to == p) else 2 * p + r
        return self.copies(p, r, at.c, first, rows, extra, self.LZ.at[n], self.RZ.at[n, i], (to, at.f))

    def once(self, zs, key, rows, got):
        if (zs, key) not in self.seen:
            self.seen.add((zs, key))
            ref = self.g.at[pl.ds(0, rows)]
            remote(ref, ref, self.S.at[0], got, (zs, self.at.fc)).wait_recv()

    def send(self, zs, op):
        for q in self.build(zs, op): q.start()
        _, _, rows, extra = self.pieces[op[2]][op[1]]
        self.sent[zs] += rows + EXTRA * extra

    def add(self, p, r, first, rows, extra, lands, final):
        a, e = self.at.span(p, r, self.at.c, first)
        g, total = self.g, self.total
        def one(s, i):
            v = g[pl.ds(s, 16), :].astype(f32)
            for land in lands:
                v = v + land[pl.ds(i, 16), :].astype(f32)
            if final:
                total[pl.ds(16 + i, 16), :] = v
            else:
                g[pl.ds(s, 16), :] = v.astype(bf16)
        def body(b, _):
            one(pl.multiple_of(a + 16 * b, 16), pl.multiple_of(first + 16 * b, 16))
            return 0
        lax.fori_loop(0, rows // 16, body, 0)
        if extra: one(e, MAIN)

    def op(self, zs, op):
        at = self.at
        kind, i, p, r = op
        unit = 4 * p + at.roles[r]
        self.once(zs, (TO_CORE, p, r), HALF, self.RD.at[unit])
        path, first, rows, extra = self.pieces[p][i]
        if kind == TO_V:
            self.add(p, r, first, rows, extra, [self.LD.at[unit]], False)
            self.send(zs, op)
            return
        n = 2 * p + r
        self.once(zs, ("v", i, p, r), rows + EXTRA * extra, self.RV.at[n, i])
        lands = [self.LD.at[unit], self.LV.at[n]]
        def arrived(land, got, key):
            self.once(zs, key, rows + EXTRA * extra, got)
            lands.append(land)
        if path == 0 or r == 0:
            if p >= zs and zs > 0: arrived(self.LZ.at[n], self.RZ.at[n, i], (UP, i, p, r))
            if p <= zs and zs < PLANES - 1:
                m = 8 + r if p == zs else n
                arrived(self.LZ.at[m], self.RZ.at[m, i], (DOWN, i, p, r))
        if r == 0 and (path == 1 or p == zs):
            arrived(self.LU.at[p], self.RU.at[p, i], (TO_U, i, p))
        self.add(p, r, first, rows, extra, lands, kind == KEEP)
        if kind != KEEP: self.send(zs, op)

    def core_copies(self, p, kk):
        a, e = self.at.span_of(p, kk, 1 - self.at.c, 0)
        land = self.LD.at[4 * p + kk]
        dev = (self.at.z, self.at.fc)
        return [remote(self.g.at[pl.ds(s, n)], land.at[pl.ds(to, n)], self.S.at[1], self.RD.at[4 * p + kk], dev)
                for s, n, to in ((a, MAIN, 0), (e, EXTRA, MAIN))]

    def to_core(self, p, kk):
        extra_rows(self.g, p, kk)
        for q in self.core_copies(p, kk): q.start()

    def drain(self):
        for zs in range(PLANES):
            @pl.when(self.at.z == zs)
            def _(): wait_sent(self.g, self.sent[zs], self.S.at[0], self.RD.at[0], (zs, self.at.fc))
        wait_sent(self.g, 4 * PLANES * HALF, self.S.at[1], self.RD.at[0], (self.at.z, self.at.fc))

class Spread:
    def __init__(self, at, own, land, zland, S, count):
        self.at, self.own, self.land, self.zland, self.S, self.count = at, own, land, zland, S, count

    def round(self, n, me, land, base, dev):
        return [remote(self.own, land.at[me], self.S.at[0, base + j], self.S.at[1, base + j], dev(lax.rem(me + j, n))) for j in range(1, n)]

    def plane(self):
        return self.round(self.count, self.at.f, self.land, 0, lambda t: (self.at.z, t))

    def planes(self):
        return self.round(PLANES, self.at.z, self.zland, self.count, lambda t: (t, self.at.f))

    def first(self):
        for q in self.plane(): q.start()

    def total(self, land, n, me):
        land[me] = self.own[...]
        v = land[0]
        for j in range(1, n): v = v + land[j]
        return v

    def second(self):
        for q in self.plane(): q.wait()
        self.own[...] = self.total(self.land, self.count, self.at.f)
        for q in self.planes(): q.start()

    def last(self):
        for q in self.planes(): q.wait()
        self.own[...] = self.total(self.zland, PLANES, self.at.z)

K2_IN = K1_OUT
K2_HERE = ("wproj", "dctx", "small", "hat1", "r1", "hat2", "r2", "gp", "ring", "normT", "attT", "q", "kT", "vv", "xT", "wq")

def backward_kernel(pieces, events, vec_ref, *rest):
    n_in = len(K2_IN)
    hbm = dict(zip(K2_IN, rest[:n_in]))
    (grad, vsum, sq, ig_out, g, vec, wproj, dctx, small, hat1, r1, hat2, r2, gp, ring, normT, attT, q, kT, vv, xT, wq,
     low1, low2, acc, tmp, dp, LD, LV, LZ, LU, total, flat, vg, vland, vzland, sqv, sland, szland,
     IS, RD, RV, RZ, RU, S, TS, TL, VS, SS) = rest[n_in:]
    here = dict(wproj=wproj, dctx=dctx, small=small, hat1=hat1, r1=r1, hat2=hat2, r2=r2, gp=gp, normT=normT, attT=attT, q=q, kT=kT, vv=vv, xT=xT)
    loads = {}
    def load(name, src=None, dst=None):
        cp = pltpu.make_async_copy(hbm[name] if src is None else src, here[name] if dst is None else dst, IS.at[len(loads)])
        cp.start()
        loads[name if src is None else (name, len(loads))] = cp
        return cp
    w = hbm["w"]
    first = [load(n) for n in ("dctx", "wproj", "hat2", "r2")]
    def second(n):
        rows = pl.ds(pl.multiple_of(6144 + n * TILE, 256), TILE)
        own = pl.ds(pl.multiple_of(n * TILE, TILE), TILE)
        pairs = ((w.at[rows], g.at[rows]), (hbm["actT"].at[own], ring.at[own]), (hbm["gp"].at[:, own], gp.at[:, own]))
        return [pltpu.make_async_copy(s, d, TL.at[3 * n + i]) for i, (s, d) in enumerate(pairs)]
    for n in range(FF // TILE - 1, -1, -1):
        for cp in second(n): cp.start()
    tail = load("tail", hbm["tail"], g.at[pl.ds(9216, 448)])
    third = [load("w", w.at[pl.ds(3072, 3072)], g.at[pl.ds(3072, 3072)]), load("normT")]
    fifth = [load("w", w.at[pl.ds(2304, 768)], g.at[pl.ds(2304, 768)]), load("attT")]
    sixth = [load("q"), load("kT"), load("vv")]
    seventh = [load("xT"), load("w", w.at[pl.ds(0, 2304)], wq)]
    def ready(cs):
        for cp in cs: cp.wait()
    at = Place()
    at.greet_all(vland.shape[0])
    re = Reduce(at, g, pieces, LD, LV, LZ, LU, total, RD, RV, RZ, RU, S)
    vs = Spread(at, vg, vland, vzland, VS, vland.shape[0])
    ss = Spread(at, sqv, sland, szland, SS, vland.shape[0])
    def slot(i, cond=None):
        for zs in range(PLANES):
            if events[zs][i]:
                @pl.when((at.z == zs) if cond is None else ((at.z == zs) & cond))
                def _():
                    for e in events[zs][i]:
                        if e[0] == SMALL: (vs.first, vs.second, vs.last)[e[1]]()
                        else: re.op(zs, e)
    for i in range(vec_ref.shape[0]):
        vec[0:1, 128 * i:128 * i + 128] = vec_ref[i:i + 1, :]
    low2[...] = jnp.zeros((T, D), bf16)
    low1[...] = jnp.zeros((T, D), bf16)
    for t in range(3):
        dp[t] = jnp.zeros((T, D), bf16)
    ready(first)
    for n in range(3):
        hat1[:, 256 * n:256 * n + 256] = mm_nt(dctx[0:LT, :], wproj[256 * n:256 * n + 256, :])
    norm_back(hat1, vec[0:1, G2:G2 + D], hat2, r2, low2, acc)
    fourth = [load("hat1"), load("r1"), load("small")]
    put_vec(vg, acc, (G2, S2, BDOWN))
    ready([tail])
    def downs(n, _):
        ready(second(3 - n))
        down_back(3 - n, low2, g, ring, gp, vg)
        for kk, last in ((3, 0), (2, 0), (1, 1), (0, 2)):
            @pl.when(n == last)
            def _(): re.to_core(3, kk)
        return 0
    lax.fori_loop(0, 3, downs, 0)
    slot(0)
    slot(1)
    ready(second(0))
    down_back(0, low2, g, ring, gp, vg)
    def head(h):
        return pltpu.make_async_copy(hbm["pT"].at[pl.ds(pl.multiple_of(h * T, T), T)], ring.at[pl.ds(pl.multiple_of((h % 6) * T, T), T)], TS.at[h % 6])
    for h in range(6): head(h).start()
    slot(2)
    ready(third)
    lax.fori_loop(0, 3, lambda n, _: (up_back_x(n, gp, g, hat2), 0)[1], 0)
    slot(3)
    weave(normT, gp, 4, 1, 3072, g, tmp, False)
    for kk in (3, 2, 1, 0): re.to_core(2, kk)
    slot(4)
    slot(5)
    slot(6)
    weave(normT, gp, 4, 0, 3072, g, tmp, False)
    re.to_core(1, 2)
    re.to_core(1, 3)
    slot(7)
    ready(fourth)
    norm_back(hat2, vec[0:1, G1:G1 + D], hat1, r1, low1, acc)
    put_vec(vg, acc, (G1, S1, BO))
    ready(fifth)
    da, dqT = low2, normT
    out_back(low1, g, attT, da)
    re.to_core(1, 0)
    re.to_core(1, 1)
    slot(8)
    slot(9)
    ready(sixth)
    def pairs(b, _):
        for p in (2 * b, 2 * b + 1):
            head(2 * p).wait()
            head(2 * p + 1).wait()
        attend_back(2 * b, da, q, kT, vv, ring, dp, dqT)
        attend_back(2 * b + 1, da, q, kT, vv, ring, dp, dqT)
        for p in (2 * b, 2 * b + 1):
            @pl.when(p < 3)
            def _():
                head(2 * p + 6).start()
                head(2 * p + 7).start()
        for i in range(3): slot(10 + i, b == i)
        return 0
    lax.fori_loop(0, H // 4, pairs, 0)
    ready(seventh)
    def wove(n, _):
        weave(xT, dp, 3, n, 0, g, tmp, True)
        for kk in range(4):
            @pl.when(n == min(kk, 1))
            def _(): re.to_core(0, kk)
        for i in range(2): slot(13 + i, n == i)
        return 0
    lax.fori_loop(0, 2, wove, 0)
    slot(15)
    slot(16)
    vg[0:1, BQ:BQ + D] = jnp.sum(dp[0].astype(f32), axis=0, keepdims=True)
    vg[0:1, BV:BV + D] = jnp.sum(dp[2].astype(f32), axis=0, keepdims=True)
    vg[0:1, BPROJ:BPROJ + 256] = small[0:1, :]
    vg[0:1, BCODE:BCODE + 256] = small[1:2, :]
    vg[0:1, BCODE + 256:BCODE + 512] = small[2:3, :]
    slot(17)
    slot(18)
    for n in range(3):
        input_back(n, dp, wq, hat1)
    put_ig = pltpu.make_async_copy(hat1.at[pl.ds(0, LEN)], ig_out.at[0], IS.at[len(loads)])
    put_ig.start()
    slot(19)
    z, c, k = at.z, at.c, at.k
    edge = remote(total.at[pl.ds(HALF, 16)], total.at[pl.ds(0, 16)], TS.at[6], TS.at[7], (z, at.fc))
    edge.start()
    row = lax.broadcasted_iota(jnp.int32, (16, D), 0)
    def square(b, acc):
        v = total[pl.ds(pl.multiple_of(16 + 16 * b, 16), 16), :]
        return acc + sum8(v * v)
    acc = lax.fori_loop(0, MAIN // 16, square, jnp.zeros((8, D), f32))
    v = jnp.where((c == 0) | (row < 12 - 4 * k) | (row >= 16 - 4 * k), total[16 + MAIN:16 + HALF, :], 0.0)
    acc = acc + sum8(v * v)
    sqv[...] = sum(acc[:, 128 * j:128 * j + 128] for j in range(6))
    ss.first()
    for i in range(vsum.shape[0]):
        vsum[i:i + 1, :] = vg[0:1, 128 * i:128 * i + 128]
    n = grad.shape[0] // 6
    edge.wait()
    for j in range(6):
        flat[pl.ds(j, 320, stride=6), :] = total[:, 128 * j:128 * j + 128]
    ss.second()
    for j in range(6):
        grad[pl.ds(j, n, stride=6), :] = flat[pl.ds(6 * (16 - 2 * c - 4 * k) + j, n, stride=6), :]
    re.drain()
    ss.last()
    sq[...] = sqv[...]
    put_ig.wait()

def backward(pieces, events, vec, hbm, count, n):
    V_ = pl.BlockSpec(memory_space=pltpu.VMEM)
    A_ = pl.BlockSpec(memory_space=pl.ANY)
    VM = pltpu.VMEM
    DMA = pltpu.SemaphoreType.DMA
    sds = jax.ShapeDtypeStruct
    most = max(len(ps) for ps in pieces)
    nv = vec.shape[0] + 256
    shape = dict(K1_SHAPE, ring=((FF, T), bf16), wq=((3 * D, D), bf16))
    return pl.pallas_call(functools.partial(backward_kernel, pieces, events),
        out_shape=[sds((n, 128), f32), sds((nv // 128, 128), f32), sds((8, 128), f32), sds((1, LEN, D), f32)],
        in_specs=[V_] + [A_] * len(K2_IN), out_specs=[V_] * 3 + [A_],
        scratch_shapes=[VM((GROW, D), bf16), VM((1, vec.shape[0]), f32)] + [VM(*shape[k]) for k in K2_HERE]
            + [VM((T, D), bf16), VM((T, D), bf16), VM((24, D), f32), VM((2, 4 * WEAVE, 128), f32), VM((3, T, D), bf16),
               VM((16, HALF, D), bf16), VM((8, HALF, D), bf16), VM((10, HALF, D), bf16), VM((4, HALF, D), bf16), VM((HALF + 16, D), f32), VM((6 * (HALF + 16), 128), f32),
               VM((1, nv), f32), VM((count, 1, nv), f32), VM((PLANES, 1, nv), f32), VM((8, 128), f32), VM((count, 8, 128), f32), VM((PLANES, 8, 128), f32),
               DMA((24,)), DMA((16,)), DMA((8, most)), DMA((10, most)), DMA((4, most)), DMA((2,)), DMA((8,)), DMA((12,)), DMA((2, count + PLANES)), DMA((2, count + PLANES))],
        compiler_params=pltpu.CompilerParams(collective_id=1, has_side_effects=True, vmem_limit_bytes=63 * 2**20),
    )(vec.reshape(-1, 128), *[hbm[k] for k in K2_IN])

def update_kernel(total, g, p, m1, m2, vg, v, v1, v2, sq, np_, low, n1, n2, nv, nv1, nv2, loss, norm, scale):
    @pl.when(pl.program_id(0) == 0)
    def _():
        n = v.shape[0]
        gv = vg[0:n, :]
        s = jnp.sum(jnp.sum(sq[...], axis=0, keepdims=True), axis=1, keepdims=True)
        s = s + jnp.sum(jnp.sum(gv * gv, axis=0, keepdims=True), axis=1, keepdims=True)
        s = jnp.sqrt(s)
        f = jnp.minimum(1.0, clip_level / (s + 1e-06))
        norm[...] = s
        loss[...] = vg[n:n + 1, 0:1] / total
        scale[...] = jnp.broadcast_to(f, (8, 128))
        nv[...], nv1[...], nv2[...] = adamw_update(v[...], v1[...], v2[...], gv * f, rate_vector)
    new, first, second = adamw_update(p[...], m1[...], m2[...], g[...] * scale[0:1, 0:1], rate_matrix)
    np_[...] = new
    low[...] = new.astype(bf16)
    n1[...] = first
    n2[...] = second

def update(total, g, p, m1, m2, vg, v, v1, v2, sq):
    n, nv = g.shape[0], v.shape[0] // 128
    sds = jax.ShapeDtypeStruct
    rows = 608
    part = pl.BlockSpec((rows, 128), lambda i: (i, 0))
    def whole(*shape): return pl.BlockSpec(shape, lambda i: (0, 0))
    flat = lambda a: a.reshape(-1, 128)
    out = pl.pallas_call(functools.partial(update_kernel, total), grid=(pl.cdiv(n, rows),),
        out_shape=[sds((n, 128), f32), sds((n, 128), bf16), sds((n, 128), f32), sds((n, 128), f32)] + [sds((nv, 128), f32)] * 3 + [sds((1, 1), f32)] * 2,
        in_specs=[part] * 4 + [whole(*vg.shape)] + [whole(nv, 128)] * 3 + [whole(8, 128)],
        out_specs=[part] * 4 + [whole(nv, 128)] * 3 + [whole(1, 1)] * 2,
        scratch_shapes=[pltpu.VMEM((8, 128), f32)],
    )(g, flat(p), flat(m1), flat(m2), vg, flat(v), flat(v1), flat(v2), sq)
    return [a.reshape(-1) for a in out[:7]] + [a.reshape(()) for a in out[7:]]

PIECES_OUT = (((0, 0, 48, False), (0, 48, 48, False), (0, 96, 48, False), (1, 144, 48, False), (1, 192, 32, False), (1, 224, 32, False), (1, 256, 32, True)),
 ((0, 0, 96, False), (0, 96, 96, False), (0, 192, 96, True)), ((1, 0, 144, False), (1, 144, 144, True)), ((0, 0, 192, False), (1, 192, 96, True)))
PIECES_BACK = (((0, 0, 48, False), (0, 48, 48, False), (0, 96, 48, False), (1, 144, 48, False), (1, 192, 32, False), (1, 224, 32, False), (1, 256, 32, True)),
 ((0, 0, 192, False), (1, 192, 48, False), (1, 240, 48, True)), ((1, 0, 96, False), (1, 96, 96, False), (1, 192, 96, True)),
 ((0, 0, 144, False), (0, 144, 144, True)))
SENDS_OUT = ((((0, 0, 0, 0), (0, 1, 0, 0), (3, 0, 0, 0), (3, 1, 0, 0), (3, 2, 0, 0)),
  ((0, 2, 0, 0), (0, 3, 0, 0), (4, 0, 0, 2), (3, 3, 0, 0), (3, 4, 0, 0), (4, 1, 0, 2), (0, 4, 0, 0), (3, 5, 0, 0), (4, 2, 0, 2), (3, 6, 0, 0),
   (0, 5, 0, 0), (4, 0, 1, 0), (2, 0, 0, 0), (2, 1, 0, 0), (0, 6, 0, 0), (2, 2, 0, 0), (4, 3, 0, 2), (2, 3, 0, 0), (4, 4, 0, 2), (2, 4, 0, 0),
   (4, 5, 0, 2), (4, 1, 1, 0), (2, 5, 0, 0), (4, 6, 0, 2), (2, 6, 0, 0), (3, 0, 1, 0), (0, 0, 0, 1), (4, 0, 0, 1), (0, 1, 0, 1), (4, 1, 0, 1),
   (3, 0, 0, 1), (0, 2, 0, 1), (4, 2, 0, 1), (4, 3, 0, 1), (3, 1, 0, 1), (4, 4, 0, 1), (3, 2, 0, 1), (4, 5, 0, 1), (4, 2, 1, 0), (3, 3, 0, 1),
   (4, 6, 0, 1), (3, 4, 0, 1), (3, 5, 0, 1), (3, 6, 0, 1), (4, 0, 1, 2), (3, 1, 1, 0), (4, 0, 0, 3), (4, 0, 2, 0), (4, 1, 0, 3), (3, 0, 2, 0),
   (4, 2, 0, 3), (4, 3, 0, 3), (4, 4, 0, 3), (4, 5, 0, 3), (2, 0, 2, 0), (4, 6, 0, 3), (4, 1, 2, 0), (4, 1, 1, 2), (3, 1, 2, 0)),
  (), ((3, 0, 2, 1), (4, 0, 1, 1), (4, 0, 2, 2), (4, 0, 2, 1), (4, 1, 1, 1), (2, 1, 2, 0)), (), ((3, 2, 1, 0), (4, 1, 2, 2)),
  ((4, 2, 1, 1), (3, 0, 1, 1), (3, 1, 1, 1), (4, 0, 2, 3), (4, 1, 2, 1)),
  ((3, 1, 2, 1), (4, 2, 1, 2), (4, 0, 3, 0), (4, 0, 1, 3), (3, 2, 1, 1), (4, 1, 1, 3), (3, 0, 3, 0), (4, 1, 3, 0), (4, 1, 2, 3), (2, 1, 3, 0),
   (4, 2, 1, 3), (3, 1, 3, 0), (4, 0, 3, 2), (4, 0, 3, 1), (3, 0, 3, 1)),
  ((4, 1, 3, 1), (3, 1, 3, 1)), ((4, 1, 3, 2),), (), (), (), ((4, 0, 3, 3),), ((4, 1, 3, 3),), (), ()),
 (((1, 0, 1, 0), (2, 0, 1, 0), (2, 1, 1, 0), (0, 0, 1, 0)),
  ((1, 1, 1, 0), (2, 2, 1, 0), (0, 1, 1, 0), (3, 0, 1, 0), (4, 0, 0, 0), (4, 0, 1, 1), (1, 2, 1, 0), (0, 0, 0, 0), (3, 0, 0, 0), (4, 1, 0, 0),
   (4, 1, 1, 1), (3, 1, 0, 0), (0, 1, 0, 0), (3, 1, 1, 0), (4, 0, 2, 0), (4, 2, 0, 0), (4, 2, 1, 1), (1, 0, 2, 0), (0, 2, 0, 0), (3, 2, 0, 0),
   (4, 3, 0, 0), (2, 3, 0, 0), (4, 0, 1, 2), (0, 3, 0, 0), (4, 4, 0, 0), (4, 0, 0, 2), (2, 4, 0, 0), (3, 3, 0, 0), (4, 1, 0, 2), (0, 4, 0, 0),
   (4, 5, 0, 0), (2, 5, 0, 0), (3, 4, 0, 0), (0, 5, 0, 0), (1, 1, 2, 0), (4, 6, 0, 0), (0, 6, 0, 0), (4, 2, 0, 2), (4, 1, 1, 2), (4, 3, 0, 1),
   (2, 6, 0, 0), (4, 4, 0, 1), (0, 0, 0, 1), (4, 0, 0, 1), (4, 3, 0, 2), (3, 5, 0, 0), (4, 5, 0, 1), (4, 1, 0, 1), (0, 1, 0, 1), (4, 4, 0, 2),
   (3, 6, 0, 0), (3, 3, 0, 1), (3, 4, 0, 1), (1, 0, 1, 1), (0, 2, 0, 1), (4, 2, 0, 1), (4, 0, 3, 0), (4, 6, 0, 1), (4, 5, 0, 2), (3, 0, 0, 1),
   (3, 5, 0, 1), (3, 1, 0, 1), (3, 2, 0, 1), (4, 6, 0, 2), (0, 2, 1, 0), (1, 1, 1, 1), (4, 3, 0, 3), (3, 6, 0, 1), (4, 4, 0, 3), (2, 1, 3, 0),
   (4, 1, 3, 0), (4, 1, 2, 0), (4, 0, 0, 3), (0, 0, 1, 1), (4, 5, 0, 3), (2, 0, 2, 0), (1, 2, 1, 1), (4, 1, 0, 3), (4, 2, 0, 3), (2, 1, 2, 0),
   (4, 6, 0, 3), (0, 1, 1, 1), (1, 0, 3, 0), (4, 1, 3, 1), (3, 0, 2, 0)),
  ((4, 0, 3, 1), (0, 2, 1, 1), (4, 0, 2, 1)), ((3, 1, 2, 0), (4, 1, 2, 1), (1, 1, 3, 0)), (), ((3, 0, 2, 1), (4, 0, 2, 2)),
  ((1, 0, 3, 1), (3, 1, 2, 1), (4, 1, 2, 2)),
  ((3, 2, 1, 0), (4, 0, 2, 3), (3, 0, 1, 1), (3, 1, 1, 1), (4, 1, 2, 3), (3, 2, 1, 1), (4, 2, 1, 2), (3, 0, 3, 0), (4, 0, 1, 3), (4, 1, 1, 3),
   (3, 1, 3, 0), (4, 2, 1, 3), (3, 1, 3, 1), (3, 0, 3, 1), (4, 0, 3, 2)),
  ((4, 1, 3, 2),), (), ((4, 1, 3, 3),), (), (), (), ((4, 0, 3, 3),), (), ()),
 (((0, 0, 2, 0), (1, 0, 2, 0), (3, 0, 2, 0)),
  ((3, 1, 2, 0), (0, 1, 2, 0), (1, 1, 2, 0), (2, 0, 2, 0), (4, 0, 2, 2), (2, 1, 2, 0), (4, 0, 1, 0), (0, 0, 1, 0), (4, 1, 2, 2), (4, 0, 3, 0),
   (3, 0, 3, 0), (4, 1, 1, 0), (1, 0, 3, 0), (4, 0, 2, 1), (4, 0, 0, 0), (0, 0, 0, 0), (3, 0, 0, 0), (4, 1, 3, 0), (0, 1, 0, 0), (3, 1, 0, 0),
   (4, 1, 2, 1), (4, 1, 0, 0), (3, 1, 3, 0), (4, 2, 0, 0), (0, 2, 0, 0), (1, 1, 3, 0), (3, 2, 0, 0), (0, 3, 0, 0), (4, 3, 0, 0), (3, 3, 0, 0),
   (4, 0, 3, 2), (4, 4, 0, 0), (3, 4, 0, 0), (0, 4, 0, 0), (4, 0, 0, 2), (3, 5, 0, 0), (4, 5, 0, 0), (0, 5, 0, 0), (3, 0, 3, 1), (4, 0, 3, 1),
   (4, 1, 0, 2), (0, 6, 0, 0), (4, 1, 3, 2), (4, 6, 0, 0), (1, 0, 3, 1), (4, 2, 0, 2), (0, 0, 0, 1), (4, 0, 0, 1), (3, 6, 0, 0), (4, 3, 0, 2),
   (4, 4, 0, 2), (3, 0, 0, 1), (0, 1, 0, 1), (4, 1, 0, 1), (3, 1, 0, 1), (4, 5, 0, 2), (2, 3, 0, 0), (4, 2, 0, 1), (0, 2, 0, 1), (3, 2, 0, 1),
   (2, 4, 0, 0), (0, 1, 1, 0), (4, 0, 3, 3), (2, 5, 0, 0), (4, 6, 0, 2), (2, 6, 0, 0), (3, 0, 2, 1), (4, 0, 0, 3), (4, 2, 1, 0), (4, 1, 0, 3),
   (0, 2, 1, 0), (4, 3, 0, 1), (3, 3, 0, 1), (4, 2, 0, 3), (4, 4, 0, 1), (3, 4, 0, 1), (4, 5, 0, 1), (3, 5, 0, 1), (4, 0, 1, 1), (3, 6, 0, 1),
   (4, 6, 0, 1), (3, 1, 2, 1), (0, 0, 1, 1), (4, 1, 1, 1), (4, 0, 2, 3), (4, 3, 0, 3), (3, 0, 1, 0), (4, 4, 0, 3), (0, 1, 1, 1), (4, 5, 0, 3),
   (3, 1, 1, 0), (4, 6, 0, 3), (4, 2, 1, 1), (3, 2, 1, 0), (0, 2, 1, 1), (4, 1, 2, 3)),
  ((3, 0, 1, 1),), ((4, 0, 1, 2), (4, 1, 1, 2), (3, 1, 1, 1), (4, 2, 1, 2), (3, 2, 1, 1)), (), ((4, 0, 1, 3), (2, 1, 3, 0)),
  ((4, 1, 1, 3), (4, 2, 1, 3)), ((3, 1, 3, 1), (4, 1, 3, 1)), (), (), (), ((4, 1, 3, 3),), (), (), (), (), ()),
 (((2, 0, 3, 0), (1, 0, 3, 0)),
  ((2, 1, 3, 0), (3, 0, 3, 0), (1, 1, 3, 0), (4, 0, 3, 1), (3, 1, 3, 0), (4, 0, 2, 0), (4, 1, 3, 1), (3, 0, 2, 0), (1, 0, 3, 1), (2, 0, 2, 0),
   (4, 0, 3, 2), (4, 1, 2, 0), (4, 1, 3, 2), (3, 1, 2, 0), (4, 0, 2, 2), (4, 0, 1, 0), (3, 0, 1, 0), (4, 0, 0, 0), (3, 0, 0, 0), (4, 0, 2, 1),
   (3, 0, 2, 1), (4, 1, 0, 0), (4, 1, 2, 2), (4, 2, 0, 0), (3, 1, 0, 0), (3, 2, 0, 0), (4, 0, 1, 2), (4, 3, 0, 0), (2, 3, 0, 0), (4, 0, 0, 2),
   (4, 4, 0, 0), (2, 4, 0, 0), (3, 3, 0, 0), (4, 5, 0, 0), (2, 5, 0, 0), (3, 4, 0, 0), (4, 0, 2, 3), (4, 6, 0, 0), (4, 1, 0, 2), (2, 6, 0, 0),
   (3, 5, 0, 0), (4, 2, 0, 2), (3, 6, 0, 0), (4, 0, 0, 1), (4, 3, 0, 1), (3, 0, 0, 1), (4, 4, 0, 1), (3, 3, 0, 1), (4, 1, 0, 1), (4, 3, 0, 2),
   (4, 5, 0, 1), (3, 4, 0, 1), (4, 4, 0, 2), (3, 1, 0, 1), (4, 2, 0, 1), (4, 6, 0, 1), (3, 5, 0, 1), (4, 5, 0, 2), (3, 2, 0, 1), (3, 6, 0, 1),
   (4, 6, 0, 2), (2, 1, 2, 0), (4, 0, 0, 3), (4, 1, 1, 0), (4, 3, 0, 3), (4, 4, 0, 3), (4, 1, 0, 3), (3, 1, 1, 0), (4, 5, 0, 3), (4, 2, 0, 3),
   (4, 2, 1, 0), (3, 2, 1, 0), (4, 6, 0, 3), (3, 0, 3, 1), (4, 1, 2, 1), (4, 0, 1, 1)),
  (), ((3, 0, 1, 1), (3, 1, 1, 1), (4, 1, 1, 2), (4, 2, 1, 2), (4, 1, 1, 1)), (),
  ((3, 2, 1, 1), (4, 2, 1, 1), (4, 0, 3, 3), (4, 0, 1, 3), (3, 1, 2, 1)), ((4, 1, 1, 3), (3, 1, 3, 1)), ((4, 2, 1, 3), (4, 1, 2, 3), (4, 1, 3, 3)),
  (), (), (), (), (), (), (), (), ()))
SENDS_BACK = (((), (), (), ((1, 0, 3, 2),), ((1, 0, 3, 3),), (), (), ((1, 1, 3, 2),), ((3, 0, 3, 0), (1, 1, 3, 3)), (), ((1, 0, 1, 2), (3, 0, 3, 1)),
  ((1, 0, 1, 3),), ((1, 1, 1, 2), (1, 1, 1, 3), (1, 2, 1, 2), (3, 1, 3, 0), (1, 2, 1, 3)), ((1, 0, 2, 2),),
  ((3, 1, 3, 1), (1, 0, 2, 3), (1, 1, 2, 2)), (), (), (), ((5, 0, 0, 0), (1, 1, 2, 3)),
  ((1, 2, 2, 2), (3, 0, 1, 0), (2, 0, 2, 1), (1, 2, 2, 3), (2, 1, 2, 1), (1, 0, 0, 2), (3, 0, 1, 1), (1, 0, 0, 3), (1, 1, 0, 2), (1, 1, 0, 3),
   (2, 2, 2, 1), (1, 2, 0, 2), (1, 2, 0, 3), (1, 3, 0, 2), (5, 1, 0, 0), (3, 0, 2, 0), (1, 3, 0, 3), (1, 4, 0, 2), (1, 4, 0, 3), (1, 5, 0, 2),
   (1, 5, 0, 3), (3, 1, 2, 0), (1, 6, 0, 2), (1, 6, 0, 3), (2, 1, 1, 1), (2, 3, 0, 1), (3, 2, 2, 0), (2, 2, 1, 1), (2, 4, 0, 1), (5, 2, 0, 0),
   (2, 5, 0, 1), (2, 0, 0, 1), (2, 6, 0, 1), (3, 1, 1, 0), (3, 2, 1, 0), (2, 1, 0, 1), (4, 0, 0, 0), (2, 2, 0, 1), (4, 1, 0, 0), (4, 3, 0, 0),
   (4, 4, 0, 0), (4, 2, 0, 0), (4, 5, 0, 0), (4, 6, 0, 0))),
 ((), (), (), ((1, 0, 3, 2),), ((1, 0, 3, 3),), (), (), ((1, 1, 3, 2),), ((1, 1, 3, 3),), (), ((1, 0, 2, 2), (1, 0, 2, 3)),
  ((1, 1, 2, 2), (1, 1, 2, 3)), ((3, 0, 3, 0), (2, 0, 2, 1), (1, 2, 2, 2)), ((2, 1, 2, 1),), ((3, 0, 3, 1), (1, 2, 2, 3)), (), (), (),
  ((5, 0, 0, 0), (1, 0, 1, 2)),
  ((1, 0, 0, 2), (3, 1, 3, 0), (1, 0, 0, 3), (2, 2, 2, 1), (1, 1, 0, 2), (1, 1, 0, 3), (1, 2, 0, 2), (3, 1, 3, 1), (1, 2, 0, 3), (1, 3, 0, 2),
   (1, 3, 0, 3), (1, 4, 0, 2), (1, 4, 0, 3), (1, 5, 0, 2), (1, 5, 0, 3), (5, 1, 0, 0), (1, 6, 0, 2), (1, 6, 0, 3), (1, 0, 1, 3), (2, 3, 0, 1),
   (2, 4, 0, 1), (2, 5, 0, 1), (3, 0, 0, 0), (2, 6, 0, 1), (1, 1, 1, 2), (3, 0, 0, 1), (1, 1, 1, 3), (1, 2, 1, 2), (3, 1, 0, 0), (2, 0, 1, 1),
   (3, 0, 2, 0), (5, 2, 0, 0), (3, 1, 0, 1), (3, 2, 0, 0), (1, 2, 1, 3), (3, 1, 2, 0), (3, 2, 0, 1), (2, 1, 1, 1), (3, 3, 0, 0), (3, 4, 0, 0),
   (3, 2, 2, 0), (4, 0, 1, 0), (3, 5, 0, 0), (2, 2, 1, 1), (3, 6, 0, 0), (4, 1, 1, 0), (4, 2, 1, 0))),
 ((), (), (), ((1, 0, 3, 2),), ((1, 0, 3, 3),), (), (), ((1, 1, 3, 2),), ((1, 1, 3, 3),), (), ((1, 0, 1, 2),), ((1, 0, 1, 3),),
  ((1, 1, 1, 2), (1, 1, 1, 3), (1, 2, 1, 2)), ((1, 2, 1, 3), (1, 0, 2, 2)), ((1, 0, 2, 3),), (), (), (), ((5, 0, 0, 0), (1, 1, 2, 2)),
  ((1, 0, 0, 2), (1, 0, 0, 3), (3, 0, 3, 0), (1, 1, 0, 2), (3, 0, 1, 0), (1, 1, 0, 3), (1, 2, 0, 2), (1, 2, 0, 3), (1, 3, 0, 2), (3, 0, 3, 1),
   (1, 3, 0, 3), (1, 4, 0, 2), (1, 4, 0, 3), (1, 5, 0, 2), (1, 5, 0, 3), (5, 1, 0, 0), (3, 0, 1, 1), (1, 6, 0, 2), (1, 6, 0, 3), (1, 1, 2, 3),
   (3, 1, 3, 0), (1, 2, 2, 2), (3, 0, 0, 0), (1, 2, 2, 3), (3, 0, 0, 1), (2, 0, 2, 1), (3, 1, 3, 1), (3, 1, 0, 0), (2, 1, 2, 1), (3, 1, 0, 1),
   (2, 3, 0, 1), (2, 4, 0, 1), (3, 2, 0, 0), (5, 2, 0, 0), (2, 2, 2, 1), (3, 2, 0, 1), (2, 5, 0, 1), (2, 6, 0, 1), (2, 1, 1, 1), (3, 3, 0, 0),
   (2, 2, 1, 1), (3, 4, 0, 0), (3, 5, 0, 0), (3, 6, 0, 0), (3, 1, 1, 0), (3, 2, 1, 0), (4, 0, 2, 0), (4, 1, 2, 0), (4, 2, 2, 0))),
 ((), (), (), ((1, 0, 3, 2),), ((1, 0, 3, 3),), (), (), ((1, 1, 3, 2),), ((1, 0, 2, 2),), ((1, 0, 2, 3),), ((1, 0, 1, 2),), ((1, 0, 1, 3),),
  ((3, 0, 1, 0), (1, 1, 1, 2), (1, 1, 1, 3), (1, 2, 1, 2)), ((1, 2, 1, 3), (1, 1, 2, 2)), ((3, 0, 1, 1), (2, 1, 1, 1), (1, 1, 2, 3)), (), (),
  ((1, 2, 2, 2),), ((5, 0, 0, 0),),
  ((1, 0, 0, 2), (1, 0, 0, 3), (1, 1, 0, 2), (1, 1, 0, 3), (3, 1, 1, 0), (1, 2, 0, 2), (1, 2, 0, 3), (1, 3, 0, 2), (3, 0, 0, 0), (1, 3, 0, 3),
   (3, 0, 0, 1), (1, 4, 0, 2), (1, 4, 0, 3), (3, 1, 0, 0), (5, 1, 0, 0), (1, 5, 0, 2), (1, 5, 0, 3), (1, 6, 0, 2), (3, 1, 0, 1), (1, 6, 0, 3),
   (2, 2, 1, 1), (3, 2, 0, 0), (2, 3, 0, 1), (3, 2, 0, 1), (2, 4, 0, 1), (1, 2, 2, 3), (2, 5, 0, 1), (2, 6, 0, 1), (3, 2, 1, 0), (2, 0, 2, 1),
   (5, 2, 0, 0), (3, 3, 0, 0), (2, 1, 2, 1), (3, 4, 0, 0), (2, 2, 2, 1), (3, 5, 0, 0), (3, 6, 0, 0), (1, 1, 3, 3), (3, 0, 2, 0), (2, 0, 3, 1),
   (3, 1, 2, 0), (3, 2, 2, 0), (2, 1, 3, 1), (4, 0, 3, 0), (4, 1, 3, 0))))

def unpack(flat_values):
    shapes = [(D, 3 * D), (D, D), (D, FF), (FF, D), (D, FINAL), (G * CD, V), (G * CD, FINAL)]
    pieces = []
    offset = 0
    for height, width in shapes:
        pieces.append(flat_values[offset : offset + height * width].reshape(height, width))
        offset = offset + height * width
    return pieces


def split_vectors(vector_all):
    lengths = [D, D, D, D, D, FF, D, D, D, FINAL, FINAL]
    pieces = []
    offset = 0
    for length in lengths:
        pieces.append(vector_all[offset : offset + length])
        offset = offset + length
    return pieces


def layer_norm(values, scale_gain, shift_bias):
    centered = values - jnp.mean(values, axis=-1, keepdims=True)
    variance = jnp.mean(centered * centered, axis=-1, keepdims=True)
    return centered * lax.rsqrt(variance + eps_norm) * scale_gain + shift_bias


def contrast_dense(chosen, targets, distract, weight):
    hi = dict(precision=lax.Precision.HIGHEST)
    frames = jnp.arange(MASKED, dtype=jnp.int32)
    allowed = jnp.any(distract[:, :, None] == frames, axis=1) | (frames[:, None] == frames)

    def agreement(chosen, targets):
        left = chosen * lax.rsqrt(jnp.sum(chosen * chosen, axis=-1, keepdims=True) + eps_cos)
        right = targets * lax.rsqrt(jnp.sum(targets * targets, axis=-1, keepdims=True) + eps_cos)
        return jnp.einsum("by,oy->bo", left, right, **hi) / softness_divisor

    similar, back = jax.vjp(agreement, chosen, targets)
    same = frames[:, None] == frames
    positive = jnp.sum(jnp.where(same, similar, 0.0), axis=1)
    top = jnp.max(jnp.where(allowed, similar, -jnp.inf), axis=1)
    parts = jnp.where(allowed, jnp.exp(similar - top[:, None]), 0.0)
    total = jnp.sum(parts, axis=1)
    loss = jnp.sum(top + jnp.log(total) - positive)
    d_similar = weight * (parts / total[:, None] - same.astype(jnp.float32))
    return (loss,) + back(d_similar)


def adamw_update(master, first_moment, second, gradient, step_rate):
    first_new = beta_one * first_moment + (1.0 - beta_one) * gradient
    second_new = beta_two * second + (1.0 - beta_two) * gradient * gradient
    first_hat = first_new / (1.0 - beta_one**STEP)
    second_hat = second_new / (1.0 - beta_two**STEP)
    master_new = master * (1.0 - step_rate * decay_rate) - step_rate * first_hat / (
        jnp.sqrt(second_hat) + adam_eps
    )
    return (master_new, first_new, second_new)


def column_sum(values):
    return jnp.sum(values.astype(jnp.float32), axis=tuple(range(values.ndim - 1)))


def finish(total_masked, square_sum, vector_sum, loss_sum, grad_shard, output, input_grad, params, moment_one, moment_two, vectors, vector_one, vector_two):
    grad_norm = jnp.sqrt(square_sum + jnp.sum(vector_sum * vector_sum))
    factor = jnp.minimum(1.0, clip_level / (grad_norm + 1e-06))
    refreshed_weights, new_one, new_two = adamw_update(params, moment_one, moment_two, grad_shard * factor, rate_matrix)
    new_vectors, new_vector_first, new_vector_second = adamw_update(vectors, vector_one, vector_two, vector_sum * factor, rate_vector)
    return (
        loss_sum / total_masked,
        grad_norm,
        output,
        input_grad,
        refreshed_weights,
        refreshed_weights.astype(bf16),
        new_one,
        new_two,
        new_vectors,
        new_vector_first,
        new_vector_second,
    )


def by_collectives(
    layer_input,
    mask_index,
    distract,
    code_choice,
    params,
    moment_one,
    moment_two,
    vectors,
    vector_one,
    vector_two,
):
    bf16 = jnp.bfloat16
    f32 = jnp.float32
    count_utts = layer_input.shape[0]
    total_masked = count_utts * lax.axis_size(("dp", "fsdp")) * MASKED
    token_rows = count_utts * LEN
    gathered = lax.all_gather(params.astype(bf16), ("dp", "fsdp"), axis=0, tiled=True)
    qkv_weight, out_weight, up_weight, down_weight, proj_weight, codebook, code_weight = unpack(
        gathered
    )
    (
        bias_query,
        bias_value,
        bias_out,
        gain_one,
        shift_one,
        bias_up,
        bias_down,
        gain_two,
        shift_two,
        bias_proj,
        bias_code,
    ) = split_vectors(vectors)
    inputs = layer_input.reshape(token_rows, D)
    projected = jnp.dot(inputs, qkv_weight, preferred_element_type=f32)
    query_heads = (projected[:, :D] + bias_query).astype(bf16).reshape(count_utts, LEN, H, HD)
    key_heads = projected[:, D : 2 * D].astype(bf16).reshape(count_utts, LEN, H, HD)
    value_heads = (projected[:, 2 * D :] + bias_value).astype(bf16).reshape(count_utts, LEN, H, HD)
    scores = (
        jnp.einsum("blhe,bmhe->bhlm", query_heads, key_heads, preferred_element_type=f32) * 0.125
    )
    attn_probs = jax.nn.softmax(scores, axis=-1)
    probs_low = attn_probs.astype(bf16)
    attended = jnp.einsum("bhlm,bmhe->blhe", probs_low, value_heads, preferred_element_type=f32)
    attended = attended.astype(bf16).reshape(token_rows, D)
    residual_one = (
        inputs.astype(f32) + jnp.dot(attended, out_weight, preferred_element_type=f32) + bias_out
    )
    normed, back_one = jax.vjp(layer_norm, residual_one, gain_one, shift_one)
    normed_low = normed.astype(bf16)
    hidden = jnp.dot(normed_low, up_weight, preferred_element_type=f32) + bias_up
    active, gelu_back = jax.vjp(functools.partial(jax.nn.gelu, approximate=False), hidden)
    active_low = active.astype(bf16)
    residual_two = normed + jnp.dot(active_low, down_weight, preferred_element_type=f32) + bias_down
    output, back_two = jax.vjp(layer_norm, residual_two, gain_two, shift_two)
    output_low = output.astype(bf16)
    place = (mask_index[0][:, None] == jnp.arange(LEN, dtype=jnp.int32)).astype(bf16)
    picked = jnp.dot(place, output_low, preferred_element_type=f32).astype(bf16)
    chosen = jnp.dot(picked, proj_weight, preferred_element_type=f32) + bias_proj
    choose = (code_choice[..., None] == jnp.arange(V, dtype=jnp.int32)).astype(bf16)
    code_vectors = jnp.einsum(
        "bmgv,gcv->bmgc", choose, codebook.reshape(G, CD, V), preferred_element_type=f32
    )
    code_vectors = code_vectors.astype(bf16).reshape(count_utts, MASKED, G * CD)
    targets = (
        jnp.einsum("bmc,cf->bmf", code_vectors, code_weight, preferred_element_type=f32) + bias_code
    )
    loss_local, d_chosen, d_targets = contrast_dense(chosen, targets[0], distract[0], 1.0 / total_masked)
    d_targets = d_targets[None]
    d_targets_low = d_targets.astype(bf16)
    quantized_offset_slope = column_sum(d_targets_low)
    d_code_weight = jnp.einsum(
        "bmc,bmf->cf", code_vectors, d_targets_low, preferred_element_type=f32
    )
    d_code_vectors = jnp.einsum(
        "bmf,cf->bmc", d_targets_low, code_weight, preferred_element_type=f32
    )
    d_codebook = jnp.einsum(
        "bmgc,bmgv->gcv",
        d_code_vectors.reshape(count_utts, MASKED, G, CD),
        choose.astype(f32),
        precision=lax.Precision.HIGHEST,
    ).reshape(G * CD, V)
    d_chosen_low = d_chosen.astype(bf16)
    d_bias_proj = column_sum(d_chosen_low)
    d_proj_weight = jnp.einsum("td,tf->df", picked, d_chosen_low, preferred_element_type=f32)
    d_context_low = jnp.einsum("mt,mf->tf", place, d_chosen_low, preferred_element_type=f32).astype(bf16)
    result_sensitivity = jnp.einsum(
        "tf,df->td", d_context_low, proj_weight, preferred_element_type=f32
    )
    d_residual_two, d_gain_two, d_shift_two = back_two(result_sensitivity)
    d_second_low = d_residual_two.astype(bf16)
    d_bias_down = column_sum(d_second_low)
    d_down_weight = jnp.einsum("th,td->hd", active_low, d_second_low, preferred_element_type=f32)
    d_active = jnp.einsum("td,hd->th", d_second_low, down_weight, preferred_element_type=f32)
    (d_hidden,) = gelu_back(d_active)
    d_hidden_low = d_hidden.astype(bf16)
    d_bias_up = column_sum(d_hidden_low)
    d_up_weight = jnp.einsum("td,th->dh", normed_low, d_hidden_low, preferred_element_type=f32)
    d_normed = d_residual_two + jnp.einsum(
        "th,dh->td", d_hidden_low, up_weight, preferred_element_type=f32
    )
    d_residual_one, d_gain_one, d_shift_one = back_one(d_normed)
    d_branch_low = d_residual_one.astype(bf16)
    d_bias_out = column_sum(d_branch_low)
    d_out_weight = jnp.einsum("td,te->de", attended, d_branch_low, preferred_element_type=f32)
    d_attended = jnp.einsum("te,de->td", d_branch_low, out_weight, preferred_element_type=f32)
    d_attended = d_attended.astype(bf16).reshape(count_utts, LEN, H, HD)
    d_value = jnp.einsum("bhlm,blhe->bmhe", probs_low, d_attended, preferred_element_type=f32)
    d_probs = jnp.einsum("blhe,bmhe->bhlm", d_attended, value_heads, preferred_element_type=f32)
    d_scores = (
        attn_probs * (d_probs - jnp.sum(attn_probs * d_probs, axis=-1, keepdims=True))
    ).astype(bf16)
    d_query = jnp.einsum("bhlm,bmhe->blhe", d_scores, key_heads, preferred_element_type=f32) * 0.125
    d_key = jnp.einsum("bhlm,blhe->bmhe", d_scores, query_heads, preferred_element_type=f32) * 0.125
    d_projected = jnp.concatenate(
        [
            d_query.reshape(token_rows, D),
            d_key.reshape(token_rows, D),
            d_value.reshape(token_rows, D),
        ],
        axis=1,
    ).astype(bf16)
    d_sums = column_sum(d_projected)
    d_qkv_weight = jnp.einsum("td,te->de", inputs, d_projected, preferred_element_type=f32)
    input_grad = d_residual_one + jnp.einsum(
        "te,de->td", d_projected, qkv_weight, preferred_element_type=f32
    )
    flat_grad = jnp.concatenate(
        [
            matrix_grad.reshape(-1)
            for matrix_grad in (
                d_qkv_weight,
                d_out_weight,
                d_up_weight,
                d_down_weight,
                d_proj_weight,
                d_codebook,
                d_code_weight,
            )
        ]
    )
    vector_gradient = jnp.concatenate(
        [
            d_sums[:D],
            d_sums[2 * D :],
            d_bias_out,
            d_gain_one,
            d_shift_one,
            d_bias_up,
            d_bias_down,
            d_gain_two,
            d_shift_two,
            d_bias_proj,
            quantized_offset_slope,
        ]
    )
    vector_sum, loss_sum = lax.psum((vector_gradient, loss_local), ("dp", "fsdp"))
    grad_shard = lax.psum_scatter(flat_grad, ("dp", "fsdp"), scatter_dimension=0, tiled=True)
    square_sum = lax.psum(jnp.sum(grad_shard * grad_shard), ("dp", "fsdp"))
    return finish(
        total_masked, square_sum, vector_sum, loss_sum, grad_shard, output_low.reshape(count_utts, LEN, D),
        input_grad.reshape(count_utts, LEN, D), params, moment_one, moment_two, vectors, vector_one, vector_two,
    )


def by_kernels(layer_input, mask_index, distract, code_choice, params, moment_one, moment_two, vectors, vector_one, vector_two):
    total_masked = layer_input.shape[0] * lax.axis_size(("dp", "fsdp")) * MASKED
    kept, output = forward(PIECES_OUT, SENDS_OUT, 1.0 / total_masked, params, layer_input, mask_index, distract, code_choice, vectors)
    grads, sums, squares, input_grad = backward(PIECES_BACK, SENDS_BACK, vectors, kept, lax.axis_size("fsdp"), params.shape[0] // 128)
    new, low, first, second, new_v, first_v, second_v, loss, norm = update(
        total_masked, grads, params, moment_one, moment_two, sums, vectors, vector_one, vector_two, squares
    )
    return loss, norm, output, input_grad, new, low, first, second, new_v, first_v, second_v


def solution(mesh):
    in_specs = (
        P(("dp", "fsdp"), None, None),
        P(("dp", "fsdp"), None),
        P(("dp", "fsdp"), None, None),
        P(("dp", "fsdp"), None, None),
        P(("dp", "fsdp")),
        P(("dp", "fsdp")),
        P(("dp", "fsdp")),
        P(),
        P(),
        P(),
    )
    out_specs = (
        P(),
        P(),
        P(("dp", "fsdp"), None, None),
        P(("dp", "fsdp"), None, None),
        P(("dp", "fsdp")),
        P(("dp", "fsdp")),
        P(("dp", "fsdp")),
        P(("dp", "fsdp")),
        P(),
        P(),
        P(),
    )
    fits = mesh.shape["dp"] == PLANES and mesh.shape["fsdp"] == 8
    return jax.shard_map(
        by_kernels if fits else by_collectives, mesh=mesh, in_specs=in_specs, out_specs=out_specs, check_vma=False
    )
```

```python
import functools

import jax
import jax.numpy as jnp
from jax import lax
from jax.experimental import pallas as pl
from jax.experimental.pallas import tpu as pltpu
from jax.sharding import PartitionSpec as P
D = 768; H = 12; HD = 64; FF = 3072; FINAL = 256; G = 2; V = 320; CD = 128; LEN = 472; MASKED = 232
NROW = 9664; GROW = NROW + 256
T = 512
LT = 480
NB = 240
TILE = 768
STEP_T = 512
bf16 = jnp.bfloat16
f32 = jnp.float32
NT = (((1,), (1,)), ((), ()))
BQ, BV, BO, G1, S1, BUP, BDOWN, G2, S2, BPROJ, BCODE = [768 * i for i in range(6)] + [3840 + 3072 + 768 * i for i in range(3)] + [9216, 9472]

def mm(a, b):
    return jnp.dot(a, b, preferred_element_type=f32)

def mm_nt(a, b, precision=None):
    return lax.dot_general(a, b, NT, preferred_element_type=f32, precision=precision)

def hi(a, b):
    return jnp.dot(a, b, preferred_element_type=f32, precision=lax.Precision.HIGHEST)

def split_rows(g, base, parts, nice, first, tmp):
    def body(b, _):
        src = pl.multiple_of(base + b * 64 * parts, 64)
        for j in range(6):
            tmp[j, 0:64 * parts, :] = g[pl.ds(src, 64 * parts), 128 * j:128 * j + 128].astype(f32)
        for t in range(parts):
            at = pl.multiple_of((first + t) * D + b * 64, 64)
            for j in range(6):
                nice[pl.ds(at, 64), 128 * j:128 * j + 128] = tmp[j, pl.ds(t, 64, stride=parts), :].astype(bf16)
        return 0
    lax.fori_loop(0, D // 64, body, 0)

def norm_rows(r, gain, shift, low, wide, hat, rstd):
    def body(b, _):
        at = pl.multiple_of(b * NB, 16)
        v = r[pl.ds(at, NB), :]
        m = jnp.mean(v, axis=-1, keepdims=True)
        c = v - m
        var = jnp.mean(c * c, axis=-1, keepdims=True)
        inv = lax.rsqrt(var + eps_norm)
        xh = c * inv
        o = xh * gain + shift
        hat[pl.ds(at, NB), :] = xh
        rstd[pl.ds(at, NB), :] = jnp.broadcast_to(inv, (NB, 128))
        if wide is not None:
            wide[pl.ds(at, NB), :] = o
        low[pl.ds(at, NB), :] = o.astype(bf16)
        return 0
    lax.fori_loop(0, LT // NB, body, 0)

def transpose_to(src, dst, rows, cols):
    step = min(STEP_T, cols // 3)
    def body(n, _):
        at = pl.multiple_of(n * step, step)
        dst[pl.ds(at, step), :] = src[:, pl.ds(at, step)].T
        return 0
    lax.fori_loop(0, cols // step, body, 0)

def prepare(x_ref, xp, xT, mask_ref, distract_ref, choice_ref, vec_ref, vec, place, placeT, allowed, choose):
    for i in range(vec_ref.shape[0]):
        vec[0:1, 128 * i:128 * i + 128] = vec_ref[i:i + 1, :]
    xp[...] = jnp.zeros((T, D), bf16)
    xp[0:LEN, :] = x_ref[0]
    transpose_to(xp, xT, T, D)
    zero = jnp.zeros((1, 256 - MASKED), jnp.int32) - 1
    def wide(row):
        return jnp.concatenate([row, zero], axis=1)
    hot = jnp.where(lax.broadcasted_iota(jnp.int32, (T, 256), 0) == wide(mask_ref[...]), 1.0, 0.0)
    placeT[...] = hot.astype(bf16)
    place[...] = hot.T.astype(bf16)
    row = lax.broadcasted_iota(jnp.int32, (256, 256), 0)
    col = lax.broadcasted_iota(jnp.int32, (256, 256), 1)
    allowed[...] = jnp.where((row == col) & (col < MASKED), 1.0, 0.0)
    rows = [wide(distract_ref[i]) for i in range(distract_ref.shape[0])]
    def body(b, _):
        at = pl.multiple_of(8 * b, 8)
        acc = allowed[pl.ds(at, 8), :]
        n = lax.broadcasted_iota(jnp.int32, (8, 256), 0) + at
        for r in rows:
            acc = jnp.where(n == r, 1.0, acc)
        allowed[pl.ds(at, 8), :] = acc
        return 0
    lax.fori_loop(0, MASKED // 8, body, 0)
    allowed[...] = allowed[...].T
    for g in range(2):
        v = jnp.where(lax.broadcasted_iota(jnp.int32, (384, 256), 0) == wide(choice_ref[0, g:g + 1, :]), 1.0, 0.0)
        choose[g] = v.T

def project(xp, nice, vec, q, kk, kT, vv, vT):
    for t, (dst, bias) in enumerate(((q, BQ), (kk, None), (vv, BV))):
        for n in range(3):
            acc = mm(xp[...], nice[t * D:(t + 1) * D, 256 * n:256 * n + 256])
            if bias is not None:
                acc = acc + vec[0:1, bias + 256 * n:bias + 256 * n + 256]
            dst[:, 256 * n:256 * n + 256] = acc.astype(bf16)
    transpose_to(kk, kT, T, D)
    transpose_to(vv, vT, T, D)

def attend(p, q, kk, vT, pT, attT):
    at = pl.multiple_of(128 * p, 128)
    qp = q[:, pl.ds(at, 128)]
    kp = kk[0:LT, pl.ds(at, 128)]
    lane = lax.broadcasted_iota(jnp.int32, (LT, 128), 1)
    for h in range(2):
        kh = jnp.where((lane < 64) == (h == 0), kp, jnp.zeros_like(kp))
        s = mm_nt(kh, qp)[0:LEN] * 0.125
        e = jnp.exp(s - jnp.max(s, axis=0, keepdims=True))
        pr = e * (1.0 / jnp.sum(e, axis=0, keepdims=True))
        pr = jnp.concatenate([pr, jnp.zeros((T - LEN, T), f32)], axis=0).astype(bf16)
        pT[pl.ds(pl.multiple_of((2 * (p % 2) + h) * T, T), T), :] = pr
        rows = pl.ds(pl.multiple_of(128 * p + 64 * h, 64), 64)
        attT[rows, :] = mm(vT[rows, :], pr).astype(bf16)

def out_project(attT, att, xp, wo, vec, res):
    for n in range(6):
        att[:, 128 * n:128 * n + 128] = attT[128 * n:128 * n + 128, :].T
    for n in range(3):
        cols = slice(256 * n, 256 * n + 256)
        acc = mm(att[0:LT, :], wo[:, cols])
        res[:, cols] = xp[0:LT, cols].astype(f32) + acc + vec[0:1, BO + 256 * n:BO + 256 * n + 256]

def up(n, norm_low, nice, vec, act, gp):
    root = 0.7071067811865476
    scale = 0.3989422804014327
    c = n * TILE // D
    at = pl.multiple_of(n * TILE, TILE)
    w = nice[pl.ds(pl.multiple_of(c * D, D), D), pl.ds(pl.multiple_of(at - c * D, TILE), TILE)]
    h = mm(norm_low[0:LT, :], w) + vec[0:1, pl.ds(pl.multiple_of(BUP + at, 256), TILE)]
    cdf = 0.5 * (1.0 + lax.erf(h * root))
    act[0:LT, pl.ds(at, TILE)] = (h * cdf).astype(bf16)
    gp[0:LT, pl.ds(at, TILE)] = (cdf + h * (scale * jnp.exp(-0.5 * h * h))).astype(bf16)

def down(act, g, vec, res, wide):
    for n in range(3):
        cols = slice(256 * n, 256 * n + 256)
        acc = mm(act[0:LT, :], g[6144:9216, cols])
        res[:, cols] = wide[:, cols] + acc + vec[0:1, BDOWN + 256 * n:BDOWN + 256 * n + 256]

def small_weights(g, fb, p32, c32, wproj, code, wcode):
    for t in range(3):
        for j in range(2):
            p32[j, pl.ds(t, 256, stride=3), :] = g[9216:9472, 256 * t + 128 * j:256 * t + 128 * j + 128].astype(f32)
    for j in range(2):
        wproj[:, 128 * j:128 * j + 128] = p32[j].astype(bf16)
    for j in range(6):
        fb[pl.ds(j, 192, stride=6), :] = g[9472:9664, 128 * j:128 * j + 128].astype(f32)
    a = [fb[pl.ds(j, 128, stride=5), :] for j in range(5)]
    lo = lax.broadcasted_iota(jnp.int32, (128, 128), 1) < 64
    r2, r3, r4 = [pltpu.roll(v, 64, 1) for v in a[2:]]
    zero = jnp.zeros((128, 128), f32)
    even = [a[0], a[1], jnp.where(lo, a[2], zero)]
    odd = [jnp.where(lo, r2, r3), jnp.where(lo, r3, r4), jnp.where(lo, r4, zero)]
    for j in range(3):
        c32[j, pl.ds(0, 128, stride=2), :] = even[j]
        c32[j, pl.ds(1, 128, stride=2), :] = odd[j]
        code[:, 128 * j:128 * j + 128] = c32[j].astype(bf16)
    for j in range(2):
        wcode[:, 128 * j:128 * j + 128] = fb[pl.ds(640 + j, 256, stride=2), :].astype(bf16)

def contrast(weight, out_low, vec, place, placeT, allowed, choose, wproj, code, wcode, fb, p32, c32, tail, dctx, small):
    picked = mm(place[...], out_low[...]).astype(bf16)
    chosen = mm(picked, wproj[...]) + vec[0:1, BPROJ:BPROJ + 256]
    cv = jnp.concatenate([mm_nt(choose[g].astype(bf16), code[128 * g:128 * g + 128, :]) for g in range(2)], axis=1).astype(bf16)
    targets = mm(cv, wcode[...]) + vec[0:1, BCODE:BCODE + 256]
    n_l = lax.rsqrt(jnp.sum(chosen * chosen, axis=1, keepdims=True) + eps_cos)
    n_r = lax.rsqrt(jnp.sum(targets * targets, axis=1, keepdims=True) + eps_cos)
    left = chosen * n_l
    right = targets * n_r
    sim = mm_nt(left, right, lax.Precision.HIGHEST) / 0.1
    ok = allowed[...] > 0.5
    row = lax.broadcasted_iota(jnp.int32, (256, 256), 0)
    col = lax.broadcasted_iota(jnp.int32, (256, 256), 1)
    eye = jnp.where((row == col) & (row < MASKED), 1.0, 0.0)
    pos = jnp.sum(eye * sim, axis=1, keepdims=True)
    top = jnp.max(jnp.where(ok, sim, -1e30), axis=1, keepdims=True)
    parts = jnp.where(ok, jnp.exp(jnp.minimum(sim - top, 0.0)), 0.0)
    real = lax.broadcasted_iota(jnp.int32, (256, 1), 0) < MASKED
    total = jnp.where(real, jnp.sum(parts, axis=1, keepdims=True), 1.0)
    loss = jnp.sum(jnp.where(real, top + jnp.log(total) - pos, 0.0))
    dsim = (weight / 0.1) * (parts / total - eye)
    dl = hi(dsim, right)
    dr = hi(dsim.T, left)
    d_chosen = (n_l * dl - chosen * (n_l * n_l * n_l) * jnp.sum(chosen * dl, axis=1, keepdims=True)).astype(bf16)
    d_target = (n_r * dr - targets * (n_r * n_r * n_r) * jnp.sum(targets * dr, axis=1, keepdims=True)).astype(bf16)
    small[0:1, :] = jnp.sum(d_chosen.astype(f32), axis=0, keepdims=True)
    small[1:2, :] = jnp.sum(d_target.astype(f32), axis=0, keepdims=True)
    small[2:3, :] = jnp.broadcast_to(loss, (1, 256))
    dctx[...] = mm(placeT[...], d_chosen).astype(bf16)
    dproj = mm(picked.T, d_chosen)
    for j in range(2):
        p32[j] = dproj[:, 128 * j:128 * j + 128]
    for t in range(3):
        for j in range(2):
            tail[0:256, 256 * t + 128 * j:256 * t + 128 * j + 128] = p32[j, pl.ds(t, 256, stride=3), :].astype(bf16)
    dwcode = mm(cv.T, d_target)
    dcv = mm_nt(d_target, wcode[...])
    for g in range(2):
        dc = hi(dcv[:, 128 * g:128 * g + 128].T, choose[g])
        for j in range(3):
            c32[j, 128 * g:128 * g + 128, :] = dc[:, 128 * j:128 * j + 128]
    e = [c32[j, pl.ds(0, 128, stride=2), :] for j in range(3)]
    o = [pltpu.roll(c32[j, pl.ds(1, 128, stride=2), :], 64, 1) for j in range(3)]
    lo = lax.broadcasted_iota(jnp.int32, (128, 128), 1) < 64
    for j, v in enumerate((e[0], e[1], jnp.where(lo, e[2], o[0]), jnp.where(lo, o[0], o[1]), jnp.where(lo, o[1], o[2]))):
        fb[pl.ds(j, 128, stride=5), :] = v
    for j in range(2):
        fb[pl.ds(640 + j, 256, stride=2), :] = dwcode[:, 128 * j:128 * j + 128]
    for j in range(6):
        tail[256:448, 128 * j:128 * j + 128] = fb[pl.ds(j, 192, stride=6), :].astype(bf16)
STEP = 10


eps_norm = 1e-05
eps_cos = 1e-06
softness_divisor = 0.1
beta_one = 0.9
beta_two = 0.98
adam_eps = 1e-08
decay_rate = 0.01
rate_matrix = 0.03
rate_vector = 0.2
clip_level = 0.001


def sum8(v):
    r, n = v.shape
    return jnp.sum(v.reshape(r // 8, 8, n), axis=0)

def norm_back_first(dctx, wproj, gain, hat, rstd, low, acc):
    acc[...] = jnp.zeros((24, D), f32)
    def body(b, _):
        at = pl.multiple_of(b * 48, 16)
        dy = mm_nt(dctx[pl.ds(at, 48), :], wproj[...])
        norm_back_rows(dy, at, gain, hat, hat, rstd, low, acc)
        return 0
    lax.fori_loop(0, LT // 48, body, 0)

def norm_back_rows(dy, at, gain, hat, dst, rstd, low, acc):
    xh = hat[pl.ds(at, NB), :]
    inv = rstd[pl.ds(at, NB), 0:1]
    a = dy * gain
    m1 = jnp.mean(a, axis=-1, keepdims=True)
    m2 = jnp.mean(a * xh, axis=-1, keepdims=True)
    dr = inv * (a - m1 - xh * m2)
    lo = dr.astype(bf16)
    dst[pl.ds(at, NB), :] = dr
    low[pl.ds(at, NB), :] = lo
    acc[0:8, :] += sum8(dy * xh)
    acc[8:16, :] += sum8(dy)
    acc[16:24, :] += sum8(lo.astype(f32))

def norm_back(dy, gain, hat, rstd, low, acc):
    acc[...] = jnp.zeros((24, D), f32)
    def body(b, _):
        at = pl.multiple_of(b * NB, 16)
        norm_back_rows(dy[pl.ds(at, NB), :], at, gain, hat, hat, rstd, low, acc)
        return 0
    lax.fori_loop(0, LT // NB, body, 0)

def put_vec(vg, acc, offsets):
    for i, o in enumerate(offsets):
        vg[0:1, o:o + D] = jnp.sum(acc[8 * i:8 * i + 8, :], axis=0, keepdims=True)

def down_back(n, low2, gg, actT, gp, vg):
    at = pl.multiple_of(n * TILE, TILE)
    rows = pl.ds(pl.multiple_of(6144 + n * TILE, 256), TILE)
    d = mm_nt(low2[0:LT, :], gg[rows, :]) * gp[0:LT, pl.ds(at, TILE)].astype(f32)
    d = d.astype(bf16)
    gp[0:LT, pl.ds(at, TILE)] = d
    vg[0:1, pl.ds(pl.multiple_of(BUP + at, 128), TILE)] = jnp.sum(d.astype(f32), axis=0, keepdims=True)
    gg[rows, :] = mm(actT[pl.ds(at, TILE), :], low2[...]).astype(bf16)

def up_back_x(n, dh, gg, dr):
    cols = pl.ds(pl.multiple_of(n * 256, 256), 256)
    v = dr[:, cols]
    for c in range(4):
        w = gg[pl.ds(pl.multiple_of(3072 + c * D + n * 256, 256), 256), :]
        v = v + mm_nt(dh[0:LT, c * D:(c + 1) * D], w)
    dr[:, cols] = v

WEAVE = 384

def weave(lhsT, rhs, parts, n, base, gg, tmp, stacked):
    def body(m, _):
        cols = pl.ds(pl.multiple_of(m * 256, 256), 256)
        for t in range(parts):
            r = rhs[t, :, cols] if stacked else rhs[:, pl.ds(pl.multiple_of(t * D + m * 256, 256), 256)]
            acc = mm(lhsT[pl.ds(pl.multiple_of(n * WEAVE, WEAVE), WEAVE), :], r)
            for j in range(2):
                tmp[j, pl.ds(t, WEAVE, stride=parts), :] = acc[:, 128 * j:128 * j + 128]
        for j in range(2):
            gg[pl.ds(pl.multiple_of(base + n * WEAVE * parts, 128), WEAVE * parts), pl.ds(pl.multiple_of(m * 256 + 128 * j, 128), 128)] = tmp[j, 0:WEAVE * parts, :].astype(bf16)
        return 0
    lax.fori_loop(0, 3, body, 0)

def out_back(low1, gg, attT, da):
    for n in range(3):
        cols = slice(256 * n, 256 * n + 256)
        da[0:LT, cols] = mm_nt(low1[0:LT, :], gg[2304 + 256 * n:2304 + 256 * n + 256, :]).astype(bf16)
    for n in range(3):
        gg[2304 + 256 * n:2304 + 256 * n + 256, :] = mm(attT[256 * n:256 * n + 256, :], low1[...]).astype(bf16)

def attend_back(p, da, q, kT, vv, ring, dp, dqT):
    at = pl.multiple_of(128 * p, 128)
    lane = lax.broadcasted_iota(jnp.int32, (T, 128), 1)
    dap = da[:, pl.ds(at, 128)]
    qp = q[:, pl.ds(at, 128)]
    vp = vv[0:LT, pl.ds(at, 128)]
    dk = dv = None
    for h in range(2):
        half = (lane < 64) == (h == 0)
        dah = jnp.where(half, dap, jnp.zeros_like(dap))
        qh = jnp.where(half, qp, jnp.zeros_like(qp))
        pr = ring[pl.ds(pl.multiple_of(((2 * p + h) % 6) * T, T), LT), :]
        dpT = mm_nt(vp, dah)
        prf = pr.astype(f32)
        w = prf * dpT
        ds = (w - prf * jnp.sum(w, axis=0, keepdims=True)).astype(bf16)
        a = mm(pr, dah)
        b = mm(ds, qh)
        dv = a if dv is None else dv + a
        dk = b if dk is None else dk + b
        rows = pl.ds(pl.multiple_of(128 * p + 64 * h, 64), 64)
        dqT[rows, :] = (mm(kT[rows, 0:LT], ds) * 0.125).astype(bf16)
    dp[1, 0:LT, pl.ds(at, 128)] = (dk * 0.125).astype(bf16)
    dp[2, 0:LT, pl.ds(at, 128)] = dv.astype(bf16)
    dp[0, :, pl.ds(at, 128)] = dqT[pl.ds(at, 128), :].T

def input_back(n, dp, wq, dr):
    cols = slice(256 * n, 256 * n + 256)
    v = dr[:, cols]
    for t in range(3):
        v = v + mm_nt(dp[t, 0:LT, :], wq[t * D + 256 * n:t * D + 256 * n + 256, :])
    dr[:, cols] = v
MESH = pl.DeviceIdType.MESH
UP, DOWN, U, V_AXIS, CORE = range(5)
PLANES = 4
MAIN = 288
EXTRA = 16
HALF = MAIN + EXTRA
RAW = 96
PLANE = 2416
UNIT = 608

class Place:
    def __init__(self):
        self.z = lax.axis_index("dp")
        self.f = f = lax.axis_index("fsdp")
        self.c = c = f % 2
        self.k = k = f // 2
        x = k % 2
        y = k // 2
        self.fc = f + 1 - 2 * c
        self.fx = f + 2 - 4 * x
        self.fy = f + 4 - 8 * y
        self.uf = self.fx * (1 - c) + self.fy * c
        self.vf = self.fy * (1 - c) + self.fx * c
        self.roles = (k, self.uf // 2, self.vf // 2, 3 - k)

    def greet(self):
        z = self.z
        bar = pltpu.get_barrier_semaphore()
        for t in (self.fc, self.fx, self.fy):
            pl.semaphore_signal(bar, inc=1, device_id=(z, t), device_id_type=MESH)
        @pl.when(z > 0)
        def _(): pl.semaphore_signal(bar, inc=1, device_id=(z - 1, self.f), device_id_type=MESH)
        @pl.when(z < PLANES - 1)
        def _(): pl.semaphore_signal(bar, inc=1, device_id=(z + 1, self.f), device_id_type=MESH)
        pl.semaphore_wait(bar, 3 + (z + PLANES - 1) // PLANES + (2 * PLANES - 2 - z) // PLANES)

    def greet_all(self, count):
        bar = pltpu.get_barrier_semaphore()
        for j in range(1, count):
            pl.semaphore_signal(bar, inc=1, device_id=(self.z, lax.rem(self.f + j, count)), device_id_type=MESH)
        for j in range(1, PLANES):
            pl.semaphore_signal(bar, inc=1, device_id=(lax.rem(self.z + j, PLANES), self.f), device_id_type=MESH)
        pl.semaphore_wait(bar, count + PLANES - 2)

    def span_of(self, p, kk, c, first):
        m = PLANE * p + UNIT * kk
        return (pl.multiple_of(m + HALF * c + first, 16),
                pl.multiple_of((m + MAIN) * (1 - c) + (NROW + EXTRA * (4 * p + kk)) * c, 16))

    def span(self, p, r, c, first):
        return self.span_of(p, self.roles[r], c, first)

def remote(src, dst, ssem, rsem, dev):
    return pltpu.make_async_remote_copy(src_ref=src, dst_ref=dst, send_sem=ssem, recv_sem=rsem, device_id=dev, device_id_type=MESH)

def shared_blocks(g, p):
    row = lax.broadcasted_iota(jnp.int32, (16, D), 0)
    e = [g[NROW + 16 * (4 * p + q):NROW + 16 * (4 * p + q) + 16, :].astype(f32) for q in range(4)]
    for q, bound in enumerate((12, 8, 4)):
        at = PLANE * p + UNIT * q + 592
        g[at:at + 16, :] = jnp.where(row < bound, e[q], e[q + 1]).astype(bf16)

def extra_rows(g, p, q):
    row = lax.broadcasted_iota(jnp.int32, (16, D), 0)
    b = [g[PLANE * p + UNIT * i + 592:PLANE * p + UNIT * i + 608, :].astype(f32) for i in range(max(q - 1, 0), min(q, 2) + 1)]
    v = b[0] if len(b) == 1 else jnp.where(row < 12 - 4 * q, b[1], b[0])
    g[NROW + 16 * (4 * p + q):NROW + 16 * (4 * p + q) + 16, :] = v.astype(bf16)

def wait_sent(g, rows, ssem, rsem, dev):
    if rows:
        ref = g.at[pl.ds(0, rows)]
        remote(ref, ref, ssem, rsem, dev).wait_send()

class Gather:
    def __init__(self, at, g, pieces, R, O, S):
        self.at, self.g, self.pieces, self.R, self.O, self.S = at, g, pieces, R, O, S
        self.sent = {z: [0, 0] for z in range(PLANES)}
        self.seen = set()

    def copies(self, i, p, r, dev, kind):
        _, first, rows, extra = self.pieces[p][i]
        a, e = self.at.span(p, r, self.at.c, first)
        unit = 4 * p + self.at.roles[r]
        out = []
        for s, n in [(a, rows)] + [(e, EXTRA)] * extra:
            ref = self.g.at[pl.ds(s, n)]
            out.append(remote(ref, ref, self.S.at[int(kind == CORE)], self.O.at[p] if kind == CORE else self.R.at[unit, i], dev))
        return out

    def op(self, zs, kind, i, p, r):
        at = self.at
        _, _, rows, extra = self.pieces[p][i]
        rows += EXTRA * extra
        if not (p == zs and r == 0) and (zs, i, p, r) not in self.seen:
            self.seen.add((zs, i, p, r))
            ref = self.g.at[pl.ds(0, rows)]
            remote(ref, ref, self.S.at[0], self.R.at[4 * p + at.roles[r], i], (zs, at.fc)).wait_recv()
        dev = ((zs + 1, at.f), (zs - 1, at.f), (zs, at.uf), (zs, at.vf), (zs, at.fc))[kind]
        for q in self.copies(i, p, r, dev, kind): q.start()
        self.sent[zs][int(kind == CORE)] += rows

    def other_core(self, zs, p):
        ref = self.g.at[pl.ds(0, HALF * (3 if p == zs else 4))]
        remote(ref, ref, self.S.at[1], self.O.at[p], (zs, self.at.fc)).wait_recv()

    def drain(self):
        for zs in range(PLANES):
            @pl.when(self.at.z == zs)
            def _():
                for i in range(2): wait_sent(self.g, self.sent[zs][i], self.S.at[i], self.O.at[0], (zs, self.at.fc))

def own_rows(at, g, p_ref, raw, sem):
    n = p_ref.shape[0]
    gap = -n % 8
    base = pl.multiple_of(RAW + (n + gap) * at.c, 8)
    mine = pltpu.make_async_copy(p_ref.at[pl.ds(0, n)], raw.at[pl.ds(base, n)], sem.at[2])
    mine.start()
    both = remote(p_ref.at[pl.ds(0, n)], raw.at[pl.ds(base, n)], sem.at[0], sem.at[1], (at.z, at.fc))
    both.start()
    mine.wait()
    both.wait()
    k = at.k
    own = pl.multiple_of(PLANE * at.z + UNIT * k, 16)
    extra = pl.multiple_of(NROW + EXTRA * (4 * at.z + k), 16)
    row = lax.broadcasted_iota(jnp.int32, (16, 128), 0)
    first_core = lax.broadcasted_iota(jnp.int32, (592, 128), 0) + 4 * k < n // 6
    for j in range(6):
        cols = slice(128 * j, 128 * j + 128)
        v = [raw[pl.ds(RAW + gap * i + 24 * k + j, 592, stride=6), :] for i in range(2)]
        g[pl.ds(own, 592), cols] = jnp.where(first_core, v[0], v[1]).astype(bf16)
        last = raw[pl.ds(RAW + gap + (592 + 4 * k) * 6 + j, 16, stride=6), :]
        first = raw[pl.ds(RAW - 96 + 24 * k + j, 16, stride=6), :]
        g[pl.ds(extra, 16), cols] = jnp.where(row < 12 - 4 * k, last, first).astype(bf16)

K1_OUT = ("w", "wproj", "tail", "dctx", "small", "hat1", "r1", "hat2", "r2", "gp", "actT", "normT", "attT", "q", "kT", "vv", "xT", "pT")
K1_SHAPE = {"w": ((NROW, D), bf16), "wproj": ((D, 256), bf16), "tail": ((448, D), bf16), "dctx": ((T, 256), bf16), "small": ((8, 256), f32),
            "hat1": ((LT, D), f32), "r1": ((LT, 128), f32), "hat2": ((LT, D), f32), "r2": ((LT, 128), f32), "gp": ((T, FF), bf16), "actT": ((FF, T), bf16),
            "normT": ((D, T), bf16), "attT": ((D, T), bf16), "q": ((T, D), bf16), "kT": ((D, T), bf16), "vv": ((T, D), bf16), "xT": ((D, T), bf16),
            "pT": ((H * T, T), bf16)}

def forward_kernel(pieces, events, weight, p_ref, x, mask, dis, cho, vec_ref, *rest):
    n_out = len(K1_OUT)
    hbm = dict(zip(K1_OUT, rest[:n_out]))
    (out, vec, g, raw, nice, tmp, wproj, tail, dctx, small, hat1, r1, hat2, r2, gp, actT, normT, attT, q, kT, vv, xT, pT,
     xp, kk, vT, act, res, wide, low1, low2, place, placeT, allowed, choose, fb, p32, c32, code, wcode,
     sem_raw, R, O, S, OS, PS) = rest[n_out:]
    here = dict(wproj=wproj, tail=tail, dctx=dctx, small=small, hat1=hat1, r1=r1, hat2=hat2, r2=r2, gp=gp, actT=actT, normT=normT, attT=attT, q=q, kT=kT, vv=vv, xT=xT, pT=pT)
    outs = []
    count = iter(range(32))
    def put(src, dst):
        cp = pltpu.make_async_copy(src, dst, OS.at[next(count)])
        cp.start()
        outs.append(cp)
    def save(*names):
        for n in names: put(here[n], hbm[n])
    at = Place()
    ga = Gather(at, g, pieces, R, O, S)
    at.greet()
    own_rows(at, g, p_ref, raw, sem_raw)
    def slot(i, cond=None):
        for zs in range(PLANES):
            if events[zs][i]:
                @pl.when((at.z == zs) if cond is None else ((at.z == zs) & cond))
                def _():
                    for e in events[zs][i]: ga.op(zs, *e)
    def plane(p):
        for zs in range(PLANES):
            @pl.when(at.z == zs)
            def _(): ga.other_core(zs, p)
        shared_blocks(g, p)
    slot(0)
    prepare(x, xp, xT, mask, dis, cho, vec_ref, vec, place, placeT, allowed, choose)
    act[LT:T, :] = jnp.zeros((T - LT, FF), bf16)
    gp[LT:T, :] = jnp.zeros((T - LT, FF), bf16)
    low1[...] = jnp.zeros((T, D), bf16)
    low2[...] = jnp.zeros((T, D), bf16)
    small[...] = jnp.zeros((8, 256), f32)
    save("xT")
    slot(1)
    plane(0)
    split_rows(g, 0, 3, nice, 0, tmp)
    slot(2)
    project(xp, nice, vec, q, kk, kT, vv, vT)
    save("q", "kT", "vv")
    put(nice.at[pl.ds(0, 2304)], hbm["w"].at[pl.ds(0, 2304)])
    nice_out = outs.pop()
    slot(3)
    slot(4)
    def pair_out(p):
        b = p % 2
        return pltpu.make_async_copy(pT.at[pl.ds(pl.multiple_of(2 * T * b, T), 2 * T)], hbm["pT"].at[pl.ds(pl.multiple_of(2 * T * p, T), 2 * T)], PS.at[b])
    def pairs(b, _):
        p = 2 * b
        @pl.when(b > 0)
        def _():
            pair_out(p - 2).wait()
            pair_out(p - 1).wait()
        attend(p, q, kk, vT, pT, attT)
        attend(p + 1, q, kk, vT, pT, attT)
        pair_out(p).start()
        pair_out(p + 1).start()
        for i in range(3): slot(5 + i, b == i)
        return 0
    lax.fori_loop(0, H // 4, pairs, 0)
    pair_out(H // 2 - 2).wait()
    pair_out(H // 2 - 1).wait()
    save("attT")
    plane(1)
    out_project(attT, kk, xp, g.at[2304:3072], vec, res)
    put(g.at[pl.ds(2304, 768)], hbm["w"].at[pl.ds(2304, 768)])
    norm_rows(res, vec[0:1, G1:G1 + D], vec[0:1, S1:S1 + D], low1, wide, hat1, r1)
    save("hat1", "r1")
    transpose_to(low1, normT, T, D)
    save("normT")
    slot(8)
    plane(2)
    nice_out.wait()
    split_rows(g, 3072, 4, nice, 0, tmp)
    put(nice, hbm["w"].at[pl.ds(3072, 3072)])
    slot(9)
    def tile(n, _):
        up(n, low1, nice, vec, act, gp)
        for i in range(3): slot(10 + i, n == i)
        return 0
    lax.fori_loop(0, FF // TILE, tile, 0)
    slot(13)
    save("gp")
    transpose_to(act, actT, T, FF)
    save("actT")
    slot(14)
    plane(3)
    put(g.at[pl.ds(6144, 3072)], hbm["w"].at[pl.ds(6144, 3072)])
    down(act, g, vec, res, wide)
    norm_rows(res, vec[0:1, G2:G2 + D], vec[0:1, S2:S2 + D], low2, None, hat2, r2)
    save("hat2", "r2")
    out[0] = low2[0:LEN, :]
    small_weights(g, fb, p32, c32, wproj, code, wcode)
    save("wproj")
    slot(15)
    contrast(weight, low2, vec, place, placeT, allowed, choose, wproj, code, wcode, fb, p32, c32, tail, dctx, small)
    save("tail", "dctx", "small")
    slot(16)
    ga.drain()
    for cp in outs: cp.wait()

def forward(pieces, events, weight, params, x, mask, dis, cho, vec):
    V_ = pl.BlockSpec(memory_space=pltpu.VMEM)
    A_ = pl.BlockSpec(memory_space=pl.ANY)
    VM = pltpu.VMEM
    DMA = pltpu.SemaphoreType.DMA
    sds = jax.ShapeDtypeStruct
    n = params.shape[0] // 128
    most = max(len(ps) for ps in pieces)
    here = [VM(*K1_SHAPE[k]) for k in K1_OUT[1:-1]] + [VM((4 * T, T), bf16)]
    outs = pl.pallas_call(functools.partial(forward_kernel, pieces, events, weight),
        out_shape=[sds(*K1_SHAPE[k]) for k in K1_OUT] + [sds((1, LEN, D), bf16)],
        in_specs=[A_] + [V_] * 5, out_specs=[A_] * len(K1_OUT) + [V_],
        scratch_shapes=[VM((1, vec.shape[0]), f32), VM((GROW, D), bf16), VM((RAW + 2 * (n + 4) + 96, 128), f32), VM((4 * D, D), bf16), VM((6, 256, 128), f32)] + here
            + [VM((T, D), bf16), VM((T, D), bf16), VM((D, T), bf16), VM((T, FF), bf16), VM((LT, D), f32), VM((LT, D), f32), VM((T, D), bf16), VM((T, D), bf16),
               VM((256, T), bf16), VM((T, 256), bf16), VM((256, 256), f32), VM((2, 256, 384), f32), VM((1152, 128), f32), VM((2, 768, 128), f32), VM((3, 256, 128), f32),
               VM((256, 384), bf16), VM((256, 256), bf16),
               DMA((3,)), DMA((16, most)), DMA((PLANES,)), DMA((2,)), DMA((24,)), DMA((2,))],
        compiler_params=pltpu.CompilerParams(collective_id=0, has_side_effects=True, vmem_limit_bytes=63 * 2**20),
    )(params.reshape(n, 128), x, mask, jnp.transpose(dis, (2, 0, 1)), jnp.swapaxes(cho, 1, 2), vec.reshape(-1, 128))
    return dict(zip(K1_OUT, outs)), outs[-1]
TO_CORE, TO_V, TO_U, TO_Z, KEEP, SMALL = range(6)

class Reduce:
    def __init__(self, at, g, pieces, LD, LV, LZ, LU, total, RD, RV, RZ, RU, S):
        self.at, self.g, self.pieces, self.total = at, g, pieces, total
        self.LD, self.LV, self.LZ, self.LU = LD, LV, LZ, LU
        self.RD, self.RV, self.RZ, self.RU, self.S = RD, RV, RZ, RU, S
        self.sent = {z: 0 for z in range(PLANES)}
        self.seen = set()

    def copies(self, p, r, c, first, rows, extra, land, got, dev):
        a, e = self.at.span(p, r, c, first)
        out = []
        for s, n, to in [(a, rows, first)] + [(e, EXTRA, MAIN)] * extra:
            out.append(remote(self.g.at[pl.ds(s, n)], land.at[pl.ds(to, n)], self.S.at[0], got, dev))
        return out

    def build(self, zs, op):
        at = self.at
        kind, i, p, r = op
        unit = 4 * p + at.roles[r]
        _, first, rows, extra = self.pieces[p][i]
        if kind == TO_V:
            n = 2 * p + r - 2
            return self.copies(p, r, at.c, first, rows, extra, self.LV.at[n], self.RV.at[n, i], (zs, at.vf))
        if kind == TO_U:
            return self.copies(p, r, at.c, first, rows, extra, self.LU.at[p], self.RU.at[p, i], (zs, at.uf))
        up = p > zs
        to = zs + 1 if up else zs - 1
        n = 8 + r if (not up and to == p) else 2 * p + r
        return self.copies(p, r, at.c, first, rows, extra, self.LZ.at[n], self.RZ.at[n, i], (to, at.f))

    def once(self, zs, key, rows, got):
        if (zs, key) not in self.seen:
            self.seen.add((zs, key))
            ref = self.g.at[pl.ds(0, rows)]
            remote(ref, ref, self.S.at[0], got, (zs, self.at.fc)).wait_recv()

    def send(self, zs, op):
        for q in self.build(zs, op): q.start()
        _, _, rows, extra = self.pieces[op[2]][op[1]]
        self.sent[zs] += rows + EXTRA * extra

    def add(self, p, r, first, rows, extra, lands, final):
        a, e = self.at.span(p, r, self.at.c, first)
        g, total = self.g, self.total
        def one(s, i):
            v = g[pl.ds(s, 16), :].astype(f32)
            for land in lands:
                v = v + land[pl.ds(i, 16), :].astype(f32)
            if final:
                total[pl.ds(16 + i, 16), :] = v
            else:
                g[pl.ds(s, 16), :] = v.astype(bf16)
        def body(b, _):
            one(pl.multiple_of(a + 16 * b, 16), pl.multiple_of(first + 16 * b, 16))
            return 0
        lax.fori_loop(0, rows // 16, body, 0)
        if extra: one(e, MAIN)

    def op(self, zs, op):
        at = self.at
        kind, i, p, r = op
        unit = 4 * p + at.roles[r]
        self.once(zs, (TO_CORE, p, r), HALF, self.RD.at[unit])
        path, first, rows, extra = self.pieces[p][i]
        if kind == TO_V:
            self.add(p, r, first, rows, extra, [self.LD.at[unit]], False)
            self.send(zs, op)
            return
        n = 2 * p + r
        self.once(zs, ("v", i, p, r), rows + EXTRA * extra, self.RV.at[n, i])
        lands = [self.LD.at[unit], self.LV.at[n]]
        def arrived(land, got, key):
            self.once(zs, key, rows + EXTRA * extra, got)
            lands.append(land)
        if path == 0 or r == 0:
            if p >= zs and zs > 0: arrived(self.LZ.at[n], self.RZ.at[n, i], (UP, i, p, r))
            if p <= zs and zs < PLANES - 1:
                m = 8 + r if p == zs else n
                arrived(self.LZ.at[m], self.RZ.at[m, i], (DOWN, i, p, r))
        if r == 0 and (path == 1 or p == zs):
            arrived(self.LU.at[p], self.RU.at[p, i], (TO_U, i, p))
        self.add(p, r, first, rows, extra, lands, kind == KEEP)
        if kind != KEEP: self.send(zs, op)

    def core_copies(self, p, kk):
        a, e = self.at.span_of(p, kk, 1 - self.at.c, 0)
        land = self.LD.at[4 * p + kk]
        dev = (self.at.z, self.at.fc)
        return [remote(self.g.at[pl.ds(s, n)], land.at[pl.ds(to, n)], self.S.at[1], self.RD.at[4 * p + kk], dev)
                for s, n, to in ((a, MAIN, 0), (e, EXTRA, MAIN))]

    def to_core(self, p, kk):
        extra_rows(self.g, p, kk)
        for q in self.core_copies(p, kk): q.start()

    def drain(self):
        for zs in range(PLANES):
            @pl.when(self.at.z == zs)
            def _(): wait_sent(self.g, self.sent[zs], self.S.at[0], self.RD.at[0], (zs, self.at.fc))
        wait_sent(self.g, 4 * PLANES * HALF, self.S.at[1], self.RD.at[0], (self.at.z, self.at.fc))

class Spread:
    def __init__(self, at, own, land, zland, S, count):
        self.at, self.own, self.land, self.zland, self.S, self.count = at, own, land, zland, S, count

    def round(self, n, me, land, base, dev):
        return [remote(self.own, land.at[me], self.S.at[0, base + j], self.S.at[1, base + j], dev(lax.rem(me + j, n))) for j in range(1, n)]

    def plane(self):
        return self.round(self.count, self.at.f, self.land, 0, lambda t: (self.at.z, t))

    def planes(self):
        return self.round(PLANES, self.at.z, self.zland, self.count, lambda t: (t, self.at.f))

    def first(self):
        for q in self.plane(): q.start()

    def total(self, land, n, me):
        land[me] = self.own[...]
        v = land[0]
        for j in range(1, n): v = v + land[j]
        return v

    def second(self):
        for q in self.plane(): q.wait()
        self.own[...] = self.total(self.land, self.count, self.at.f)
        for q in self.planes(): q.start()

    def last(self):
        for q in self.planes(): q.wait()
        self.own[...] = self.total(self.zland, PLANES, self.at.z)

K2_IN = K1_OUT
K2_HERE = ("wproj", "dctx", "small", "hat1", "r1", "hat2", "r2", "gp", "ring", "normT", "attT", "q", "kT", "vv", "xT", "wq")

def backward_kernel(pieces, events, vec_ref, *rest):
    n_in = len(K2_IN)
    hbm = dict(zip(K2_IN, rest[:n_in]))
    (grad, vsum, sq, ig_out, g, vec, wproj, dctx, small, hat1, r1, hat2, r2, gp, ring, normT, attT, q, kT, vv, xT, wq,
     low1, low2, acc, tmp, dp, LD, LV, LZ, LU, total, flat, vg, vland, vzland, sqv, sland, szland,
     IS, RD, RV, RZ, RU, S, TS, TL, VS, SS) = rest[n_in:]
    here = dict(wproj=wproj, dctx=dctx, small=small, hat1=hat1, r1=r1, hat2=hat2, r2=r2, gp=gp, normT=normT, attT=attT, q=q, kT=kT, vv=vv, xT=xT)
    loads = {}
    def load(name, src=None, dst=None):
        cp = pltpu.make_async_copy(hbm[name] if src is None else src, here[name] if dst is None else dst, IS.at[len(loads)])
        cp.start()
        loads[name if src is None else (name, len(loads))] = cp
        return cp
    w = hbm["w"]
    first = [load(n) for n in ("dctx", "wproj", "hat2", "r2")]
    def second(n):
        rows = pl.ds(pl.multiple_of(6144 + n * TILE, 256), TILE)
        own = pl.ds(pl.multiple_of(n * TILE, TILE), TILE)
        pairs = ((w.at[rows], g.at[rows]), (hbm["actT"].at[own], ring.at[own]), (hbm["gp"].at[:, own], gp.at[:, own]))
        return [pltpu.make_async_copy(s, d, TL.at[3 * n + i]) for i, (s, d) in enumerate(pairs)]
    for n in range(FF // TILE - 1, -1, -1):
        for cp in second(n): cp.start()
    tail = load("tail", hbm["tail"], g.at[pl.ds(9216, 448)])
    third = [load("w", w.at[pl.ds(3072, 3072)], g.at[pl.ds(3072, 3072)]), load("normT")]
    fifth = [load("w", w.at[pl.ds(2304, 768)], g.at[pl.ds(2304, 768)]), load("attT")]
    sixth = [load("q"), load("kT"), load("vv")]
    seventh = [load("xT"), load("w", w.at[pl.ds(0, 2304)], wq)]
    def ready(cs):
        for cp in cs: cp.wait()
    at = Place()
    at.greet_all(vland.shape[0])
    re = Reduce(at, g, pieces, LD, LV, LZ, LU, total, RD, RV, RZ, RU, S)
    vs = Spread(at, vg, vland, vzland, VS, vland.shape[0])
    ss = Spread(at, sqv, sland, szland, SS, vland.shape[0])
    def slot(i, cond=None):
        for zs in range(PLANES):
            if events[zs][i]:
                @pl.when((at.z == zs) if cond is None else ((at.z == zs) & cond))
                def _():
                    for e in events[zs][i]:
                        if e[0] == SMALL: (vs.first, vs.second, vs.last)[e[1]]()
                        else: re.op(zs, e)
    for i in range(vec_ref.shape[0]):
        vec[0:1, 128 * i:128 * i + 128] = vec_ref[i:i + 1, :]
    low2[...] = jnp.zeros((T, D), bf16)
    low1[...] = jnp.zeros((T, D), bf16)
    for t in range(3):
        dp[t] = jnp.zeros((T, D), bf16)
    ready(first)
    for n in range(3):
        hat1[:, 256 * n:256 * n + 256] = mm_nt(dctx[0:LT, :], wproj[256 * n:256 * n + 256, :])
    norm_back(hat1, vec[0:1, G2:G2 + D], hat2, r2, low2, acc)
    fourth = [load("hat1"), load("r1"), load("small")]
    put_vec(vg, acc, (G2, S2, BDOWN))
    ready([tail])
    def downs(n, _):
        ready(second(3 - n))
        down_back(3 - n, low2, g, ring, gp, vg)
        for kk, last in ((3, 0), (2, 0), (1, 1), (0, 2)):
            @pl.when(n == last)
            def _(): re.to_core(3, kk)
        return 0
    lax.fori_loop(0, 3, downs, 0)
    slot(0)
    slot(1)
    ready(second(0))
    down_back(0, low2, g, ring, gp, vg)
    def head(h):
        return pltpu.make_async_copy(hbm["pT"].at[pl.ds(pl.multiple_of(h * T, T), T)], ring.at[pl.ds(pl.multiple_of((h % 6) * T, T), T)], TS.at[h % 6])
    for h in range(6): head(h).start()
    slot(2)
    ready(third)
    lax.fori_loop(0, 3, lambda n, _: (up_back_x(n, gp, g, hat2), 0)[1], 0)
    slot(3)
    weave(normT, gp, 4, 1, 3072, g, tmp, False)
    for kk in (3, 2, 1, 0): re.to_core(2, kk)
    slot(4)
    slot(5)
    slot(6)
    weave(normT, gp, 4, 0, 3072, g, tmp, False)
    re.to_core(1, 2)
    re.to_core(1, 3)
    slot(7)
    ready(fourth)
    norm_back(hat2, vec[0:1, G1:G1 + D], hat1, r1, low1, acc)
    put_vec(vg, acc, (G1, S1, BO))
    ready(fifth)
    da, dqT = low2, normT
    out_back(low1, g, attT, da)
    re.to_core(1, 0)
    re.to_core(1, 1)
    slot(8)
    slot(9)
    ready(sixth)
    def pairs(b, _):
        for p in (2 * b, 2 * b + 1):
            head(2 * p).wait()
            head(2 * p + 1).wait()
        attend_back(2 * b, da, q, kT, vv, ring, dp, dqT)
        attend_back(2 * b + 1, da, q, kT, vv, ring, dp, dqT)
        for p in (2 * b, 2 * b + 1):
            @pl.when(p < 3)
            def _():
                head(2 * p + 6).start()
                head(2 * p + 7).start()
        for i in range(3): slot(10 + i, b == i)
        return 0
    lax.fori_loop(0, H // 4, pairs, 0)
    ready(seventh)
    def wove(n, _):
        weave(xT, dp, 3, n, 0, g, tmp, True)
        for kk in range(4):
            @pl.when(n == min(kk, 1))
            def _(): re.to_core(0, kk)
        for i in range(2): slot(13 + i, n == i)
        return 0
    lax.fori_loop(0, 2, wove, 0)
    slot(15)
    slot(16)
    vg[0:1, BQ:BQ + D] = jnp.sum(dp[0].astype(f32), axis=0, keepdims=True)
    vg[0:1, BV:BV + D] = jnp.sum(dp[2].astype(f32), axis=0, keepdims=True)
    vg[0:1, BPROJ:BPROJ + 256] = small[0:1, :]
    vg[0:1, BCODE:BCODE + 256] = small[1:2, :]
    vg[0:1, BCODE + 256:BCODE + 512] = small[2:3, :]
    slot(17)
    slot(18)
    for n in range(3):
        input_back(n, dp, wq, hat1)
    put_ig = pltpu.make_async_copy(hat1.at[pl.ds(0, LEN)], ig_out.at[0], IS.at[len(loads)])
    put_ig.start()
    slot(19)
    z, c, k = at.z, at.c, at.k
    edge = remote(total.at[pl.ds(HALF, 16)], total.at[pl.ds(0, 16)], TS.at[6], TS.at[7], (z, at.fc))
    edge.start()
    row = lax.broadcasted_iota(jnp.int32, (16, D), 0)
    def square(b, acc):
        v = total[pl.ds(pl.multiple_of(16 + 16 * b, 16), 16), :]
        return acc + sum8(v * v)
    acc = lax.fori_loop(0, MAIN // 16, square, jnp.zeros((8, D), f32))
    v = jnp.where((c == 0) | (row < 12 - 4 * k) | (row >= 16 - 4 * k), total[16 + MAIN:16 + HALF, :], 0.0)
    acc = acc + sum8(v * v)
    sqv[...] = sum(acc[:, 128 * j:128 * j + 128] for j in range(6))
    ss.first()
    for i in range(vsum.shape[0]):
        vsum[i:i + 1, :] = vg[0:1, 128 * i:128 * i + 128]
    n = grad.shape[0] // 6
    edge.wait()
    for j in range(6):
        flat[pl.ds(j, 320, stride=6), :] = total[:, 128 * j:128 * j + 128]
    ss.second()
    for j in range(6):
        grad[pl.ds(j, n, stride=6), :] = flat[pl.ds(6 * (16 - 2 * c - 4 * k) + j, n, stride=6), :]
    re.drain()
    ss.last()
    sq[...] = sqv[...]
    put_ig.wait()

def backward(pieces, events, vec, hbm, count, n):
    V_ = pl.BlockSpec(memory_space=pltpu.VMEM)
    A_ = pl.BlockSpec(memory_space=pl.ANY)
    VM = pltpu.VMEM
    DMA = pltpu.SemaphoreType.DMA
    sds = jax.ShapeDtypeStruct
    most = max(len(ps) for ps in pieces)
    nv = vec.shape[0] + 256
    shape = dict(K1_SHAPE, ring=((FF, T), bf16), wq=((3 * D, D), bf16))
    return pl.pallas_call(functools.partial(backward_kernel, pieces, events),
        out_shape=[sds((n, 128), f32), sds((nv // 128, 128), f32), sds((8, 128), f32), sds((1, LEN, D), f32)],
        in_specs=[V_] + [A_] * len(K2_IN), out_specs=[V_] * 3 + [A_],
        scratch_shapes=[VM((GROW, D), bf16), VM((1, vec.shape[0]), f32)] + [VM(*shape[k]) for k in K2_HERE]
            + [VM((T, D), bf16), VM((T, D), bf16), VM((24, D), f32), VM((2, 4 * WEAVE, 128), f32), VM((3, T, D), bf16),
               VM((16, HALF, D), bf16), VM((8, HALF, D), bf16), VM((10, HALF, D), bf16), VM((4, HALF, D), bf16), VM((HALF + 16, D), f32), VM((6 * (HALF + 16), 128), f32),
               VM((1, nv), f32), VM((count, 1, nv), f32), VM((PLANES, 1, nv), f32), VM((8, 128), f32), VM((count, 8, 128), f32), VM((PLANES, 8, 128), f32),
               DMA((24,)), DMA((16,)), DMA((8, most)), DMA((10, most)), DMA((4, most)), DMA((2,)), DMA((8,)), DMA((12,)), DMA((2, count + PLANES)), DMA((2, count + PLANES))],
        compiler_params=pltpu.CompilerParams(collective_id=1, has_side_effects=True, vmem_limit_bytes=63 * 2**20),
    )(vec.reshape(-1, 128), *[hbm[k] for k in K2_IN])

def update_kernel(total, g, p, m1, m2, vg, v, v1, v2, sq, np_, low, n1, n2, nv, nv1, nv2, loss, norm, scale):
    @pl.when(pl.program_id(0) == 0)
    def _():
        n = v.shape[0]
        gv = vg[0:n, :]
        s = jnp.sum(jnp.sum(sq[...], axis=0, keepdims=True), axis=1, keepdims=True)
        s = s + jnp.sum(jnp.sum(gv * gv, axis=0, keepdims=True), axis=1, keepdims=True)
        s = jnp.sqrt(s)
        f = jnp.minimum(1.0, clip_level / (s + 1e-06))
        norm[...] = s
        loss[...] = vg[n:n + 1, 0:1] / total
        scale[...] = jnp.broadcast_to(f, (8, 128))
        nv[...], nv1[...], nv2[...] = adamw_update(v[...], v1[...], v2[...], gv * f, rate_vector)
    new, first, second = adamw_update(p[...], m1[...], m2[...], g[...] * scale[0:1, 0:1], rate_matrix)
    np_[...] = new
    low[...] = new.astype(bf16)
    n1[...] = first
    n2[...] = second

def update(total, g, p, m1, m2, vg, v, v1, v2, sq):
    n, nv = g.shape[0], v.shape[0] // 128
    sds = jax.ShapeDtypeStruct
    rows = 464
    part = pl.BlockSpec((rows, 128), lambda i: (i, 0))
    def whole(*shape): return pl.BlockSpec(shape, lambda i: (0, 0))
    flat = lambda a: a.reshape(-1, 128)
    out = pl.pallas_call(functools.partial(update_kernel, total), grid=(pl.cdiv(n, rows),),
        out_shape=[sds((n, 128), f32), sds((n, 128), bf16), sds((n, 128), f32), sds((n, 128), f32)] + [sds((nv, 128), f32)] * 3 + [sds((1, 1), f32)] * 2,
        in_specs=[part] * 4 + [whole(*vg.shape)] + [whole(nv, 128)] * 3 + [whole(8, 128)],
        out_specs=[part] * 4 + [whole(nv, 128)] * 3 + [whole(1, 1)] * 2,
        scratch_shapes=[pltpu.VMEM((8, 128), f32)],
    )(g, flat(p), flat(m1), flat(m2), vg, flat(v), flat(v1), flat(v2), sq)
    return [a.reshape(-1) for a in out[:7]] + [a.reshape(()) for a in out[7:]]

PIECES_OUT = (((0, 0, 48, False), (0, 48, 48, False), (0, 96, 48, False), (1, 144, 48, False), (1, 192, 32, False), (1, 224, 32, False), (1, 256, 32, True)),
 ((0, 0, 96, False), (0, 96, 96, False), (0, 192, 96, True)), ((1, 0, 144, False), (1, 144, 144, True)), ((0, 0, 192, False), (1, 192, 96, True)))
PIECES_BACK = (((0, 0, 48, False), (0, 48, 48, False), (0, 96, 48, False), (1, 144, 48, False), (1, 192, 32, False), (1, 224, 32, False), (1, 256, 32, True)),
 ((0, 0, 192, False), (1, 192, 48, False), (1, 240, 48, True)), ((1, 0, 96, False), (1, 96, 96, False), (1, 192, 96, True)),
 ((0, 0, 144, False), (0, 144, 144, True)))
SENDS_OUT = ((((0, 0, 0, 0), (0, 1, 0, 0), (3, 0, 0, 0), (3, 1, 0, 0), (3, 2, 0, 0)),
  ((0, 2, 0, 0), (0, 3, 0, 0), (4, 0, 0, 2), (3, 3, 0, 0), (3, 4, 0, 0), (4, 1, 0, 2), (0, 4, 0, 0), (3, 5, 0, 0), (4, 2, 0, 2), (3, 6, 0, 0),
   (0, 5, 0, 0), (4, 0, 1, 0), (2, 0, 0, 0), (2, 1, 0, 0), (0, 6, 0, 0), (2, 2, 0, 0), (4, 3, 0, 2), (2, 3, 0, 0), (4, 4, 0, 2), (2, 4, 0, 0),
   (4, 5, 0, 2), (4, 1, 1, 0), (2, 5, 0, 0), (4, 6, 0, 2), (2, 6, 0, 0), (3, 0, 1, 0), (0, 0, 0, 1), (4, 0, 0, 1), (0, 1, 0, 1), (4, 1, 0, 1),
   (3, 0, 0, 1), (0, 2, 0, 1), (4, 2, 0, 1), (4, 3, 0, 1), (3, 1, 0, 1), (4, 4, 0, 1), (3, 2, 0, 1), (4, 5, 0, 1), (4, 2, 1, 0), (3, 3, 0, 1),
   (4, 6, 0, 1), (3, 4, 0, 1), (3, 5, 0, 1), (3, 6, 0, 1), (4, 0, 1, 2), (3, 1, 1, 0), (4, 0, 0, 3), (4, 0, 2, 0), (4, 1, 0, 3), (3, 0, 2, 0),
   (4, 2, 0, 3), (4, 3, 0, 3), (4, 4, 0, 3), (4, 5, 0, 3), (2, 0, 2, 0), (4, 6, 0, 3), (4, 1, 2, 0), (4, 1, 1, 2), (3, 1, 2, 0)),
  (), ((3, 0, 2, 1), (4, 0, 1, 1), (4, 0, 2, 2), (4, 0, 2, 1), (4, 1, 1, 1), (2, 1, 2, 0)), (), ((3, 2, 1, 0), (4, 1, 2, 2)),
  ((4, 2, 1, 1), (3, 0, 1, 1), (3, 1, 1, 1), (4, 0, 2, 3), (4, 1, 2, 1)),
  ((3, 1, 2, 1), (4, 2, 1, 2), (4, 0, 3, 0), (4, 0, 1, 3), (3, 2, 1, 1), (4, 1, 1, 3), (3, 0, 3, 0), (4, 1, 3, 0), (4, 1, 2, 3), (2, 1, 3, 0),
   (4, 2, 1, 3), (3, 1, 3, 0), (4, 0, 3, 2), (4, 0, 3, 1), (3, 0, 3, 1)),
  ((4, 1, 3, 1), (3, 1, 3, 1)), ((4, 1, 3, 2),), (), (), (), ((4, 0, 3, 3),), ((4, 1, 3, 3),), (), ()),
 (((1, 0, 1, 0), (2, 0, 1, 0), (2, 1, 1, 0), (0, 0, 1, 0)),
  ((1, 1, 1, 0), (2, 2, 1, 0), (0, 1, 1, 0), (3, 0, 1, 0), (4, 0, 0, 0), (4, 0, 1, 1), (1, 2, 1, 0), (0, 0, 0, 0), (3, 0, 0, 0), (4, 1, 0, 0),
   (4, 1, 1, 1), (3, 1, 0, 0), (0, 1, 0, 0), (3, 1, 1, 0), (4, 0, 2, 0), (4, 2, 0, 0), (4, 2, 1, 1), (1, 0, 2, 0), (0, 2, 0, 0), (3, 2, 0, 0),
   (4, 3, 0, 0), (2, 3, 0, 0), (4, 0, 1, 2), (0, 3, 0, 0), (4, 4, 0, 0), (4, 0, 0, 2), (2, 4, 0, 0), (3, 3, 0, 0), (4, 1, 0, 2), (0, 4, 0, 0),
   (4, 5, 0, 0), (2, 5, 0, 0), (3, 4, 0, 0), (0, 5, 0, 0), (1, 1, 2, 0), (4, 6, 0, 0), (0, 6, 0, 0), (4, 2, 0, 2), (4, 1, 1, 2), (4, 3, 0, 1),
   (2, 6, 0, 0), (4, 4, 0, 1), (0, 0, 0, 1), (4, 0, 0, 1), (4, 3, 0, 2), (3, 5, 0, 0), (4, 5, 0, 1), (4, 1, 0, 1), (0, 1, 0, 1), (4, 4, 0, 2),
   (3, 6, 0, 0), (3, 3, 0, 1), (3, 4, 0, 1), (1, 0, 1, 1), (0, 2, 0, 1), (4, 2, 0, 1), (4, 0, 3, 0), (4, 6, 0, 1), (4, 5, 0, 2), (3, 0, 0, 1),
   (3, 5, 0, 1), (3, 1, 0, 1), (3, 2, 0, 1), (4, 6, 0, 2), (0, 2, 1, 0), (1, 1, 1, 1), (4, 3, 0, 3), (3, 6, 0, 1), (4, 4, 0, 3), (2, 1, 3, 0),
   (4, 1, 3, 0), (4, 1, 2, 0), (4, 0, 0, 3), (0, 0, 1, 1), (4, 5, 0, 3), (2, 0, 2, 0), (1, 2, 1, 1), (4, 1, 0, 3), (4, 2, 0, 3), (2, 1, 2, 0),
   (4, 6, 0, 3), (0, 1, 1, 1), (1, 0, 3, 0), (4, 1, 3, 1), (3, 0, 2, 0)),
  ((4, 0, 3, 1), (0, 2, 1, 1), (4, 0, 2, 1)), ((3, 1, 2, 0), (4, 1, 2, 1), (1, 1, 3, 0)), (), ((3, 0, 2, 1), (4, 0, 2, 2)),
  ((1, 0, 3, 1), (3, 1, 2, 1), (4, 1, 2, 2)),
  ((3, 2, 1, 0), (4, 0, 2, 3), (3, 0, 1, 1), (3, 1, 1, 1), (4, 1, 2, 3), (3, 2, 1, 1), (4, 2, 1, 2), (3, 0, 3, 0), (4, 0, 1, 3), (4, 1, 1, 3),
   (3, 1, 3, 0), (4, 2, 1, 3), (3, 1, 3, 1), (3, 0, 3, 1), (4, 0, 3, 2)),
  ((4, 1, 3, 2),), (), ((4, 1, 3, 3),), (), (), (), ((4, 0, 3, 3),), (), ()),
 (((0, 0, 2, 0), (1, 0, 2, 0), (3, 0, 2, 0)),
  ((3, 1, 2, 0), (0, 1, 2, 0), (1, 1, 2, 0), (2, 0, 2, 0), (4, 0, 2, 2), (2, 1, 2, 0), (4, 0, 1, 0), (0, 0, 1, 0), (4, 1, 2, 2), (4, 0, 3, 0),
   (3, 0, 3, 0), (4, 1, 1, 0), (1, 0, 3, 0), (4, 0, 2, 1), (4, 0, 0, 0), (0, 0, 0, 0), (3, 0, 0, 0), (4, 1, 3, 0), (0, 1, 0, 0), (3, 1, 0, 0),
   (4, 1, 2, 1), (4, 1, 0, 0), (3, 1, 3, 0), (4, 2, 0, 0), (0, 2, 0, 0), (1, 1, 3, 0), (3, 2, 0, 0), (0, 3, 0, 0), (4, 3, 0, 0), (3, 3, 0, 0),
   (4, 0, 3, 2), (4, 4, 0, 0), (3, 4, 0, 0), (0, 4, 0, 0), (4, 0, 0, 2), (3, 5, 0, 0), (4, 5, 0, 0), (0, 5, 0, 0), (3, 0, 3, 1), (4, 0, 3, 1),
   (4, 1, 0, 2), (0, 6, 0, 0), (4, 1, 3, 2), (4, 6, 0, 0), (1, 0, 3, 1), (4, 2, 0, 2), (0, 0, 0, 1), (4, 0, 0, 1), (3, 6, 0, 0), (4, 3, 0, 2),
   (4, 4, 0, 2), (3, 0, 0, 1), (0, 1, 0, 1), (4, 1, 0, 1), (3, 1, 0, 1), (4, 5, 0, 2), (2, 3, 0, 0), (4, 2, 0, 1), (0, 2, 0, 1), (3, 2, 0, 1),
   (2, 4, 0, 0), (0, 1, 1, 0), (4, 0, 3, 3), (2, 5, 0, 0), (4, 6, 0, 2), (2, 6, 0, 0), (3, 0, 2, 1), (4, 0, 0, 3), (4, 2, 1, 0), (4, 1, 0, 3),
   (0, 2, 1, 0), (4, 3, 0, 1), (3, 3, 0, 1), (4, 2, 0, 3), (4, 4, 0, 1), (3, 4, 0, 1), (4, 5, 0, 1), (3, 5, 0, 1), (4, 0, 1, 1), (3, 6, 0, 1),
   (4, 6, 0, 1), (3, 1, 2, 1), (0, 0, 1, 1), (4, 1, 1, 1), (4, 0, 2, 3), (4, 3, 0, 3), (3, 0, 1, 0), (4, 4, 0, 3), (0, 1, 1, 1), (4, 5, 0, 3),
   (3, 1, 1, 0), (4, 6, 0, 3), (4, 2, 1, 1), (3, 2, 1, 0), (0, 2, 1, 1), (4, 1, 2, 3)),
  ((3, 0, 1, 1),), ((4, 0, 1, 2), (4, 1, 1, 2), (3, 1, 1, 1), (4, 2, 1, 2), (3, 2, 1, 1)), (), ((4, 0, 1, 3), (2, 1, 3, 0)),
  ((4, 1, 1, 3), (4, 2, 1, 3)), ((3, 1, 3, 1), (4, 1, 3, 1)), (), (), (), ((4, 1, 3, 3),), (), (), (), (), ()),
 (((2, 0, 3, 0), (1, 0, 3, 0)),
  ((2, 1, 3, 0), (3, 0, 3, 0), (1, 1, 3, 0), (4, 0, 3, 1), (3, 1, 3, 0), (4, 0, 2, 0), (4, 1, 3, 1), (3, 0, 2, 0), (1, 0, 3, 1), (2, 0, 2, 0),
   (4, 0, 3, 2), (4, 1, 2, 0), (4, 1, 3, 2), (3, 1, 2, 0), (4, 0, 2, 2), (4, 0, 1, 0), (3, 0, 1, 0), (4, 0, 0, 0), (3, 0, 0, 0), (4, 0, 2, 1),
   (3, 0, 2, 1), (4, 1, 0, 0), (4, 1, 2, 2), (4, 2, 0, 0), (3, 1, 0, 0), (3, 2, 0, 0), (4, 0, 1, 2), (4, 3, 0, 0), (2, 3, 0, 0), (4, 0, 0, 2),
   (4, 4, 0, 0), (2, 4, 0, 0), (3, 3, 0, 0), (4, 5, 0, 0), (2, 5, 0, 0), (3, 4, 0, 0), (4, 0, 2, 3), (4, 6, 0, 0), (4, 1, 0, 2), (2, 6, 0, 0),
   (3, 5, 0, 0), (4, 2, 0, 2), (3, 6, 0, 0), (4, 0, 0, 1), (4, 3, 0, 1), (3, 0, 0, 1), (4, 4, 0, 1), (3, 3, 0, 1), (4, 1, 0, 1), (4, 3, 0, 2),
   (4, 5, 0, 1), (3, 4, 0, 1), (4, 4, 0, 2), (3, 1, 0, 1), (4, 2, 0, 1), (4, 6, 0, 1), (3, 5, 0, 1), (4, 5, 0, 2), (3, 2, 0, 1), (3, 6, 0, 1),
   (4, 6, 0, 2), (2, 1, 2, 0), (4, 0, 0, 3), (4, 1, 1, 0), (4, 3, 0, 3), (4, 4, 0, 3), (4, 1, 0, 3), (3, 1, 1, 0), (4, 5, 0, 3), (4, 2, 0, 3),
   (4, 2, 1, 0), (3, 2, 1, 0), (4, 6, 0, 3), (3, 0, 3, 1), (4, 1, 2, 1), (4, 0, 1, 1)),
  (), ((3, 0, 1, 1), (3, 1, 1, 1), (4, 1, 1, 2), (4, 2, 1, 2), (4, 1, 1, 1)), (),
  ((3, 2, 1, 1), (4, 2, 1, 1), (4, 0, 3, 3), (4, 0, 1, 3), (3, 1, 2, 1)), ((4, 1, 1, 3), (3, 1, 3, 1)), ((4, 2, 1, 3), (4, 1, 2, 3), (4, 1, 3, 3)),
  (), (), (), (), (), (), (), (), ()))
SENDS_BACK = (((), (), (), ((1, 0, 3, 2),), ((1, 0, 3, 3),), (), (), ((1, 1, 3, 2),), ((3, 0, 3, 0), (1, 1, 3, 3)), (), ((1, 0, 1, 2), (3, 0, 3, 1)),
  ((1, 0, 1, 3),), ((1, 1, 1, 2), (1, 1, 1, 3), (1, 2, 1, 2), (3, 1, 3, 0), (1, 2, 1, 3)), ((1, 0, 2, 2),),
  ((3, 1, 3, 1), (1, 0, 2, 3), (1, 1, 2, 2)), (), (), (), ((5, 0, 0, 0), (1, 1, 2, 3)),
  ((1, 2, 2, 2), (3, 0, 1, 0), (2, 0, 2, 1), (1, 2, 2, 3), (2, 1, 2, 1), (1, 0, 0, 2), (3, 0, 1, 1), (1, 0, 0, 3), (1, 1, 0, 2), (1, 1, 0, 3),
   (2, 2, 2, 1), (1, 2, 0, 2), (1, 2, 0, 3), (1, 3, 0, 2), (5, 1, 0, 0), (3, 0, 2, 0), (1, 3, 0, 3), (1, 4, 0, 2), (1, 4, 0, 3), (1, 5, 0, 2),
   (1, 5, 0, 3), (3, 1, 2, 0), (1, 6, 0, 2), (1, 6, 0, 3), (2, 1, 1, 1), (2, 3, 0, 1), (3, 2, 2, 0), (2, 2, 1, 1), (2, 4, 0, 1), (5, 2, 0, 0),
   (2, 5, 0, 1), (2, 0, 0, 1), (2, 6, 0, 1), (3, 1, 1, 0), (3, 2, 1, 0), (2, 1, 0, 1), (4, 0, 0, 0), (2, 2, 0, 1), (4, 1, 0, 0), (4, 3, 0, 0),
   (4, 4, 0, 0), (4, 2, 0, 0), (4, 5, 0, 0), (4, 6, 0, 0))),
 ((), (), (), ((1, 0, 3, 2),), ((1, 0, 3, 3),), (), (), ((1, 1, 3, 2),), ((1, 1, 3, 3),), (), ((1, 0, 2, 2), (1, 0, 2, 3)),
  ((1, 1, 2, 2), (1, 1, 2, 3)), ((3, 0, 3, 0), (2, 0, 2, 1), (1, 2, 2, 2)), ((2, 1, 2, 1),), ((3, 0, 3, 1), (1, 2, 2, 3)), (), (), (),
  ((5, 0, 0, 0), (1, 0, 1, 2)),
  ((1, 0, 0, 2), (3, 1, 3, 0), (1, 0, 0, 3), (2, 2, 2, 1), (1, 1, 0, 2), (1, 1, 0, 3), (1, 2, 0, 2), (3, 1, 3, 1), (1, 2, 0, 3), (1, 3, 0, 2),
   (1, 3, 0, 3), (1, 4, 0, 2), (1, 4, 0, 3), (1, 5, 0, 2), (1, 5, 0, 3), (5, 1, 0, 0), (1, 6, 0, 2), (1, 6, 0, 3), (1, 0, 1, 3), (2, 3, 0, 1),
   (2, 4, 0, 1), (2, 5, 0, 1), (3, 0, 0, 0), (2, 6, 0, 1), (1, 1, 1, 2), (3, 0, 0, 1), (1, 1, 1, 3), (1, 2, 1, 2), (3, 1, 0, 0), (2, 0, 1, 1),
   (3, 0, 2, 0), (5, 2, 0, 0), (3, 1, 0, 1), (3, 2, 0, 0), (1, 2, 1, 3), (3, 1, 2, 0), (3, 2, 0, 1), (2, 1, 1, 1), (3, 3, 0, 0), (3, 4, 0, 0),
   (3, 2, 2, 0), (4, 0, 1, 0), (3, 5, 0, 0), (2, 2, 1, 1), (3, 6, 0, 0), (4, 1, 1, 0), (4, 2, 1, 0))),
 ((), (), (), ((1, 0, 3, 2),), ((1, 0, 3, 3),), (), (), ((1, 1, 3, 2),), ((1, 1, 3, 3),), (), ((1, 0, 1, 2),), ((1, 0, 1, 3),),
  ((1, 1, 1, 2), (1, 1, 1, 3), (1, 2, 1, 2)), ((1, 2, 1, 3), (1, 0, 2, 2)), ((1, 0, 2, 3),), (), (), (), ((5, 0, 0, 0), (1, 1, 2, 2)),
  ((1, 0, 0, 2), (1, 0, 0, 3), (3, 0, 3, 0), (1, 1, 0, 2), (3, 0, 1, 0), (1, 1, 0, 3), (1, 2, 0, 2), (1, 2, 0, 3), (1, 3, 0, 2), (3, 0, 3, 1),
   (1, 3, 0, 3), (1, 4, 0, 2), (1, 4, 0, 3), (1, 5, 0, 2), (1, 5, 0, 3), (5, 1, 0, 0), (3, 0, 1, 1), (1, 6, 0, 2), (1, 6, 0, 3), (1, 1, 2, 3),
   (3, 1, 3, 0), (1, 2, 2, 2), (3, 0, 0, 0), (1, 2, 2, 3), (3, 0, 0, 1), (2, 0, 2, 1), (3, 1, 3, 1), (3, 1, 0, 0), (2, 1, 2, 1), (3, 1, 0, 1),
   (2, 3, 0, 1), (2, 4, 0, 1), (3, 2, 0, 0), (5, 2, 0, 0), (2, 2, 2, 1), (3, 2, 0, 1), (2, 5, 0, 1), (2, 6, 0, 1), (2, 1, 1, 1), (3, 3, 0, 0),
   (2, 2, 1, 1), (3, 4, 0, 0), (3, 5, 0, 0), (3, 6, 0, 0), (3, 1, 1, 0), (3, 2, 1, 0), (4, 0, 2, 0), (4, 1, 2, 0), (4, 2, 2, 0))),
 ((), (), (), ((1, 0, 3, 2),), ((1, 0, 3, 3),), (), (), ((1, 1, 3, 2),), ((1, 0, 2, 2),), ((1, 0, 2, 3),), ((1, 0, 1, 2),), ((1, 0, 1, 3),),
  ((3, 0, 1, 0), (1, 1, 1, 2), (1, 1, 1, 3), (1, 2, 1, 2)), ((1, 2, 1, 3), (1, 1, 2, 2)), ((3, 0, 1, 1), (2, 1, 1, 1), (1, 1, 2, 3)), (), (),
  ((1, 2, 2, 2),), ((5, 0, 0, 0),),
  ((1, 0, 0, 2), (1, 0, 0, 3), (1, 1, 0, 2), (1, 1, 0, 3), (3, 1, 1, 0), (1, 2, 0, 2), (1, 2, 0, 3), (1, 3, 0, 2), (3, 0, 0, 0), (1, 3, 0, 3),
   (3, 0, 0, 1), (1, 4, 0, 2), (1, 4, 0, 3), (3, 1, 0, 0), (5, 1, 0, 0), (1, 5, 0, 2), (1, 5, 0, 3), (1, 6, 0, 2), (3, 1, 0, 1), (1, 6, 0, 3),
   (2, 2, 1, 1), (3, 2, 0, 0), (2, 3, 0, 1), (3, 2, 0, 1), (2, 4, 0, 1), (1, 2, 2, 3), (2, 5, 0, 1), (2, 6, 0, 1), (3, 2, 1, 0), (2, 0, 2, 1),
   (5, 2, 0, 0), (3, 3, 0, 0), (2, 1, 2, 1), (3, 4, 0, 0), (2, 2, 2, 1), (3, 5, 0, 0), (3, 6, 0, 0), (1, 1, 3, 3), (3, 0, 2, 0), (2, 0, 3, 1),
   (3, 1, 2, 0), (3, 2, 2, 0), (2, 1, 3, 1), (4, 0, 3, 0), (4, 1, 3, 0))))

def unpack(flat_values):
    shapes = [(D, 3 * D), (D, D), (D, FF), (FF, D), (D, FINAL), (G * CD, V), (G * CD, FINAL)]
    pieces = []
    offset = 0
    for height, width in shapes:
        pieces.append(flat_values[offset : offset + height * width].reshape(height, width))
        offset = offset + height * width
    return pieces


def split_vectors(vector_all):
    lengths = [D, D, D, D, D, FF, D, D, D, FINAL, FINAL]
    pieces = []
    offset = 0
    for length in lengths:
        pieces.append(vector_all[offset : offset + length])
        offset = offset + length
    return pieces


def layer_norm(values, scale_gain, shift_bias):
    centered = values - jnp.mean(values, axis=-1, keepdims=True)
    variance = jnp.mean(centered * centered, axis=-1, keepdims=True)
    return centered * lax.rsqrt(variance + eps_norm) * scale_gain + shift_bias


def contrast_dense(chosen, targets, distract, weight):
    hi = dict(precision=lax.Precision.HIGHEST)
    frames = jnp.arange(MASKED, dtype=jnp.int32)
    allowed = jnp.any(distract[:, :, None] == frames, axis=1) | (frames[:, None] == frames)

    def agreement(chosen, targets):
        left = chosen * lax.rsqrt(jnp.sum(chosen * chosen, axis=-1, keepdims=True) + eps_cos)
        right = targets * lax.rsqrt(jnp.sum(targets * targets, axis=-1, keepdims=True) + eps_cos)
        return jnp.einsum("by,oy->bo", left, right, **hi) / softness_divisor

    similar, back = jax.vjp(agreement, chosen, targets)
    same = frames[:, None] == frames
    positive = jnp.sum(jnp.where(same, similar, 0.0), axis=1)
    top = jnp.max(jnp.where(allowed, similar, -jnp.inf), axis=1)
    parts = jnp.where(allowed, jnp.exp(similar - top[:, None]), 0.0)
    total = jnp.sum(parts, axis=1)
    loss = jnp.sum(top + jnp.log(total) - positive)
    d_similar = weight * (parts / total[:, None] - same.astype(jnp.float32))
    return (loss,) + back(d_similar)


def adamw_update(master, first_moment, second, gradient, step_rate):
    first_new = beta_one * first_moment + (1.0 - beta_one) * gradient
    second_new = beta_two * second + (1.0 - beta_two) * gradient * gradient
    first_hat = first_new / (1.0 - beta_one**STEP)
    second_hat = second_new / (1.0 - beta_two**STEP)
    master_new = master * (1.0 - step_rate * decay_rate) - step_rate * first_hat / (
        jnp.sqrt(second_hat) + adam_eps
    )
    return (master_new, first_new, second_new)


def column_sum(values):
    return jnp.sum(values.astype(jnp.float32), axis=tuple(range(values.ndim - 1)))


def finish(total_masked, square_sum, vector_sum, loss_sum, grad_shard, output, input_grad, params, moment_one, moment_two, vectors, vector_one, vector_two):
    grad_norm = jnp.sqrt(square_sum + jnp.sum(vector_sum * vector_sum))
    factor = jnp.minimum(1.0, clip_level / (grad_norm + 1e-06))
    refreshed_weights, new_one, new_two = adamw_update(params, moment_one, moment_two, grad_shard * factor, rate_matrix)
    new_vectors, new_vector_first, new_vector_second = adamw_update(vectors, vector_one, vector_two, vector_sum * factor, rate_vector)
    return (
        loss_sum / total_masked,
        grad_norm,
        output,
        input_grad,
        refreshed_weights,
        refreshed_weights.astype(bf16),
        new_one,
        new_two,
        new_vectors,
        new_vector_first,
        new_vector_second,
    )


def by_collectives(
    layer_input,
    mask_index,
    distract,
    code_choice,
    params,
    moment_one,
    moment_two,
    vectors,
    vector_one,
    vector_two,
):
    bf16 = jnp.bfloat16
    f32 = jnp.float32
    count_utts = layer_input.shape[0]
    total_masked = count_utts * lax.axis_size(("dp", "fsdp")) * MASKED
    token_rows = count_utts * LEN
    gathered = lax.all_gather(params.astype(bf16), ("dp", "fsdp"), axis=0, tiled=True)
    qkv_weight, out_weight, up_weight, down_weight, proj_weight, codebook, code_weight = unpack(
        gathered
    )
    (
        bias_query,
        bias_value,
        bias_out,
        gain_one,
        shift_one,
        bias_up,
        bias_down,
        gain_two,
        shift_two,
        bias_proj,
        bias_code,
    ) = split_vectors(vectors)
    inputs = layer_input.reshape(token_rows, D)
    projected = jnp.dot(inputs, qkv_weight, preferred_element_type=f32)
    query_heads = (projected[:, :D] + bias_query).astype(bf16).reshape(count_utts, LEN, H, HD)
    key_heads = projected[:, D : 2 * D].astype(bf16).reshape(count_utts, LEN, H, HD)
    value_heads = (projected[:, 2 * D :] + bias_value).astype(bf16).reshape(count_utts, LEN, H, HD)
    scores = (
        jnp.einsum("blhe,bmhe->bhlm", query_heads, key_heads, preferred_element_type=f32) * 0.125
    )
    attn_probs = jax.nn.softmax(scores, axis=-1)
    probs_low = attn_probs.astype(bf16)
    attended = jnp.einsum("bhlm,bmhe->blhe", probs_low, value_heads, preferred_element_type=f32)
    attended = attended.astype(bf16).reshape(token_rows, D)
    residual_one = (
        inputs.astype(f32) + jnp.dot(attended, out_weight, preferred_element_type=f32) + bias_out
    )
    normed, back_one = jax.vjp(layer_norm, residual_one, gain_one, shift_one)
    normed_low = normed.astype(bf16)
    hidden = jnp.dot(normed_low, up_weight, preferred_element_type=f32) + bias_up
    active, gelu_back = jax.vjp(functools.partial(jax.nn.gelu, approximate=False), hidden)
    active_low = active.astype(bf16)
    residual_two = normed + jnp.dot(active_low, down_weight, preferred_element_type=f32) + bias_down
    output, back_two = jax.vjp(layer_norm, residual_two, gain_two, shift_two)
    output_low = output.astype(bf16)
    place = (mask_index[0][:, None] == jnp.arange(LEN, dtype=jnp.int32)).astype(bf16)
    picked = jnp.dot(place, output_low, preferred_element_type=f32).astype(bf16)
    chosen = jnp.dot(picked, proj_weight, preferred_element_type=f32) + bias_proj
    choose = (code_choice[..., None] == jnp.arange(V, dtype=jnp.int32)).astype(bf16)
    code_vectors = jnp.einsum(
        "bmgv,gcv->bmgc", choose, codebook.reshape(G, CD, V), preferred_element_type=f32
    )
    code_vectors = code_vectors.astype(bf16).reshape(count_utts, MASKED, G * CD)
    targets = (
        jnp.einsum("bmc,cf->bmf", code_vectors, code_weight, preferred_element_type=f32) + bias_code
    )
    loss_local, d_chosen, d_targets = contrast_dense(chosen, targets[0], distract[0], 1.0 / total_masked)
    d_targets = d_targets[None]
    d_targets_low = d_targets.astype(bf16)
    quantized_offset_slope = column_sum(d_targets_low)
    d_code_weight = jnp.einsum(
        "bmc,bmf->cf", code_vectors, d_targets_low, preferred_element_type=f32
    )
    d_code_vectors = jnp.einsum(
        "bmf,cf->bmc", d_targets_low, code_weight, preferred_element_type=f32
    )
    d_codebook = jnp.einsum(
        "bmgc,bmgv->gcv",
        d_code_vectors.reshape(count_utts, MASKED, G, CD),
        choose.astype(f32),
        precision=lax.Precision.HIGHEST,
    ).reshape(G * CD, V)
    d_chosen_low = d_chosen.astype(bf16)
    d_bias_proj = column_sum(d_chosen_low)
    d_proj_weight = jnp.einsum("td,tf->df", picked, d_chosen_low, preferred_element_type=f32)
    d_context_low = jnp.einsum("mt,mf->tf", place, d_chosen_low, preferred_element_type=f32).astype(bf16)
    result_sensitivity = jnp.einsum(
        "tf,df->td", d_context_low, proj_weight, preferred_element_type=f32
    )
    d_residual_two, d_gain_two, d_shift_two = back_two(result_sensitivity)
    d_second_low = d_residual_two.astype(bf16)
    d_bias_down = column_sum(d_second_low)
    d_down_weight = jnp.einsum("th,td->hd", active_low, d_second_low, preferred_element_type=f32)
    d_active = jnp.einsum("td,hd->th", d_second_low, down_weight, preferred_element_type=f32)
    (d_hidden,) = gelu_back(d_active)
    d_hidden_low = d_hidden.astype(bf16)
    d_bias_up = column_sum(d_hidden_low)
    d_up_weight = jnp.einsum("td,th->dh", normed_low, d_hidden_low, preferred_element_type=f32)
    d_normed = d_residual_two + jnp.einsum(
        "th,dh->td", d_hidden_low, up_weight, preferred_element_type=f32
    )
    d_residual_one, d_gain_one, d_shift_one = back_one(d_normed)
    d_branch_low = d_residual_one.astype(bf16)
    d_bias_out = column_sum(d_branch_low)
    d_out_weight = jnp.einsum("td,te->de", attended, d_branch_low, preferred_element_type=f32)
    d_attended = jnp.einsum("te,de->td", d_branch_low, out_weight, preferred_element_type=f32)
    d_attended = d_attended.astype(bf16).reshape(count_utts, LEN, H, HD)
    d_value = jnp.einsum("bhlm,blhe->bmhe", probs_low, d_attended, preferred_element_type=f32)
    d_probs = jnp.einsum("blhe,bmhe->bhlm", d_attended, value_heads, preferred_element_type=f32)
    d_scores = (
        attn_probs * (d_probs - jnp.sum(attn_probs * d_probs, axis=-1, keepdims=True))
    ).astype(bf16)
    d_query = jnp.einsum("bhlm,bmhe->blhe", d_scores, key_heads, preferred_element_type=f32) * 0.125
    d_key = jnp.einsum("bhlm,blhe->bmhe", d_scores, query_heads, preferred_element_type=f32) * 0.125
    d_projected = jnp.concatenate(
        [
            d_query.reshape(token_rows, D),
            d_key.reshape(token_rows, D),
            d_value.reshape(token_rows, D),
        ],
        axis=1,
    ).astype(bf16)
    d_sums = column_sum(d_projected)
    d_qkv_weight = jnp.einsum("td,te->de", inputs, d_projected, preferred_element_type=f32)
    input_grad = d_residual_one + jnp.einsum(
        "te,de->td", d_projected, qkv_weight, preferred_element_type=f32
    )
    flat_grad = jnp.concatenate(
        [
            matrix_grad.reshape(-1)
            for matrix_grad in (
                d_qkv_weight,
                d_out_weight,
                d_up_weight,
                d_down_weight,
                d_proj_weight,
                d_codebook,
                d_code_weight,
            )
        ]
    )
    vector_gradient = jnp.concatenate(
        [
            d_sums[:D],
            d_sums[2 * D :],
            d_bias_out,
            d_gain_one,
            d_shift_one,
            d_bias_up,
            d_bias_down,
            d_gain_two,
            d_shift_two,
            d_bias_proj,
            quantized_offset_slope,
        ]
    )
    vector_sum, loss_sum = lax.psum((vector_gradient, loss_local), ("dp", "fsdp"))
    grad_shard = lax.psum_scatter(flat_grad, ("dp", "fsdp"), scatter_dimension=0, tiled=True)
    square_sum = lax.psum(jnp.sum(grad_shard * grad_shard), ("dp", "fsdp"))
    return finish(
        total_masked, square_sum, vector_sum, loss_sum, grad_shard, output_low.reshape(count_utts, LEN, D),
        input_grad.reshape(count_utts, LEN, D), params, moment_one, moment_two, vectors, vector_one, vector_two,
    )


def by_kernels(layer_input, mask_index, distract, code_choice, params, moment_one, moment_two, vectors, vector_one, vector_two):
    total_masked = layer_input.shape[0] * lax.axis_size(("dp", "fsdp")) * MASKED
    kept, output = forward(PIECES_OUT, SENDS_OUT, 1.0 / total_masked, params, layer_input, mask_index, distract, code_choice, vectors)
    grads, sums, squares, input_grad = backward(PIECES_BACK, SENDS_BACK, vectors, kept, lax.axis_size("fsdp"), params.shape[0] // 128)
    new, low, first, second, new_v, first_v, second_v, loss, norm = update(
        total_masked, grads, params, moment_one, moment_two, sums, vectors, vector_one, vector_two, squares
    )
    return loss, norm, output, input_grad, new, low, first, second, new_v, first_v, second_v


def solution(mesh):
    in_specs = (
        P(("dp", "fsdp"), None, None),
        P(("dp", "fsdp"), None),
        P(("dp", "fsdp"), None, None),
        P(("dp", "fsdp"), None, None),
        P(("dp", "fsdp")),
        P(("dp", "fsdp")),
        P(("dp", "fsdp")),
        P(),
        P(),
        P(),
    )
    out_specs = (
        P(),
        P(),
        P(("dp", "fsdp"), None, None),
        P(("dp", "fsdp"), None, None),
        P(("dp", "fsdp")),
        P(("dp", "fsdp")),
        P(("dp", "fsdp")),
        P(("dp", "fsdp")),
        P(),
        P(),
        P(),
    )
    fits = mesh.shape["dp"] == PLANES and mesh.shape["fsdp"] == 8
    return jax.shard_map(
        by_kernels if fits else by_collectives, mesh=mesh, in_specs=in_specs, out_specs=out_specs, check_vma=False
    )
```
